32 devices in a mesh: groups: 2 (over x), dp: 16 (over z, y, core).
Axes of the slice: x: 2, y: 2, z: 4, core: 2. Of those that a mesh axis runs over, the one named last changes fastest.
Arguments:
- tokens: bfloat16 [4096, 8192], P(('groups', 'dp')), parts along dimension 0, may hold values from -6 to 6
- output_gradient: bfloat16 [4096, 1024], P(('groups', 'dp')), parts along dimension 0, may hold values from -6 to 6
- value_weight: bfloat16 [1024, 8192], P(None, 'dp'), may hold values from -0.1875 to 0.1875
- down_maps: bfloat16 [64, 128, 8192], P(None, None, 'dp'), may hold values from -0.1875 to 0.1875
- up_maps: bfloat16 [64, 1024, 128], P(None, 'dp'), may hold values from -0.1875 to 0.1875
- adapter_per_block: int32 [32], P('groups'), parts along dimension 0, may hold values from 0 to 63
- ranks: int32 [64], replicated, may hold values from 16 to 128
Outputs:
- input_grad: bfloat16 [4096, 8192], P(('groups', 'dp')), parts along dimension 0
- down_gradient: bfloat16 [128, 128, 8192], P('groups', None, 'dp'), parts along dimension 0
- up_gradient: bfloat16 [128, 1024, 128], P('groups', 'dp'), parts along dimension 0
The draws below stay inside these ranges and needn't reach their ends.
There are 2 independent parts, one for each index of `groups`. The reference program is written for one: setup_inputs(seed, part) draws one part's arguments, and reference() takes and returns one part's arrays. A program takes and returns all parts, laid end to end along the dimension named above; an argument that names none is the same for every part. Nothing has to cross between parts.
All inputs are finite; a program needn't handle non-finite values.
Results may differ from the reference program's by a relative error of at most 0.0049.
Values may be sent and summed in bfloat16 or wider, within the bound.
No kernel may reach another device: no remote copies, remote signals or barrier semaphores. Data moves between devices by JAX's collectives and lax.ppermute only.
A program may use at most 128 MiB of HBM per device.

```python
import math
import jax
import jax.numpy as jnp
import numpy as np
from jax import lax

MODEL_WIDTH = 8192
VALUE_WIDTH = 1024
MAX_RANK = 128
ADAPTER_POOL = 64
BLOCK = 128
TOKENS = 2048
BLOCKS = 16


def touch_ends(result, rng, low, high):
    longest = result.shape.index(max(result.shape))
    spots = []
    for shift in (0, 1):
        where = [jax.random.randint(jax.random.fold_in(rng, axis), (), 0, length) for axis, length in enumerate(result.shape)]
        where[longest] = (where[longest] + shift) % result.shape[longest]
        spots.append(tuple(where))
    return result.at[spots[0]].set(low).at[spots[1]].set(high)


def shard_levels(stream_key, extent, pieces, least, top_value):
    def one(axis_at, blocks):
        heights = jax.random.uniform(jax.random.fold_in(jax.random.fold_in(stream_key, 6), axis_at), (blocks,), jnp.float32, least / len(pieces), top_value / len(pieces))
        return jnp.repeat(jnp.exp(heights), extent[axis_at] // blocks).reshape((-1,) + (1,) * (len(extent) - axis_at - 1))

    gain = one(*pieces[0])
    for cut in pieces[1:]:
        gain = gain * one(*cut)
    return gain


def cumulative_ranks(number_of, slope):
    portions = [(1 << 20) // math.isqrt(rank ** slope) + 1 for rank in range(1, number_of + 1)]
    deviation = 1 + sum(portions) // (1 << 30)
    return np.cumsum(np.array([max(1, weight // deviation) for weight in portions]))


def skewed_ids(own_key, dims, amount, lean):
    table = cumulative_ranks(amount, lean)
    ticket = jax.random.randint(jax.random.fold_in(own_key, 1), dims, 0, int(table[amount - 1]))
    standing = jnp.searchsorted(jnp.asarray(table, jnp.int32), ticket, side="right")
    return jax.random.permutation(jax.random.fold_in(own_key, 2), amount)[standing].astype(jnp.int32)


def centred(own_key, shape, spread, limit, shards=(), held_as=jnp.bfloat16):
    entries = spread * jax.random.normal(own_key, shape, jnp.float32)
    if shards:
        entries = entries * shard_levels(own_key, shape, shards, -0.22, 0.18)
    return jnp.clip(entries, -limit, limit).astype(held_as)


def setup_inputs(seed: int = 0, part: int = 0) -> dict:
    key_of = jax.random.split(jax.random.key(seed), 8)
    part_keys = jax.random.split(jax.random.fold_in(key_of[7], part), 8)
    return {
        "tokens": centred(part_keys[0], (TOKENS, MODEL_WIDTH), 1.0, 6.0, ((0, 16),)),
        "output_gradient": centred(part_keys[1], (TOKENS, VALUE_WIDTH), 1.0, 6.0, ((0, 16),)),
        "value_weight": centred(key_of[2], (VALUE_WIDTH, MODEL_WIDTH), VALUE_WIDTH ** -0.5, 0.1875, ((1, 16),)),
        "down_maps": centred(key_of[3], (ADAPTER_POOL, MAX_RANK, MODEL_WIDTH), VALUE_WIDTH ** -0.5, 0.1875, ((2, 16),)),
        "up_maps": centred(key_of[4], (ADAPTER_POOL, VALUE_WIDTH, MAX_RANK), VALUE_WIDTH ** -0.5, 0.1875, ((1, 16),)),
        "adapter_per_block": touch_ends(skewed_ids(part_keys[5], (BLOCKS,), ADAPTER_POOL, 2), jax.random.fold_in(part_keys[5], 3), 0, ADAPTER_POOL - 1).astype(jnp.int32),
        "ranks": touch_ends(jax.random.randint(key_of[6], (ADAPTER_POOL,), MAX_RANK // 8, MAX_RANK + 1), jax.random.fold_in(key_of[6], 1), MAX_RANK // 8, MAX_RANK).astype(jnp.int32),
    }


adapter_alpha = 32.0


def reference(tokens, output_gradient, value_weight, down_maps, up_maps, adapter_per_block, ranks):
    alive_mask = (jnp.arange(MAX_RANK, dtype=jnp.int32)[None, :] < ranks[:, None]).astype(jnp.float32)
    adapter_scale = adapter_alpha / ranks.astype(jnp.float32)
    token_block_rows = tokens.reshape(BLOCKS, BLOCK, MODEL_WIDTH)
    grad_blocks = output_gradient.reshape(BLOCKS, BLOCK, VALUE_WIDTH)

    def per_block(totals, block_item):
        total_a, total_b = totals
        x_block, g_block, adapter_index = block_item
        down_rows = down_maps[adapter_index]
        up_rows = up_maps[adapter_index]
        rank_mask = alive_mask[adapter_index][None, :]
        factor = adapter_scale[adapter_index]
        hidden = jnp.dot(x_block, down_rows.T, preferred_element_type=jnp.float32)
        back = jnp.dot(g_block, up_rows, preferred_element_type=jnp.float32)
        hidden_low = (hidden * rank_mask).astype(jnp.bfloat16)
        rank_backward = (factor * back * rank_mask).astype(jnp.bfloat16)
        down_piece = jnp.dot(rank_backward.T, x_block, preferred_element_type=jnp.float32)
        part_b = factor * jnp.dot(g_block.T, hidden_low, preferred_element_type=jnp.float32)
        total_a = total_a.at[adapter_index].add(down_piece)
        total_b = total_b.at[adapter_index].add(part_b)
        block_grad = jnp.dot(g_block, value_weight, preferred_element_type=jnp.float32) + jnp.dot(rank_backward, down_rows, preferred_element_type=jnp.float32)
        return (total_a, total_b), block_grad.astype(jnp.bfloat16)

    start_totals = (jnp.zeros((ADAPTER_POOL, MAX_RANK, MODEL_WIDTH), jnp.float32), jnp.zeros((ADAPTER_POOL, VALUE_WIDTH, MAX_RANK), jnp.float32))
    (total_a, total_b), grads = lax.scan(per_block, start_totals, (token_block_rows, grad_blocks, adapter_per_block))
    return grads.reshape(TOKENS, MODEL_WIDTH), total_a.astype(jnp.bfloat16), total_b.astype(jnp.bfloat16)
```

```python
import functools

import jax
import jax.numpy as jnp
from jax import lax
from jax.experimental import pallas as pl
from jax.experimental.pallas import tpu as pltpu
from jax.sharding import PartitionSpec as P

adapter_alpha = 32.0
vmem_limit = 48 * 1024 * 1024


def group_of(count):
    return 4 if count % 4 == 0 else 1


def gather_up_kernel(adapters, up_maps, out, sems):
    count = out.shape[0]
    copies = [
        pltpu.make_async_copy(up_maps.at[adapters[block]], out.at[block], sems.at[block])
        for block in range(count)
    ]
    for copy in copies:
        copy.start()
    for copy in copies:
        copy.wait()


def gather_up(adapters, up_maps):
    count = adapters.shape[0]
    return pl.pallas_call(
        gather_up_kernel,
        out_shape=jax.ShapeDtypeStruct((count,) + up_maps.shape[1:], up_maps.dtype),
        grid_spec=pltpu.PrefetchScalarGridSpec(
            num_scalar_prefetch=1,
            grid=(),
            in_specs=[pl.BlockSpec(memory_space=pl.ANY)],
            out_specs=pl.BlockSpec(memory_space=pl.ANY),
            scratch_shapes=[pltpu.SemaphoreType.DMA((count,))],
        ),
        name="gather_up",
    )(adapters, up_maps)


def split_kernel(source, out):
    width = out.shape[2]
    for piece in range(out.shape[0]):
        out[piece] = source[:, piece * width : (piece + 1) * width]


def split_columns(source, pieces):
    rows, columns = source.shape
    width = columns // pieces
    step = group_of(pieces)
    return pl.pallas_call(
        split_kernel,
        out_shape=jax.ShapeDtypeStruct((pieces, rows, width), source.dtype),
        grid=(pieces // step,),
        in_specs=[pl.BlockSpec((rows, step * width), lambda i: (0, i))],
        out_specs=pl.BlockSpec((step, rows, width), lambda i: (i, 0, 0)),
        name="split_columns",
    )(source)


def join_kernel(source, out):
    width = source.shape[2]
    for piece in range(source.shape[0]):
        out[:, piece * width : (piece + 1) * width] = source[piece]


def join_columns(source):
    pieces, rows, width = source.shape
    step = group_of(pieces)
    return pl.pallas_call(
        join_kernel,
        out_shape=jax.ShapeDtypeStruct((rows, pieces * width), source.dtype),
        grid=(pieces // step,),
        in_specs=[pl.BlockSpec((step, rows, width), lambda i: (i, 0, 0))],
        out_specs=pl.BlockSpec((rows, step * width), lambda i: (0, i)),
        name="join_columns",
    )(source)


def rank_row(ranks, adapter, extent):
    rank = jnp.full((1, extent), ranks[adapter], jnp.int32)
    alive = (lax.broadcasted_iota(jnp.int32, (1, extent), 1) < rank).astype(jnp.float32)
    return alive, adapter_alpha / rank.astype(jnp.float32)


def back_kernel(adapters, ranks, place, gradient, up, out):
    alive, factor = rank_row(ranks, adapters[place[0]], up.shape[1])
    back = jnp.dot(gradient[...], up[...], preferred_element_type=jnp.float32)
    width = gradient.shape[1]
    out[:, :width] = gradient[...]
    out[:, width:] = (factor * back * alive).astype(out.dtype)


def back_beside_gradient(adapters, ranks, place, gradient, up):
    rows, width = gradient.shape
    return pl.pallas_call(
        back_kernel,
        out_shape=jax.ShapeDtypeStruct((rows, width + up.shape[1]), gradient.dtype),
        grid_spec=pltpu.PrefetchScalarGridSpec(
            num_scalar_prefetch=3,
            grid=(1,),
            in_specs=[
                pl.BlockSpec(gradient.shape, lambda i, *_: (0, 0)),
                pl.BlockSpec(up.shape, lambda i, *_: (0, 0)),
            ],
            out_specs=pl.BlockSpec((rows, width + up.shape[1]), lambda i, *_: (0, 0)),
        ),
        compiler_params=pltpu.CompilerParams(vmem_limit_bytes=vmem_limit),
        name="back_low",
    )(adapters, ranks, place, gradient, up)


def down_specs(step, down_maps):
    def spec(offset):
        return pl.BlockSpec(
            (1,) + down_maps.shape[1:],
            lambda i, adapters: (adapters[i * step + offset], 0, 0),
        )

    return [spec(offset) for offset in range(step)]


def hidden_kernel(adapters, tokens, *refs):
    out = refs[-1]
    for offset in range(tokens.shape[0]):
        out[offset] = lax.dot_general(
            tokens[offset],
            refs[offset][0],
            (((1,), (1,)), ((), ())),
            preferred_element_type=jnp.float32,
        ).astype(out.dtype)


def hidden_parts(adapters, tokens, down_maps):
    count, rows, width = tokens.shape
    step = group_of(count)
    extent = down_maps.shape[1]
    return pl.pallas_call(
        hidden_kernel,
        out_shape=jax.ShapeDtypeStruct((count, rows, extent), jnp.bfloat16),
        grid_spec=pltpu.PrefetchScalarGridSpec(
            num_scalar_prefetch=1,
            grid=(count // step,),
            in_specs=[pl.BlockSpec((step, rows, width), lambda i, _: (i, 0, 0))]
            + down_specs(step, down_maps),
            out_specs=pl.BlockSpec((step, rows, extent), lambda i, _: (i, 0, 0)),
        ),
        compiler_params=pltpu.CompilerParams(vmem_limit_bytes=vmem_limit),
        name="hidden_parts",
    )(adapters, tokens, *([down_maps] * step))


def input_kernel(adapters, gathered, weight, *refs):
    out = refs[-1]
    step, rows, _ = out.shape
    depth = weight.shape[0]
    frozen = jnp.dot(gathered[:, :depth], weight[...], preferred_element_type=jnp.float32)
    for offset in range(step):
        low = gathered[offset * rows : (offset + 1) * rows, depth:]
        adapter = jnp.dot(low, refs[offset][0], preferred_element_type=jnp.float32)
        out[offset] = (frozen[offset * rows : (offset + 1) * rows] + adapter).astype(out.dtype)


def input_slices(adapters, gathered, weight, down_maps):
    count = adapters.shape[0]
    step = group_of(count)
    rows = gathered.shape[0] // count
    width = weight.shape[1]
    return pl.pallas_call(
        input_kernel,
        out_shape=jax.ShapeDtypeStruct((count, rows, width), jnp.bfloat16),
        grid_spec=pltpu.PrefetchScalarGridSpec(
            num_scalar_prefetch=1,
            grid=(count // step,),
            in_specs=[
                pl.BlockSpec((step * rows, gathered.shape[1]), lambda i, _: (i, 0)),
                pl.BlockSpec(weight.shape, lambda i, _: (0, 0)),
            ]
            + down_specs(step, down_maps),
            out_specs=pl.BlockSpec((step, rows, width), lambda i, _: (i, 0, 0)),
        ),
        compiler_params=pltpu.CompilerParams(vmem_limit_bytes=vmem_limit),
        name="input_slices",
    )(adapters, gathered, weight, *([down_maps] * step))


def up_piece_kernel(adapters, ranks, place, parts, gradient, out):
    extent = parts.shape[2]
    alive, factor = rank_row(ranks, adapters[place[0]], extent)
    hidden = parts[0].astype(jnp.float32)
    for part in range(1, parts.shape[0]):
        hidden += parts[part].astype(jnp.float32)
    hidden_low = (hidden * alive).astype(jnp.bfloat16)
    piece = lax.dot_general(
        gradient[...], hidden_low, (((0,), (0,)), ((), ())), preferred_element_type=jnp.float32
    )
    out[...] = (factor * piece).astype(out.dtype)


def up_piece(adapters, ranks, place, parts, gradient):
    width = gradient.shape[1]
    extent = parts.shape[2]
    return pl.pallas_call(
        up_piece_kernel,
        out_shape=jax.ShapeDtypeStruct((width, extent), jnp.bfloat16),
        grid_spec=pltpu.PrefetchScalarGridSpec(
            num_scalar_prefetch=3,
            grid=(1,),
            in_specs=[
                pl.BlockSpec(parts.shape, lambda i, *_: (0, 0, 0)),
                pl.BlockSpec(gradient.shape, lambda i, *_: (0, 0)),
            ],
            out_specs=pl.BlockSpec((width, extent), lambda i, *_: (0, 0)),
        ),
        compiler_params=pltpu.CompilerParams(vmem_limit_bytes=vmem_limit),
        name="up_piece",
    )(adapters, ranks, place, parts, gradient)


def list_members(adapters, head, following):
    def clear(adapter, carry):
        head[adapter] = -1
        return carry

    lax.fori_loop(0, head.shape[0], clear, 0)

    def link(step, carry):
        block = following.shape[0] - 1 - step
        adapter = adapters[block]
        following[block] = head[adapter]
        head[adapter] = block
        return carry

    lax.fori_loop(0, following.shape[0], link, 0)


def sum_members(head, following, total, out, term):
    chunk = out.shape[0]

    def per_adapter(slot, carry):
        first = head[pl.program_id(0) * chunk + slot]

        @pl.when(first < 0)
        def _():
            out[slot] = jnp.zeros(out.shape[1:], out.dtype)

        @pl.when(first >= 0)
        def _():
            total[...] = term(first)

            def more(block):
                total[...] += term(block)
                return following[block]

            lax.while_loop(lambda block: block >= 0, more, following[first])
            out[slot] = total[...].astype(out.dtype)

        return carry

    lax.fori_loop(0, chunk, per_adapter, 0)


def down_gradient_kernel(adapters, gathered, tokens, out, head, following, total):
    rows = tokens.shape[1]

    @pl.when(pl.program_id(0) == 0)
    def _():
        list_members(adapters, head, following)

    def term(block):
        low = gathered[pl.ds(pl.multiple_of(block * rows, rows), rows), :]
        return lax.dot_general(
            low, tokens[block], (((0,), (0,)), ((), ())), preferred_element_type=jnp.float32
        )

    sum_members(head, following, total, out, term)


def down_gradients(adapters, gathered, tokens, num_adapters, extent):
    count, rows, width = tokens.shape
    chunk = 8 if num_adapters % 8 == 0 else 1
    low_at = gathered.shape[1] // extent - 1
    return pl.pallas_call(
        down_gradient_kernel,
        out_shape=jax.ShapeDtypeStruct((num_adapters, extent, width), jnp.bfloat16),
        grid_spec=pltpu.PrefetchScalarGridSpec(
            num_scalar_prefetch=1,
            grid=(num_adapters // chunk,),
            in_specs=[
                pl.BlockSpec((count * rows, extent), lambda i, _: (0, low_at)),
                pl.BlockSpec(tokens.shape, lambda i, _: (0, 0, 0)),
            ],
            out_specs=pl.BlockSpec((chunk, extent, width), lambda i, _: (i, 0, 0)),
            scratch_shapes=[
                pltpu.SMEM((num_adapters,), jnp.int32),
                pltpu.SMEM((count,), jnp.int32),
                pltpu.VMEM((extent, width), jnp.float32),
            ],
        ),
        compiler_params=pltpu.CompilerParams(vmem_limit_bytes=vmem_limit),
        name="down_gradients",
    )(adapters, gathered, tokens)


def up_gradient_kernel(adapters, pieces, out, head, following, total):
    @pl.when(pl.program_id(0) == 0)
    def _():
        list_members(adapters, head, following)

    sum_members(
        head, following, total, out, lambda block: pieces[block].astype(jnp.float32)
    )


def up_gradients(adapters, pieces, num_adapters):
    count, width, extent = pieces.shape
    chunk = 32 if num_adapters % 32 == 0 else 1
    return pl.pallas_call(
        up_gradient_kernel,
        out_shape=jax.ShapeDtypeStruct((num_adapters, width, extent), jnp.bfloat16),
        grid_spec=pltpu.PrefetchScalarGridSpec(
            num_scalar_prefetch=1,
            grid=(num_adapters // chunk,),
            in_specs=[pl.BlockSpec(pieces.shape, lambda i, _: (0, 0, 0))],
            out_specs=pl.BlockSpec((chunk, width, extent), lambda i, _: (i, 0, 0)),
            scratch_shapes=[
                pltpu.SMEM((num_adapters,), jnp.int32),
                pltpu.SMEM((count,), jnp.int32),
                pltpu.VMEM((width, extent), jnp.float32),
            ],
        ),
        compiler_params=pltpu.CompilerParams(vmem_limit_bytes=vmem_limit),
        name="up_gradients",
    )(adapters, pieces)


def exchange(pieces):
    return lax.all_to_all(pieces, "dp", split_axis=0, concat_axis=0, tiled=True)


def local(tokens, output_gradient, value_weight, down_maps, up_maps, adapter_per_block, ranks):
    devices = lax.axis_size("dp")
    num_adapters, extent, _ = down_maps.shape
    width = output_gradient.shape[1]
    place = lax.axis_index("dp").astype(jnp.int32).reshape(1)

    own_up = exchange(gather_up(adapter_per_block, up_maps)).reshape(width, extent)
    token_pieces = split_columns(tokens, devices)
    token_pieces, own_up = lax.optimization_barrier((token_pieces, own_up))
    token_blocks = exchange(token_pieces)

    beside = back_beside_gradient(adapter_per_block, ranks, place, output_gradient, own_up)
    gathered = lax.all_gather(beside, "dp", axis=0, tiled=True)
    slices = input_slices(adapter_per_block, gathered, value_weight, down_maps)

    parts = exchange(hidden_parts(adapter_per_block, token_blocks, down_maps))
    slices, parts = lax.optimization_barrier((slices, parts))
    input_grad = join_columns(exchange(slices))

    piece = up_piece(adapter_per_block, ranks, place, parts, output_gradient)
    pieces = exchange(piece.reshape(devices, width // devices, extent))
    down_gradient = down_gradients(
        adapter_per_block, gathered, token_blocks, num_adapters, extent
    )
    up_gradient = up_gradients(adapter_per_block, pieces, num_adapters)
    return (input_grad, down_gradient, up_gradient)


def solution(mesh):
    in_specs = (
        P(("groups", "dp"), None),
        P(("groups", "dp"), None),
        P(None, "dp"),
        P(None, None, "dp"),
        P(None, "dp", None),
        P("groups"),
        P(),
    )
    out_specs = (P(("groups", "dp"), None), P("groups", None, "dp"), P("groups", "dp", None))
    return jax.shard_map(local, mesh=mesh, in_specs=in_specs, out_specs=out_specs, check_vma=False)
```

```python
import functools

import jax
import jax.numpy as jnp
from jax import lax
from jax.experimental import pallas as pl
from jax.experimental.pallas import tpu as pltpu
from jax.sharding import PartitionSpec as P

adapter_alpha = 32.0
vmem_limit = 48 * 1024 * 1024


def group_of(count):
    return 4 if count % 4 == 0 else 1


def order_of(slot, place, count):
    block = place
    bits = count.bit_length() - 1
    for bit in range(bits):
        block = block ^ (((slot >> bit) & 1) << (bits - 1 - bit))
    return block


def gather_up_kernel(adapters, *refs):
    out = refs[-1]
    for offset in range(out.shape[0]):
        out[offset] = refs[offset][0]


def gather_up(adapters, up_maps):
    count = adapters.shape[0]
    step = 16 if count % 16 == 0 else 1

    def spec(offset):
        return pl.BlockSpec(
            (1,) + up_maps.shape[1:], lambda i, adapters: (adapters[i * step + offset], 0, 0)
        )

    return pl.pallas_call(
        gather_up_kernel,
        out_shape=jax.ShapeDtypeStruct((count,) + up_maps.shape[1:], up_maps.dtype),
        grid_spec=pltpu.PrefetchScalarGridSpec(
            num_scalar_prefetch=1,
            grid=(count // step,),
            in_specs=[spec(offset) for offset in range(step)],
            out_specs=pl.BlockSpec((step,) + up_maps.shape[1:], lambda i, _: (i, 0, 0)),
        ),
        name="gather_up",
    )(adapters, *([up_maps] * step))


def split_kernel(source, out):
    width = out.shape[2]
    for piece in range(out.shape[0]):
        out[piece] = source[:, piece * width : (piece + 1) * width]


def split_columns(source, pieces):
    rows, columns = source.shape
    width = columns // pieces
    step = group_of(pieces)
    return pl.pallas_call(
        split_kernel,
        out_shape=jax.ShapeDtypeStruct((pieces, rows, width), source.dtype),
        grid=(pieces // step,),
        in_specs=[pl.BlockSpec((rows, step * width), lambda i: (0, i))],
        out_specs=pl.BlockSpec((step, rows, width), lambda i: (i, 0, 0)),
        name="split_columns",
    )(source)


def join_kernel(source, out):
    width = source.shape[2]
    for piece in range(source.shape[0]):
        out[:, piece * width : (piece + 1) * width] = source[piece]


def join_columns(source):
    pieces, rows, width = source.shape
    step = group_of(pieces)
    return pl.pallas_call(
        join_kernel,
        out_shape=jax.ShapeDtypeStruct((rows, pieces * width), source.dtype),
        grid=(pieces // step,),
        in_specs=[pl.BlockSpec((step, rows, width), lambda i: (i, 0, 0))],
        out_specs=pl.BlockSpec((rows, step * width), lambda i: (0, i)),
        name="join_columns",
    )(source)


def rank_row(ranks, adapter, extent):
    rank = jnp.full((1, extent), ranks[adapter], jnp.int32)
    alive = (lax.broadcasted_iota(jnp.int32, (1, extent), 1) < rank).astype(jnp.float32)
    return alive, adapter_alpha / rank.astype(jnp.float32)


def back_kernel(adapters, ranks, place, gradient, up, out):
    alive, factor = rank_row(ranks, adapters[place[0]], up.shape[1])
    back = jnp.dot(gradient[...], up[...], preferred_element_type=jnp.float32)
    out[0] = (factor * back * alive).astype(out.dtype)


def back_rows(adapters, ranks, place, gradient, up):
    rows = gradient.shape[0]
    extent = up.shape[1]
    return pl.pallas_call(
        back_kernel,
        out_shape=jax.ShapeDtypeStruct((1, rows, extent), jnp.bfloat16),
        grid_spec=pltpu.PrefetchScalarGridSpec(
            num_scalar_prefetch=3,
            grid=(1,),
            in_specs=[
                pl.BlockSpec(gradient.shape, lambda i, *_: (0, 0)),
                pl.BlockSpec(up.shape, lambda i, *_: (0, 0)),
            ],
            out_specs=pl.BlockSpec((1, rows, extent), lambda i, *_: (0, 0, 0)),
        ),
        compiler_params=pltpu.CompilerParams(vmem_limit_bytes=vmem_limit),
        name="back_low",
    )(adapters, ranks, place, gradient, up)


def down_specs(step, count, down_maps):
    def spec(offset):
        return pl.BlockSpec(
            (1,) + down_maps.shape[1:],
            lambda i, adapters, place: (
                adapters[order_of(i * step + offset, place[0], count)],
                0,
                0,
            ),
        )

    return [spec(offset) for offset in range(step)]


def hidden_kernel(adapters, place, tokens, *refs):
    out = refs[-1]
    step = out.shape[0]
    count = tokens.shape[0]
    for offset in range(step):
        block = order_of(pl.program_id(0) * step + offset, place[0], count)
        out[offset] = lax.dot_general(
            tokens[block],
            refs[offset][0],
            (((1,), (1,)), ((), ())),
            preferred_element_type=jnp.float32,
        )


def hidden_parts(adapters, place, tokens, down_maps):
    count, rows, width = tokens.shape
    step = group_of(count)
    extent = down_maps.shape[1]
    return pl.pallas_call(
        hidden_kernel,
        out_shape=jax.ShapeDtypeStruct((count, rows, extent), jnp.float32),
        grid_spec=pltpu.PrefetchScalarGridSpec(
            num_scalar_prefetch=2,
            grid=(count // step,),
            in_specs=[pl.BlockSpec((count, rows, width), lambda i, *_: (0, 0, 0))]
            + down_specs(step, count, down_maps),
            out_specs=pl.BlockSpec((step, rows, extent), lambda i, *_: (i, 0, 0)),
        ),
        compiler_params=pltpu.CompilerParams(vmem_limit_bytes=vmem_limit),
        name="hidden_parts",
    )(adapters, place, tokens, *([down_maps] * step))


def input_kernel(adapters, place, gradients, backs, weight, *refs):
    out = refs[-1]
    count = out.shape[0]
    step, rows, depth = gradients.shape
    frozen = jnp.dot(
        gradients[...].reshape(step * rows, depth),
        weight[...],
        preferred_element_type=jnp.float32,
    )
    for offset in range(step):
        block = order_of(pl.program_id(0) * step + offset, place[0], count)
        adapter = jnp.dot(backs[offset], refs[offset][0], preferred_element_type=jnp.float32)
        out[block] = (frozen[offset * rows : (offset + 1) * rows] + adapter).astype(out.dtype)


def input_slices(adapters, place, gradients, backs, weight, down_maps):
    count, rows, depth = gradients.shape
    step = group_of(count)
    extent = backs.shape[2]
    width = weight.shape[1]
    return pl.pallas_call(
        input_kernel,
        out_shape=jax.ShapeDtypeStruct((count, rows, width), jnp.bfloat16),
        grid_spec=pltpu.PrefetchScalarGridSpec(
            num_scalar_prefetch=2,
            grid=(count // step,),
            in_specs=[
                pl.BlockSpec((step, rows, depth), lambda i, *_: (i, 0, 0)),
                pl.BlockSpec((step, rows, extent), lambda i, *_: (i, 0, 0)),
                pl.BlockSpec(weight.shape, lambda i, *_: (0, 0)),
            ]
            + down_specs(step, count, down_maps),
            out_specs=pl.BlockSpec((count, rows, width), lambda i, *_: (0, 0, 0)),
        ),
        compiler_params=pltpu.CompilerParams(vmem_limit_bytes=vmem_limit),
        name="input_slices",
    )(adapters, place, gradients, backs, weight, *([down_maps] * step))


def hidden_low_kernel(adapters, ranks, place, kept, received, out):
    alive, _ = rank_row(ranks, adapters[place[0]], out.shape[2])
    out[0] = ((kept[0] + received[0]) * alive).astype(out.dtype)


def hidden_rows(adapters, ranks, place, kept, received):
    whole = pl.BlockSpec(kept.shape, lambda i, *_: (0, 0, 0))
    return pl.pallas_call(
        hidden_low_kernel,
        out_shape=jax.ShapeDtypeStruct(kept.shape, jnp.bfloat16),
        grid_spec=pltpu.PrefetchScalarGridSpec(
            num_scalar_prefetch=3, grid=(1,), in_specs=[whole, whole], out_specs=whole
        ),
        name="hidden_low",
    )(adapters, ranks, place, kept, received)


def list_members(adapters, place, head, following):
    count = following.shape[0]

    def clear(adapter, carry):
        head[adapter] = -1
        return carry

    lax.fori_loop(0, head.shape[0], clear, 0)

    def link(step, carry):
        slot = count - 1 - step
        adapter = adapters[order_of(slot, place[0], count)]
        following[slot] = head[adapter]
        head[adapter] = slot
        return carry

    lax.fori_loop(0, count, link, 0)


def sum_members(head, following, total, out, term, finish):
    chunk = out.shape[0]

    def per_adapter(entry, carry):
        adapter = pl.program_id(0) * chunk + entry
        first = head[adapter]

        @pl.when(first < 0)
        def _():
            out[entry] = jnp.zeros(out.shape[1:], out.dtype)

        @pl.when(first >= 0)
        def _():
            total[...] = term(first)

            def more(slot):
                total[...] += term(slot)
                return following[slot]

            lax.while_loop(lambda slot: slot >= 0, more, following[first])
            out[entry] = finish(adapter).astype(out.dtype)

        return carry

    lax.fori_loop(0, chunk, per_adapter, 0)


def down_gradient_kernel(adapters, place, backs, tokens, out, head, following, total):
    count = tokens.shape[0]

    @pl.when(pl.program_id(0) == 0)
    def _():
        list_members(adapters, place, head, following)

    def term(slot):
        return lax.dot_general(
            backs[slot],
            tokens[order_of(slot, place[0], count)],
            (((0,), (0,)), ((), ())),
            preferred_element_type=jnp.float32,
        )

    sum_members(head, following, total, out, term, lambda adapter: total[...])


def down_gradients(adapters, place, backs, tokens, num_adapters):
    count, rows, width = tokens.shape
    extent = backs.shape[2]
    chunk = 8 if num_adapters % 8 == 0 else 1
    return pl.pallas_call(
        down_gradient_kernel,
        out_shape=jax.ShapeDtypeStruct((num_adapters, extent, width), jnp.bfloat16),
        grid_spec=pltpu.PrefetchScalarGridSpec(
            num_scalar_prefetch=2,
            grid=(num_adapters // chunk,),
            in_specs=[
                pl.BlockSpec(backs.shape, lambda i, *_: (0, 0, 0)),
                pl.BlockSpec(tokens.shape, lambda i, *_: (0, 0, 0)),
            ],
            out_specs=pl.BlockSpec((chunk, extent, width), lambda i, *_: (i, 0, 0)),
            scratch_shapes=[
                pltpu.SMEM((num_adapters,), jnp.int32),
                pltpu.SMEM((count,), jnp.int32),
                pltpu.VMEM((extent, width), jnp.float32),
            ],
        ),
        compiler_params=pltpu.CompilerParams(vmem_limit_bytes=vmem_limit),
        name="down_gradients",
    )(adapters, place, backs, tokens)


def up_gradient_kernel(
    adapters, place, ranks, gradients, hiddens, out, head, following, total
):
    width = out.shape[1]
    lanes = gradients.shape[2]
    extent = out.shape[2]

    @pl.when(pl.program_id(0) == 0)
    def _():
        list_members(adapters, place, head, following)

    def term(slot):
        return lax.dot_general(
            gradients[slot],
            hiddens[slot],
            (((0,), (0,)), ((), ())),
            preferred_element_type=jnp.float32,
        )

    def finish(adapter):
        _, factor = rank_row(ranks, adapter, extent)
        inside = lax.rem(place[0], lanes // width) * width
        return factor * total[pl.ds(pl.multiple_of(inside, width), width), :]

    sum_members(head, following, total, out, term, finish)


def up_gradients(adapters, place, ranks, gradients, hiddens, width):
    count, rows, _ = gradients.shape
    extent = hiddens.shape[2]
    num_adapters = ranks.shape[0]
    lanes = 128 if width < 128 else width
    chunk = 32 if num_adapters % 32 == 0 else 1
    return pl.pallas_call(
        up_gradient_kernel,
        out_shape=jax.ShapeDtypeStruct((num_adapters, width, extent), jnp.bfloat16),
        grid_spec=pltpu.PrefetchScalarGridSpec(
            num_scalar_prefetch=3,
            grid=(num_adapters // chunk,),
            in_specs=[
                pl.BlockSpec(
                    (count, rows, lanes),
                    lambda i, adapters, place, ranks: (0, 0, place[0] * width // lanes),
                ),
                pl.BlockSpec(hiddens.shape, lambda i, *_: (0, 0, 0)),
            ],
            out_specs=pl.BlockSpec((chunk, width, extent), lambda i, *_: (i, 0, 0)),
            scratch_shapes=[
                pltpu.SMEM((num_adapters,), jnp.int32),
                pltpu.SMEM((count,), jnp.int32),
                pltpu.VMEM((lanes, extent), jnp.float32),
            ],
        ),
        compiler_params=pltpu.CompilerParams(vmem_limit_bytes=vmem_limit),
        name="up_gradients",
    )(adapters, place, ranks, gradients, hiddens)


def exchange(pieces):
    return lax.all_to_all(pieces, "dp", split_axis=0, concat_axis=0, tiled=True)


def swap(array, distance):
    devices = lax.axis_size("dp")
    return lax.ppermute(array, "dp", [(i, i ^ distance) for i in range(devices)])


def gather_blocks(own):
    distance = lax.axis_size("dp") // 2
    while distance:
        own = jnp.concatenate([own, swap(own, distance)], axis=0)
        distance //= 2
    return own


def reduce_blocks(parts):
    devices = lax.axis_size("dp")
    distance = 1
    while True:
        half = parts.shape[0] // 2
        kept, received = parts[:half], swap(parts[half:], distance)
        distance *= 2
        if distance == devices:
            return kept, received
        parts = kept + received


def local(tokens, output_gradient, value_weight, down_maps, up_maps, adapter_per_block, ranks):
    devices = lax.axis_size("dp")
    num_adapters, extent, _ = down_maps.shape
    rows, width = output_gradient.shape
    place = lax.axis_index("dp").astype(jnp.int32).reshape(1)

    own_up = exchange(gather_up(adapter_per_block, up_maps)).reshape(width, extent)
    gradients = gather_blocks(output_gradient.reshape(1, rows, width))
    token_pieces = split_columns(tokens, devices)
    token_pieces, own_up = lax.optimization_barrier((token_pieces, own_up))
    token_blocks = exchange(token_pieces)

    backs = gather_blocks(back_rows(adapter_per_block, ranks, place, output_gradient, own_up))
    slices = input_slices(adapter_per_block, place, gradients, backs, value_weight, down_maps)
    slices, token_blocks = lax.optimization_barrier((slices, token_blocks))
    input_grad = join_columns(exchange(slices))

    parts = hidden_parts(adapter_per_block, place, token_blocks, down_maps)
    kept, received = reduce_blocks(parts)
    hiddens = gather_blocks(hidden_rows(adapter_per_block, ranks, place, kept, received))
    down_gradient = down_gradients(
        adapter_per_block, place, backs, token_blocks, num_adapters
    )
    up_gradient = up_gradients(
        adapter_per_block, place, ranks, gradients, hiddens, width // devices
    )
    return (input_grad, down_gradient, up_gradient)


def solution(mesh):
    in_specs = (
        P(("groups", "dp"), None),
        P(("groups", "dp"), None),
        P(None, "dp"),
        P(None, None, "dp"),
        P(None, "dp", None),
        P("groups"),
        P(),
    )
    out_specs = (P(("groups", "dp"), None), P("groups", None, "dp"), P("groups", "dp", None))
    return jax.shard_map(local, mesh=mesh, in_specs=in_specs, out_specs=out_specs, check_vma=False)
```

```python
import jax
import jax.numpy as jnp
from jax import lax
from jax.experimental import pallas as pl
from jax.experimental.pallas import tpu as pltpu
from jax.sharding import PartitionSpec as P

adapter_alpha = 32.0
vmem_limit = 48 * 1024 * 1024
pair_bit = 2


def line_offset(slot, members):
    bits = members.bit_length() - 1
    line = 0
    for bit in range(bits):
        line |= ((slot >> bit) & 1) << (bits - 1 - bit)
    return ((line // pair_bit) * 2 * pair_bit) | (line % pair_bit)


def params():
    return pltpu.CompilerParams(vmem_limit_bytes=vmem_limit)


def whole(shape):
    return pl.BlockSpec(shape, lambda *_: (0,) * len(shape))


def picked(maps, flip):
    return pl.BlockSpec(
        (1,) + maps.shape[1:], lambda i, adapters, place, *_: (adapters[place[0] ^ flip], 0, 0)
    )


def call(kernel, name, prefetch, operands, in_specs, out_shapes, scratch=(), grid=(1,), out_specs=None):
    if out_specs is None:
        out_specs = [whole(shape.shape) for shape in out_shapes]
    return pl.pallas_call(
        kernel,
        out_shape=out_shapes,
        grid_spec=pltpu.PrefetchScalarGridSpec(
            num_scalar_prefetch=len(prefetch),
            grid=grid,
            in_specs=in_specs,
            out_specs=out_specs,
            scratch_shapes=list(scratch),
        ),
        compiler_params=params(),
        name=name,
    )(*prefetch, *operands)


def collect_kernel(adapters, place, *refs):
    out = refs[-1]
    for entry in range(out.shape[0]):
        out[entry] = refs[entry][0]


def collect(adapters, place, maps, flips, name):
    shape = jax.ShapeDtypeStruct((len(flips),) + maps.shape[1:], maps.dtype)
    return call(
        collect_kernel,
        name,
        (adapters, place),
        [maps] * len(flips),
        [picked(maps, flip) for flip in flips],
        [shape],
    )[0]


def gather_up_kernel(adapters, place, *refs):
    out = refs[-1]
    for entry in range(out.shape[0]):
        out[entry] = refs[entry][0]


def gather_up(adapters, place, up_maps):
    count = adapters.shape[0]

    def spec(block):
        return pl.BlockSpec(
            (1,) + up_maps.shape[1:], lambda i, adapters, place: (adapters[block], 0, 0)
        )

    shape = jax.ShapeDtypeStruct((count,) + up_maps.shape[1:], up_maps.dtype)
    return call(
        gather_up_kernel,
        "gather_up",
        (adapters, place),
        [up_maps] * count,
        [spec(block) for block in range(count)],
        [shape],
    )[0]


def pack_kernel(place, *refs):
    count = len(refs) // 3
    for slot in range(count):
        out = refs[2 * count + slot]
        out[0] = refs[2 * slot][...]
        out[1] = refs[2 * slot + 1][...]


def pack_tokens(place, tokens, members, width):
    rows = tokens.shape[0]

    def spec(flip):
        return pl.BlockSpec((rows, width), lambda i, place: (0, place[0] ^ flip))

    specs = []
    for slot in range(members):
        offset = line_offset(slot, members)
        specs += [spec(offset), spec(offset ^ pair_bit)]
    shape = jax.ShapeDtypeStruct((2, rows, width), tokens.dtype)
    return call(
        pack_kernel, "pack_tokens", (place,), [tokens] * len(specs), specs, [shape] * members
    )


def rank_row(ranks, adapter, extent):
    rank = jnp.full((1, extent), ranks[adapter], jnp.int32)
    alive = (lax.broadcasted_iota(jnp.int32, (1, extent), 1) < rank).astype(jnp.float32)
    return alive, adapter_alpha / rank.astype(jnp.float32)


def back_kernel(adapters, place, ranks, gradient, up, out):
    alive, factor = rank_row(ranks, adapters[place[0]], up.shape[1])
    back = jnp.dot(gradient[...], up[...], preferred_element_type=jnp.float32)
    out[0] = (factor * back * alive).astype(out.dtype)


def back_rows(adapters, place, ranks, gradient, up):
    shape = jax.ShapeDtypeStruct((1, gradient.shape[0], up.shape[1]), jnp.bfloat16)
    return call(
        back_kernel,
        "back_low",
        (adapters, place, ranks),
        (gradient, up),
        [whole(gradient.shape), whole(up.shape)],
        [shape],
    )[0]


def input_kernel(adapters, place, gradients, backs, weight, weight_pair, down_pair, *refs):
    members, rows, depth = gradients.shape
    downs, outs = refs[:members], refs[members:]
    for first in range(0, members, 4):
        some = min(4, members - first)
        lines = gradients[first : first + some].reshape(some * rows, depth)
        for half in range(2):
            frozen = jnp.dot(
                lines, (weight, weight_pair)[half][...], preferred_element_type=jnp.float32
            )
            for slot in range(first, first + some):
                down = downs[slot][0] if half == 0 else down_pair[slot]
                low = jnp.dot(backs[slot], down, preferred_element_type=jnp.float32)
                at = (slot - first) * rows
                outs[slot][half] = (frozen[at : at + rows] + low).astype(jnp.bfloat16)


def input_slices(adapters, place, gradients, backs, weight, weight_pair, down_maps, down_pair):
    members, rows, _ = gradients.shape
    operands = (gradients, backs, weight, weight_pair, down_pair)
    shape = jax.ShapeDtypeStruct((2, rows, weight.shape[1]), jnp.bfloat16)
    return call(
        input_kernel,
        "input_slices",
        (adapters, place),
        operands + (down_maps,) * members,
        [whole(operand.shape) for operand in operands]
        + [picked(down_maps, line_offset(slot, members)) for slot in range(members)],
        [shape] * members,
    )


def hidden_kernel(adapters, place, down_pair, *refs):
    members = down_pair.shape[0]
    downs, tokens = refs[:members], refs[members : 2 * members]
    parts, own, pair = refs[2 * members :]
    across = (((1,), (1,)), ((), ()))
    for slot in range(members):
        own[slot] = tokens[slot][0]
        pair[slot] = tokens[slot][1]
        parts[slot] = lax.dot_general(
            tokens[slot][0], downs[slot][0], across, preferred_element_type=jnp.float32
        ) + lax.dot_general(
            tokens[slot][1], down_pair[slot], across, preferred_element_type=jnp.float32
        )


def hidden_parts(adapters, place, down_maps, down_pair, tokens):
    members = len(tokens)
    _, rows, width = tokens[0].shape
    extent = down_maps.shape[1]
    tokens_shape = jax.ShapeDtypeStruct((members, rows, width), tokens[0].dtype)
    return call(
        hidden_kernel,
        "hidden_parts",
        (adapters, place),
        [down_pair] + [down_maps] * members + list(tokens),
        [whole(down_pair.shape)]
        + [picked(down_maps, line_offset(slot, members)) for slot in range(members)]
        + [whole(tokens[0].shape)] * members,
        [
            jax.ShapeDtypeStruct((members, rows, extent), jnp.float32),
            tokens_shape,
            tokens_shape,
        ],
    )


def hidden_low_kernel(adapters, place, ranks, kept, received, out):
    alive, _ = rank_row(ranks, adapters[place[0]], out.shape[2])
    out[0] = ((kept[0] + received[0]) * alive).astype(out.dtype)


def hidden_rows(adapters, place, ranks, kept, received):
    return call(
        hidden_low_kernel,
        "hidden_low",
        (adapters, place, ranks),
        (kept, received),
        [whole(kept.shape)] * 2,
        [jax.ShapeDtypeStruct(kept.shape, jnp.bfloat16)],
    )[0]


def join_kernel(place, *refs):
    out = refs[-1]
    members = len(refs) - 1
    width = refs[0].shape[2]
    for slot in range(members):
        for half in range(2):
            source = place[0] ^ line_offset(slot, members) ^ (half * pair_bit)
            columns = pl.ds(pl.multiple_of(source * width, width), width)
            out[:, columns] = refs[slot][half]


def join_columns(place, pieces):
    members = len(pieces)
    _, rows, width = pieces[0].shape
    return call(
        join_kernel,
        "join_columns",
        (place,),
        pieces,
        [whole(pieces[0].shape)] * members,
        [jax.ShapeDtypeStruct((rows, 2 * members * width), pieces[0].dtype)],
    )[0]


def list_members(adapters, place, members, head, following):
    num_adapters = head.shape[1]

    def clear(adapter, carry):
        head[0, adapter] = -1
        head[1, adapter] = -1
        return carry

    lax.fori_loop(0, num_adapters, clear, 0)
    for side in range(2):
        for slot in reversed(range(members)):
            adapter = adapters[place[0] ^ line_offset(slot, members) ^ (side * pair_bit)]
            following[side, slot] = head[side, adapter]
            head[side, adapter] = slot


def sum_members(head, following, total, out, terms, finish):
    chunk = out.shape[0]

    def per_adapter(entry, carry):
        adapter = pl.program_id(0) * chunk + entry
        firsts = [head[0, adapter], head[1, adapter]]
        used = jnp.logical_or(firsts[0] >= 0, firsts[1] >= 0)

        @pl.when(jnp.logical_not(used))
        def _():
            out[entry] = jnp.zeros(out.shape[1:], out.dtype)

        @pl.when(used)
        def _():
            total[...] = jnp.zeros_like(total)
            for side in range(2):

                def more(slot, side=side):
                    total[...] += terms[side](slot)
                    return following[side, slot]

                lax.while_loop(lambda slot: slot >= 0, more, firsts[side])
            out[entry] = finish(adapter).astype(out.dtype)

        return carry

    lax.fori_loop(0, chunk, per_adapter, 0)


def by_rows(left, right):
    return lax.dot_general(
        left, right, (((0,), (0,)), ((), ())), preferred_element_type=jnp.float32
    )


def down_gradient_kernel(
    adapters, place, backs, backs_pair, own, other, out, head, following, total
):
    @pl.when(pl.program_id(0) == 0)
    def _():
        list_members(adapters, place, own.shape[0], head, following)

    terms = (
        lambda slot: by_rows(backs[slot], own[slot]),
        lambda slot: by_rows(backs_pair[slot], other[slot]),
    )
    sum_members(head, following, total, out, terms, lambda adapter: total[...])


def down_gradients(adapters, place, backs, backs_pair, own, other, num_adapters):
    members, _, width = own.shape
    extent = backs.shape[2]
    chunk = 8 if num_adapters % 8 == 0 else 1
    operands = (backs, backs_pair, own, other)
    return call(
        down_gradient_kernel,
        "down_gradients",
        (adapters, place),
        operands,
        [whole(operand.shape) for operand in operands],
        [jax.ShapeDtypeStruct((num_adapters, extent, width), jnp.bfloat16)],
        scratch=[
            pltpu.SMEM((2, num_adapters), jnp.int32),
            pltpu.SMEM((2, members), jnp.int32),
            pltpu.VMEM((extent, width), jnp.float32),
        ],
        grid=(num_adapters // chunk,),
        out_specs=[pl.BlockSpec((chunk, extent, width), lambda i, *_: (i, 0, 0))],
    )[0]


def up_gradient_kernel(
    adapters, place, ranks, gradients, gradients_pair, hiddens, hiddens_pair, out, head, following, total
):
    width, extent = out.shape[1:]
    lanes = gradients.shape[2]

    @pl.when(pl.program_id(0) == 0)
    def _():
        list_members(adapters, place, gradients.shape[0], head, following)

    def finish(adapter):
        _, factor = rank_row(ranks, adapter, extent)
        inside = lax.rem(place[0], lanes // width) * width
        return factor * total[pl.ds(pl.multiple_of(inside, width), width), :]

    terms = (
        lambda slot: by_rows(gradients[slot], hiddens[slot]),
        lambda slot: by_rows(gradients_pair[slot], hiddens_pair[slot]),
    )
    sum_members(head, following, total, out, terms, finish)


def up_gradients(adapters, place, ranks, gradients, gradients_pair, hiddens, hiddens_pair, width):
    members, rows, lanes = gradients_pair.shape
    extent = hiddens.shape[2]
    num_adapters = ranks.shape[0]
    chunk = 32 if num_adapters % 32 == 0 else 1
    return call(
        up_gradient_kernel,
        "up_gradients",
        (adapters, place, ranks),
        (gradients, gradients_pair, hiddens, hiddens_pair),
        [
            pl.BlockSpec(
                (members, rows, lanes),
                lambda i, adapters, place, ranks: (0, 0, place[0] * width // lanes),
            ),
            whole(gradients_pair.shape),
            whole(hiddens.shape),
            whole(hiddens.shape),
        ],
        [jax.ShapeDtypeStruct((num_adapters, width, extent), jnp.bfloat16)],
        scratch=[
            pltpu.SMEM((2, num_adapters), jnp.int32),
            pltpu.SMEM((2, members), jnp.int32),
            pltpu.VMEM((lanes, extent), jnp.float32),
        ],
        grid=(num_adapters // chunk,),
        out_specs=[pl.BlockSpec((chunk, width, extent), lambda i, *_: (i, 0, 0))],
    )[0]


def exchange(pieces):
    return lax.all_to_all(pieces, "dp", split_axis=0, concat_axis=0, tiled=True)


def swap(array, flip):
    devices = lax.axis_size("dp")
    return lax.ppermute(array, "dp", [(i, i ^ flip) for i in range(devices)])


def tie(first, second):
    return lax.optimization_barrier((first, second))


def gather_step(held, members):
    return jnp.concatenate([held, swap(held, line_offset(held.shape[0], members))], axis=0)


def gather_line(held, members):
    while held.shape[0] < members:
        held = gather_step(held, members)
    return held


def reduce_line(parts, members):
    while True:
        half = parts.shape[0] // 2
        kept, received = parts[:half], swap(parts[half:], line_offset(half, members))
        if half == 1:
            return kept, received
        parts = kept + received


def local(tokens, output_gradient, value_weight, down_maps, up_maps, adapter_per_block, ranks):
    devices = lax.axis_size("dp")
    members = devices // 2
    num_adapters, extent, width = down_maps.shape
    rows, depth = output_gradient.shape
    value_width = depth // devices
    place = lax.axis_index("dp").astype(jnp.int32).reshape(1)
    adapters = adapter_per_block
    offsets = [line_offset(slot, members) for slot in range(members)]
    far = [slot for slot in range(members) if slot % 2]
    near = [slot for slot in range(1, members) if slot % 2 == 0]

    gradients = gather_step(output_gradient.reshape(1, rows, depth), members)
    own_up = exchange(gather_up(adapters, place, up_maps)).reshape(depth, extent)
    down_pair = swap(
        collect(adapters, place, down_maps, [o ^ pair_bit for o in offsets], "collect_down"),
        pair_bit,
    )
    weight_pair = swap(value_weight, pair_bit)

    packs = list(pack_tokens(place, tokens, members, width))
    arrived = [packs[0]] + [None] * (members - 1)
    early = far[: len(far) // 2]
    for slot in early:
        arrived[slot] = swap(packs[slot], offsets[slot])
    gradients = gather_step(gradients, members)
    gradients, packs = tie(gradients, packs)
    for slot in near + far[len(far) // 2 :]:
        arrived[slot] = swap(packs[slot], offsets[slot])
    gradients = gather_line(gradients, members)

    backs = gather_line(back_rows(adapters, place, ranks, output_gradient, own_up), members)
    slices = list(
        input_slices(
            adapters, place, gradients, backs, value_weight, weight_pair, down_maps, down_pair
        )
    )
    results = [slices[0]] + [None] * (members - 1)
    for slot in early:
        results[slot] = swap(slices[slot], offsets[slot])

    slices, arrived = tie(slices, arrived)
    parts, tokens_own, tokens_pair = hidden_parts(
        adapters, place, down_maps, down_pair, arrived
    )
    kept, received = reduce_line(parts, members)
    received, slices = tie(received, slices)
    for slot in near + far[len(far) // 2 :]:
        results[slot] = swap(slices[slot], offsets[slot])
    input_grad = join_columns(place, results)

    tokens_other = swap(tokens_pair, pair_bit)
    backs_pair = swap(backs, pair_bit)
    down_gradient = down_gradients(
        adapters, place, backs, backs_pair, tokens_own, tokens_other, num_adapters
    )

    lanes = max(128, value_width)
    column = (place[0] ^ pair_bit) * value_width // lanes * lanes
    gradients_pair = swap(
        lax.dynamic_slice(gradients, (0, 0, column), (members, rows, lanes)), pair_bit
    )
    hiddens = gather_line(hidden_rows(adapters, place, ranks, kept, received), members)
    hiddens_pair = swap(hiddens, pair_bit)
    up_gradient = up_gradients(
        adapters, place, ranks, gradients, gradients_pair, hiddens, hiddens_pair, value_width
    )
    return (input_grad, down_gradient, up_gradient)


def solution(mesh):
    in_specs = (
        P(("groups", "dp"), None),
        P(("groups", "dp"), None),
        P(None, "dp"),
        P(None, None, "dp"),
        P(None, "dp", None),
        P("groups"),
        P(),
    )
    out_specs = (P(("groups", "dp"), None), P("groups", None, "dp"), P("groups", "dp", None))
    return jax.shard_map(local, mesh=mesh, in_specs=in_specs, out_specs=out_specs, check_vma=False)
```

```python
import jax
import jax.numpy as jnp
from jax import lax
from jax.experimental import pallas as pl
from jax.experimental.pallas import tpu as pltpu
from jax.sharding import PartitionSpec as P

adapter_alpha = 32.0
vmem_limit = 48 * 1024 * 1024
pair_bit = 2


def line_offset(slot, members):
    bits = members.bit_length() - 1
    line = 0
    for bit in range(bits):
        line |= ((slot >> bit) & 1) << (bits - 1 - bit)
    return ((line // pair_bit) * 2 * pair_bit) | (line % pair_bit)


def line_index(place):
    return (place // (2 * pair_bit)) * pair_bit + place % pair_bit


def line_place(index, side):
    return (index // pair_bit) * 2 * pair_bit + side * pair_bit + index % pair_bit


def slot_index(place, slot, members):
    return line_index(place) ^ line_index(line_offset(slot, members))


def side_of(place):
    return (place // pair_bit) % 2


def params():
    return pltpu.CompilerParams(vmem_limit_bytes=vmem_limit)


def whole(shape):
    return pl.BlockSpec(shape, lambda *_: (0,) * len(shape))


def picked(maps, flip):
    return pl.BlockSpec(
        (1,) + maps.shape[1:], lambda i, adapters, place, *_: (adapters[place[0] ^ flip], 0, 0)
    )


def call(kernel, name, prefetch, operands, in_specs, out_shapes, scratch=(), grid=(1,), out_specs=None):
    if out_specs is None:
        out_specs = [whole(shape.shape) for shape in out_shapes]
    return pl.pallas_call(
        kernel,
        out_shape=out_shapes,
        grid_spec=pltpu.PrefetchScalarGridSpec(
            num_scalar_prefetch=len(prefetch),
            grid=grid,
            in_specs=in_specs,
            out_specs=out_specs,
            scratch_shapes=list(scratch),
        ),
        compiler_params=params(),
        name=name,
    )(*prefetch, *operands)


def collect_kernel(adapters, place, *refs):
    out = refs[-1]
    for entry in range(out.shape[0]):
        out[entry] = refs[entry][0]


def collect(adapters, place, maps, flips, name):
    shape = jax.ShapeDtypeStruct((len(flips),) + maps.shape[1:], maps.dtype)
    return call(
        collect_kernel,
        name,
        (adapters, place),
        [maps] * len(flips),
        [picked(maps, flip) for flip in flips],
        [shape],
    )[0]


def gather_up_kernel(adapters, place, *refs):
    out = refs[-1]
    for entry in range(out.shape[0]):
        out[entry] = refs[entry][0]


def gather_up(adapters, place, up_maps):
    count = adapters.shape[0]

    def spec(block):
        return pl.BlockSpec(
            (1,) + up_maps.shape[1:], lambda i, adapters, place: (adapters[block], 0, 0)
        )

    shape = jax.ShapeDtypeStruct((count,) + up_maps.shape[1:], up_maps.dtype)
    return call(
        gather_up_kernel,
        "gather_up",
        (adapters, place),
        [up_maps] * count,
        [spec(block) for block in range(count)],
        [shape],
    )[0]


def pack_kernel(place, *refs):
    out = refs[-1]
    for index in range(out.shape[0]):
        for half in range(2):
            out[index, half] = refs[2 * index + half][...]


def pack_tokens(place, tokens, members, width):
    rows = tokens.shape[0]

    def spec(index, half):
        return pl.BlockSpec(
            (rows, width),
            lambda i, place: (0, line_place(index, side_of(place[0]) ^ half)),
        )

    return call(
        pack_kernel,
        "pack_tokens",
        (place,),
        [tokens] * (2 * members),
        [spec(index, half) for index in range(members) for half in range(2)],
        [jax.ShapeDtypeStruct((members, 2, rows, width), tokens.dtype)],
    )[0]


def rank_row(ranks, adapter, extent):
    rank = jnp.full((1, extent), ranks[adapter], jnp.int32)
    alive = (lax.broadcasted_iota(jnp.int32, (1, extent), 1) < rank).astype(jnp.float32)
    return alive, adapter_alpha / rank.astype(jnp.float32)


def back_kernel(adapters, place, ranks, gradient, up, out):
    alive, factor = rank_row(ranks, adapters[place[0]], up.shape[1])
    back = jnp.dot(gradient[...], up[...], preferred_element_type=jnp.float32)
    out[0] = (factor * back * alive).astype(out.dtype)


def back_rows(adapters, place, ranks, gradient, up):
    shape = jax.ShapeDtypeStruct((1, gradient.shape[0], up.shape[1]), jnp.bfloat16)
    return call(
        back_kernel,
        "back_low",
        (adapters, place, ranks),
        (gradient, up),
        [whole(gradient.shape), whole(up.shape)],
        [shape],
    )[0]


def column_of(place, width, lanes):
    return pl.multiple_of(place * width // lanes * lanes, lanes)


def input_kernel(adapters, place, backs, weight, weight_pair, down_pair, *refs):
    members, rows, _ = backs.shape
    gradients, downs, outs = refs[:members], refs[members : 2 * members], refs[2 * members : -2]
    columns = refs[-2:]
    lanes = columns[0].shape[2]
    value_width = gradients[0].shape[2] // (2 * members)
    piece = rows // len(outs)
    some = min(4, members)
    for first in range(0, members, some):
        slots = range(first, first + some)
        lines = jnp.concatenate([gradients[slot][0] for slot in slots], axis=0)
        for half in range(2):
            frozen = jnp.dot(
                lines, (weight, weight_pair)[half][...], preferred_element_type=jnp.float32
            )
            for slot in slots:
                down = downs[slot][0] if half == 0 else down_pair[slot]
                low = jnp.dot(backs[slot], down, preferred_element_type=jnp.float32)
                at = (slot - first) * rows
                result = (frozen[at : at + rows] + low).astype(jnp.bfloat16)
                index = slot_index(place[0], slot, members)
                for part, out in enumerate(outs):
                    out[index, half] = result[part * piece : (part + 1) * piece]
    for side in range(2):
        column = column_of(place[0] ^ (side * pair_bit), value_width, lanes)
        for slot in range(members):
            columns[side][slot] = gradients[slot][0, :, pl.ds(column, lanes)]


def input_slices(
    adapters, place, gradients, backs, weight, weight_pair, down_maps, down_pair, pieces
):
    members, rows, _ = backs.shape
    width = weight.shape[1]
    lanes = max(128, gradients[0].shape[2] // (2 * members))
    operands = (backs, weight, weight_pair, down_pair) + tuple(gradients)
    shape = jax.ShapeDtypeStruct((members, 2, rows // pieces, width), jnp.bfloat16)
    columns = jax.ShapeDtypeStruct((members, rows, lanes), jnp.bfloat16)
    return call(
        input_kernel,
        "input_slices",
        (adapters, place),
        operands + (down_maps,) * members,
        [whole(operand.shape) for operand in operands]
        + [picked(down_maps, line_offset(slot, members)) for slot in range(members)],
        [shape] * pieces + [columns] * 2,
    )


def hidden_kernel(adapters, place, down_pair, tokens, *refs):
    members = down_pair.shape[0]
    downs = refs[:members]
    parts, own, pair = refs[members:]
    across = (((1,), (1,)), ((), ()))
    for slot in reversed(range(members)):
        index = slot_index(place[0], slot, members)
        own[slot] = tokens[index, 0]
        pair[slot] = tokens[index, 1]
        parts[slot] = lax.dot_general(
            tokens[index, 0], downs[slot][0], across, preferred_element_type=jnp.float32
        ) + lax.dot_general(
            tokens[index, 1], down_pair[slot], across, preferred_element_type=jnp.float32
        )


def hidden_parts(adapters, place, down_maps, down_pair, tokens):
    members, _, rows, width = tokens.shape
    extent = down_maps.shape[1]
    tokens_shape = jax.ShapeDtypeStruct((members, rows, width), tokens.dtype)
    return call(
        hidden_kernel,
        "hidden_parts",
        (adapters, place),
        [down_pair, tokens] + [down_maps] * members,
        [whole(down_pair.shape), whole(tokens.shape)]
        + [picked(down_maps, line_offset(slot, members)) for slot in range(members)],
        [
            jax.ShapeDtypeStruct((members, rows, extent), jnp.float32),
            tokens_shape,
            tokens_shape,
        ],
    )


def hidden_low_kernel(adapters, place, ranks, kept, received, out):
    alive, _ = rank_row(ranks, adapters[place[0]], out.shape[2])
    out[0] = ((kept[0] + received[0]) * alive).astype(out.dtype)


def hidden_rows(adapters, place, ranks, kept, received):
    return call(
        hidden_low_kernel,
        "hidden_low",
        (adapters, place, ranks),
        (kept, received),
        [whole(kept.shape)] * 2,
        [jax.ShapeDtypeStruct(kept.shape, jnp.bfloat16)],
    )[0]


def join_kernel(place, source, *refs):
    out = refs[-1]
    members, _, _, width = source.shape
    for index in range(members):
        for half in range(2):
            column = line_place(index, side_of(place[0]) ^ half) * width
            out[:, pl.ds(pl.multiple_of(column, width), width)] = source[index, half]


def join_columns(place, source, part, parts, before=None):
    members, _, rows, width = source.shape
    operands, specs, aliases = [source], [whole(source.shape)], {}
    if before is not None:
        operands, specs = operands + [before], specs + [pl.BlockSpec(memory_space=pl.ANY)]
        aliases = {2: 0}
    return pl.pallas_call(
        join_kernel,
        out_shape=jax.ShapeDtypeStruct((parts * rows, 2 * members * width), source.dtype),
        grid_spec=pltpu.PrefetchScalarGridSpec(
            num_scalar_prefetch=1,
            grid=(1,),
            in_specs=specs,
            out_specs=pl.BlockSpec((rows, 2 * members * width), lambda i, place: (part, 0)),
        ),
        input_output_aliases=aliases,
        compiler_params=params(),
        name="join_columns",
    )(place, *operands)


def list_members(adapters, place, members, head, following):
    num_adapters = head.shape[1]

    def clear(adapter, carry):
        head[0, adapter] = -1
        head[1, adapter] = -1
        return carry

    lax.fori_loop(0, num_adapters, clear, 0)
    for side in range(2):
        for slot in reversed(range(members)):
            adapter = adapters[place[0] ^ line_offset(slot, members) ^ (side * pair_bit)]
            following[side, slot] = head[side, adapter]
            head[side, adapter] = slot


def sum_members(head, following, total, out, terms, finish):
    chunk = out.shape[0]

    def per_adapter(entry, carry):
        adapter = pl.program_id(0) * chunk + entry
        firsts = [head[0, adapter], head[1, adapter]]
        used = jnp.logical_or(firsts[0] >= 0, firsts[1] >= 0)

        @pl.when(jnp.logical_not(used))
        def _():
            out[entry] = jnp.zeros(out.shape[1:], out.dtype)

        @pl.when(used)
        def _():
            total[...] = jnp.zeros_like(total)
            for side in range(2):

                def more(slot, side=side):
                    total[...] += terms[side](slot)
                    return following[side, slot]

                lax.while_loop(lambda slot: slot >= 0, more, firsts[side])
            out[entry] = finish(adapter).astype(out.dtype)

        return carry

    lax.fori_loop(0, chunk, per_adapter, 0)


def by_rows(left, right):
    return lax.dot_general(
        left, right, (((0,), (0,)), ((), ())), preferred_element_type=jnp.float32
    )


def down_gradient_kernel(
    adapters, place, backs, backs_pair, own, other, out, head, following, total
):
    @pl.when(pl.program_id(0) == 0)
    def _():
        list_members(adapters, place, own.shape[0], head, following)

    terms = (
        lambda slot: by_rows(backs[slot], own[slot]),
        lambda slot: by_rows(backs_pair[slot], other[slot]),
    )
    sum_members(head, following, total, out, terms, lambda adapter: total[...])


def down_gradients(adapters, place, backs, backs_pair, own, other, num_adapters):
    members, _, width = own.shape
    extent = backs.shape[2]
    chunk = 8 if num_adapters % 8 == 0 else 1
    operands = (backs, backs_pair, own, other)
    return call(
        down_gradient_kernel,
        "down_gradients",
        (adapters, place),
        operands,
        [whole(operand.shape) for operand in operands],
        [jax.ShapeDtypeStruct((num_adapters, extent, width), jnp.bfloat16)],
        scratch=[
            pltpu.SMEM((2, num_adapters), jnp.int32),
            pltpu.SMEM((2, members), jnp.int32),
            pltpu.VMEM((extent, width), jnp.float32),
        ],
        grid=(num_adapters // chunk,),
        out_specs=[pl.BlockSpec((chunk, extent, width), lambda i, *_: (i, 0, 0))],
    )[0]


def up_gradient_kernel(
    adapters, place, ranks, gradients, gradients_pair, hiddens, hiddens_pair, out, head, following, total
):
    width, extent = out.shape[1:]
    lanes = gradients.shape[2]

    @pl.when(pl.program_id(0) == 0)
    def _():
        list_members(adapters, place, gradients.shape[0], head, following)

    def finish(adapter):
        _, factor = rank_row(ranks, adapter, extent)
        inside = lax.rem(place[0], lanes // width) * width
        return factor * total[pl.ds(pl.multiple_of(inside, width), width), :]

    terms = (
        lambda slot: by_rows(gradients[slot], hiddens[slot]),
        lambda slot: by_rows(gradients_pair[slot], hiddens_pair[slot]),
    )
    sum_members(head, following, total, out, terms, finish)


def up_gradients(adapters, place, ranks, gradients, gradients_pair, hiddens, hiddens_pair, width):
    members, _, lanes = gradients.shape
    extent = hiddens.shape[2]
    num_adapters = ranks.shape[0]
    chunk = 32 if num_adapters % 32 == 0 else 1
    operands = (gradients, gradients_pair, hiddens, hiddens_pair)
    return call(
        up_gradient_kernel,
        "up_gradients",
        (adapters, place, ranks),
        operands,
        [whole(operand.shape) for operand in operands],
        [jax.ShapeDtypeStruct((num_adapters, width, extent), jnp.bfloat16)],
        scratch=[
            pltpu.SMEM((2, num_adapters), jnp.int32),
            pltpu.SMEM((2, members), jnp.int32),
            pltpu.VMEM((lanes, extent), jnp.float32),
        ],
        grid=(num_adapters // chunk,),
        out_specs=[pl.BlockSpec((chunk, width, extent), lambda i, *_: (i, 0, 0))],
    )[0]


def exchange(pieces):
    return lax.all_to_all(pieces, "dp", split_axis=0, concat_axis=0, tiled=True)


def exchange_line(pieces):
    members = pieces.shape[0]
    groups = [[line_place(index, side) for index in range(members)] for side in range(2)]
    return lax.all_to_all(
        pieces, "dp", split_axis=0, concat_axis=0, axis_index_groups=groups, tiled=True
    )


def swap(array, flip):
    devices = lax.axis_size("dp")
    return lax.ppermute(array, "dp", [(i, i ^ flip) for i in range(devices)])


def tie(first, second):
    return lax.optimization_barrier((first, second))


def gather_line(held, members):
    while held.shape[0] < members:
        arrived = swap(held, line_offset(held.shape[0], members))
        held = jnp.concatenate([held, arrived], axis=0)
    return held


def gather_apart(own, members):
    held = [own]
    while len(held) < members:
        offset = line_offset(len(held), members)
        held = held + [swap(block, offset) for block in held]
    return held


def reduce_line(parts, members):
    while True:
        half = parts.shape[0] // 2
        kept, received = parts[:half], swap(parts[half:], line_offset(half, members))
        if half == 1:
            return kept, received
        parts = kept + received


def local(tokens, output_gradient, value_weight, down_maps, up_maps, adapter_per_block, ranks):
    devices = lax.axis_size("dp")
    members = devices // 2
    num_adapters, extent, width = down_maps.shape
    rows, depth = output_gradient.shape
    place = lax.axis_index("dp").astype(jnp.int32).reshape(1)
    adapters = adapter_per_block
    offsets = [line_offset(slot, members) for slot in range(members)]

    gradients = gather_apart(output_gradient.reshape(1, rows, depth), members)
    own_up = exchange(gather_up(adapters, place, up_maps)).reshape(depth, extent)
    arrived = exchange_line(pack_tokens(place, tokens, members, width))
    weight_pair = swap(value_weight, pair_bit)
    down_pair = swap(
        collect(adapters, place, down_maps, [o ^ pair_bit for o in offsets], "collect_down"),
        pair_bit,
    )

    backs = gather_line(back_rows(adapters, place, ranks, output_gradient, own_up), members)
    first, second, columns, columns_pair = input_slices(
        adapters, place, gradients, backs, value_weight, weight_pair, down_maps, down_pair, 2
    )
    first_result = exchange_line(first)

    second, arrived = tie(second, arrived)
    parts, tokens_own, tokens_pair = hidden_parts(
        adapters, place, down_maps, down_pair, arrived
    )
    kept, received = reduce_line(parts, members)
    received, second = tie(received, second)
    second_result = exchange_line(second)

    columns_other = swap(columns_pair, pair_bit)
    backs_pair = swap(backs, pair_bit)
    tokens_other = swap(tokens_pair, pair_bit)
    down_gradient = down_gradients(
        adapters, place, backs, backs_pair, tokens_own, tokens_other, num_adapters
    )
    hiddens = gather_line(hidden_rows(adapters, place, ranks, kept, received), members)
    hiddens_pair = swap(hiddens, pair_bit)
    up_gradient = up_gradients(
        adapters, place, ranks, columns, columns_other, hiddens, hiddens_pair, depth // devices
    )
    half_joined = join_columns(place, first_result, 0, 2)
    down_gradient, second_result = tie(down_gradient, second_result)
    input_grad = join_columns(place, second_result, 1, 2, half_joined)
    return (input_grad, down_gradient, up_gradient)


def solution(mesh):
    in_specs = (
        P(("groups", "dp"), None),
        P(("groups", "dp"), None),
        P(None, "dp"),
        P(None, None, "dp"),
        P(None, "dp", None),
        P("groups"),
        P(),
    )
    out_specs = (P(("groups", "dp"), None), P("groups", None, "dp"), P("groups", "dp", None))
    return jax.shard_map(local, mesh=mesh, in_specs=in_specs, out_specs=out_specs, check_vma=False)
```

```python
import functools

import jax
import jax.numpy as jnp
from jax import lax
from jax.experimental import pallas as pl
from jax.experimental.pallas import tpu as pltpu
from jax.sharding import PartitionSpec as P

adapter_alpha = 32.0
vmem_limit = 48 * 1024 * 1024
pair_bit = 2


def line_offset(slot, members):
    bits = members.bit_length() - 1
    line = 0
    for bit in range(bits):
        line |= ((slot >> bit) & 1) << (bits - 1 - bit)
    return ((line // pair_bit) * 2 * pair_bit) | (line % pair_bit)


def params():
    return pltpu.CompilerParams(vmem_limit_bytes=vmem_limit)


def whole(shape):
    return pl.BlockSpec(shape, lambda *_: (0,) * len(shape))


def picked(maps, flip):
    return pl.BlockSpec(
        (1,) + maps.shape[1:], lambda i, adapters, place, *_: (adapters[place[0] ^ flip], 0, 0)
    )


def call(kernel, name, prefetch, operands, in_specs, out_shapes, scratch=(), grid=(1,), out_specs=None):
    if out_specs is None:
        out_specs = [whole(shape.shape) for shape in out_shapes]
    return pl.pallas_call(
        kernel,
        out_shape=out_shapes,
        grid_spec=pltpu.PrefetchScalarGridSpec(
            num_scalar_prefetch=len(prefetch),
            grid=grid,
            in_specs=in_specs,
            out_specs=out_specs,
            scratch_shapes=list(scratch),
        ),
        compiler_params=params(),
        name=name,
    )(*prefetch, *operands)


def pair_kernel(adapters, place, weight, *refs):
    out = refs[-1]
    count, extent, _ = refs[0].shape[0] * (len(refs) - 1), *refs[0].shape[1:]
    for entry in range(count):
        out[entry * extent : (entry + 1) * extent] = refs[entry][0]
    out[count * extent :] = weight[...]


def for_pair(adapters, place, weight, down_maps, members):
    extent, width = down_maps.shape[1:]
    shape = jax.ShapeDtypeStruct((members * extent + weight.shape[0], width), weight.dtype)
    return call(
        pair_kernel,
        "for_pair",
        (adapters, place),
        [weight] + [down_maps] * members,
        [whole(weight.shape)]
        + [picked(down_maps, line_offset(slot, members) ^ pair_bit) for slot in range(members)],
        [shape],
    )[0]


def gather_up_kernel(adapters, up_maps, out, sems):
    copies = [
        pltpu.make_async_copy(up_maps.at[adapters[block]], out.at[block], sems.at[block])
        for block in range(out.shape[0])
    ]
    for copy in copies:
        copy.start()
    for copy in copies:
        copy.wait()


def gather_up(adapters, up_maps):
    shape = (adapters.shape[0],) + up_maps.shape[1:]
    return call(
        gather_up_kernel,
        "gather_up",
        (adapters,),
        [up_maps],
        [pl.BlockSpec(memory_space=pltpu.HBM)],
        [jax.ShapeDtypeStruct(shape, up_maps.dtype)],
        scratch=[pltpu.SemaphoreType.DMA((shape[0],))],
    )[0]


def pack_kernel(place, *refs):
    count = len(refs) // 3
    for slot in range(count):
        out = refs[2 * count + slot]
        out[0] = refs[2 * slot][...]
        out[1] = refs[2 * slot + 1][...]


def pack_tokens(place, tokens, members, width):
    rows = tokens.shape[0]

    def spec(flip):
        return pl.BlockSpec((rows, width), lambda i, place: (0, place[0] ^ flip))

    specs = []
    for slot in range(members):
        offset = line_offset(slot, members)
        specs += [spec(offset), spec(offset ^ pair_bit)]
    shape = jax.ShapeDtypeStruct((2, rows, width), tokens.dtype)
    return call(
        pack_kernel, "pack_tokens", (place,), [tokens] * len(specs), specs, [shape] * members
    )


def rank_row(ranks, adapter, extent):
    rank = jnp.full((1, extent), ranks[adapter], jnp.int32)
    alive = (lax.broadcasted_iota(jnp.int32, (1, extent), 1) < rank).astype(jnp.float32)
    return alive, adapter_alpha / rank.astype(jnp.float32)


def back_kernel(adapters, place, ranks, gradient, up, out):
    alive, factor = rank_row(ranks, adapters[place[0]], up.shape[1])
    back = jnp.dot(gradient[...], up[...], preferred_element_type=jnp.float32)
    out[0] = (factor * back * alive).astype(out.dtype)


def back_rows(adapters, place, ranks, gradient, up):
    shape = jax.ShapeDtypeStruct((1, gradient.shape[0], up.shape[1]), jnp.bfloat16)
    return call(
        back_kernel,
        "back_low",
        (adapters, place, ranks),
        (gradient, up),
        [whole(gradient.shape), whole(up.shape)],
        [shape],
    )[0]


def input_kernel(adapters, place, backs, pair, *refs):
    members, rows, _ = backs.shape
    gradients, downs = refs[:members], refs[members : 2 * members]
    weight = refs[2 * members]
    outs, columns = refs[2 * members + 1 : -2], refs[-2:]
    extent = downs[0].shape[1]
    lanes = columns[0].shape[2]
    value_width = gradients[0].shape[2] // (2 * members)
    some = min(4, members)
    for first in range(0, members, some):
        slots = range(first, first + some)
        lines = jnp.concatenate([gradients[slot][0] for slot in slots], axis=0)
        for half in range(2):
            right = weight[...] if half == 0 else pair[members * extent :]
            frozen = jnp.dot(lines, right, preferred_element_type=jnp.float32)
            for slot in slots:
                down = downs[slot][0] if half == 0 else pair[slot * extent : (slot + 1) * extent]
                low = jnp.dot(backs[slot], down, preferred_element_type=jnp.float32)
                at = (slot - first) * rows
                outs[slot][half] = (frozen[at : at + rows] + low).astype(jnp.bfloat16)
    for side in range(2):
        column = (place[0] ^ (side * pair_bit)) * value_width // lanes * lanes
        for slot in range(members):
            columns[side][slot] = gradients[slot][0, :, pl.ds(pl.multiple_of(column, lanes), lanes)]


def input_slices(adapters, place, gradients, backs, weight, pair, down_maps):
    members, rows, _ = backs.shape
    width = weight.shape[1]
    lanes = max(128, gradients[0].shape[2] // (2 * members))
    shape = jax.ShapeDtypeStruct((2, rows, width), jnp.bfloat16)
    columns = jax.ShapeDtypeStruct((members, rows, lanes), jnp.bfloat16)
    return call(
        input_kernel,
        "input_slices",
        (adapters, place),
        [backs, pair] + list(gradients) + [down_maps] * members + [weight],
        [whole(backs.shape), whole(pair.shape)]
        + [whole(gradients[0].shape)] * members
        + [picked(down_maps, line_offset(slot, members)) for slot in range(members)]
        + [whole(weight.shape)],
        [shape] * members + [columns] * 2,
    )


def hidden_kernel(adapters, place, pair, *refs):
    parts, own, other = refs[-3:]
    members = own.shape[0]
    downs, tokens = refs[:members], refs[members : 2 * members]
    extent = downs[0].shape[1]
    across = (((1,), (1,)), ((), ()))
    for slot in range(members):
        own[slot] = tokens[slot][0]
        other[slot] = tokens[slot][1]
        parts[slot] = lax.dot_general(
            tokens[slot][0], downs[slot][0], across, preferred_element_type=jnp.float32
        ) + lax.dot_general(
            tokens[slot][1],
            pair[slot * extent : (slot + 1) * extent],
            across,
            preferred_element_type=jnp.float32,
        )


def hidden_parts(adapters, place, down_maps, pair, tokens):
    members = len(tokens)
    _, rows, width = tokens[0].shape
    extent = down_maps.shape[1]
    tokens_shape = jax.ShapeDtypeStruct((members, rows, width), tokens[0].dtype)
    return call(
        hidden_kernel,
        "hidden_parts",
        (adapters, place),
        [pair] + [down_maps] * members + list(tokens),
        [whole(pair.shape)]
        + [picked(down_maps, line_offset(slot, members)) for slot in range(members)]
        + [whole(tokens[0].shape)] * members,
        [
            jax.ShapeDtypeStruct((members, rows, extent), jnp.float32),
            tokens_shape,
            tokens_shape,
        ],
    )


def hidden_low_kernel(adapters, place, ranks, kept, received, out):
    alive, _ = rank_row(ranks, adapters[place[0]], out.shape[2])
    out[0] = ((kept[0] + received[0]) * alive).astype(out.dtype)


def hidden_rows(adapters, place, ranks, kept, received):
    return call(
        hidden_low_kernel,
        "hidden_low",
        (adapters, place, ranks),
        (kept, received),
        [whole(kept.shape)] * 2,
        [jax.ShapeDtypeStruct(kept.shape, jnp.bfloat16)],
    )[0]


def join_kernel(place, *refs, offsets, aliased):
    pieces = refs[: len(offsets)]
    out, sems = refs[len(offsets) + aliased :]
    width = pieces[0].shape[2]
    copies = []
    for entry, offset in enumerate(offsets):
        for half in range(2):
            column = (place[0] ^ offset ^ (half * pair_bit)) * width
            copies.append(
                pltpu.make_async_copy(
                    pieces[entry].at[half],
                    out.at[:, pl.ds(pl.multiple_of(column, width), width)],
                    sems.at[2 * entry + half],
                )
            )
    for copy in copies:
        copy.start()
    for copy in copies:
        copy.wait()


def join_columns(place, pieces, offsets, columns, before=None):
    rows = pieces[0].shape[1]
    anywhere = pl.BlockSpec(memory_space=pl.ANY)
    rest = [] if before is None else [before]
    return pl.pallas_call(
        functools.partial(join_kernel, offsets=offsets, aliased=len(rest)),
        out_shape=jax.ShapeDtypeStruct((rows, columns), pieces[0].dtype),
        grid_spec=pltpu.PrefetchScalarGridSpec(
            num_scalar_prefetch=1,
            grid=(1,),
            in_specs=[anywhere] * (len(pieces) + len(rest)),
            out_specs=pl.BlockSpec(memory_space=pltpu.HBM),
            scratch_shapes=[pltpu.SemaphoreType.DMA((2 * len(pieces),))],
        ),
        input_output_aliases={1 + len(pieces): 0} if rest else {},
        compiler_params=params(),
        name="join_columns",
    )(place, *pieces, *rest)


def list_members(adapters, place, members, head, following):
    def clear(adapter, carry):
        head[adapter] = -1
        return carry

    lax.fori_loop(0, head.shape[0], clear, 0)
    for entry in reversed(range(2 * members)):
        side, slot = divmod(entry, members)
        adapter = adapters[place[0] ^ line_offset(slot, members) ^ (side * pair_bit)]
        following[entry] = head[adapter]
        head[adapter] = entry


def write_sums(head, following, products, ready, zero, out, sems, finish):
    num_adapters = out.shape[0]
    zero[...] = jnp.zeros_like(zero)

    def write(adapter, carry):
        first = head[adapter]

        @pl.when(first < 0)
        def _():
            pltpu.make_async_copy(zero, out.at[adapter], sems.at[adapter]).start()

        @pl.when(first >= 0)
        def _():
            def more(entry):
                products[first] += products[entry]
                return following[entry]

            lax.while_loop(lambda entry: entry >= 0, more, following[first])
            ready[first] = finish(adapter, products[first]).astype(out.dtype)
            pltpu.make_async_copy(ready.at[first], out.at[adapter], sems.at[adapter]).start()

        return carry

    lax.fori_loop(0, num_adapters, write, 0)

    def wait(adapter, carry):
        pltpu.make_async_copy(zero, out.at[adapter], sems.at[adapter]).wait()
        return carry

    lax.fori_loop(0, num_adapters, wait, 0)


def by_rows(left, right):
    return lax.dot_general(
        left, right, (((0,), (0,)), ((), ())), preferred_element_type=jnp.float32
    )


def sums_call(kernel, name, prefetch, operands, num_adapters, entries, product, scratch=()):
    return pl.pallas_call(
        kernel,
        out_shape=jax.ShapeDtypeStruct((num_adapters,) + product, jnp.bfloat16),
        grid_spec=pltpu.PrefetchScalarGridSpec(
            num_scalar_prefetch=len(prefetch),
            grid=(1,),
            in_specs=[whole(operand.shape) for operand in operands],
            out_specs=pl.BlockSpec(memory_space=pltpu.HBM),
            scratch_shapes=[
                pltpu.SMEM((num_adapters,), jnp.int32),
                pltpu.SMEM((entries,), jnp.int32),
                pltpu.VMEM((entries,) + product, jnp.float32),
                pltpu.VMEM((entries,) + product, jnp.bfloat16),
                pltpu.VMEM(product, jnp.bfloat16),
                pltpu.SemaphoreType.DMA((num_adapters,)),
                *scratch,
            ],
        ),
        compiler_params=params(),
        name=name,
    )(*prefetch, *operands)


def down_gradient_kernel(
    adapters, place, backs, backs_pair, own, other, out, head, following, products, ready, zero, sems
):
    members = own.shape[0]
    list_members(adapters, place, members, head, following)
    for slot in range(members):
        products[slot] = by_rows(backs[slot], own[slot])
        products[members + slot] = by_rows(backs_pair[slot], other[slot])
    write_sums(
        head, following, products, ready, zero, out, sems, lambda adapter, total: total
    )


def down_gradients(adapters, place, backs, backs_pair, own, other, num_adapters):
    members, _, width = own.shape
    return sums_call(
        down_gradient_kernel,
        "down_gradients",
        (adapters, place),
        (backs, backs_pair, own, other),
        num_adapters,
        2 * members,
        (backs.shape[2], width),
    )


def up_gradient_kernel(
    adapters,
    place,
    ranks,
    gradients,
    gradients_pair,
    hiddens,
    hiddens_pair,
    out,
    head,
    following,
    products,
    ready,
    zero,
    sems,
    lines,
):
    members, _, lanes = gradients.shape
    width, extent = out.shape[1:]
    list_members(adapters, place, members, head, following)
    inside = pl.multiple_of(lax.rem(place[0], lanes // width) * width, width)
    for slot in range(members):
        lines[slot] = by_rows(gradients[slot], hiddens[slot])
        lines[members + slot] = by_rows(gradients_pair[slot], hiddens_pair[slot])
    for entry in range(2 * members):
        products[entry] = lines[entry, pl.ds(inside, width), :]

    def finish(adapter, total):
        _, factor = rank_row(ranks, adapter, extent)
        return factor * total

    write_sums(head, following, products, ready, zero, out, sems, finish)


def up_gradients(adapters, place, ranks, gradients, gradients_pair, hiddens, hiddens_pair, width):
    members, _, lanes = gradients.shape
    extent = hiddens.shape[2]
    return sums_call(
        up_gradient_kernel,
        "up_gradients",
        (adapters, place, ranks),
        (gradients, gradients_pair, hiddens, hiddens_pair),
        ranks.shape[0],
        2 * members,
        (width, extent),
        [pltpu.VMEM((2 * members, lanes, extent), jnp.float32)],
    )


def exchange(pieces):
    return lax.all_to_all(pieces, "dp", split_axis=0, concat_axis=0, tiled=True)


def swap(array, flip):
    devices = lax.axis_size("dp")
    return lax.ppermute(array, "dp", [(i, i ^ flip) for i in range(devices)])


def tie(first, second):
    return lax.optimization_barrier((first, second))


def gather_step(held, members):
    arrived = swap(held, line_offset(held.shape[0], members))
    return jnp.concatenate([held, arrived], axis=0)


def reduce_step(parts, members):
    half = parts.shape[0] // 2
    return parts[:half], swap(parts[half:], line_offset(half, members))


def local(tokens, output_gradient, value_weight, down_maps, up_maps, adapter_per_block, ranks):
    devices = lax.axis_size("dp")
    members = devices // 2
    steps = members.bit_length() - 1
    num_adapters, extent, width = down_maps.shape
    rows, depth = output_gradient.shape
    place = lax.axis_index("dp").astype(jnp.int32).reshape(1)
    adapters = adapter_per_block
    offsets = [line_offset(slot, members) for slot in range(members)]

    far = [slot for slot in range(members) if slot % 2]
    near = [slot for slot in range(2, members, 2)]
    quarter = max(1, len(far) // 4)
    portions = [far[at : at + quarter] for at in range(0, len(far), quarter)]
    portions[2] = portions[2] + near[: len(near) // 2]
    portions[3] = portions[3] + near[len(near) // 2 :]

    def send(packs, portion):
        return {slot: swap(packs[slot], offsets[slot]) for slot in portion}

    own_gradient = output_gradient.reshape(1, rows, depth)
    gradients = [own_gradient] + [None] * (members - 1)
    for step in range(steps):
        gradients[1 << step] = swap(own_gradient, offsets[1 << step])
    own_up = exchange(gather_up(adapters, up_maps)).reshape(depth, extent)
    pair = swap(for_pair(adapters, place, value_weight, down_maps, members), pair_bit)
    packs = pack_tokens(place, tokens, members, width)
    arrived = {0: packs[0]}
    arrived.update(send(packs, portions[0]))

    first = [gradients[1 << step] for step in range(steps)]
    first, own_up, packs = lax.optimization_barrier((first, own_up, packs))
    for step in range(steps):
        gradients[1 << step] = first[step]

    backs = back_rows(adapters, place, ranks, output_gradient, own_up)
    for step in range(1, steps):
        for slot in range(1, 1 << step):
            gradients[slot + (1 << step)] = swap(gradients[slot], offsets[1 << step])
        backs = gather_step(backs, members)
        arrived.update(send(packs, portions[step]))
        done = [arrived[slot] for slot in portions[step - 1]]
        backs, gradients, packs, done = lax.optimization_barrier(
            (backs, gradients, packs, done)
        )
        arrived.update(zip(portions[step - 1], done))
        if step == 2:
            break
    for step in range(3, steps):
        for slot in range(1, 1 << step):
            gradients[slot + (1 << step)] = swap(gradients[slot], offsets[1 << step])
        backs = gather_step(backs, members)
    backs = gather_step(backs, members)
    arrived.update(send(packs, portions[3]))

    *slices, columns, columns_pair = input_slices(
        adapters, place, gradients, backs, value_weight, pair, down_maps
    )
    results = {0: slices[0]}
    results.update(send(slices, portions[0]))
    results.update(send(slices, portions[1]))

    columns_other = swap(columns_pair, pair_bit)
    backs_pair = swap(backs, pair_bit)
    arrived = [arrived[slot] for slot in range(members)]
    slices, arrived = lax.optimization_barrier((slices, arrived))
    parts, tokens_own, tokens_pair = hidden_parts(adapters, place, down_maps, pair, arrived)
    tokens_other = swap(tokens_pair, pair_bit)
    while parts.shape[0] > 2:
        kept, received = reduce_step(parts, members)
        parts = kept + received
    done = [results[slot] for slot in portions[0]]
    parts, done, columns_other, backs_pair, slices = lax.optimization_barrier(
        (parts, done, columns_other, backs_pair, slices)
    )
    results.update(zip(portions[0], done))
    results.update(send(slices, portions[2]))
    kept, received = reduce_step(parts, members)
    done = [results[slot] for slot in portions[1]]
    received, done, slices = lax.optimization_barrier((received, done, slices))
    results.update(zip(portions[1], done))
    results.update(send(slices, portions[3]))

    hiddens = hidden_rows(adapters, place, ranks, kept, received)
    hiddens = gather_step(gather_step(hiddens, members), members)
    down_gradient = down_gradients(
        adapters, place, backs, backs_pair, tokens_own, tokens_other, num_adapters
    )
    done = [results[slot] for slot in portions[2]]
    hiddens, done, down_gradient = lax.optimization_barrier((hiddens, done, down_gradient))
    results.update(zip(portions[2], done))
    while hiddens.shape[0] < members:
        hiddens = gather_step(hiddens, members)
    hiddens_pair = swap(hiddens, pair_bit)
    up_gradient = up_gradients(
        adapters, place, ranks, columns, columns_other, hiddens, hiddens_pair, depth // devices
    )

    def joined(slots, before=None):
        return join_columns(
            place,
            [results[slot] for slot in slots],
            [offsets[slot] for slot in slots],
            tokens.shape[1],
            before,
        )

    most = joined([0] + portions[0] + portions[1] + portions[2])
    up_gradient, most = lax.optimization_barrier((up_gradient, most))
    input_grad = joined(portions[3], most)
    return (input_grad, down_gradient, up_gradient)


def solution(mesh):
    in_specs = (
        P(("groups", "dp"), None),
        P(("groups", "dp"), None),
        P(None, "dp"),
        P(None, None, "dp"),
        P(None, "dp", None),
        P("groups"),
        P(),
    )
    out_specs = (P(("groups", "dp"), None), P("groups", None, "dp"), P("groups", "dp", None))
    return jax.shard_map(local, mesh=mesh, in_specs=in_specs, out_specs=out_specs, check_vma=False)
```

```python
import functools

import jax
import jax.numpy as jnp
from jax import lax
from jax.experimental import pallas as pl
from jax.experimental.pallas import tpu as pltpu
from jax.sharding import PartitionSpec as P

adapter_alpha = 32.0
vmem_limit = 48 * 1024 * 1024
pair_bit = 2
line_bit = 4


def line_offset(slot, members):
    bits = members.bit_length() - 1
    order = 0
    for bit in range(bits):
        order |= ((slot >> bit) & 1) << (bits - 1 - bit)
    return ((order // 2) * line_bit) | (order % 2)


def entry_of(place, slot, members):
    offset = line_offset(slot, members)
    return (offset % 2) * (members // 2) + ((place ^ offset) // line_bit)


def place_of(entry, place, side, members):
    core, line = divmod(entry, members // 2)
    return line * line_bit + ((place % line_bit) ^ core ^ (side * pair_bit))


def params():
    return pltpu.CompilerParams(vmem_limit_bytes=vmem_limit)


def whole(shape):
    return pl.BlockSpec(shape, lambda *_: (0,) * len(shape))


def picked(maps, flip):
    return pl.BlockSpec(
        (1,) + maps.shape[1:], lambda i, adapters, place, *_: (adapters[place[0] ^ flip], 0, 0)
    )


def call(kernel, name, prefetch, operands, in_specs, out_shapes, scratch=(), grid=(1,), out_specs=None):
    if out_specs is None:
        out_specs = [whole(shape.shape) for shape in out_shapes]
    return pl.pallas_call(
        kernel,
        out_shape=out_shapes,
        grid_spec=pltpu.PrefetchScalarGridSpec(
            num_scalar_prefetch=len(prefetch),
            grid=grid,
            in_specs=in_specs,
            out_specs=out_specs,
            scratch_shapes=list(scratch),
        ),
        compiler_params=params(),
        name=name,
    )(*prefetch, *operands)


def run(copies):
    for copy in copies:
        copy.start()
    for copy in copies:
        copy.wait()


def copy_call(kernel, name, prefetch, operands, out_shapes, copies):
    hbm = pl.BlockSpec(memory_space=pltpu.HBM)
    return pl.pallas_call(
        kernel,
        out_shape=out_shapes,
        grid_spec=pltpu.PrefetchScalarGridSpec(
            num_scalar_prefetch=len(prefetch),
            grid=(1,),
            in_specs=[hbm] * len(operands),
            out_specs=[hbm] * len(out_shapes),
            scratch_shapes=[pltpu.SemaphoreType.DMA((copies,))],
        ),
        compiler_params=params(),
        name=name,
    )(*prefetch, *operands)


weight_cuts = 8


def pair_kernel(adapters, place, weight, down_maps, out, sems):
    extent = down_maps.shape[1]
    depth = weight.shape[0]
    members = (out.shape[0] - depth) // extent
    copies = []
    for slot in range(members):
        block = place[0] ^ line_offset(slot, members) ^ pair_bit
        copies.append((down_maps.at[adapters[block]], slot * extent, extent))
    cut = depth // weight_cuts
    for at in range(0, depth, cut):
        copies.append((weight.at[pl.ds(at, cut)], members * extent + at, cut))
    run(
        [
            pltpu.make_async_copy(source, out.at[pl.ds(at, rows)], sems.at[number])
            for number, (source, at, rows) in enumerate(copies)
        ]
    )


def for_pair(adapters, place, weight, down_maps, members):
    extent, width = down_maps.shape[1:]
    shape = jax.ShapeDtypeStruct((members * extent + weight.shape[0], width), weight.dtype)
    return copy_call(
        pair_kernel,
        "for_pair",
        (adapters, place),
        (weight, down_maps),
        [shape],
        members + weight_cuts,
    )[0]


def gather_up_kernel(adapters, up_maps, out, sems):
    run(
        [
            pltpu.make_async_copy(up_maps.at[adapters[block]], out.at[block], sems.at[block])
            for block in range(out.shape[0])
        ]
    )


def gather_up(adapters, up_maps):
    shape = jax.ShapeDtypeStruct((adapters.shape[0],) + up_maps.shape[1:], up_maps.dtype)
    return copy_call(
        gather_up_kernel, "gather_up", (adapters,), (up_maps,), [shape], adapters.shape[0]
    )[0]


def pack_kernel(place, tokens, *refs):
    outs, sems = refs[:-1], refs[-1]
    members = len(outs)
    width = outs[0].shape[2]
    copies = []
    for slot in range(members):
        for half in range(2):
            column = (place[0] ^ line_offset(slot, members) ^ (half * pair_bit)) * width
            copies.append(
                pltpu.make_async_copy(
                    tokens.at[:, pl.ds(pl.multiple_of(column, width), width)],
                    outs[slot].at[half],
                    sems.at[2 * slot + half],
                )
            )
    run(copies)


def pack_tokens(place, tokens, members, width):
    shape = jax.ShapeDtypeStruct((2, tokens.shape[0], width), tokens.dtype)
    return copy_call(
        pack_kernel, "pack_tokens", (place,), (tokens,), [shape] * members, 2 * members
    )


def rank_row(ranks, adapter, extent):
    rank = jnp.full((1, extent), ranks[adapter], jnp.int32)
    alive = (lax.broadcasted_iota(jnp.int32, (1, extent), 1) < rank).astype(jnp.float32)
    return alive, adapter_alpha / rank.astype(jnp.float32)


def back_kernel(adapters, place, ranks, gradient, up, out):
    alive, factor = rank_row(ranks, adapters[place[0]], up.shape[1])
    back = jnp.dot(gradient[...], up[...], preferred_element_type=jnp.float32)
    low = (factor * back * alive).astype(out.dtype)
    for line in range(out.shape[0]):
        out[line] = low


def back_rows(adapters, place, ranks, gradient, up, lines):
    shape = jax.ShapeDtypeStruct((lines, gradient.shape[0], up.shape[1]), jnp.bfloat16)
    return call(
        back_kernel,
        "back_low",
        (adapters, place, ranks),
        (gradient, up),
        [whole(gradient.shape), whole(up.shape)],
        [shape],
    )[0]


def input_kernel(adapters, place, backs, pair, *refs):
    members, rows, _ = backs.shape
    gradients, downs = refs[:members], refs[members : 2 * members]
    weight = refs[2 * members]
    outs, columns = refs[2 * members + 1 : -2], refs[-2:]
    extent = downs[0].shape[1]
    lanes = columns[0].shape[2]
    value_width = gradients[0].shape[2] // (2 * members)
    some = min(4, members)
    for first in range(0, members, some):
        slots = range(first, first + some)
        lines = jnp.concatenate([gradients[slot][0] for slot in slots], axis=0)
        for half in range(2):
            right = weight[...] if half == 0 else pair[members * extent :]
            frozen = jnp.dot(lines, right, preferred_element_type=jnp.float32)
            for slot in slots:
                down = downs[slot][0] if half == 0 else pair[slot * extent : (slot + 1) * extent]
                entry = entry_of(place[0], slot, members)
                low = jnp.dot(backs[entry], down, preferred_element_type=jnp.float32)
                at = (slot - first) * rows
                outs[slot][half] = (frozen[at : at + rows] + low).astype(jnp.bfloat16)
    for side in range(2):
        column = (place[0] ^ (side * pair_bit)) * value_width // lanes * lanes
        for slot in range(members):
            entry = entry_of(place[0], slot, members)
            columns[side][entry] = gradients[slot][0, :, pl.ds(pl.multiple_of(column, lanes), lanes)]


def input_slices(adapters, place, gradients, backs, weight, pair, down_maps):
    members, rows, _ = backs.shape
    width = weight.shape[1]
    lanes = max(128, gradients[0].shape[2] // (2 * members))
    shape = jax.ShapeDtypeStruct((2, rows, width), jnp.bfloat16)
    columns = jax.ShapeDtypeStruct((members, rows, lanes), jnp.bfloat16)
    return call(
        input_kernel,
        "input_slices",
        (adapters, place),
        [backs, pair] + list(gradients) + [down_maps] * members + [weight],
        [whole(backs.shape), whole(pair.shape)]
        + [whole(gradients[0].shape)] * members
        + [picked(down_maps, line_offset(slot, members)) for slot in range(members)]
        + [whole(weight.shape)],
        [shape] * members + [columns] * 2,
    )


def hidden_kernel(adapters, place, pair, *refs):
    parts, own, other = refs[-3:]
    members = own.shape[0]
    downs, tokens = refs[:members], refs[members : 2 * members]
    extent = downs[0].shape[1]
    across = (((1,), (1,)), ((), ()))
    for slot in range(members):
        entry = entry_of(place[0], slot, members)
        own[entry] = tokens[slot][0]
        other[entry] = tokens[slot][1]
        parts[entry] = lax.dot_general(
            tokens[slot][0], downs[slot][0], across, preferred_element_type=jnp.float32
        ) + lax.dot_general(
            tokens[slot][1],
            pair[slot * extent : (slot + 1) * extent],
            across,
            preferred_element_type=jnp.float32,
        )


def hidden_parts(adapters, place, down_maps, pair, tokens):
    members = len(tokens)
    _, rows, width = tokens[0].shape
    extent = down_maps.shape[1]
    tokens_shape = jax.ShapeDtypeStruct((members, rows, width), tokens[0].dtype)
    return call(
        hidden_kernel,
        "hidden_parts",
        (adapters, place),
        [pair] + [down_maps] * members + list(tokens),
        [whole(pair.shape)]
        + [picked(down_maps, line_offset(slot, members)) for slot in range(members)]
        + [whole(tokens[0].shape)] * members,
        [
            jax.ShapeDtypeStruct((members, rows, extent), jnp.float32),
            tokens_shape,
            tokens_shape,
        ],
    )


def hidden_low_kernel(adapters, place, ranks, parts, out):
    alive, _ = rank_row(ranks, adapters[place[0]], out.shape[2])
    total = parts[0]
    for line in range(1, parts.shape[0]):
        total += parts[line]
    low = (total * alive).astype(out.dtype)
    for line in range(out.shape[0]):
        out[line] = low


def hidden_rows(adapters, place, ranks, parts):
    return call(
        hidden_low_kernel,
        "hidden_low",
        (adapters, place, ranks),
        (parts,),
        [whole(parts.shape)],
        [jax.ShapeDtypeStruct(parts.shape, jnp.bfloat16)],
    )[0]


def join_kernel(place, *refs, offsets, aliased):
    pieces = refs[: len(offsets)]
    out, sems = refs[len(offsets) + aliased :]
    width = pieces[0].shape[2]
    copies = []
    for entry, offset in enumerate(offsets):
        for half in range(2):
            column = (place[0] ^ offset ^ (half * pair_bit)) * width
            copies.append(
                pltpu.make_async_copy(
                    pieces[entry].at[half],
                    out.at[:, pl.ds(pl.multiple_of(column, width), width)],
                    sems.at[2 * entry + half],
                )
            )
    run(copies)


def join_columns(place, pieces, offsets, columns, before=None):
    rows = pieces[0].shape[1]
    anywhere = pl.BlockSpec(memory_space=pl.ANY)
    rest = [] if before is None else [before]
    return pl.pallas_call(
        functools.partial(join_kernel, offsets=offsets, aliased=len(rest)),
        out_shape=jax.ShapeDtypeStruct((rows, columns), pieces[0].dtype),
        grid_spec=pltpu.PrefetchScalarGridSpec(
            num_scalar_prefetch=1,
            grid=(1,),
            in_specs=[anywhere] * (len(pieces) + len(rest)),
            out_specs=pl.BlockSpec(memory_space=pltpu.HBM),
            scratch_shapes=[pltpu.SemaphoreType.DMA((2 * len(pieces),))],
        ),
        input_output_aliases={1 + len(pieces): 0} if rest else {},
        compiler_params=params(),
        name="join_columns",
    )(place, *pieces, *rest)


def list_members(adapters, place, members, head, following):
    def clear(adapter, carry):
        head[adapter] = -1
        return carry

    lax.fori_loop(0, head.shape[0], clear, 0)
    for entry in reversed(range(2 * members)):
        side, own = divmod(entry, members)
        adapter = adapters[place_of(own, place[0], side, members)]
        following[entry] = head[adapter]
        head[adapter] = entry


def write_sums(head, following, products, ready, zero, out, sems, finish):
    num_adapters = out.shape[0]
    zero[...] = jnp.zeros_like(zero)

    def write(adapter, carry):
        first = head[adapter]

        @pl.when(first < 0)
        def _():
            pltpu.make_async_copy(zero, out.at[adapter], sems.at[adapter]).start()

        @pl.when(first >= 0)
        def _():
            def more(entry):
                products[first] += products[entry]
                return following[entry]

            lax.while_loop(lambda entry: entry >= 0, more, following[first])
            ready[first] = finish(adapter, products[first]).astype(out.dtype)
            pltpu.make_async_copy(ready.at[first], out.at[adapter], sems.at[adapter]).start()

        return carry

    lax.fori_loop(0, num_adapters, write, 0)

    def wait(adapter, carry):
        pltpu.make_async_copy(zero, out.at[adapter], sems.at[adapter]).wait()
        return carry

    lax.fori_loop(0, num_adapters, wait, 0)


def by_rows(left, right):
    return lax.dot_general(
        left, right, (((0,), (0,)), ((), ())), preferred_element_type=jnp.float32
    )


def sums_call(kernel, name, prefetch, operands, num_adapters, entries, product, scratch=()):
    return pl.pallas_call(
        kernel,
        out_shape=jax.ShapeDtypeStruct((num_adapters,) + product, jnp.bfloat16),
        grid_spec=pltpu.PrefetchScalarGridSpec(
            num_scalar_prefetch=len(prefetch),
            grid=(1,),
            in_specs=[whole(operand.shape) for operand in operands],
            out_specs=pl.BlockSpec(memory_space=pltpu.HBM),
            scratch_shapes=[
                pltpu.SMEM((num_adapters,), jnp.int32),
                pltpu.SMEM((entries,), jnp.int32),
                pltpu.VMEM((entries,) + product, jnp.float32),
                pltpu.VMEM((entries,) + product, jnp.bfloat16),
                pltpu.VMEM(product, jnp.bfloat16),
                pltpu.SemaphoreType.DMA((num_adapters,)),
                *scratch,
            ],
        ),
        compiler_params=params(),
        name=name,
    )(*prefetch, *operands)


def down_gradient_kernel(
    adapters, place, backs, backs_pair, own, other, out, head, following, products, ready, zero, sems
):
    members = own.shape[0]
    list_members(adapters, place, members, head, following)
    for slot in range(members):
        products[slot] = by_rows(backs[slot], own[slot])
        products[members + slot] = by_rows(backs_pair[slot], other[slot])
    write_sums(
        head, following, products, ready, zero, out, sems, lambda adapter, total: total
    )


def down_gradients(adapters, place, backs, backs_pair, own, other, num_adapters):
    members, _, width = own.shape
    return sums_call(
        down_gradient_kernel,
        "down_gradients",
        (adapters, place),
        (backs, backs_pair, own, other),
        num_adapters,
        2 * members,
        (backs.shape[2], width),
    )


def up_gradient_kernel(
    adapters,
    place,
    ranks,
    gradients,
    gradients_pair,
    hiddens,
    hiddens_pair,
    out,
    head,
    following,
    products,
    ready,
    zero,
    sems,
    lines,
):
    members, _, lanes = gradients.shape
    width, extent = out.shape[1:]
    list_members(adapters, place, members, head, following)
    inside = pl.multiple_of(lax.rem(place[0], lanes // width) * width, width)
    for slot in range(members):
        lines[slot] = by_rows(gradients[slot], hiddens[slot])
        lines[members + slot] = by_rows(gradients_pair[slot], hiddens_pair[slot])
    for entry in range(2 * members):
        products[entry] = lines[entry, pl.ds(inside, width), :]

    def finish(adapter, total):
        _, factor = rank_row(ranks, adapter, extent)
        return factor * total

    write_sums(head, following, products, ready, zero, out, sems, finish)


def up_gradients(adapters, place, ranks, gradients, gradients_pair, hiddens, hiddens_pair, width):
    members, _, lanes = gradients.shape
    extent = hiddens.shape[2]
    return sums_call(
        up_gradient_kernel,
        "up_gradients",
        (adapters, place, ranks),
        (gradients, gradients_pair, hiddens, hiddens_pair),
        ranks.shape[0],
        2 * members,
        (width, extent),
        [pltpu.VMEM((2 * members, lanes, extent), jnp.float32)],
    )


def exchange(pieces):
    return lax.all_to_all(pieces, "dp", split_axis=0, concat_axis=0, tiled=True)


def exchange_line(pieces):
    lines = pieces.shape[0]
    groups = [[line * line_bit + first for line in range(lines)] for first in range(line_bit)]
    return lax.all_to_all(
        pieces, "dp", split_axis=0, concat_axis=0, axis_index_groups=groups, tiled=True
    )


def swap(array, flip):
    devices = lax.axis_size("dp")
    return lax.ppermute(array, "dp", [(i, i ^ flip) for i in range(devices)])


def tie(first, second):
    return lax.optimization_barrier((first, second))


def both_cores(held):
    return jnp.concatenate([held, swap(held, 1)], axis=0)


def local(tokens, output_gradient, value_weight, down_maps, up_maps, adapter_per_block, ranks):
    devices = lax.axis_size("dp")
    members = devices // 2
    lines = members // 2
    steps = members.bit_length() - 1
    num_adapters, extent, width = down_maps.shape
    rows, depth = output_gradient.shape
    place = lax.axis_index("dp").astype(jnp.int32).reshape(1)
    adapters = adapter_per_block
    offsets = [line_offset(slot, members) for slot in range(members)]
    barrier = lax.optimization_barrier

    far = [slot for slot in range(members) if slot % 2]
    near = [slot for slot in range(2, members, 2)]
    quarter = max(1, len(far) // 4)
    portions = [far[at : at + quarter] for at in range(0, len(far), quarter)]
    portions[2] = portions[2] + near[: len(near) // 2]
    portions[3] = portions[3] + near[len(near) // 2 :]

    def send(packs, portion):
        return {slot: swap(packs[slot], offsets[slot]) for slot in portion}

    def taken(pieces, portion):
        return [pieces[slot] for slot in portion]

    own_gradient = output_gradient.reshape(1, rows, depth)
    gradients = [own_gradient] + [None] * (members - 1)
    for step in range(steps):
        gradients[1 << step] = swap(own_gradient, offsets[1 << step])
    own_up = exchange(gather_up(adapters, up_maps)).reshape(depth, extent)
    pair = for_pair(adapters, place, value_weight, down_maps, members)
    gradients[2], pair = barrier((gradients[2], pair))
    pair = swap(pair, pair_bit)
    packs = pack_tokens(place, tokens, members, width)
    gradients[1], packs = barrier((gradients[1], packs))
    arrived = {0: packs[0]}
    arrived.update(send(packs, portions[0]))
    for step in range(1, steps):
        for slot in range(1, 1 << step):
            gradients[slot + (1 << step)] = swap(gradients[slot], offsets[1 << step])
    gradients[: members // 2], own_up, packs = barrier(
        (gradients[: members // 2], own_up, packs)
    )

    backs = exchange_line(back_rows(adapters, place, ranks, output_gradient, own_up, lines))
    arrived.update(send(packs, portions[1]))
    backs, gradients, packs, done = barrier(
        (backs, gradients, packs, taken(arrived, portions[0] + portions[1]))
    )
    arrived.update(zip(portions[0] + portions[1], done))
    backs = both_cores(backs)
    arrived.update(send(packs, portions[2]))
    arrived.update(send(packs, portions[3]))

    *slices, columns, columns_pair = input_slices(
        adapters, place, gradients, backs, value_weight, pair, down_maps
    )
    results = {0: slices[0]}
    results.update(send(slices, portions[0]))
    results.update(send(slices, portions[1]))
    columns_other = swap(columns_pair, pair_bit)
    backs_pair = swap(backs, pair_bit)
    slices, arrived = barrier((slices, taken(arrived, range(members))))
    parts, tokens_own, tokens_pair = hidden_parts(adapters, place, down_maps, pair, arrived)
    parts = parts[:lines] + swap(parts[lines:], 1)
    parts, tokens_pair, columns_other, backs_pair = barrier(
        (parts, tokens_pair, columns_other, backs_pair)
    )
    tokens_other = swap(tokens_pair, pair_bit)
    parts = exchange_line(parts)
    parts, done, slices = barrier((parts, taken(results, portions[0]), slices))
    results.update(zip(portions[0], done))
    results.update(send(slices, portions[2]))

    hiddens = exchange_line(hidden_rows(adapters, place, ranks, parts))
    hiddens, done, slices = barrier((hiddens, taken(results, portions[1]), slices))
    results.update(zip(portions[1], done))
    results.update(send(slices, portions[3]))
    hiddens = both_cores(hiddens)
    hiddens_pair = swap(hiddens, pair_bit)
    down_gradient = down_gradients(
        adapters, place, backs, backs_pair, tokens_own, tokens_other, num_adapters
    )
    hiddens_pair, done, down_gradient = barrier(
        (hiddens_pair, taken(results, portions[2]), down_gradient)
    )
    results.update(zip(portions[2], done))
    up_gradient = up_gradients(
        adapters, place, ranks, columns, columns_other, hiddens, hiddens_pair, depth // devices
    )

    def joined(slots, before=None):
        return join_columns(
            place, taken(results, slots), taken(offsets, slots), tokens.shape[1], before
        )

    most = joined([0] + portions[0] + portions[1] + portions[2])
    up_gradient, most = barrier((up_gradient, most))
    input_grad = joined(portions[3], most)
    return (input_grad, down_gradient, up_gradient)


def solution(mesh):
    in_specs = (
        P(("groups", "dp"), None),
        P(("groups", "dp"), None),
        P(None, "dp"),
        P(None, None, "dp"),
        P(None, "dp", None),
        P("groups"),
        P(),
    )
    out_specs = (P(("groups", "dp"), None), P("groups", None, "dp"), P("groups", "dp", None))
    return jax.shard_map(local, mesh=mesh, in_specs=in_specs, out_specs=out_specs, check_vma=False)
```

```python
import functools

import jax
import jax.numpy as jnp
from jax import lax
from jax.experimental import pallas as pl
from jax.experimental.pallas import tpu as pltpu
from jax.sharding import PartitionSpec as P

adapter_alpha = 32.0
vmem_limit = 48 * 1024 * 1024
pair_bit = 2
line_bit = 4


def line_offset(slot, members):
    bits = members.bit_length() - 1
    order = 0
    for bit in range(bits):
        order |= ((slot >> bit) & 1) << (bits - 1 - bit)
    return ((order // 2) * line_bit) | (order % 2)


def entry_of(place, slot, members):
    offset = line_offset(slot, members)
    return (offset % 2) * (members // 2) + ((place ^ offset) // line_bit)


def place_of(entry, place, side, members):
    core, line = divmod(entry, members // 2)
    return line * line_bit + ((place % line_bit) ^ core ^ (side * pair_bit))


def params():
    return pltpu.CompilerParams(vmem_limit_bytes=vmem_limit)


def whole(shape):
    return pl.BlockSpec(shape, lambda *_: (0,) * len(shape))


def picked(maps, flip):
    return pl.BlockSpec(
        (1,) + maps.shape[1:], lambda i, adapters, place, *_: (adapters[place[0] ^ flip], 0, 0)
    )


def call(kernel, name, prefetch, operands, in_specs, out_shapes, scratch=(), grid=(1,), out_specs=None):
    if out_specs is None:
        out_specs = [whole(shape.shape) for shape in out_shapes]
    return pl.pallas_call(
        kernel,
        out_shape=out_shapes,
        grid_spec=pltpu.PrefetchScalarGridSpec(
            num_scalar_prefetch=len(prefetch),
            grid=grid,
            in_specs=in_specs,
            out_specs=out_specs,
            scratch_shapes=list(scratch),
        ),
        compiler_params=params(),
        name=name,
    )(*prefetch, *operands)


def run(copies):
    for copy in copies:
        copy.start()
    for copy in copies:
        copy.wait()


def copy_call(kernel, name, prefetch, operands, out_shapes, copies):
    return pl.pallas_call(
        kernel,
        out_shape=out_shapes,
        grid_spec=pltpu.PrefetchScalarGridSpec(
            num_scalar_prefetch=len(prefetch),
            grid=(1,),
            in_specs=[pl.BlockSpec(memory_space=pl.ANY)] * len(operands),
            out_specs=[whole(shape.shape) for shape in out_shapes],
            scratch_shapes=[pltpu.SemaphoreType.DMA((copies,))],
        ),
        compiler_params=params(),
        name=name,
    )(*prefetch, *operands)


weight_cuts = 4


def pair_kernel(adapters, place, weight, down_maps, out, sems):
    extent = down_maps.shape[1]
    depth = weight.shape[0]
    members = (out.shape[0] - depth) // extent
    copies = []
    for slot in range(members):
        block = place[0] ^ line_offset(slot, members) ^ pair_bit
        copies.append((down_maps.at[adapters[block]], slot * extent, extent))
    cut = depth // weight_cuts
    for at in range(0, depth, cut):
        copies.append((weight.at[pl.ds(at, cut)], members * extent + at, cut))
    run(
        [
            pltpu.make_async_copy(source, out.at[pl.ds(at, rows)], sems.at[number])
            for number, (source, at, rows) in enumerate(copies)
        ]
    )


def for_pair(adapters, place, weight, down_maps, members):
    extent, width = down_maps.shape[1:]
    shape = jax.ShapeDtypeStruct((members * extent + weight.shape[0], width), weight.dtype)
    return copy_call(
        pair_kernel,
        "for_pair",
        (adapters, place),
        (weight, down_maps),
        [shape],
        members + weight_cuts,
    )[0]


def gather_up_kernel(adapters, place, up_maps, own, pair, sems):
    members = own.shape[0]
    copies = []
    for index in range(members):
        block = (index // 2) * line_bit + place[0] % line_bit // pair_bit * pair_bit + index % 2
        for side, out in enumerate((own, pair)):
            source = up_maps.at[adapters[block ^ (side * pair_bit)]]
            copies.append(
                pltpu.make_async_copy(source, out.at[index], sems.at[2 * index + side])
            )
    run(copies)


def gather_up(adapters, place, up_maps, members):
    shape = jax.ShapeDtypeStruct((members,) + up_maps.shape[1:], up_maps.dtype)
    return copy_call(
        gather_up_kernel, "gather_up", (adapters, place), (up_maps,), [shape] * 2, 2 * members
    )


def pack_kernel(place, tokens, *refs):
    outs, sems = refs[:-1], refs[-1]
    members = len(outs)
    width = outs[0].shape[2]
    copies = []
    for slot in range(members):
        for half in range(2):
            column = (place[0] ^ line_offset(slot, members) ^ (half * pair_bit)) * width
            copies.append(
                pltpu.make_async_copy(
                    tokens.at[:, pl.ds(pl.multiple_of(column, width), width)],
                    outs[slot].at[half],
                    sems.at[2 * slot + half],
                )
            )
    run(copies)


def pack_tokens(place, tokens, members, width):
    shape = jax.ShapeDtypeStruct((2, tokens.shape[0], width), tokens.dtype)
    return copy_call(
        pack_kernel, "pack_tokens", (place,), (tokens,), [shape] * members, 2 * members
    )


def rank_row(ranks, adapter, extent):
    rank = jnp.full((1, extent), ranks[adapter], jnp.int32)
    alive = (lax.broadcasted_iota(jnp.int32, (1, extent), 1) < rank).astype(jnp.float32)
    return alive, adapter_alpha / rank.astype(jnp.float32)


def back_kernel(adapters, place, ranks, gradient, ups, out, up):
    members, _, value_width, extent = ups.shape
    side = place[0] % line_bit // pair_bit
    for index in range(members):
        for half in range(2):
            owner = (index // 2) * line_bit + (side ^ half) * pair_bit + index % 2
            rows = pl.ds(pl.multiple_of(owner * value_width, value_width), value_width)
            up[rows, :] = ups[index, half]
    alive, factor = rank_row(ranks, adapters[place[0]], extent)
    back = jnp.dot(gradient[...], up[...], preferred_element_type=jnp.float32)
    low = (factor * back * alive).astype(out.dtype)
    for line in range(out.shape[0]):
        out[line] = low


def back_rows(adapters, place, ranks, gradient, ups):
    members, _, _, extent = ups.shape
    rows, depth = gradient.shape
    return call(
        back_kernel,
        "back_low",
        (adapters, place, ranks),
        (gradient, ups),
        [whole(gradient.shape), whole(ups.shape)],
        [jax.ShapeDtypeStruct((members // 2, rows, extent), jnp.bfloat16)],
        scratch=[pltpu.VMEM((depth, extent), jnp.bfloat16)],
    )[0]


def input_kernel(adapters, place, backs, pair, *refs):
    members, rows, _ = backs.shape
    gradients, downs = refs[:members], refs[members : 2 * members]
    weight = refs[2 * members]
    outs, columns = refs[2 * members + 1 : -2], refs[-2:]
    extent = downs[0].shape[1]
    lanes = columns[0].shape[2]
    value_width = gradients[0].shape[2] // (2 * members)
    some = min(4, members)
    for first in range(0, members, some):
        slots = range(first, first + some)
        lines = jnp.concatenate([gradients[slot][0] for slot in slots], axis=0)
        for half in range(2):
            right = weight[...] if half == 0 else pair[members * extent :]
            frozen = jnp.dot(lines, right, preferred_element_type=jnp.float32)
            for slot in slots:
                down = downs[slot][0] if half == 0 else pair[slot * extent : (slot + 1) * extent]
                entry = entry_of(place[0], slot, members)
                low = jnp.dot(backs[entry], down, preferred_element_type=jnp.float32)
                at = (slot - first) * rows
                outs[slot][half] = (frozen[at : at + rows] + low).astype(jnp.bfloat16)
    for side in range(2):
        column = (place[0] ^ (side * pair_bit)) * value_width // lanes * lanes
        for slot in range(members):
            entry = entry_of(place[0], slot, members)
            columns[side][entry] = gradients[slot][0, :, pl.ds(pl.multiple_of(column, lanes), lanes)]


def input_slices(adapters, place, gradients, backs, weight, pair, down_maps):
    members, rows, _ = backs.shape
    width = weight.shape[1]
    lanes = max(128, gradients[0].shape[2] // (2 * members))
    shape = jax.ShapeDtypeStruct((2, rows, width), jnp.bfloat16)
    columns = jax.ShapeDtypeStruct((members, rows, lanes), jnp.bfloat16)
    return call(
        input_kernel,
        "input_slices",
        (adapters, place),
        [backs, pair] + list(gradients) + [down_maps] * members + [weight],
        [whole(backs.shape), whole(pair.shape)]
        + [whole(gradients[0].shape)] * members
        + [picked(down_maps, line_offset(slot, members)) for slot in range(members)]
        + [whole(weight.shape)],
        [shape] * members + [columns] * 2,
    )


def hidden_kernel(adapters, place, pair, *refs):
    parts, own, other = refs[-3:]
    members = own.shape[0]
    downs, tokens = refs[:members], refs[members : 2 * members]
    extent = downs[0].shape[1]
    across = (((1,), (1,)), ((), ()))
    for slot in range(members):
        entry = entry_of(place[0], slot, members)
        own[entry] = tokens[slot][0]
        other[entry] = tokens[slot][1]
        parts[entry] = lax.dot_general(
            tokens[slot][0], downs[slot][0], across, preferred_element_type=jnp.float32
        ) + lax.dot_general(
            tokens[slot][1],
            pair[slot * extent : (slot + 1) * extent],
            across,
            preferred_element_type=jnp.float32,
        )


def hidden_parts(adapters, place, down_maps, pair, tokens):
    members = len(tokens)
    _, rows, width = tokens[0].shape
    extent = down_maps.shape[1]
    tokens_shape = jax.ShapeDtypeStruct((members, rows, width), tokens[0].dtype)
    return call(
        hidden_kernel,
        "hidden_parts",
        (adapters, place),
        [pair] + [down_maps] * members + list(tokens),
        [whole(pair.shape)]
        + [picked(down_maps, line_offset(slot, members)) for slot in range(members)]
        + [whole(tokens[0].shape)] * members,
        [
            jax.ShapeDtypeStruct((members, rows, extent), jnp.float32),
            tokens_shape,
            tokens_shape,
        ],
    )


def hidden_low_kernel(adapters, place, ranks, parts, out):
    alive, _ = rank_row(ranks, adapters[place[0]], out.shape[2])
    total = parts[0]
    for line in range(1, parts.shape[0]):
        total += parts[line]
    low = (total * alive).astype(out.dtype)
    for line in range(out.shape[0]):
        out[line] = low


def hidden_rows(adapters, place, ranks, parts):
    return call(
        hidden_low_kernel,
        "hidden_low",
        (adapters, place, ranks),
        (parts,),
        [whole(parts.shape)],
        [jax.ShapeDtypeStruct(parts.shape, jnp.bfloat16)],
    )[0]


def join_kernel(place, *refs, offsets, aliased):
    pieces = refs[: len(offsets)]
    out, sems = refs[len(offsets) + aliased :]
    width = pieces[0].shape[2]
    copies = []
    for entry, offset in enumerate(offsets):
        for half in range(2):
            column = (place[0] ^ offset ^ (half * pair_bit)) * width
            copies.append(
                pltpu.make_async_copy(
                    pieces[entry].at[half],
                    out.at[:, pl.ds(pl.multiple_of(column, width), width)],
                    sems.at[2 * entry + half],
                )
            )
    run(copies)


def join_columns(place, pieces, offsets, columns, before=None):
    rows = pieces[0].shape[1]
    rest = [] if before is None else [before]
    return pl.pallas_call(
        functools.partial(join_kernel, offsets=offsets, aliased=len(rest)),
        out_shape=jax.ShapeDtypeStruct((rows, columns), pieces[0].dtype),
        grid_spec=pltpu.PrefetchScalarGridSpec(
            num_scalar_prefetch=1,
            grid=(1,),
            in_specs=[whole(piece.shape) for piece in pieces]
            + [pl.BlockSpec(memory_space=pl.ANY)] * len(rest),
            out_specs=pl.BlockSpec(memory_space=pltpu.HBM),
            scratch_shapes=[pltpu.SemaphoreType.DMA((2 * len(pieces),))],
        ),
        input_output_aliases={1 + len(pieces): 0} if rest else {},
        compiler_params=params(),
        name="join_columns",
    )(place, *pieces, *rest)


def list_members(adapters, place, members, head, following):
    def clear(adapter, carry):
        head[adapter] = -1
        return carry

    lax.fori_loop(0, head.shape[0], clear, 0)
    for entry in reversed(range(2 * members)):
        side, own = divmod(entry, members)
        adapter = adapters[place_of(own, place[0], side, members)]
        following[entry] = head[adapter]
        head[adapter] = entry


def write_sums(head, following, products, ready, zero, out, sems, finish):
    num_adapters = out.shape[0]
    zero[...] = jnp.zeros_like(zero)

    def write(adapter, carry):
        first = head[adapter]

        @pl.when(first < 0)
        def _():
            pltpu.make_async_copy(zero, out.at[adapter], sems.at[adapter]).start()

        @pl.when(first >= 0)
        def _():
            def more(entry):
                products[first] += products[entry]
                return following[entry]

            lax.while_loop(lambda entry: entry >= 0, more, following[first])
            ready[first] = finish(adapter, products[first]).astype(out.dtype)
            pltpu.make_async_copy(ready.at[first], out.at[adapter], sems.at[adapter]).start()

        return carry

    lax.fori_loop(0, num_adapters, write, 0)

    def wait(adapter, carry):
        pltpu.make_async_copy(zero, out.at[adapter], sems.at[adapter]).wait()
        return carry

    lax.fori_loop(0, num_adapters, wait, 0)


def by_rows(left, right):
    return lax.dot_general(
        left, right, (((0,), (0,)), ((), ())), preferred_element_type=jnp.float32
    )


def sums_call(kernel, name, prefetch, operands, num_adapters, entries, product, scratch=()):
    return pl.pallas_call(
        kernel,
        out_shape=jax.ShapeDtypeStruct((num_adapters,) + product, jnp.bfloat16),
        grid_spec=pltpu.PrefetchScalarGridSpec(
            num_scalar_prefetch=len(prefetch),
            grid=(1,),
            in_specs=[whole(operand.shape) for operand in operands],
            out_specs=pl.BlockSpec(memory_space=pltpu.HBM),
            scratch_shapes=[
                pltpu.SMEM((num_adapters,), jnp.int32),
                pltpu.SMEM((entries,), jnp.int32),
                pltpu.VMEM((entries,) + product, jnp.float32),
                pltpu.VMEM((entries,) + product, jnp.bfloat16),
                pltpu.VMEM(product, jnp.bfloat16),
                pltpu.SemaphoreType.DMA((num_adapters,)),
                *scratch,
            ],
        ),
        compiler_params=params(),
        name=name,
    )(*prefetch, *operands)


def down_gradient_kernel(
    adapters, place, backs, backs_pair, own, other, out, head, following, products, ready, zero, sems
):
    members = own.shape[0]
    list_members(adapters, place, members, head, following)
    for slot in range(members):
        products[slot] = by_rows(backs[slot], own[slot])
        products[members + slot] = by_rows(backs_pair[slot], other[slot])
    write_sums(
        head, following, products, ready, zero, out, sems, lambda adapter, total: total
    )


def down_gradients(adapters, place, backs, backs_pair, own, other, num_adapters):
    members, _, width = own.shape
    return sums_call(
        down_gradient_kernel,
        "down_gradients",
        (adapters, place),
        (backs, backs_pair, own, other),
        num_adapters,
        2 * members,
        (backs.shape[2], width),
    )


def up_gradient_kernel(
    adapters,
    place,
    ranks,
    gradients,
    gradients_pair,
    hiddens,
    hiddens_pair,
    out,
    head,
    following,
    products,
    ready,
    zero,
    sems,
    lines,
):
    members, _, lanes = gradients.shape
    width, extent = out.shape[1:]
    list_members(adapters, place, members, head, following)
    inside = pl.multiple_of(lax.rem(place[0], lanes // width) * width, width)
    for slot in range(members):
        lines[slot] = by_rows(gradients[slot], hiddens[slot])
        lines[members + slot] = by_rows(gradients_pair[slot], hiddens_pair[slot])
    for entry in range(2 * members):
        products[entry] = lines[entry, pl.ds(inside, width), :]

    def finish(adapter, total):
        _, factor = rank_row(ranks, adapter, extent)
        return factor * total

    write_sums(head, following, products, ready, zero, out, sems, finish)


def up_gradients(adapters, place, ranks, gradients, gradients_pair, hiddens, hiddens_pair, width):
    members, _, lanes = gradients.shape
    extent = hiddens.shape[2]
    return sums_call(
        up_gradient_kernel,
        "up_gradients",
        (adapters, place, ranks),
        (gradients, gradients_pair, hiddens, hiddens_pair),
        ranks.shape[0],
        2 * members,
        (width, extent),
        [pltpu.VMEM((2 * members, lanes, extent), jnp.float32)],
    )


def exchange(pieces, groups):
    return lax.all_to_all(
        pieces, "dp", split_axis=0, concat_axis=0, axis_index_groups=groups, tiled=True
    )


def exchange_line(pieces):
    groups = [
        [line * line_bit + first for line in range(pieces.shape[0])] for first in range(line_bit)
    ]
    return exchange(pieces, groups)


def exchange_side(pieces):
    members = pieces.shape[0]
    groups = [
        [(index // 2) * line_bit + side * pair_bit + index % 2 for index in range(members)]
        for side in range(2)
    ]
    return exchange(pieces, groups)


def swap(array, flip):
    devices = lax.axis_size("dp")
    return lax.ppermute(array, "dp", [(i, i ^ flip) for i in range(devices)])


def tie(first, second):
    return lax.optimization_barrier((first, second))


def both_cores(held):
    return jnp.concatenate([held, swap(held, 1)], axis=0)


def local(tokens, output_gradient, value_weight, down_maps, up_maps, adapter_per_block, ranks):
    devices = lax.axis_size("dp")
    members = devices // 2
    lines = members // 2
    steps = members.bit_length() - 1
    num_adapters, extent, width = down_maps.shape
    rows, depth = output_gradient.shape
    place = lax.axis_index("dp").astype(jnp.int32).reshape(1)
    adapters = adapter_per_block
    offsets = [line_offset(slot, members) for slot in range(members)]
    barrier = lax.optimization_barrier

    far = [slot for slot in range(members) if slot % 2]
    near = [slot for slot in range(2, members, 2)]
    quarter = max(1, len(far) // 4)
    portions = [far[at : at + quarter] for at in range(0, len(far), quarter)]
    portions[2] = portions[2] + near[: len(near) // 2]
    portions[3] = portions[3] + near[len(near) // 2 :]

    def send(packs, portion):
        return {slot: swap(packs[slot], offsets[slot]) for slot in portion}

    def taken(pieces, portion):
        return [pieces[slot] for slot in portion]

    own_gradient = output_gradient.reshape(1, rows, depth)
    gradients = [own_gradient] + [None] * (members - 1)
    for step in range(steps):
        gradients[1 << step] = swap(own_gradient, offsets[1 << step])
    ups, ups_pair = gather_up(adapters, place, up_maps, members)
    ups_other = swap(ups_pair, pair_bit)
    pair = for_pair(adapters, place, value_weight, down_maps, members)
    ups_other, pair = barrier((ups_other, pair))
    pair = swap(pair, pair_bit)
    ups = exchange_side(jnp.stack([ups, ups_other], axis=1))
    packs = pack_tokens(place, tokens, members, width)
    gradients[1], packs = barrier((gradients[1], packs))
    arrived = {0: packs[0]}
    arrived.update(send(packs, portions[0]))
    for step in range(1, steps):
        for slot in range(1, 1 << step):
            gradients[slot + (1 << step)] = swap(gradients[slot], offsets[1 << step])
    gradients[: members // 2], ups, packs = barrier((gradients[: members // 2], ups, packs))

    backs = exchange_line(back_rows(adapters, place, ranks, output_gradient, ups))
    backs, gradients, packs, done = barrier(
        (backs, gradients, packs, taken(arrived, portions[0]))
    )
    arrived.update(zip(portions[0], done))
    for portion in portions[1:]:
        arrived.update(send(packs, portion))
    backs = both_cores(backs)
    *slices, columns, columns_pair = input_slices(
        adapters, place, gradients, backs, value_weight, pair, down_maps
    )
    results = {0: slices[0]}
    results.update(send(slices, portions[0]))
    columns_other = swap(columns_pair, pair_bit)
    backs_pair = swap(backs, pair_bit)
    slices, arrived = barrier((slices, taken(arrived, range(members))))
    parts, tokens_own, tokens_pair = hidden_parts(adapters, place, down_maps, pair, arrived)
    parts = parts[:lines] + swap(parts[lines:], 1)
    parts, done = barrier((parts, taken(results, portions[0])))
    results.update(zip(portions[0], done))
    hiddens = exchange_line(
        hidden_rows(adapters, place, ranks, exchange_line(parts))
    )
    hiddens, slices, columns_other, backs_pair, tokens_pair = barrier(
        (hiddens, slices, columns_other, backs_pair, tokens_pair)
    )
    for portion in portions[1:]:
        results.update(send(slices, portion))
    hiddens = both_cores(hiddens)
    hiddens_pair = swap(hiddens, pair_bit)
    tokens_other = swap(tokens_pair, pair_bit)
    up_gradient = up_gradients(
        adapters, place, ranks, columns, columns_other, hiddens, hiddens_pair, depth // devices
    )
    down_gradient = down_gradients(
        adapters, place, backs, backs_pair, tokens_own, tokens_other, num_adapters
    )

    def joined(slots, before=None):
        return join_columns(
            place, taken(results, slots), taken(offsets, slots), tokens.shape[1], before
        )

    most = joined([0] + portions[0] + portions[1] + portions[2])
    up_gradient, down_gradient, most = barrier((up_gradient, down_gradient, most))
    input_grad = joined(portions[3], most)
    return (input_grad, down_gradient, up_gradient)


def solution(mesh):
    in_specs = (
        P(("groups", "dp"), None),
        P(("groups", "dp"), None),
        P(None, "dp"),
        P(None, None, "dp"),
        P(None, "dp", None),
        P("groups"),
        P(),
    )
    out_specs = (P(("groups", "dp"), None), P("groups", None, "dp"), P("groups", "dp", None))
    return jax.shard_map(local, mesh=mesh, in_specs=in_specs, out_specs=out_specs, check_vma=False)
```

```python
import functools

import jax
import jax.numpy as jnp
from jax import lax
from jax.experimental import pallas as pl
from jax.experimental.pallas import tpu as pltpu
from jax.sharding import PartitionSpec as P

adapter_alpha = 32.0
vmem_limit = 48 * 1024 * 1024
pair_bit = 2
line_bit = 4


def line_offset(slot, members):
    bits = members.bit_length() - 1
    order = 0
    for bit in range(bits):
        order |= ((slot >> bit) & 1) << (bits - 1 - bit)
    return ((order // 2) * line_bit) | (order % 2)


def entry_of(place, slot, members):
    offset = line_offset(slot, members)
    return (offset % 2) * (members // 2) + ((place ^ offset) // line_bit)


def place_of(entry, place, side, members):
    core, line = divmod(entry, members // 2)
    return line * line_bit + ((place % line_bit) ^ core ^ (side * pair_bit))


def params():
    return pltpu.CompilerParams(vmem_limit_bytes=vmem_limit)


def whole(shape):
    return pl.BlockSpec(shape, lambda *_: (0,) * len(shape))


def picked(maps, flip):
    return pl.BlockSpec(
        (1,) + maps.shape[1:], lambda i, adapters, place, *_: (adapters[place[0] ^ flip], 0, 0)
    )


def call(kernel, name, prefetch, operands, in_specs, out_shapes, scratch=(), grid=(1,), out_specs=None):
    if out_specs is None:
        out_specs = [whole(shape.shape) for shape in out_shapes]
    return pl.pallas_call(
        kernel,
        out_shape=out_shapes,
        grid_spec=pltpu.PrefetchScalarGridSpec(
            num_scalar_prefetch=len(prefetch),
            grid=grid,
            in_specs=in_specs,
            out_specs=out_specs,
            scratch_shapes=list(scratch),
        ),
        compiler_params=params(),
        name=name,
    )(*prefetch, *operands)


def run(copies):
    for copy in copies:
        copy.start()
    for copy in copies:
        copy.wait()


def copy_call(kernel, name, prefetch, operands, out_shapes, copies):
    return pl.pallas_call(
        kernel,
        out_shape=out_shapes,
        grid_spec=pltpu.PrefetchScalarGridSpec(
            num_scalar_prefetch=len(prefetch),
            grid=(1,),
            in_specs=[pl.BlockSpec(memory_space=pl.ANY)] * len(operands),
            out_specs=[whole(shape.shape) for shape in out_shapes],
            scratch_shapes=[pltpu.SemaphoreType.DMA((copies,))],
        ),
        compiler_params=params(),
        name=name,
    )(*prefetch, *operands)


weight_cuts = 4


def pair_kernel(adapters, place, weight, down_maps, out, sems):
    extent = down_maps.shape[1]
    depth = weight.shape[0]
    members = (out.shape[0] - depth) // extent
    copies = []
    for slot in range(members):
        block = place[0] ^ line_offset(slot, members) ^ pair_bit
        copies.append((down_maps.at[adapters[block]], slot * extent, extent))
    cut = depth // weight_cuts
    for at in range(0, depth, cut):
        copies.append((weight.at[pl.ds(at, cut)], members * extent + at, cut))
    run(
        [
            pltpu.make_async_copy(source, out.at[pl.ds(at, rows)], sems.at[number])
            for number, (source, at, rows) in enumerate(copies)
        ]
    )


def for_pair(adapters, place, weight, down_maps, members):
    extent, width = down_maps.shape[1:]
    shape = jax.ShapeDtypeStruct((members * extent + weight.shape[0], width), weight.dtype)
    return copy_call(
        pair_kernel,
        "for_pair",
        (adapters, place),
        (weight, down_maps),
        [shape],
        members + weight_cuts,
    )[0]


def gather_up_kernel(adapters, place, up_maps, own, pair, sems):
    members = own.shape[0]
    copies = []
    for index in range(members):
        block = (index // 2) * line_bit + place[0] % line_bit // pair_bit * pair_bit + index % 2
        for side, out in enumerate((own, pair)):
            source = up_maps.at[adapters[block ^ (side * pair_bit)]]
            copies.append(
                pltpu.make_async_copy(source, out.at[index], sems.at[2 * index + side])
            )
    run(copies)


def gather_up(adapters, place, up_maps, members):
    shape = jax.ShapeDtypeStruct((members,) + up_maps.shape[1:], up_maps.dtype)
    return copy_call(
        gather_up_kernel, "gather_up", (adapters, place), (up_maps,), [shape] * 2, 2 * members
    )


def pack_kernel(place, tokens, *refs):
    outs, sems = refs[:-1], refs[-1]
    members = len(outs)
    width = outs[0].shape[2]
    copies = []
    for slot in range(members):
        for half in range(2):
            column = (place[0] ^ line_offset(slot, members) ^ (half * pair_bit)) * width
            copies.append(
                pltpu.make_async_copy(
                    tokens.at[:, pl.ds(pl.multiple_of(column, width), width)],
                    outs[slot].at[half],
                    sems.at[2 * slot + half],
                )
            )
    run(copies)


def pack_tokens(place, tokens, members, width):
    shape = jax.ShapeDtypeStruct((2, tokens.shape[0], width), tokens.dtype)
    return copy_call(
        pack_kernel, "pack_tokens", (place,), (tokens,), [shape] * members, 2 * members
    )


def rank_row(ranks, adapter, extent):
    rank = jnp.full((1, extent), ranks[adapter], jnp.int32)
    alive = (lax.broadcasted_iota(jnp.int32, (1, extent), 1) < rank).astype(jnp.float32)
    return alive, adapter_alpha / rank.astype(jnp.float32)


def back_kernel(adapters, place, ranks, gradient, ups, out, up):
    members, _, value_width, extent = ups.shape
    side = place[0] % line_bit // pair_bit
    for index in range(members):
        for half in range(2):
            owner = (index // 2) * line_bit + (side ^ half) * pair_bit + index % 2
            rows = pl.ds(pl.multiple_of(owner * value_width, value_width), value_width)
            up[rows, :] = ups[index, half]
    alive, factor = rank_row(ranks, adapters[place[0]], extent)
    back = jnp.dot(gradient[...], up[...], preferred_element_type=jnp.float32)
    low = (factor * back * alive).astype(out.dtype)
    for line in range(out.shape[0]):
        out[line] = low


def back_rows(adapters, place, ranks, gradient, ups):
    members, _, _, extent = ups.shape
    rows, depth = gradient.shape
    return call(
        back_kernel,
        "back_low",
        (adapters, place, ranks),
        (gradient, ups),
        [whole(gradient.shape), whole(ups.shape)],
        [jax.ShapeDtypeStruct((members // 2, rows, extent), jnp.bfloat16)],
        scratch=[pltpu.VMEM((depth, extent), jnp.bfloat16)],
    )[0]


def input_kernel(adapters, place, backs, pair, *refs):
    members, rows, _ = backs.shape
    apart = members // 2
    gradients = [ref.at[0] for ref in refs[:apart]]
    gradients += [refs[apart].at[slot] for slot in range(members - apart)]
    downs = refs[apart + 1 : apart + 1 + members]
    weight = refs[apart + 1 + members]
    outs, columns = refs[apart + 2 + members : -2], refs[-2:]
    extent = downs[0].shape[1]
    lanes = columns[0].shape[2]
    value_width = gradients[0].shape[1] // (2 * members)
    some = min(4, members)
    for first in range(0, members, some):
        slots = range(first, first + some)
        lines = jnp.concatenate([gradients[slot][...] for slot in slots], axis=0)
        for half in range(2):
            right = weight[...] if half == 0 else pair[members * extent :]
            frozen = jnp.dot(lines, right, preferred_element_type=jnp.float32)
            for slot in slots:
                down = downs[slot][0] if half == 0 else pair[slot * extent : (slot + 1) * extent]
                entry = entry_of(place[0], slot, members)
                low = jnp.dot(backs[entry], down, preferred_element_type=jnp.float32)
                at = (slot - first) * rows
                outs[slot][half] = (frozen[at : at + rows] + low).astype(jnp.bfloat16)
    for side in range(2):
        column = (place[0] ^ (side * pair_bit)) * value_width // lanes * lanes
        for slot in range(members):
            entry = entry_of(place[0], slot, members)
            columns[side][entry] = gradients[slot][:, pl.ds(pl.multiple_of(column, lanes), lanes)]


def input_slices(adapters, place, gradients, backs, weight, pair, down_maps):
    members, rows, _ = backs.shape
    width = weight.shape[1]
    lanes = max(128, gradients[0].shape[2] // (2 * members))
    shape = jax.ShapeDtypeStruct((2, rows, width), jnp.bfloat16)
    columns = jax.ShapeDtypeStruct((members, rows, lanes), jnp.bfloat16)
    return call(
        input_kernel,
        "input_slices",
        (adapters, place),
        [backs, pair] + list(gradients) + [down_maps] * members + [weight],
        [whole(backs.shape), whole(pair.shape)]
        + [whole(gradient.shape) for gradient in gradients]
        + [picked(down_maps, line_offset(slot, members)) for slot in range(members)]
        + [whole(weight.shape)],
        [shape] * members + [columns] * 2,
    )


def hidden_kernel(adapters, place, pair, *refs):
    parts, own, *others = refs[-4:]
    members = own.shape[0]
    downs, tokens = refs[:members], refs[members : 2 * members]
    extent = downs[0].shape[1]
    across = (((1,), (1,)), ((), ()))
    for slot in range(members):
        entry = entry_of(place[0], slot, members)
        own[entry] = tokens[slot][0]
        core = line_offset(slot, members) % 2
        others[core][entry - core * (members // 2)] = tokens[slot][1]
        parts[entry] = lax.dot_general(
            tokens[slot][0], downs[slot][0], across, preferred_element_type=jnp.float32
        ) + lax.dot_general(
            tokens[slot][1],
            pair[slot * extent : (slot + 1) * extent],
            across,
            preferred_element_type=jnp.float32,
        )


def hidden_parts(adapters, place, down_maps, pair, tokens):
    members = len(tokens)
    _, rows, width = tokens[0].shape
    extent = down_maps.shape[1]
    others = jax.ShapeDtypeStruct((members // 2, rows, width), tokens[0].dtype)
    return call(
        hidden_kernel,
        "hidden_parts",
        (adapters, place),
        [pair] + [down_maps] * members + list(tokens),
        [whole(pair.shape)]
        + [picked(down_maps, line_offset(slot, members)) for slot in range(members)]
        + [whole(tokens[0].shape)] * members,
        [
            jax.ShapeDtypeStruct((members, rows, extent), jnp.float32),
            jax.ShapeDtypeStruct((members, rows, width), tokens[0].dtype),
            others,
            others,
        ],
    )


def hidden_low_kernel(adapters, place, ranks, parts, out):
    alive, _ = rank_row(ranks, adapters[place[0]], out.shape[2])
    total = parts[0]
    for line in range(1, parts.shape[0]):
        total += parts[line]
    low = (total * alive).astype(out.dtype)
    for line in range(out.shape[0]):
        out[line] = low


def hidden_rows(adapters, place, ranks, parts):
    return call(
        hidden_low_kernel,
        "hidden_low",
        (adapters, place, ranks),
        (parts,),
        [whole(parts.shape)],
        [jax.ShapeDtypeStruct(parts.shape, jnp.bfloat16)],
    )[0]


def join_kernel(place, *refs, offsets, aliased):
    pieces = refs[: len(offsets)]
    out, sems = refs[len(offsets) + aliased :]
    width = pieces[0].shape[2]
    copies = []
    for entry, offset in enumerate(offsets):
        for half in range(2):
            column = (place[0] ^ offset ^ (half * pair_bit)) * width
            copies.append(
                pltpu.make_async_copy(
                    pieces[entry].at[half],
                    out.at[:, pl.ds(pl.multiple_of(column, width), width)],
                    sems.at[2 * entry + half],
                )
            )
    run(copies)


def join_columns(place, pieces, offsets, columns, before=None):
    rows = pieces[0].shape[1]
    rest = [] if before is None else [before]
    return pl.pallas_call(
        functools.partial(join_kernel, offsets=offsets, aliased=len(rest)),
        out_shape=jax.ShapeDtypeStruct((rows, columns), pieces[0].dtype),
        grid_spec=pltpu.PrefetchScalarGridSpec(
            num_scalar_prefetch=1,
            grid=(1,),
            in_specs=[whole(piece.shape) for piece in pieces]
            + [pl.BlockSpec(memory_space=pl.ANY)] * len(rest),
            out_specs=pl.BlockSpec(memory_space=pltpu.HBM),
            scratch_shapes=[pltpu.SemaphoreType.DMA((2 * len(pieces),))],
        ),
        input_output_aliases={1 + len(pieces): 0} if rest else {},
        compiler_params=params(),
        name="join_columns",
    )(place, *pieces, *rest)


def list_members(adapters, place, members, head, following):
    def clear(adapter, carry):
        head[adapter] = -1
        return carry

    lax.fori_loop(0, head.shape[0], clear, 0)
    for entry in reversed(range(2 * members)):
        side, own = divmod(entry, members)
        adapter = adapters[place_of(own, place[0], side, members)]
        following[entry] = head[adapter]
        head[adapter] = entry


def write_sums(head, following, products, ready, zero, out, sems, finish):
    num_adapters = out.shape[0]
    zero[...] = jnp.zeros_like(zero)

    def write(adapter, carry):
        first = head[adapter]

        @pl.when(first < 0)
        def _():
            pltpu.make_async_copy(zero, out.at[adapter], sems.at[adapter]).start()

        @pl.when(first >= 0)
        def _():
            def more(entry):
                products[first] += products[entry]
                return following[entry]

            lax.while_loop(lambda entry: entry >= 0, more, following[first])
            ready[first] = finish(adapter, products[first]).astype(out.dtype)
            pltpu.make_async_copy(ready.at[first], out.at[adapter], sems.at[adapter]).start()

        return carry

    lax.fori_loop(0, num_adapters, write, 0)

    def wait(adapter, carry):
        pltpu.make_async_copy(zero, out.at[adapter], sems.at[adapter]).wait()
        return carry

    lax.fori_loop(0, num_adapters, wait, 0)


def by_rows(left, right):
    return lax.dot_general(
        left, right, (((0,), (0,)), ((), ())), preferred_element_type=jnp.float32
    )


def sums_call(kernel, name, prefetch, operands, num_adapters, entries, product, scratch=()):
    return pl.pallas_call(
        kernel,
        out_shape=jax.ShapeDtypeStruct((num_adapters,) + product, jnp.bfloat16),
        grid_spec=pltpu.PrefetchScalarGridSpec(
            num_scalar_prefetch=len(prefetch),
            grid=(1,),
            in_specs=[whole(operand.shape) for operand in operands],
            out_specs=pl.BlockSpec(memory_space=pltpu.HBM),
            scratch_shapes=[
                pltpu.SMEM((num_adapters,), jnp.int32),
                pltpu.SMEM((entries,), jnp.int32),
                pltpu.VMEM((entries,) + product, jnp.float32),
                pltpu.VMEM((entries,) + product, jnp.bfloat16),
                pltpu.VMEM(product, jnp.bfloat16),
                pltpu.SemaphoreType.DMA((num_adapters,)),
                *scratch,
            ],
        ),
        compiler_params=params(),
        name=name,
    )(*prefetch, *operands)


def down_gradient_kernel(
    adapters,
    place,
    backs,
    backs_pair,
    own,
    other_first,
    other_second,
    out,
    head,
    following,
    products,
    ready,
    zero,
    sems,
):
    members = own.shape[0]
    others = (other_first, other_second)
    list_members(adapters, place, members, head, following)
    for slot in range(members):
        products[slot] = by_rows(backs[slot], own[slot])
        core, line = divmod(slot, members // 2)
        products[members + slot] = by_rows(backs_pair[slot], others[core][line])
    write_sums(
        head, following, products, ready, zero, out, sems, lambda adapter, total: total
    )


def down_gradients(adapters, place, backs, backs_pair, own, others, num_adapters):
    members, _, width = own.shape
    return sums_call(
        down_gradient_kernel,
        "down_gradients",
        (adapters, place),
        (backs, backs_pair, own, *others),
        num_adapters,
        2 * members,
        (backs.shape[2], width),
    )


def up_gradient_kernel(
    adapters,
    place,
    ranks,
    gradients,
    gradients_pair,
    hiddens,
    hiddens_pair,
    out,
    head,
    following,
    products,
    ready,
    zero,
    sems,
    lines,
):
    members, _, lanes = gradients.shape
    width, extent = out.shape[1:]
    list_members(adapters, place, members, head, following)
    inside = pl.multiple_of(lax.rem(place[0], lanes // width) * width, width)
    for slot in range(members):
        lines[slot] = by_rows(gradients[slot], hiddens[slot])
        lines[members + slot] = by_rows(gradients_pair[slot], hiddens_pair[slot])
    for entry in range(2 * members):
        products[entry] = lines[entry, pl.ds(inside, width), :]

    def finish(adapter, total):
        _, factor = rank_row(ranks, adapter, extent)
        return factor * total

    write_sums(head, following, products, ready, zero, out, sems, finish)


def up_gradients(adapters, place, ranks, gradients, gradients_pair, hiddens, hiddens_pair, width):
    members, _, lanes = gradients.shape
    extent = hiddens.shape[2]
    return sums_call(
        up_gradient_kernel,
        "up_gradients",
        (adapters, place, ranks),
        (gradients, gradients_pair, hiddens, hiddens_pair),
        ranks.shape[0],
        2 * members,
        (width, extent),
        [pltpu.VMEM((2 * members, lanes, extent), jnp.float32)],
    )


def exchange(pieces, groups):
    return lax.all_to_all(
        pieces, "dp", split_axis=0, concat_axis=0, axis_index_groups=groups, tiled=True
    )


def exchange_line(pieces):
    groups = [
        [line * line_bit + first for line in range(pieces.shape[0])] for first in range(line_bit)
    ]
    return exchange(pieces, groups)


def exchange_side(pieces):
    members = pieces.shape[0]
    groups = [
        [(index // 2) * line_bit + side * pair_bit + index % 2 for index in range(members)]
        for side in range(2)
    ]
    return exchange(pieces, groups)


def swap(array, flip):
    devices = lax.axis_size("dp")
    return lax.ppermute(array, "dp", [(i, i ^ flip) for i in range(devices)])


def tie(first, second):
    return lax.optimization_barrier((first, second))


def both_cores(held):
    return jnp.concatenate([held, swap(held, 1)], axis=0)


def local(tokens, output_gradient, value_weight, down_maps, up_maps, adapter_per_block, ranks):
    devices = lax.axis_size("dp")
    members = devices // 2
    lines = members // 2
    steps = members.bit_length() - 1
    num_adapters, extent, width = down_maps.shape
    rows, depth = output_gradient.shape
    place = lax.axis_index("dp").astype(jnp.int32).reshape(1)
    adapters = adapter_per_block
    offsets = [line_offset(slot, members) for slot in range(members)]
    barrier = lax.optimization_barrier

    far = [slot for slot in range(members) if slot % 2]
    near = [slot for slot in range(2, members, 2)]
    quarter = max(1, len(far) // 4)
    portions = [far[at : at + quarter] for at in range(0, len(far), quarter)]
    for number, slot in enumerate(near):
        portions[number % 3] = portions[number % 3] + [slot]

    def send(packs, portion):
        return {slot: swap(packs[slot], offsets[slot]) for slot in portion}

    def taken(pieces, portion):
        return [pieces[slot] for slot in portion]

    own_gradient = output_gradient.reshape(1, rows, depth)
    gradients = [own_gradient] + [None] * (lines - 1)
    for step in range(steps - 1):
        gradients[1 << step] = swap(own_gradient, offsets[1 << step])
    ups, ups_pair = gather_up(adapters, place, up_maps, members)
    ups_other = swap(ups_pair, pair_bit)
    pair = for_pair(adapters, place, value_weight, down_maps, members)
    ups_other, pair = barrier((ups_other, pair))
    pair = swap(pair, pair_bit)
    packs = pack_tokens(place, tokens, members, width)
    gradients[1], ups_other, packs = barrier((gradients[1], ups_other, packs))

    ups = exchange_side(jnp.stack([ups, ups_other], axis=1))
    arrived = {0: packs[0]}
    arrived.update(send(packs, portions[0][:1]))
    for step in range(1, steps - 1):
        for slot in range(1, 1 << step):
            gradients[slot + (1 << step)] = swap(gradients[slot], offsets[1 << step])
    ups, packs, done = barrier((ups, packs, taken(arrived, portions[0][:1])))
    arrived.update(zip(portions[0][:1], done))

    backs = exchange_line(back_rows(adapters, place, ranks, output_gradient, ups))
    arrived.update(send(packs, portions[1][:1]))
    backs, gradients, packs, done = barrier(
        (backs, gradients, packs, taken(arrived, portions[1][:1]))
    )
    arrived.update(zip(portions[1][:1], done))

    backs = both_cores(backs)
    gradients.append(swap(jnp.concatenate(gradients, axis=0), 1))
    for portion in (portions[2], portions[3], portions[0][1:], portions[1][1:]):
        arrived.update(send(packs, portion))
    *slices, columns, columns_pair = input_slices(
        adapters, place, gradients, backs, value_weight, pair, down_maps
    )
    slices, arrived = barrier((slices, taken(arrived, range(members))))

    parts, tokens_own, *tokens_pair = hidden_parts(
        adapters, place, down_maps, pair, arrived
    )
    results = {0: slices[0]}
    results.update(send(slices, portions[0]))
    parts = parts[:lines] + swap(parts[lines:], 1)
    tokens_other = [swap(tokens_pair[0], pair_bit)]
    parts, done, slices, tokens_other, tokens_pair = barrier(
        (parts, taken(results, portions[0]), slices, tokens_other, tokens_pair)
    )
    results.update(zip(portions[0], done))

    results.update(send(slices, portions[1]))
    parts = exchange_line(parts)
    tokens_other.append(swap(tokens_pair[1], pair_bit))
    parts, done, slices, tokens_other, columns_pair = barrier(
        (parts, taken(results, portions[1]), slices, tokens_other, columns_pair)
    )
    results.update(zip(portions[1], done))

    results.update(send(slices, portions[2]))
    hiddens = exchange_line(hidden_rows(adapters, place, ranks, parts))
    columns_other = swap(columns_pair, pair_bit)
    backs_pair = swap(backs, pair_bit)
    hiddens, done, slices, columns_other, backs_pair = barrier(
        (hiddens, taken(results, portions[2]), slices, columns_other, backs_pair)
    )
    results.update(zip(portions[2], done))

    results.update(send(slices, portions[3]))
    hiddens = both_cores(hiddens)
    hiddens_pair = swap(hiddens, pair_bit)
    down_gradient = down_gradients(
        adapters, place, backs, backs_pair, tokens_own, tokens_other, num_adapters
    )
    up_gradient = up_gradients(
        adapters, place, ranks, columns, columns_other, hiddens, hiddens_pair, depth // devices
    )

    def joined(slots, before=None):
        return join_columns(
            place, taken(results, slots), taken(offsets, slots), tokens.shape[1], before
        )

    most = joined([0] + portions[0] + portions[1] + portions[2])
    up_gradient, down_gradient, most = barrier((up_gradient, down_gradient, most))
    input_grad = joined(portions[3], most)
    return (input_grad, down_gradient, up_gradient)


def solution(mesh):
    in_specs = (
        P(("groups", "dp"), None),
        P(("groups", "dp"), None),
        P(None, "dp"),
        P(None, None, "dp"),
        P(None, "dp", None),
        P("groups"),
        P(),
    )
    out_specs = (P(("groups", "dp"), None), P("groups", None, "dp"), P("groups", "dp", None))
    return jax.shard_map(local, mesh=mesh, in_specs=in_specs, out_specs=out_specs, check_vma=False)
```

```python
import functools

import jax
import jax.numpy as jnp
from jax import lax
from jax.experimental import pallas as pl
from jax.experimental.pallas import tpu as pltpu
from jax.sharding import PartitionSpec as P

adapter_alpha = 32.0
vmem_limit = 48 * 1024 * 1024
pair_bit = 2
line_bit = 4


def line_offset(slot, members):
    bits = members.bit_length() - 1
    order = 0
    for bit in range(bits):
        order |= ((slot >> bit) & 1) << (bits - 1 - bit)
    return ((order // 2) * line_bit) | (order % 2)


def entry_of(slot, members):
    offset = line_offset(slot, members)
    return (offset % 2) * (members // 2) + offset // line_bit


def entry_offset(entry, members):
    core, line = divmod(entry, members // 2)
    return line * line_bit ^ core


def params():
    return pltpu.CompilerParams(vmem_limit_bytes=vmem_limit)


def whole(shape):
    return pl.BlockSpec(shape, lambda *_: (0,) * len(shape))


def picked(maps, flip):
    return pl.BlockSpec(
        (1,) + maps.shape[1:], lambda i, adapters, place, *_: (adapters[place[0] ^ flip], 0, 0)
    )


def call(kernel, name, prefetch, operands, in_specs, out_shapes, scratch=(), grid=(1,), out_specs=None):
    if out_specs is None:
        out_specs = [whole(shape.shape) for shape in out_shapes]
    return pl.pallas_call(
        kernel,
        out_shape=out_shapes,
        grid_spec=pltpu.PrefetchScalarGridSpec(
            num_scalar_prefetch=len(prefetch),
            grid=grid,
            in_specs=in_specs,
            out_specs=out_specs,
            scratch_shapes=list(scratch),
        ),
        compiler_params=params(),
        name=name,
    )(*prefetch, *operands)


def run(copies):
    for copy in copies:
        copy.start()
    for copy in copies:
        copy.wait()


def copy_call(kernel, name, prefetch, operands, out_shapes, copies):
    return pl.pallas_call(
        kernel,
        out_shape=out_shapes,
        grid_spec=pltpu.PrefetchScalarGridSpec(
            num_scalar_prefetch=len(prefetch),
            grid=(1,),
            in_specs=[pl.BlockSpec(memory_space=pl.ANY)] * len(operands),
            out_specs=[whole(shape.shape) for shape in out_shapes],
            scratch_shapes=[pltpu.SemaphoreType.DMA((copies,))],
        ),
        compiler_params=params(),
        name=name,
    )(*prefetch, *operands)


weight_cuts = 4


def pair_kernel(adapters, place, weight, down_maps, out, sems):
    extent = down_maps.shape[1]
    depth = weight.shape[0]
    members = (out.shape[0] - depth) // extent
    copies = []
    for slot in range(members):
        block = place[0] ^ line_offset(slot, members) ^ pair_bit
        copies.append((down_maps.at[adapters[block]], slot * extent, extent))
    cut = depth // weight_cuts
    for at in range(0, depth, cut):
        copies.append((weight.at[pl.ds(at, cut)], members * extent + at, cut))
    run(
        [
            pltpu.make_async_copy(source, out.at[pl.ds(at, rows)], sems.at[number])
            for number, (source, at, rows) in enumerate(copies)
        ]
    )


def for_pair(adapters, place, weight, down_maps, members):
    extent, width = down_maps.shape[1:]
    shape = jax.ShapeDtypeStruct((members * extent + weight.shape[0], width), weight.dtype)
    return copy_call(
        pair_kernel,
        "for_pair",
        (adapters, place),
        (weight, down_maps),
        [shape],
        members + weight_cuts,
    )[0]


def gather_up_kernel(adapters, place, up_maps, own, pair, sems):
    members = own.shape[0]
    copies = []
    for index in range(members):
        block = (index // 2) * line_bit + place[0] % line_bit // pair_bit * pair_bit + index % 2
        for side, out in enumerate((own, pair)):
            source = up_maps.at[adapters[block ^ (side * pair_bit)]]
            copies.append(
                pltpu.make_async_copy(source, out.at[index], sems.at[2 * index + side])
            )
    run(copies)


def gather_up(adapters, place, up_maps, members):
    shape = jax.ShapeDtypeStruct((members,) + up_maps.shape[1:], up_maps.dtype)
    return copy_call(
        gather_up_kernel, "gather_up", (adapters, place), (up_maps,), [shape] * 2, 2 * members
    )


def pack_kernel(place, tokens, *refs, flips):
    outs, sems = refs[:-1], refs[-1]
    width = outs[0].shape[2]
    copies = []
    for number, out in enumerate(outs):
        for half in range(2):
            column = (place[0] ^ flips[number] ^ (half * pair_bit)) * width
            copies.append(
                pltpu.make_async_copy(
                    tokens.at[:, pl.ds(pl.multiple_of(column, width), width)],
                    out.at[half],
                    sems.at[2 * number + half],
                )
            )
    run(copies)


def pack_tokens(place, tokens, flips, width):
    shape = jax.ShapeDtypeStruct((2, tokens.shape[0], width), tokens.dtype)
    return copy_call(
        functools.partial(pack_kernel, flips=flips),
        "pack_tokens",
        (place,),
        (tokens,),
        [shape] * len(flips),
        2 * len(flips),
    )


def rank_row(ranks, adapter, extent):
    rank = jnp.full((1, extent), ranks[adapter], jnp.int32)
    alive = (lax.broadcasted_iota(jnp.int32, (1, extent), 1) < rank).astype(jnp.float32)
    return alive, adapter_alpha / rank.astype(jnp.float32)


def back_kernel(adapters, place, ranks, gradient, ups, out, up):
    members, _, value_width, extent = ups.shape
    side = place[0] % line_bit // pair_bit
    for index in range(members):
        for half in range(2):
            owner = (index // 2) * line_bit + (side ^ half) * pair_bit + index % 2
            rows = pl.ds(pl.multiple_of(owner * value_width, value_width), value_width)
            up[rows, :] = ups[index, half]
    alive, factor = rank_row(ranks, adapters[place[0]], extent)
    back = jnp.dot(gradient[...], up[...], preferred_element_type=jnp.float32)
    out[0] = (factor * back * alive).astype(out.dtype)


def back_rows(adapters, place, ranks, gradient, ups):
    _, _, _, extent = ups.shape
    rows, depth = gradient.shape
    return call(
        back_kernel,
        "back_low",
        (adapters, place, ranks),
        (gradient, ups),
        [whole(gradient.shape), whole(ups.shape)],
        [jax.ShapeDtypeStruct((1, rows, extent), jnp.bfloat16)],
        scratch=[pltpu.VMEM((depth, extent), jnp.bfloat16)],
    )[0]


def input_kernel(adapters, place, backs, pair, *refs):
    members, rows, _ = backs.shape
    apart = members // 2
    gradients = [ref.at[0] for ref in refs[:apart]]
    gradients += [refs[apart].at[slot] for slot in range(members - apart)]
    downs = refs[apart + 1 : apart + 1 + members]
    weight = refs[apart + 1 + members]
    outs, columns = refs[apart + 2 + members : -2], refs[-2:]
    extent = downs[0].shape[1]
    lanes = columns[0].shape[2]
    value_width = gradients[0].shape[1] // (2 * members)
    some = min(4, members)
    for first in range(0, members, some):
        slots = range(first, first + some)
        lines = jnp.concatenate([gradients[slot][...] for slot in slots], axis=0)
        for half in range(2):
            right = weight[...] if half == 0 else pair[members * extent :]
            frozen = jnp.dot(lines, right, preferred_element_type=jnp.float32)
            for slot in slots:
                down = downs[slot][0] if half == 0 else pair[slot * extent : (slot + 1) * extent]
                entry = entry_of(slot, members)
                low = jnp.dot(backs[entry], down, preferred_element_type=jnp.float32)
                at = (slot - first) * rows
                outs[slot][half] = (frozen[at : at + rows] + low).astype(jnp.bfloat16)
    for side in range(2):
        column = (place[0] ^ (side * pair_bit)) * value_width // lanes * lanes
        for slot in range(members):
            entry = entry_of(slot, members)
            columns[side][entry] = gradients[slot][:, pl.ds(pl.multiple_of(column, lanes), lanes)]


def input_slices(adapters, place, gradients, backs, weight, pair, down_maps):
    members, rows, _ = backs.shape
    width = weight.shape[1]
    lanes = max(128, gradients[0].shape[2] // (2 * members))
    shape = jax.ShapeDtypeStruct((2, rows, width), jnp.bfloat16)
    columns = jax.ShapeDtypeStruct((members, rows, lanes), jnp.bfloat16)
    return call(
        input_kernel,
        "input_slices",
        (adapters, place),
        [backs, pair] + list(gradients) + [down_maps] * members + [weight],
        [whole(backs.shape), whole(pair.shape)]
        + [whole(gradient.shape) for gradient in gradients]
        + [picked(down_maps, line_offset(slot, members)) for slot in range(members)]
        + [whole(weight.shape)],
        [shape] * members + [columns] * 2,
    )


def hidden_kernel(adapters, place, pair, *refs):
    parts, own, *others = refs[-4:]
    members = own.shape[0]
    downs, tokens = refs[:members], refs[members : 2 * members]
    extent = downs[0].shape[1]
    across = (((1,), (1,)), ((), ()))
    for slot in range(members):
        entry = entry_of(slot, members)
        own[entry] = tokens[slot][0]
        core = line_offset(slot, members) % 2
        others[core][entry - core * (members // 2)] = tokens[slot][1]
        parts[entry] = lax.dot_general(
            tokens[slot][0], downs[slot][0], across, preferred_element_type=jnp.float32
        ) + lax.dot_general(
            tokens[slot][1],
            pair[slot * extent : (slot + 1) * extent],
            across,
            preferred_element_type=jnp.float32,
        )


def hidden_parts(adapters, place, down_maps, pair, tokens):
    members = len(tokens)
    _, rows, width = tokens[0].shape
    extent = down_maps.shape[1]
    others = jax.ShapeDtypeStruct((members // 2, rows, width), tokens[0].dtype)
    return call(
        hidden_kernel,
        "hidden_parts",
        (adapters, place),
        [pair] + [down_maps] * members + list(tokens),
        [whole(pair.shape)]
        + [picked(down_maps, line_offset(slot, members)) for slot in range(members)]
        + [whole(tokens[0].shape)] * members,
        [
            jax.ShapeDtypeStruct((members, rows, extent), jnp.float32),
            jax.ShapeDtypeStruct((members, rows, width), tokens[0].dtype),
            others,
            others,
        ],
    )


def core_sum_kernel(parts, received, *outs):
    for line, out in enumerate(outs):
        out[0] = parts[line] + received[line]


def core_sums(parts, received):
    lines, rows, extent = received.shape
    shape = jax.ShapeDtypeStruct((1, rows, extent), jnp.float32)
    return call(
        core_sum_kernel,
        "core_sums",
        (),
        (parts, received),
        [whole(received.shape)] * 2,
        [shape] * lines,
    )


def hidden_low_kernel(adapters, place, ranks, *refs):
    out = refs[-1]
    alive, _ = rank_row(ranks, adapters[place[0]], out.shape[2])
    total = refs[0][0]
    for part in refs[1:-1]:
        total += part[0]
    out[0] = (total * alive).astype(out.dtype)


def hidden_rows(adapters, place, ranks, parts):
    return call(
        hidden_low_kernel,
        "hidden_low",
        (adapters, place, ranks),
        parts,
        [whole(part.shape) for part in parts],
        [jax.ShapeDtypeStruct(parts[0].shape, jnp.bfloat16)],
    )[0]


def join_kernel(place, *refs, offsets, aliased):
    pieces = refs[: len(offsets)]
    out, sems = refs[len(offsets) + aliased :]
    width = pieces[0].shape[2]
    copies = []
    for entry, offset in enumerate(offsets):
        for half in range(2):
            column = (place[0] ^ offset ^ (half * pair_bit)) * width
            copies.append(
                pltpu.make_async_copy(
                    pieces[entry].at[half],
                    out.at[:, pl.ds(pl.multiple_of(column, width), width)],
                    sems.at[2 * entry + half],
                )
            )
    run(copies)


def join_columns(place, pieces, offsets, columns, before=None):
    rows = pieces[0].shape[1]
    rest = [] if before is None else [before]
    return pl.pallas_call(
        functools.partial(join_kernel, offsets=offsets, aliased=len(rest)),
        out_shape=jax.ShapeDtypeStruct((rows, columns), pieces[0].dtype),
        grid_spec=pltpu.PrefetchScalarGridSpec(
            num_scalar_prefetch=1,
            grid=(1,),
            in_specs=[whole(piece.shape) for piece in pieces]
            + [pl.BlockSpec(memory_space=pl.ANY)] * len(rest),
            out_specs=pl.BlockSpec(memory_space=pltpu.HBM),
            scratch_shapes=[pltpu.SemaphoreType.DMA((2 * len(pieces),))],
        ),
        input_output_aliases={1 + len(pieces): 0} if rest else {},
        compiler_params=params(),
        name="join_columns",
    )(place, *pieces, *rest)


def list_members(adapters, place, members, head, following):
    def clear(adapter, carry):
        head[adapter] = -1
        return carry

    lax.fori_loop(0, head.shape[0], clear, 0)
    for entry in reversed(range(2 * members)):
        side, own = divmod(entry, members)
        adapter = adapters[place[0] ^ entry_offset(own, members) ^ (side * pair_bit)]
        following[entry] = head[adapter]
        head[adapter] = entry


def write_sums(head, following, products, ready, zero, out, sems, finish):
    num_adapters = out.shape[0]
    zero[...] = jnp.zeros_like(zero)

    def write(adapter, carry):
        first = head[adapter]

        @pl.when(first < 0)
        def _():
            pltpu.make_async_copy(zero, out.at[adapter], sems.at[adapter]).start()

        @pl.when(first >= 0)
        def _():
            def more(entry):
                products[first] += products[entry]
                return following[entry]

            lax.while_loop(lambda entry: entry >= 0, more, following[first])
            ready[first] = finish(adapter, products[first]).astype(out.dtype)
            pltpu.make_async_copy(ready.at[first], out.at[adapter], sems.at[adapter]).start()

        return carry

    lax.fori_loop(0, num_adapters, write, 0)

    def wait(adapter, carry):
        pltpu.make_async_copy(zero, out.at[adapter], sems.at[adapter]).wait()
        return carry

    lax.fori_loop(0, num_adapters, wait, 0)


def by_rows(left, right):
    return lax.dot_general(
        left, right, (((0,), (0,)), ((), ())), preferred_element_type=jnp.float32
    )


def sums_call(kernel, name, prefetch, operands, num_adapters, entries, product, scratch=()):
    return pl.pallas_call(
        kernel,
        out_shape=jax.ShapeDtypeStruct((num_adapters,) + product, jnp.bfloat16),
        grid_spec=pltpu.PrefetchScalarGridSpec(
            num_scalar_prefetch=len(prefetch),
            grid=(1,),
            in_specs=[whole(operand.shape) for operand in operands],
            out_specs=pl.BlockSpec(memory_space=pltpu.HBM),
            scratch_shapes=[
                pltpu.SMEM((num_adapters,), jnp.int32),
                pltpu.SMEM((entries,), jnp.int32),
                pltpu.VMEM((entries,) + product, jnp.float32),
                pltpu.VMEM((entries,) + product, jnp.bfloat16),
                pltpu.VMEM(product, jnp.bfloat16),
                pltpu.SemaphoreType.DMA((num_adapters,)),
                *scratch,
            ],
        ),
        compiler_params=params(),
        name=name,
    )(*prefetch, *operands)


def down_gradient_kernel(
    adapters,
    place,
    backs,
    backs_pair,
    own,
    other_first,
    other_second,
    out,
    head,
    following,
    products,
    ready,
    zero,
    sems,
):
    members = own.shape[0]
    others = (other_first, other_second)
    list_members(adapters, place, members, head, following)
    for slot in range(members):
        products[slot] = by_rows(backs[slot], own[slot])
        core, line = divmod(slot, members // 2)
        products[members + slot] = by_rows(backs_pair[slot], others[core][line])
    write_sums(
        head, following, products, ready, zero, out, sems, lambda adapter, total: total
    )


def down_gradients(adapters, place, backs, backs_pair, own, others, num_adapters):
    members, _, width = own.shape
    return sums_call(
        down_gradient_kernel,
        "down_gradients",
        (adapters, place),
        (backs, backs_pair, own, *others),
        num_adapters,
        2 * members,
        (backs.shape[2], width),
    )


def up_gradient_kernel(
    adapters,
    place,
    ranks,
    gradients,
    gradients_pair,
    hiddens,
    hiddens_pair,
    out,
    head,
    following,
    products,
    ready,
    zero,
    sems,
    lines,
):
    members, _, lanes = gradients.shape
    width, extent = out.shape[1:]
    list_members(adapters, place, members, head, following)
    inside = pl.multiple_of(lax.rem(place[0], lanes // width) * width, width)
    for slot in range(members):
        lines[slot] = by_rows(gradients[slot], hiddens[slot])
        lines[members + slot] = by_rows(gradients_pair[slot], hiddens_pair[slot])
    for entry in range(2 * members):
        products[entry] = lines[entry, pl.ds(inside, width), :]

    def finish(adapter, total):
        _, factor = rank_row(ranks, adapter, extent)
        return factor * total

    write_sums(head, following, products, ready, zero, out, sems, finish)


def up_gradients(adapters, place, ranks, gradients, gradients_pair, hiddens, hiddens_pair, width):
    members, _, lanes = gradients.shape
    extent = hiddens.shape[2]
    return sums_call(
        up_gradient_kernel,
        "up_gradients",
        (adapters, place, ranks),
        (gradients, gradients_pair, hiddens, hiddens_pair),
        ranks.shape[0],
        2 * members,
        (width, extent),
        [pltpu.VMEM((2 * members, lanes, extent), jnp.float32)],
    )


def exchange(pieces, groups):
    return lax.all_to_all(
        pieces, "dp", split_axis=0, concat_axis=0, axis_index_groups=groups, tiled=True
    )


def exchange_side(pieces):
    members = pieces.shape[0]
    groups = [
        [(index // 2) * line_bit + side * pair_bit + index % 2 for index in range(members)]
        for side in range(2)
    ]
    return exchange(pieces, groups)


def swap(array, flip):
    devices = lax.axis_size("dp")
    return lax.ppermute(array, "dp", [(i, i ^ flip) for i in range(devices)])


def tie(first, second):
    return lax.optimization_barrier((first, second))


def along_line(pieces):
    return [pieces[0]] + [
        swap(piece, line * line_bit) for line, piece in enumerate(pieces) if line
    ]


def both_cores(held):
    return jnp.concatenate([held, swap(held, 1)], axis=0)


def local(tokens, output_gradient, value_weight, down_maps, up_maps, adapter_per_block, ranks):
    devices = lax.axis_size("dp")
    members = devices // 2
    lines = members // 2
    steps = members.bit_length() - 1
    num_adapters, extent, width = down_maps.shape
    rows, depth = output_gradient.shape
    place = lax.axis_index("dp").astype(jnp.int32).reshape(1)
    adapters = adapter_per_block
    offsets = [line_offset(slot, members) for slot in range(members)]
    barrier = lax.optimization_barrier

    far = [slot for slot in range(members) if slot % 2]
    near = [slot for slot in range(2, members, 2)]
    quarter = max(1, len(far) // 4)
    portions = [far[at : at + quarter] for at in range(0, len(far), quarter)]
    for number, slot in enumerate(near):
        portions[1 + number % 2] = portions[1 + number % 2] + [slot]

    def send(packs, portion):
        return {slot: swap(packs[slot], offsets[slot]) for slot in portion}

    def taken(pieces, portion):
        return [pieces[slot] for slot in portion]

    own_gradient = output_gradient.reshape(1, rows, depth)
    gradients = [own_gradient] + [None] * (lines - 1)
    for step in range(steps - 1):
        gradients[1 << step] = swap(own_gradient, offsets[1 << step])
    ups, ups_pair = gather_up(adapters, place, up_maps, members)
    ups_other = swap(ups_pair, pair_bit)
    pair = for_pair(adapters, place, value_weight, down_maps, members)
    ups_other, pair = barrier((ups_other, pair))
    pair = swap(pair, pair_bit)
    packs = dict(zip(portions[0], pack_tokens(place, tokens, taken(offsets, portions[0]), width)))
    gradients[1], ups_other, packs = barrier((gradients[1], ups_other, packs))

    ups = exchange_side(jnp.stack([ups, ups_other], axis=1))
    arrived = send(packs, portions[0])
    for step in range(1, steps - 1):
        for slot in range(1, 1 << step):
            gradients[slot + (1 << step)] = swap(gradients[slot], offsets[1 << step])
    ups, tokens, done = barrier((ups, tokens, taken(arrived, portions[0])))
    arrived.update(zip(portions[0], done))

    rest = [slot for slot in range(members) if slot not in portions[0]]
    packs = dict(zip(rest, pack_tokens(place, tokens, taken(offsets, rest), width)))
    arrived[0] = packs[0]
    backs = back_rows(adapters, place, ranks, output_gradient, ups)
    backs = along_line([backs] * lines)
    arrived.update(send(packs, portions[1]))
    backs, gradients, packs, done = barrier(
        (backs, gradients, packs, taken(arrived, portions[1]))
    )
    arrived.update(zip(portions[1], done))

    backs = both_cores(jnp.concatenate(backs, axis=0))
    gradients.append(swap(jnp.concatenate(gradients, axis=0), 1))
    for portion in portions[2:]:
        arrived.update(send(packs, portion))
    *slices, columns, columns_pair = input_slices(
        adapters, place, gradients, backs, value_weight, pair, down_maps
    )
    slices, arrived = barrier((slices, taken(arrived, range(members))))

    parts, tokens_own, *tokens_pair = hidden_parts(
        adapters, place, down_maps, pair, arrived
    )
    results = {0: slices[0]}
    results.update(send(slices, portions[0]))
    parts = core_sums(parts, swap(parts[lines:], 1))
    tokens_other = [swap(tokens_pair[0], pair_bit)]
    parts, done, slices, tokens_other, tokens_pair = barrier(
        (parts, taken(results, portions[0]), slices, tokens_other, tokens_pair)
    )
    results.update(zip(portions[0], done))

    results.update(send(slices, portions[1]))
    parts = along_line(parts)
    tokens_other.append(swap(tokens_pair[1], pair_bit))
    parts, done, slices, tokens_other, columns_pair = barrier(
        (parts, taken(results, portions[1]), slices, tokens_other, columns_pair)
    )
    results.update(zip(portions[1], done))

    results.update(send(slices, portions[2]))
    hiddens = along_line([hidden_rows(adapters, place, ranks, parts)] * lines)
    columns_other = swap(columns_pair, pair_bit)
    backs_pair = swap(backs, pair_bit)
    hiddens, done, slices, columns_other, backs_pair = barrier(
        (hiddens, taken(results, portions[2]), slices, columns_other, backs_pair)
    )
    results.update(zip(portions[2], done))

    results.update(send(slices, portions[3]))
    hiddens = both_cores(jnp.concatenate(hiddens, axis=0))
    hiddens_pair = swap(hiddens, pair_bit)
    down_gradient = down_gradients(
        adapters, place, backs, backs_pair, tokens_own, tokens_other, num_adapters
    )
    up_gradient = up_gradients(
        adapters, place, ranks, columns, columns_other, hiddens, hiddens_pair, depth // devices
    )

    def joined(slots, before=None):
        return join_columns(
            place, taken(results, slots), taken(offsets, slots), tokens.shape[1], before
        )

    most = joined([0] + portions[0] + portions[1] + portions[2])
    up_gradient, down_gradient, most = barrier((up_gradient, down_gradient, most))
    input_grad = joined(portions[3], most)
    return (input_grad, down_gradient, up_gradient)


def solution(mesh):
    in_specs = (
        P(("groups", "dp"), None),
        P(("groups", "dp"), None),
        P(None, "dp"),
        P(None, None, "dp"),
        P(None, "dp", None),
        P("groups"),
        P(),
    )
    out_specs = (P(("groups", "dp"), None), P("groups", None, "dp"), P("groups", "dp", None))
    return jax.shard_map(local, mesh=mesh, in_specs=in_specs, out_specs=out_specs, check_vma=False)
```

```python
import functools

import jax
import jax.numpy as jnp
from jax import lax
from jax.experimental import pallas as pl
from jax.experimental.pallas import tpu as pltpu
from jax.sharding import PartitionSpec as P

adapter_alpha = 32.0
vmem_limit = 48 * 1024 * 1024
pair_bit = 2
line_bit = 4


def line_offset(slot, members):
    bits = members.bit_length() - 1
    order = 0
    for bit in range(bits):
        order |= ((slot >> bit) & 1) << (bits - 1 - bit)
    return ((order // 2) * line_bit) | (order % 2)


def entry_of(place, slot, members):
    offset = line_offset(slot, members)
    return (offset % 2) * (members // 2) + ((place ^ offset) // line_bit)


def place_of(entry, place, side, members):
    core, line = divmod(entry, members // 2)
    return line * line_bit + ((place % line_bit) ^ core ^ (side * pair_bit))


def params():
    return pltpu.CompilerParams(vmem_limit_bytes=vmem_limit)


def whole(shape):
    return pl.BlockSpec(shape, lambda *_: (0,) * len(shape))


def picked(maps, flip):
    return pl.BlockSpec(
        (1,) + maps.shape[1:], lambda i, adapters, place, *_: (adapters[place[0] ^ flip], 0, 0)
    )


def call(kernel, name, prefetch, operands, in_specs, out_shapes, scratch=(), grid=(1,), out_specs=None):
    if out_specs is None:
        out_specs = [whole(shape.shape) for shape in out_shapes]
    return pl.pallas_call(
        kernel,
        out_shape=out_shapes,
        grid_spec=pltpu.PrefetchScalarGridSpec(
            num_scalar_prefetch=len(prefetch),
            grid=grid,
            in_specs=in_specs,
            out_specs=out_specs,
            scratch_shapes=list(scratch),
        ),
        compiler_params=params(),
        name=name,
    )(*prefetch, *operands)


def run(copies):
    for copy in copies:
        copy.start()
    for copy in copies:
        copy.wait()


def copy_call(kernel, name, prefetch, operands, out_shapes, copies):
    return pl.pallas_call(
        kernel,
        out_shape=out_shapes,
        grid_spec=pltpu.PrefetchScalarGridSpec(
            num_scalar_prefetch=len(prefetch),
            grid=(1,),
            in_specs=[pl.BlockSpec(memory_space=pl.ANY)] * len(operands),
            out_specs=[whole(shape.shape) for shape in out_shapes],
            scratch_shapes=[pltpu.SemaphoreType.DMA((copies,))],
        ),
        compiler_params=params(),
        name=name,
    )(*prefetch, *operands)


weight_cuts = 4


def pair_kernel(adapters, place, weight, down_maps, out, sems):
    extent = down_maps.shape[1]
    depth = weight.shape[0]
    members = (out.shape[0] - depth) // extent
    copies = []
    for slot in range(members):
        block = place[0] ^ line_offset(slot, members) ^ pair_bit
        copies.append((down_maps.at[adapters[block]], slot * extent, extent))
    cut = depth // weight_cuts
    for at in range(0, depth, cut):
        copies.append((weight.at[pl.ds(at, cut)], members * extent + at, cut))
    run(
        [
            pltpu.make_async_copy(source, out.at[pl.ds(at, rows)], sems.at[number])
            for number, (source, at, rows) in enumerate(copies)
        ]
    )


def for_pair(adapters, place, weight, down_maps, members):
    extent, width = down_maps.shape[1:]
    shape = jax.ShapeDtypeStruct((members * extent + weight.shape[0], width), weight.dtype)
    return copy_call(
        pair_kernel,
        "for_pair",
        (adapters, place),
        (weight, down_maps),
        [shape],
        members + weight_cuts,
    )[0]


def gather_up_kernel(adapters, place, up_maps, own, pair, sems):
    members = own.shape[0]
    copies = []
    for index in range(members):
        block = (index // 2) * line_bit + place[0] % line_bit // pair_bit * pair_bit + index % 2
        for side, out in enumerate((own, pair)):
            source = up_maps.at[adapters[block ^ (side * pair_bit)]]
            copies.append(
                pltpu.make_async_copy(source, out.at[index], sems.at[2 * index + side])
            )
    run(copies)


def gather_up(adapters, place, up_maps, members):
    shape = jax.ShapeDtypeStruct((members,) + up_maps.shape[1:], up_maps.dtype)
    return copy_call(
        gather_up_kernel, "gather_up", (adapters, place), (up_maps,), [shape] * 2, 2 * members
    )


def pack_kernel(place, tokens, *refs, flips):
    outs, sems = refs[:-1], refs[-1]
    width = outs[0].shape[2]
    copies = []
    for number, out in enumerate(outs):
        for half in range(2):
            column = (place[0] ^ flips[number] ^ (half * pair_bit)) * width
            copies.append(
                pltpu.make_async_copy(
                    tokens.at[:, pl.ds(pl.multiple_of(column, width), width)],
                    out.at[half],
                    sems.at[2 * number + half],
                )
            )
    run(copies)


def pack_tokens(place, tokens, flips, width):
    shape = jax.ShapeDtypeStruct((2, tokens.shape[0], width), tokens.dtype)
    return copy_call(
        functools.partial(pack_kernel, flips=flips),
        "pack_tokens",
        (place,),
        (tokens,),
        [shape] * len(flips),
        2 * len(flips),
    )


def rank_row(ranks, adapter, extent):
    rank = jnp.full((1, extent), ranks[adapter], jnp.int32)
    alive = (lax.broadcasted_iota(jnp.int32, (1, extent), 1) < rank).astype(jnp.float32)
    return alive, adapter_alpha / rank.astype(jnp.float32)


def back_kernel(adapters, place, ranks, gradient, ups, out, up):
    members, _, value_width, extent = ups.shape
    side = place[0] % line_bit // pair_bit
    for index in range(members):
        for half in range(2):
            owner = (index // 2) * line_bit + (side ^ half) * pair_bit + index % 2
            rows = pl.ds(pl.multiple_of(owner * value_width, value_width), value_width)
            up[rows, :] = ups[index, half]
    alive, factor = rank_row(ranks, adapters[place[0]], extent)
    back = jnp.dot(gradient[...], up[...], preferred_element_type=jnp.float32)
    low = (factor * back * alive).astype(out.dtype)
    for line in range(out.shape[0]):
        out[line] = low


def back_rows(adapters, place, ranks, gradient, ups):
    members, _, _, extent = ups.shape
    rows, depth = gradient.shape
    return call(
        back_kernel,
        "back_low",
        (adapters, place, ranks),
        (gradient, ups),
        [whole(gradient.shape), whole(ups.shape)],
        [jax.ShapeDtypeStruct((members // 2, rows, extent), jnp.bfloat16)],
        scratch=[pltpu.VMEM((depth, extent), jnp.bfloat16)],
    )[0]


def input_kernel(adapters, place, backs, pair, *refs):
    members, rows, _ = backs.shape
    apart = members // 2
    gradients = [ref.at[0] for ref in refs[:apart]]
    gradients += [refs[apart].at[slot] for slot in range(members - apart)]
    downs = refs[apart + 1 : apart + 1 + members]
    weight = refs[apart + 1 + members]
    outs, columns = refs[apart + 2 + members : -2], refs[-2:]
    extent = downs[0].shape[1]
    lanes = columns[0].shape[2]
    value_width = gradients[0].shape[1] // (2 * members)
    some = min(4, members)
    for first in range(0, members, some):
        slots = range(first, first + some)
        lines = jnp.concatenate([gradients[slot][...] for slot in slots], axis=0)
        for half in range(2):
            right = weight[...] if half == 0 else pair[members * extent :]
            frozen = jnp.dot(lines, right, preferred_element_type=jnp.float32)
            for slot in slots:
                down = downs[slot][0] if half == 0 else pair[slot * extent : (slot + 1) * extent]
                entry = entry_of(place[0], slot, members)
                low = jnp.dot(backs[entry], down, preferred_element_type=jnp.float32)
                at = (slot - first) * rows
                outs[slot][half] = (frozen[at : at + rows] + low).astype(jnp.bfloat16)
    for side in range(2):
        column = (place[0] ^ (side * pair_bit)) * value_width // lanes * lanes
        for slot in range(members):
            entry = entry_of(place[0], slot, members)
            columns[side][entry] = gradients[slot][:, pl.ds(pl.multiple_of(column, lanes), lanes)]


def input_slices(adapters, place, gradients, backs, weight, pair, down_maps):
    members, rows, _ = backs.shape
    width = weight.shape[1]
    lanes = max(128, gradients[0].shape[2] // (2 * members))
    shape = jax.ShapeDtypeStruct((2, rows, width), jnp.bfloat16)
    columns = jax.ShapeDtypeStruct((members, rows, lanes), jnp.bfloat16)
    return call(
        input_kernel,
        "input_slices",
        (adapters, place),
        [backs, pair] + list(gradients) + [down_maps] * members + [weight],
        [whole(backs.shape), whole(pair.shape)]
        + [whole(gradient.shape) for gradient in gradients]
        + [picked(down_maps, line_offset(slot, members)) for slot in range(members)]
        + [whole(weight.shape)],
        [shape] * members + [columns] * 2,
    )


def hidden_kernel(adapters, place, pair, *refs):
    parts, own, other = refs[-3:]
    members = own.shape[0]
    downs, tokens = refs[:members], refs[members : 2 * members]
    extent = downs[0].shape[1]
    across = (((1,), (1,)), ((), ()))
    for slot in range(members):
        entry = entry_of(place[0], slot, members)
        own[entry] = tokens[slot][0]
        other[entry] = tokens[slot][1]
        parts[entry] = lax.dot_general(
            tokens[slot][0], downs[slot][0], across, preferred_element_type=jnp.float32
        ) + lax.dot_general(
            tokens[slot][1],
            pair[slot * extent : (slot + 1) * extent],
            across,
            preferred_element_type=jnp.float32,
        )


def hidden_parts(adapters, place, down_maps, pair, tokens):
    members = len(tokens)
    _, rows, width = tokens[0].shape
    extent = down_maps.shape[1]
    tokens_shape = jax.ShapeDtypeStruct((members, rows, width), tokens[0].dtype)
    return call(
        hidden_kernel,
        "hidden_parts",
        (adapters, place),
        [pair] + [down_maps] * members + list(tokens),
        [whole(pair.shape)]
        + [picked(down_maps, line_offset(slot, members)) for slot in range(members)]
        + [whole(tokens[0].shape)] * members,
        [
            jax.ShapeDtypeStruct((members, rows, extent), jnp.float32),
            tokens_shape,
            tokens_shape,
        ],
    )


def hidden_low_kernel(adapters, place, ranks, parts, out):
    alive, _ = rank_row(ranks, adapters[place[0]], out.shape[2])
    total = parts[0]
    for line in range(1, parts.shape[0]):
        total += parts[line]
    low = (total * alive).astype(out.dtype)
    for line in range(out.shape[0]):
        out[line] = low


def hidden_rows(adapters, place, ranks, parts):
    return call(
        hidden_low_kernel,
        "hidden_low",
        (adapters, place, ranks),
        (parts,),
        [whole(parts.shape)],
        [jax.ShapeDtypeStruct(parts.shape, jnp.bfloat16)],
    )[0]


def join_kernel(place, *refs, offsets, aliased):
    pieces = refs[: len(offsets)]
    out, sems = refs[len(offsets) + aliased :]
    width = pieces[0].shape[2]
    copies = []
    for entry, offset in enumerate(offsets):
        for half in range(2):
            column = (place[0] ^ offset ^ (half * pair_bit)) * width
            copies.append(
                pltpu.make_async_copy(
                    pieces[entry].at[half],
                    out.at[:, pl.ds(pl.multiple_of(column, width), width)],
                    sems.at[2 * entry + half],
                )
            )
    run(copies)


def join_columns(place, pieces, offsets, columns, before=None):
    rows = pieces[0].shape[1]
    rest = [] if before is None else [before]
    return pl.pallas_call(
        functools.partial(join_kernel, offsets=offsets, aliased=len(rest)),
        out_shape=jax.ShapeDtypeStruct((rows, columns), pieces[0].dtype),
        grid_spec=pltpu.PrefetchScalarGridSpec(
            num_scalar_prefetch=1,
            grid=(1,),
            in_specs=[whole(piece.shape) for piece in pieces]
            + [pl.BlockSpec(memory_space=pl.ANY)] * len(rest),
            out_specs=pl.BlockSpec(memory_space=pltpu.HBM),
            scratch_shapes=[pltpu.SemaphoreType.DMA((2 * len(pieces),))],
        ),
        input_output_aliases={1 + len(pieces): 0} if rest else {},
        compiler_params=params(),
        name="join_columns",
    )(place, *pieces, *rest)


def list_members(adapters, place, members, head, following):
    def clear(adapter, carry):
        head[adapter] = -1
        return carry

    lax.fori_loop(0, head.shape[0], clear, 0)
    for entry in reversed(range(2 * members)):
        side, own = divmod(entry, members)
        adapter = adapters[place_of(own, place[0], side, members)]
        following[entry] = head[adapter]
        head[adapter] = entry


def write_sums(head, following, products, ready, zero, out, sems, finish):
    num_adapters = out.shape[0]
    zero[...] = jnp.zeros_like(zero)

    def write(adapter, carry):
        first = head[adapter]

        @pl.when(first < 0)
        def _():
            pltpu.make_async_copy(zero, out.at[adapter], sems.at[adapter]).start()

        @pl.when(first >= 0)
        def _():
            def more(entry):
                products[first] += products[entry]
                return following[entry]

            lax.while_loop(lambda entry: entry >= 0, more, following[first])
            ready[first] = finish(adapter, products[first]).astype(out.dtype)
            pltpu.make_async_copy(ready.at[first], out.at[adapter], sems.at[adapter]).start()

        return carry

    lax.fori_loop(0, num_adapters, write, 0)

    def wait(adapter, carry):
        pltpu.make_async_copy(zero, out.at[adapter], sems.at[adapter]).wait()
        return carry

    lax.fori_loop(0, num_adapters, wait, 0)


def by_rows(left, right):
    return lax.dot_general(
        left, right, (((0,), (0,)), ((), ())), preferred_element_type=jnp.float32
    )


def sums_call(kernel, name, prefetch, operands, num_adapters, entries, product, scratch=()):
    return pl.pallas_call(
        kernel,
        out_shape=jax.ShapeDtypeStruct((num_adapters,) + product, jnp.bfloat16),
        grid_spec=pltpu.PrefetchScalarGridSpec(
            num_scalar_prefetch=len(prefetch),
            grid=(1,),
            in_specs=[whole(operand.shape) for operand in operands],
            out_specs=pl.BlockSpec(memory_space=pltpu.HBM),
            scratch_shapes=[
                pltpu.SMEM((num_adapters,), jnp.int32),
                pltpu.SMEM((entries,), jnp.int32),
                pltpu.VMEM((entries,) + product, jnp.float32),
                pltpu.VMEM((entries,) + product, jnp.bfloat16),
                pltpu.VMEM(product, jnp.bfloat16),
                pltpu.SemaphoreType.DMA((num_adapters,)),
                *scratch,
            ],
        ),
        compiler_params=params(),
        name=name,
    )(*prefetch, *operands)


def down_gradient_kernel(
    adapters, place, backs, backs_pair, own, other, out, head, following, products, ready, zero, sems
):
    members = own.shape[0]
    list_members(adapters, place, members, head, following)
    for slot in range(members):
        products[slot] = by_rows(backs[slot], own[slot])
        products[members + slot] = by_rows(backs_pair[slot], other[slot])
    write_sums(
        head, following, products, ready, zero, out, sems, lambda adapter, total: total
    )


def down_gradients(adapters, place, backs, backs_pair, own, other, num_adapters):
    members, _, width = own.shape
    return sums_call(
        down_gradient_kernel,
        "down_gradients",
        (adapters, place),
        (backs, backs_pair, own, other),
        num_adapters,
        2 * members,
        (backs.shape[2], width),
    )


def up_gradient_kernel(
    adapters,
    place,
    ranks,
    gradients,
    gradients_pair,
    hiddens,
    hiddens_pair,
    out,
    head,
    following,
    products,
    ready,
    zero,
    sems,
    lines,
):
    members, _, lanes = gradients.shape
    width, extent = out.shape[1:]
    list_members(adapters, place, members, head, following)
    inside = pl.multiple_of(lax.rem(place[0], lanes // width) * width, width)
    for slot in range(members):
        lines[slot] = by_rows(gradients[slot], hiddens[slot])
        lines[members + slot] = by_rows(gradients_pair[slot], hiddens_pair[slot])
    for entry in range(2 * members):
        products[entry] = lines[entry, pl.ds(inside, width), :]

    def finish(adapter, total):
        _, factor = rank_row(ranks, adapter, extent)
        return factor * total

    write_sums(head, following, products, ready, zero, out, sems, finish)


def up_gradients(adapters, place, ranks, gradients, gradients_pair, hiddens, hiddens_pair, width):
    members, _, lanes = gradients.shape
    extent = hiddens.shape[2]
    return sums_call(
        up_gradient_kernel,
        "up_gradients",
        (adapters, place, ranks),
        (gradients, gradients_pair, hiddens, hiddens_pair),
        ranks.shape[0],
        2 * members,
        (width, extent),
        [pltpu.VMEM((2 * members, lanes, extent), jnp.float32)],
    )


def exchange(pieces, groups):
    return lax.all_to_all(
        pieces, "dp", split_axis=0, concat_axis=0, axis_index_groups=groups, tiled=True
    )


def exchange_line(pieces):
    groups = [
        [line * line_bit + first for line in range(pieces.shape[0])] for first in range(line_bit)
    ]
    return exchange(pieces, groups)


def exchange_side(pieces):
    members = pieces.shape[0]
    groups = [
        [(index // 2) * line_bit + side * pair_bit + index % 2 for index in range(members)]
        for side in range(2)
    ]
    return exchange(pieces, groups)


def swap(array, flip):
    devices = lax.axis_size("dp")
    return lax.ppermute(array, "dp", [(i, i ^ flip) for i in range(devices)])


def tie(first, second):
    return lax.optimization_barrier((first, second))


def both_cores(held):
    return jnp.concatenate([held, swap(held, 1)], axis=0)


def local(tokens, output_gradient, value_weight, down_maps, up_maps, adapter_per_block, ranks):
    devices = lax.axis_size("dp")
    members = devices // 2
    lines = members // 2
    steps = members.bit_length() - 1
    num_adapters, extent, width = down_maps.shape
    rows, depth = output_gradient.shape
    place = lax.axis_index("dp").astype(jnp.int32).reshape(1)
    adapters = adapter_per_block
    offsets = [line_offset(slot, members) for slot in range(members)]
    barrier = lax.optimization_barrier

    far = [slot for slot in range(members) if slot % 2]
    quarter = max(1, len(far) // 4)
    far = [far[at : at + quarter] for at in range(0, len(far), quarter)]
    near = [slot for slot in range(2, members, 2)]

    def send(packs, portion):
        return {slot: swap(packs[slot], offsets[slot]) for slot in portion}

    def taken(pieces, portion):
        return [pieces[slot] for slot in portion]

    own_gradient = output_gradient.reshape(1, rows, depth)
    gradients = [own_gradient] + [None] * (lines - 1)
    for step in range(steps - 1):
        gradients[1 << step] = swap(own_gradient, offsets[1 << step])
    ups, ups_pair = gather_up(adapters, place, up_maps, members)
    ups_other = swap(ups_pair, pair_bit)
    pair = for_pair(adapters, place, value_weight, down_maps, members)
    ups_other, pair = barrier((ups_other, pair))
    pair = swap(pair, pair_bit)
    packs = dict(zip(far[0], pack_tokens(place, tokens, taken(offsets, far[0]), width)))
    firsts = [gradients[1 << step] for step in range(steps - 1)]
    firsts, ups_other, packs = barrier((firsts, ups_other, packs))
    for step in range(steps - 1):
        gradients[1 << step] = firsts[step]

    ups = exchange_side(jnp.stack([ups, ups_other], axis=1))
    arrived = send(packs, far[0])
    for step in range(1, steps - 1):
        for slot in range(1, 1 << step):
            gradients[slot + (1 << step)] = swap(gradients[slot], offsets[1 << step])
    ups, tokens, done = barrier((ups, tokens, taken(arrived, far[0])))
    arrived.update(zip(far[0], done))

    rest = [slot for slot in range(members) if slot not in far[0]]
    packs = dict(zip(rest, pack_tokens(place, tokens, taken(offsets, rest), width)))
    arrived[0] = packs[0]
    backs = exchange_line(back_rows(adapters, place, ranks, output_gradient, ups))
    window = far[1] + near[:1]
    arrived.update(send(packs, window))
    backs, gradients, packs, done = barrier((backs, gradients, packs, taken(arrived, window)))
    arrived.update(zip(window, done))

    backs = both_cores(backs)
    gradients.append(swap(jnp.concatenate(gradients, axis=0), 1))
    arrived.update(send(packs, near[1:] + far[2] + far[3]))
    *slices, columns, columns_pair = input_slices(
        adapters, place, gradients, backs, value_weight, pair, down_maps
    )
    slices, arrived = barrier((slices, taken(arrived, range(members))))

    parts, tokens_own, tokens_pair = hidden_parts(adapters, place, down_maps, pair, arrived)
    results = {0: slices[0]}
    window = near[:1] + far[0] + far[1]
    results.update(send(slices, window))
    tokens_other = swap(tokens_pair, pair_bit)
    parts = exchange_line(parts[:lines] + swap(parts[lines:], 1))
    parts, done, slices, tokens_other, columns_pair = barrier(
        (parts, taken(results, window), slices, tokens_other, columns_pair)
    )
    results.update(zip(window, done))

    window = near[1:2] + far[2]
    results.update(send(slices, window))
    hiddens = exchange_line(hidden_rows(adapters, place, ranks, parts))
    columns_other = swap(columns_pair, pair_bit)
    backs_pair = swap(backs, pair_bit)
    hiddens, done, slices, columns_other, backs_pair = barrier(
        (hiddens, taken(results, window), slices, columns_other, backs_pair)
    )
    results.update(zip(window, done))

    results.update(send(slices, near[2:] + far[3]))
    hiddens = both_cores(hiddens)
    hiddens_pair = swap(hiddens, pair_bit)
    down_gradient = down_gradients(
        adapters, place, backs, backs_pair, tokens_own, tokens_other, num_adapters
    )
    up_gradient = up_gradients(
        adapters, place, ranks, columns, columns_other, hiddens, hiddens_pair, depth // devices
    )

    def joined(slots, before=None):
        return join_columns(
            place, taken(results, slots), taken(offsets, slots), tokens.shape[1], before
        )

    most = joined([slot for slot in range(members) if slot not in far[3]])
    up_gradient, down_gradient, most = barrier((up_gradient, down_gradient, most))
    input_grad = joined(far[3], most)
    return (input_grad, down_gradient, up_gradient)


def solution(mesh):
    in_specs = (
        P(("groups", "dp"), None),
        P(("groups", "dp"), None),
        P(None, "dp"),
        P(None, None, "dp"),
        P(None, "dp", None),
        P("groups"),
        P(),
    )
    out_specs = (P(("groups", "dp"), None), P("groups", None, "dp"), P("groups", "dp", None))
    return jax.shard_map(local, mesh=mesh, in_specs=in_specs, out_specs=out_specs, check_vma=False)
```

```python
import functools

import jax
import jax.numpy as jnp
from jax import lax
from jax.experimental import pallas as pl
from jax.experimental.pallas import tpu as pltpu
from jax.sharding import PartitionSpec as P

adapter_alpha = 32.0
vmem_limit = 48 * 1024 * 1024
pair_bit = 2
line_bit = 4


def line_offset(slot, members):
    bits = members.bit_length() - 1
    order = 0
    for bit in range(bits):
        order |= ((slot >> bit) & 1) << (bits - 1 - bit)
    return ((order // 2) * line_bit) | (order % 2)


def entry_of(place, slot, members):
    offset = line_offset(slot, members)
    return (offset % 2) * (members // 2) + ((place ^ offset) // line_bit)


def place_of(entry, place, side, members):
    core, line = divmod(entry, members // 2)
    return line * line_bit + ((place % line_bit) ^ core ^ (side * pair_bit))


def params():
    return pltpu.CompilerParams(vmem_limit_bytes=vmem_limit)


def whole(shape):
    return pl.BlockSpec(shape, lambda *_: (0,) * len(shape))


def picked(maps, flip):
    return pl.BlockSpec(
        (1,) + maps.shape[1:], lambda i, adapters, place, *_: (adapters[place[0] ^ flip], 0, 0)
    )


def call(kernel, name, prefetch, operands, in_specs, out_shapes, scratch=(), grid=(1,), out_specs=None):
    if out_specs is None:
        out_specs = [whole(shape.shape) for shape in out_shapes]
    return pl.pallas_call(
        kernel,
        out_shape=out_shapes,
        grid_spec=pltpu.PrefetchScalarGridSpec(
            num_scalar_prefetch=len(prefetch),
            grid=grid,
            in_specs=in_specs,
            out_specs=out_specs,
            scratch_shapes=list(scratch),
        ),
        compiler_params=params(),
        name=name,
    )(*prefetch, *operands)


def run(copies):
    for copy in copies:
        copy.start()
    for copy in copies:
        copy.wait()


def copy_call(kernel, name, prefetch, operands, out_shapes, copies):
    return pl.pallas_call(
        kernel,
        out_shape=out_shapes,
        grid_spec=pltpu.PrefetchScalarGridSpec(
            num_scalar_prefetch=len(prefetch),
            grid=(1,),
            in_specs=[pl.BlockSpec(memory_space=pl.ANY)] * len(operands),
            out_specs=[whole(shape.shape) for shape in out_shapes],
            scratch_shapes=[pltpu.SemaphoreType.DMA((copies,))],
        ),
        compiler_params=params(),
        name=name,
    )(*prefetch, *operands)


weight_cuts = 4


def pair_kernel(adapters, place, weight, down_maps, out, sems):
    extent = down_maps.shape[1]
    depth = weight.shape[0]
    members = (out.shape[0] - depth) // extent
    copies = []
    for slot in range(members):
        block = place[0] ^ line_offset(slot, members) ^ pair_bit
        copies.append((down_maps.at[adapters[block]], slot * extent, extent))
    cut = depth // weight_cuts
    for at in range(0, depth, cut):
        copies.append((weight.at[pl.ds(at, cut)], members * extent + at, cut))
    run(
        [
            pltpu.make_async_copy(source, out.at[pl.ds(at, rows)], sems.at[number])
            for number, (source, at, rows) in enumerate(copies)
        ]
    )


def for_pair(adapters, place, weight, down_maps, members):
    extent, width = down_maps.shape[1:]
    shape = jax.ShapeDtypeStruct((members * extent + weight.shape[0], width), weight.dtype)
    return copy_call(
        pair_kernel,
        "for_pair",
        (adapters, place),
        (weight, down_maps),
        [shape],
        members + weight_cuts,
    )[0]


def gather_up_kernel(adapters, place, up_maps, own, pair, sems):
    members = own.shape[0]
    copies = []
    for index in range(members):
        block = (index // 2) * line_bit + place[0] % line_bit // pair_bit * pair_bit + index % 2
        for side, out in enumerate((own, pair)):
            source = up_maps.at[adapters[block ^ (side * pair_bit)]]
            copies.append(
                pltpu.make_async_copy(source, out.at[index], sems.at[2 * index + side])
            )
    run(copies)


def gather_up(adapters, place, up_maps, members):
    shape = jax.ShapeDtypeStruct((members,) + up_maps.shape[1:], up_maps.dtype)
    return copy_call(
        gather_up_kernel, "gather_up", (adapters, place), (up_maps,), [shape] * 2, 2 * members
    )


def pack_kernel(place, tokens, *refs, flips):
    outs, sems = refs[:-1], refs[-1]
    width = outs[0].shape[2]
    copies = []
    for number, out in enumerate(outs):
        for half in range(2):
            column = (place[0] ^ flips[number] ^ (half * pair_bit)) * width
            copies.append(
                pltpu.make_async_copy(
                    tokens.at[:, pl.ds(pl.multiple_of(column, width), width)],
                    out.at[half],
                    sems.at[2 * number + half],
                )
            )
    run(copies)


def pack_tokens(place, tokens, flips, width):
    shape = jax.ShapeDtypeStruct((2, tokens.shape[0], width), tokens.dtype)
    return copy_call(
        functools.partial(pack_kernel, flips=flips),
        "pack_tokens",
        (place,),
        (tokens,),
        [shape] * len(flips),
        2 * len(flips),
    )


def rank_row(ranks, adapter, extent):
    rank = jnp.full((1, extent), ranks[adapter], jnp.int32)
    alive = (lax.broadcasted_iota(jnp.int32, (1, extent), 1) < rank).astype(jnp.float32)
    return alive, adapter_alpha / rank.astype(jnp.float32)


def back_kernel(adapters, place, ranks, gradient, ups, out, up):
    members, _, value_width, extent = ups.shape
    side = place[0] % line_bit // pair_bit
    for index in range(members):
        for half in range(2):
            owner = (index // 2) * line_bit + (side ^ half) * pair_bit + index % 2
            rows = pl.ds(pl.multiple_of(owner * value_width, value_width), value_width)
            up[rows, :] = ups[index, half]
    alive, factor = rank_row(ranks, adapters[place[0]], extent)
    back = jnp.dot(gradient[...], up[...], preferred_element_type=jnp.float32)
    low = (factor * back * alive).astype(out.dtype)
    for line in range(out.shape[0]):
        out[line] = low


def back_rows(adapters, place, ranks, gradient, ups):
    members, _, _, extent = ups.shape
    rows, depth = gradient.shape
    return call(
        back_kernel,
        "back_low",
        (adapters, place, ranks),
        (gradient, ups),
        [whole(gradient.shape), whole(ups.shape)],
        [jax.ShapeDtypeStruct((members // 2, rows, extent), jnp.bfloat16)],
        scratch=[pltpu.VMEM((depth, extent), jnp.bfloat16)],
    )[0]


def input_kernel(adapters, place, backs, pair, *refs):
    members, rows, _ = backs.shape
    apart = members // 2
    gradients = [ref.at[0] for ref in refs[:apart]]
    gradients += [refs[apart].at[slot] for slot in range(members - apart)]
    downs = refs[apart + 1 : apart + 1 + members]
    weight = refs[apart + 1 + members]
    outs, columns = refs[apart + 2 + members : -2], refs[-2:]
    extent = downs[0].shape[1]
    lanes = columns[0].shape[2]
    value_width = gradients[0].shape[1] // (2 * members)
    some = min(4, members)
    for first in range(0, members, some):
        slots = range(first, first + some)
        lines = jnp.concatenate([gradients[slot][...] for slot in slots], axis=0)
        for half in range(2):
            right = weight[...] if half == 0 else pair[members * extent :]
            frozen = jnp.dot(lines, right, preferred_element_type=jnp.float32)
            for slot in slots:
                down = downs[slot][0] if half == 0 else pair[slot * extent : (slot + 1) * extent]
                entry = entry_of(place[0], slot, members)
                low = jnp.dot(backs[entry], down, preferred_element_type=jnp.float32)
                at = (slot - first) * rows
                outs[slot][half] = (frozen[at : at + rows] + low).astype(jnp.bfloat16)
    for side in range(2):
        column = (place[0] ^ (side * pair_bit)) * value_width // lanes * lanes
        for slot in range(members):
            entry = entry_of(place[0], slot, members)
            columns[side][entry] = gradients[slot][:, pl.ds(pl.multiple_of(column, lanes), lanes)]


def input_slices(adapters, place, gradients, backs, weight, pair, down_maps):
    members, rows, _ = backs.shape
    width = weight.shape[1]
    lanes = max(128, gradients[0].shape[2] // (2 * members))
    shape = jax.ShapeDtypeStruct((2, rows, width), jnp.bfloat16)
    columns = jax.ShapeDtypeStruct((members, rows, lanes), jnp.bfloat16)
    return call(
        input_kernel,
        "input_slices",
        (adapters, place),
        [backs, pair] + list(gradients) + [down_maps] * members + [weight],
        [whole(backs.shape), whole(pair.shape)]
        + [whole(gradient.shape) for gradient in gradients]
        + [picked(down_maps, line_offset(slot, members)) for slot in range(members)]
        + [whole(weight.shape)],
        [shape] * members + [columns] * 2,
    )


def hidden_kernel(adapters, place, pair, *refs):
    parts, own, other = refs[-3:]
    members = own.shape[0]
    downs, tokens = refs[:members], refs[members : 2 * members]
    extent = downs[0].shape[1]
    across = (((1,), (1,)), ((), ()))
    for slot in range(members):
        entry = entry_of(place[0], slot, members)
        own[entry] = tokens[slot][0]
        other[entry] = tokens[slot][1]
        parts[entry] = lax.dot_general(
            tokens[slot][0], downs[slot][0], across, preferred_element_type=jnp.float32
        ) + lax.dot_general(
            tokens[slot][1],
            pair[slot * extent : (slot + 1) * extent],
            across,
            preferred_element_type=jnp.float32,
        )


def hidden_parts(adapters, place, down_maps, pair, tokens):
    members = len(tokens)
    _, rows, width = tokens[0].shape
    extent = down_maps.shape[1]
    tokens_shape = jax.ShapeDtypeStruct((members, rows, width), tokens[0].dtype)
    return call(
        hidden_kernel,
        "hidden_parts",
        (adapters, place),
        [pair] + [down_maps] * members + list(tokens),
        [whole(pair.shape)]
        + [picked(down_maps, line_offset(slot, members)) for slot in range(members)]
        + [whole(tokens[0].shape)] * members,
        [
            jax.ShapeDtypeStruct((members, rows, extent), jnp.float32),
            tokens_shape,
            tokens_shape,
        ],
    )


def hidden_low_kernel(adapters, place, ranks, parts, out):
    alive, _ = rank_row(ranks, adapters[place[0]], out.shape[2])
    total = parts[0]
    for line in range(1, parts.shape[0]):
        total += parts[line]
    low = (total * alive).astype(out.dtype)
    for line in range(out.shape[0]):
        out[line] = low


def hidden_rows(adapters, place, ranks, parts):
    return call(
        hidden_low_kernel,
        "hidden_low",
        (adapters, place, ranks),
        (parts,),
        [whole(parts.shape)],
        [jax.ShapeDtypeStruct(parts.shape, jnp.bfloat16)],
    )[0]


def join_kernel(place, *refs, offsets, aliased):
    pieces = refs[: len(offsets)]
    out, sems = refs[len(offsets) + aliased :]
    width = pieces[0].shape[2]
    copies = []
    for entry, offset in enumerate(offsets):
        for half in range(2):
            column = (place[0] ^ offset ^ (half * pair_bit)) * width
            copies.append(
                pltpu.make_async_copy(
                    pieces[entry].at[half],
                    out.at[:, pl.ds(pl.multiple_of(column, width), width)],
                    sems.at[2 * entry + half],
                )
            )
    run(copies)


def join_columns(place, pieces, offsets, columns, before=None):
    rows = pieces[0].shape[1]
    rest = [] if before is None else [before]
    return pl.pallas_call(
        functools.partial(join_kernel, offsets=offsets, aliased=len(rest)),
        out_shape=jax.ShapeDtypeStruct((rows, columns), pieces[0].dtype),
        grid_spec=pltpu.PrefetchScalarGridSpec(
            num_scalar_prefetch=1,
            grid=(1,),
            in_specs=[whole(piece.shape) for piece in pieces]
            + [pl.BlockSpec(memory_space=pl.ANY)] * len(rest),
            out_specs=pl.BlockSpec(memory_space=pltpu.HBM),
            scratch_shapes=[pltpu.SemaphoreType.DMA((2 * len(pieces),))],
        ),
        input_output_aliases={1 + len(pieces): 0} if rest else {},
        compiler_params=params(),
        name="join_columns",
    )(place, *pieces, *rest)


def list_members(adapters, place, members, head, following):
    def clear(adapter, carry):
        head[adapter] = -1
        return carry

    lax.fori_loop(0, head.shape[0], clear, 0)
    for entry in reversed(range(2 * members)):
        side, own = divmod(entry, members)
        adapter = adapters[place_of(own, place[0], side, members)]
        following[entry] = head[adapter]
        head[adapter] = entry


def write_sums(head, following, products, ready, zero, out, sems, finish):
    num_adapters = out.shape[0]
    zero[...] = jnp.zeros_like(zero)

    def write(adapter, carry):
        first = head[adapter]

        @pl.when(first < 0)
        def _():
            pltpu.make_async_copy(zero, out.at[adapter], sems.at[adapter]).start()

        @pl.when(first >= 0)
        def _():
            def more(entry):
                products[first] += products[entry]
                return following[entry]

            lax.while_loop(lambda entry: entry >= 0, more, following[first])
            ready[first] = finish(adapter, products[first]).astype(out.dtype)
            pltpu.make_async_copy(ready.at[first], out.at[adapter], sems.at[adapter]).start()

        return carry

    lax.fori_loop(0, num_adapters, write, 0)

    def wait(adapter, carry):
        pltpu.make_async_copy(zero, out.at[adapter], sems.at[adapter]).wait()
        return carry

    lax.fori_loop(0, num_adapters, wait, 0)


def by_rows(left, right):
    return lax.dot_general(
        left, right, (((0,), (0,)), ((), ())), preferred_element_type=jnp.float32
    )


def sums_call(kernel, name, prefetch, operands, num_adapters, entries, product, scratch=()):
    return pl.pallas_call(
        kernel,
        out_shape=jax.ShapeDtypeStruct((num_adapters,) + product, jnp.bfloat16),
        grid_spec=pltpu.PrefetchScalarGridSpec(
            num_scalar_prefetch=len(prefetch),
            grid=(1,),
            in_specs=[whole(operand.shape) for operand in operands],
            out_specs=pl.BlockSpec(memory_space=pltpu.HBM),
            scratch_shapes=[
                pltpu.SMEM((num_adapters,), jnp.int32),
                pltpu.SMEM((entries,), jnp.int32),
                pltpu.VMEM((entries,) + product, jnp.float32),
                pltpu.VMEM((entries,) + product, jnp.bfloat16),
                pltpu.VMEM(product, jnp.bfloat16),
                pltpu.SemaphoreType.DMA((num_adapters,)),
                *scratch,
            ],
        ),
        compiler_params=params(),
        name=name,
    )(*prefetch, *operands)


def down_gradient_kernel(
    adapters, place, backs, backs_pair, own, other, out, head, following, products, ready, zero, sems
):
    members = own.shape[0]
    list_members(adapters, place, members, head, following)
    for slot in range(members):
        products[slot] = by_rows(backs[slot], own[slot])
        products[members + slot] = by_rows(backs_pair[slot], other[slot])
    write_sums(
        head, following, products, ready, zero, out, sems, lambda adapter, total: total
    )


def down_gradients(adapters, place, backs, backs_pair, own, other, num_adapters):
    members, _, width = own.shape
    return sums_call(
        down_gradient_kernel,
        "down_gradients",
        (adapters, place),
        (backs, backs_pair, own, other),
        num_adapters,
        2 * members,
        (backs.shape[2], width),
    )


def up_gradient_kernel(
    adapters,
    place,
    ranks,
    gradients,
    gradients_pair,
    hiddens,
    hiddens_pair,
    out,
    head,
    following,
    products,
    ready,
    zero,
    sems,
    lines,
):
    members, _, lanes = gradients.shape
    width, extent = out.shape[1:]
    list_members(adapters, place, members, head, following)
    inside = pl.multiple_of(lax.rem(place[0], lanes // width) * width, width)
    for slot in range(members):
        lines[slot] = by_rows(gradients[slot], hiddens[slot])
        lines[members + slot] = by_rows(gradients_pair[slot], hiddens_pair[slot])
    for entry in range(2 * members):
        products[entry] = lines[entry, pl.ds(inside, width), :]

    def finish(adapter, total):
        _, factor = rank_row(ranks, adapter, extent)
        return factor * total

    write_sums(head, following, products, ready, zero, out, sems, finish)


def up_gradients(adapters, place, ranks, gradients, gradients_pair, hiddens, hiddens_pair, width):
    members, _, lanes = gradients.shape
    extent = hiddens.shape[2]
    return sums_call(
        up_gradient_kernel,
        "up_gradients",
        (adapters, place, ranks),
        (gradients, gradients_pair, hiddens, hiddens_pair),
        ranks.shape[0],
        2 * members,
        (width, extent),
        [pltpu.VMEM((2 * members, lanes, extent), jnp.float32)],
    )


def exchange(pieces, groups):
    return lax.all_to_all(
        pieces, "dp", split_axis=0, concat_axis=0, axis_index_groups=groups, tiled=True
    )


def exchange_line(pieces):
    groups = [
        [line * line_bit + first for line in range(pieces.shape[0])] for first in range(line_bit)
    ]
    return exchange(pieces, groups)


def exchange_side(pieces):
    members = pieces.shape[0]
    groups = [
        [(index // 2) * line_bit + side * pair_bit + index % 2 for index in range(members)]
        for side in range(2)
    ]
    return exchange(pieces, groups)


def swap(array, flip):
    devices = lax.axis_size("dp")
    return lax.ppermute(array, "dp", [(i, i ^ flip) for i in range(devices)])


def tie(first, second):
    return lax.optimization_barrier((first, second))


def both_cores(held):
    return jnp.concatenate([held, swap(held, 1)], axis=0)


def local(tokens, output_gradient, value_weight, down_maps, up_maps, adapter_per_block, ranks):
    devices = lax.axis_size("dp")
    members = devices // 2
    lines = members // 2
    steps = members.bit_length() - 1
    num_adapters, extent, width = down_maps.shape
    rows, depth = output_gradient.shape
    place = lax.axis_index("dp").astype(jnp.int32).reshape(1)
    adapters = adapter_per_block
    offsets = [line_offset(slot, members) for slot in range(members)]
    barrier = lax.optimization_barrier

    far = [slot for slot in range(members) if slot % 2]
    quarter = max(1, len(far) // 4)
    far = [far[at : at + quarter] for at in range(0, len(far), quarter)]
    near = [slot for slot in range(2, members, 2)]

    def send(packs, portion):
        return {slot: swap(packs[slot], offsets[slot]) for slot in portion}

    def taken(pieces, portion):
        return [pieces[slot] for slot in portion]

    own_gradient = output_gradient.reshape(1, rows, depth)
    gradients = [own_gradient] + [None] * (lines - 1)
    for step in range(steps - 1):
        gradients[1 << step] = swap(own_gradient, offsets[1 << step])
    ups, ups_pair = gather_up(adapters, place, up_maps, members)
    ups_other = swap(ups_pair, pair_bit)
    pair = for_pair(adapters, place, value_weight, down_maps, members)
    ups_other, pair = barrier((ups_other, pair))
    pair = swap(pair, pair_bit)
    early = near[:1] + far[0] + far[1]
    packs = dict(zip(early, pack_tokens(place, tokens, taken(offsets, early), width)))
    ups = exchange_side(jnp.stack([ups, ups_other], axis=1))
    firsts = [gradients[1 << step] for step in range(steps - 1)]
    firsts, packs = barrier((firsts, packs))
    for step in range(steps - 1):
        gradients[1 << step] = firsts[step]
    window = near[:1] + far[0]
    arrived = send(packs, window)
    ups, gradients, packs, tokens, done = barrier(
        (ups, [gradients[0]] + firsts, packs, tokens, taken(arrived, window))
    )
    arrived.update(zip(window, done))
    gradients = {0: gradients[0], **{1 << step: gradients[1 + step] for step in range(steps - 1)}}

    backs = exchange_line(back_rows(adapters, place, ranks, output_gradient, ups))
    arrived.update(send(packs, far[1]))
    for step in range(1, steps - 1):
        for slot in range(1, 1 << step):
            gradients[slot + (1 << step)] = swap(gradients[slot], offsets[1 << step])
    gradients = taken(gradients, range(lines))
    rest = [slot for slot in range(members) if slot not in early]
    packs.update(zip(rest, pack_tokens(place, tokens, taken(offsets, rest), width)))
    arrived[0] = packs[0]
    backs, gradients, packs, done = barrier((backs, gradients, packs, taken(arrived, far[1])))
    arrived.update(zip(far[1], done))

    backs = both_cores(backs)
    backs_pair = swap(backs, pair_bit)
    gradients.append(swap(jnp.concatenate(gradients, axis=0), 1))
    arrived.update(send(packs, near[1:] + far[2] + far[3]))
    *slices, columns, columns_pair = input_slices(
        adapters, place, gradients, backs, value_weight, pair, down_maps
    )
    slices, arrived, backs_pair = barrier((slices, taken(arrived, range(members)), backs_pair))

    parts, tokens_own, tokens_pair = hidden_parts(adapters, place, down_maps, pair, arrived)
    results = {0: slices[0]}
    results.update(send(slices, far[0]))
    parts, done, slices = barrier((parts, taken(results, far[0]), slices))
    results.update(zip(far[0], done))

    window = near[:1] + far[1]
    results.update(send(slices, window))
    tokens_other = swap(tokens_pair, pair_bit)
    parts = exchange_line(parts[:lines] + swap(parts[lines:], 1))
    parts, done, slices, tokens_other, columns_pair = barrier(
        (parts, taken(results, window), slices, tokens_other, columns_pair)
    )
    results.update(zip(window, done))

    window = near[1:2] + far[2]
    results.update(send(slices, window))
    hiddens = exchange_line(hidden_rows(adapters, place, ranks, parts))
    columns_other = swap(columns_pair, pair_bit)
    down_gradient = down_gradients(
        adapters, place, backs, backs_pair, tokens_own, tokens_other, num_adapters
    )
    hiddens, done, slices, columns_other, down_gradient = barrier(
        (hiddens, taken(results, window), slices, columns_other, down_gradient)
    )
    results.update(zip(window, done))

    results.update(send(slices, near[2:] + far[3]))
    hiddens = both_cores(hiddens)
    hiddens_pair = swap(hiddens, pair_bit)
    up_gradient = up_gradients(
        adapters, place, ranks, columns, columns_other, hiddens, hiddens_pair, depth // devices
    )

    def joined(slots, before=None):
        return join_columns(
            place, taken(results, slots), taken(offsets, slots), tokens.shape[1], before
        )

    most = joined([slot for slot in range(members) if slot not in far[3]])
    up_gradient, most = barrier((up_gradient, most))
    input_grad = joined(far[3], most)
    return (input_grad, down_gradient, up_gradient)


def solution(mesh):
    in_specs = (
        P(("groups", "dp"), None),
        P(("groups", "dp"), None),
        P(None, "dp"),
        P(None, None, "dp"),
        P(None, "dp", None),
        P("groups"),
        P(),
    )
    out_specs = (P(("groups", "dp"), None), P("groups", None, "dp"), P("groups", "dp", None))
    return jax.shard_map(local, mesh=mesh, in_specs=in_specs, out_specs=out_specs, check_vma=False)
```

```python
import functools

import jax
import jax.numpy as jnp
from jax import lax
from jax.experimental import pallas as pl
from jax.experimental.pallas import tpu as pltpu
from jax.sharding import PartitionSpec as P

adapter_alpha = 32.0
vmem_limit = 48 * 1024 * 1024
pair_bit = 2
line_bit = 4


def line_offset(slot, members):
    bits = members.bit_length() - 1
    order = 0
    for bit in range(bits):
        order |= ((slot >> bit) & 1) << (bits - 1 - bit)
    return ((order // 2) * line_bit) | (order % 2)


def entry_of(place, slot, members):
    offset = line_offset(slot, members)
    return (offset % 2) * (members // 2) + ((place ^ offset) // line_bit)


def place_of(entry, place, side, members):
    core, line = divmod(entry, members // 2)
    return line * line_bit + ((place % line_bit) ^ core ^ (side * pair_bit))


def params():
    return pltpu.CompilerParams(vmem_limit_bytes=vmem_limit)


def whole(shape):
    return pl.BlockSpec(shape, lambda *_: (0,) * len(shape))


def picked(maps, flip):
    return pl.BlockSpec(
        (1,) + maps.shape[1:], lambda i, adapters, place, *_: (adapters[place[0] ^ flip], 0, 0)
    )


def call(kernel, name, prefetch, operands, in_specs, out_shapes, scratch=(), grid=(1,), out_specs=None):
    if out_specs is None:
        out_specs = [whole(shape.shape) for shape in out_shapes]
    return pl.pallas_call(
        kernel,
        out_shape=out_shapes,
        grid_spec=pltpu.PrefetchScalarGridSpec(
            num_scalar_prefetch=len(prefetch),
            grid=grid,
            in_specs=in_specs,
            out_specs=out_specs,
            scratch_shapes=list(scratch),
        ),
        compiler_params=params(),
        name=name,
    )(*prefetch, *operands)


def run(copies):
    for copy in copies:
        copy.start()
    for copy in copies:
        copy.wait()


def copy_call(kernel, name, prefetch, operands, out_shapes, copies):
    return pl.pallas_call(
        kernel,
        out_shape=out_shapes,
        grid_spec=pltpu.PrefetchScalarGridSpec(
            num_scalar_prefetch=len(prefetch),
            grid=(1,),
            in_specs=[pl.BlockSpec(memory_space=pl.ANY)] * len(operands),
            out_specs=[whole(shape.shape) for shape in out_shapes],
            scratch_shapes=[pltpu.SemaphoreType.DMA((copies,))],
        ),
        compiler_params=params(),
        name=name,
    )(*prefetch, *operands)


weight_cuts = 4


def pair_kernel(adapters, place, weight, down_maps, out, sems):
    extent = down_maps.shape[1]
    depth = weight.shape[0]
    members = (out.shape[0] - depth) // extent
    copies = []
    for slot in range(members):
        block = place[0] ^ line_offset(slot, members) ^ pair_bit
        copies.append((down_maps.at[adapters[block]], slot * extent, extent))
    cut = depth // weight_cuts
    for at in range(0, depth, cut):
        copies.append((weight.at[pl.ds(at, cut)], members * extent + at, cut))
    run(
        [
            pltpu.make_async_copy(source, out.at[pl.ds(at, rows)], sems.at[number])
            for number, (source, at, rows) in enumerate(copies)
        ]
    )


def for_pair(adapters, place, weight, down_maps, members):
    extent, width = down_maps.shape[1:]
    shape = jax.ShapeDtypeStruct((members * extent + weight.shape[0], width), weight.dtype)
    return copy_call(
        pair_kernel,
        "for_pair",
        (adapters, place),
        (weight, down_maps),
        [shape],
        members + weight_cuts,
    )[0]


def gather_up_kernel(adapters, place, up_maps, own, pair, sems):
    members = own.shape[0]
    copies = []
    for index in range(members):
        block = (index // 2) * line_bit + place[0] % line_bit // pair_bit * pair_bit + index % 2
        for side, out in enumerate((own, pair)):
            source = up_maps.at[adapters[block ^ (side * pair_bit)]]
            copies.append(
                pltpu.make_async_copy(source, out.at[index], sems.at[2 * index + side])
            )
    run(copies)


def gather_up(adapters, place, up_maps, members):
    shape = jax.ShapeDtypeStruct((members,) + up_maps.shape[1:], up_maps.dtype)
    return copy_call(
        gather_up_kernel, "gather_up", (adapters, place), (up_maps,), [shape] * 2, 2 * members
    )


def pack_kernel(place, tokens, *refs, flips):
    outs, sems = refs[:-1], refs[-1]
    width = outs[0].shape[2]
    copies = []
    for number, out in enumerate(outs):
        for half in range(2):
            column = (place[0] ^ flips[number] ^ (half * pair_bit)) * width
            copies.append(
                pltpu.make_async_copy(
                    tokens.at[:, pl.ds(pl.multiple_of(column, width), width)],
                    out.at[half],
                    sems.at[2 * number + half],
                )
            )
    run(copies)


def pack_tokens(place, tokens, flips, width):
    shape = jax.ShapeDtypeStruct((2, tokens.shape[0], width), tokens.dtype)
    return copy_call(
        functools.partial(pack_kernel, flips=flips),
        "pack_tokens",
        (place,),
        (tokens,),
        [shape] * len(flips),
        2 * len(flips),
    )


def rank_row(ranks, adapter, extent):
    rank = jnp.full((1, extent), ranks[adapter], jnp.int32)
    alive = (lax.broadcasted_iota(jnp.int32, (1, extent), 1) < rank).astype(jnp.float32)
    return alive, adapter_alpha / rank.astype(jnp.float32)


def back_kernel(adapters, place, ranks, gradient, ups, out, up):
    members, _, value_width, extent = ups.shape
    side = place[0] % line_bit // pair_bit
    for index in range(members):
        for half in range(2):
            owner = (index // 2) * line_bit + (side ^ half) * pair_bit + index % 2
            rows = pl.ds(pl.multiple_of(owner * value_width, value_width), value_width)
            up[rows, :] = ups[index, half]
    alive, factor = rank_row(ranks, adapters[place[0]], extent)
    back = jnp.dot(gradient[...], up[...], preferred_element_type=jnp.float32)
    low = (factor * back * alive).astype(out.dtype)
    for line in range(out.shape[0]):
        out[line] = low


def back_rows(adapters, place, ranks, gradient, ups):
    members, _, _, extent = ups.shape
    rows, depth = gradient.shape
    return call(
        back_kernel,
        "back_low",
        (adapters, place, ranks),
        (gradient, ups),
        [whole(gradient.shape), whole(ups.shape)],
        [jax.ShapeDtypeStruct((members // 2, rows, extent), jnp.bfloat16)],
        scratch=[pltpu.VMEM((depth, extent), jnp.bfloat16)],
    )[0]


def input_kernel(adapters, place, backs, pair, *refs):
    members, rows, _ = backs.shape
    apart = members // 2
    gradients = [ref.at[0] for ref in refs[:apart]]
    gradients += [refs[apart].at[slot] for slot in range(members - apart)]
    downs = refs[apart + 1 : apart + 1 + members]
    weight = refs[apart + 1 + members]
    outs, columns = refs[apart + 2 + members : -2], refs[-2:]
    extent = downs[0].shape[1]
    lanes = columns[0].shape[2]
    value_width = gradients[0].shape[1] // (2 * members)
    some = min(4, members)
    for first in range(0, members, some):
        slots = range(first, first + some)
        lines = jnp.concatenate([gradients[slot][...] for slot in slots], axis=0)
        for half in range(2):
            right = weight[...] if half == 0 else pair[members * extent :]
            frozen = jnp.dot(lines, right, preferred_element_type=jnp.float32)
            for slot in slots:
                down = downs[slot][0] if half == 0 else pair[slot * extent : (slot + 1) * extent]
                entry = entry_of(place[0], slot, members)
                low = jnp.dot(backs[entry], down, preferred_element_type=jnp.float32)
                at = (slot - first) * rows
                outs[slot][half] = (frozen[at : at + rows] + low).astype(jnp.bfloat16)
    for side in range(2):
        column = (place[0] ^ (side * pair_bit)) * value_width // lanes * lanes
        for slot in range(members):
            entry = entry_of(place[0], slot, members)
            columns[side][entry] = gradients[slot][:, pl.ds(pl.multiple_of(column, lanes), lanes)]


def input_slices(adapters, place, gradients, backs, weight, pair, down_maps):
    members, rows, _ = backs.shape
    width = weight.shape[1]
    lanes = max(128, gradients[0].shape[2] // (2 * members))
    shape = jax.ShapeDtypeStruct((2, rows, width), jnp.bfloat16)
    columns = jax.ShapeDtypeStruct((members, rows, lanes), jnp.bfloat16)
    return call(
        input_kernel,
        "input_slices",
        (adapters, place),
        [backs, pair] + list(gradients) + [down_maps] * members + [weight],
        [whole(backs.shape), whole(pair.shape)]
        + [whole(gradient.shape) for gradient in gradients]
        + [picked(down_maps, line_offset(slot, members)) for slot in range(members)]
        + [whole(weight.shape)],
        [shape] * members + [columns] * 2,
    )


def hidden_kernel(adapters, place, pair, *refs):
    parts, own, other = refs[-3:]
    members = own.shape[0]
    downs, tokens = refs[:members], refs[members : 2 * members]
    extent = downs[0].shape[1]
    across = (((1,), (1,)), ((), ()))
    for slot in range(members):
        entry = entry_of(place[0], slot, members)
        own[entry] = tokens[slot][0]
        other[entry] = tokens[slot][1]
        parts[entry] = lax.dot_general(
            tokens[slot][0], downs[slot][0], across, preferred_element_type=jnp.float32
        ) + lax.dot_general(
            tokens[slot][1],
            pair[slot * extent : (slot + 1) * extent],
            across,
            preferred_element_type=jnp.float32,
        )


def hidden_parts(adapters, place, down_maps, pair, tokens):
    members = len(tokens)
    _, rows, width = tokens[0].shape
    extent = down_maps.shape[1]
    tokens_shape = jax.ShapeDtypeStruct((members, rows, width), tokens[0].dtype)
    return call(
        hidden_kernel,
        "hidden_parts",
        (adapters, place),
        [pair] + [down_maps] * members + list(tokens),
        [whole(pair.shape)]
        + [picked(down_maps, line_offset(slot, members)) for slot in range(members)]
        + [whole(tokens[0].shape)] * members,
        [
            jax.ShapeDtypeStruct((members, rows, extent), jnp.float32),
            tokens_shape,
            tokens_shape,
        ],
    )


def hidden_low_kernel(adapters, place, ranks, parts, out):
    alive, _ = rank_row(ranks, adapters[place[0]], out.shape[2])
    total = parts[0]
    for line in range(1, parts.shape[0]):
        total += parts[line]
    low = (total * alive).astype(out.dtype)
    for line in range(out.shape[0]):
        out[line] = low


def hidden_rows(adapters, place, ranks, parts):
    return call(
        hidden_low_kernel,
        "hidden_low",
        (adapters, place, ranks),
        (parts,),
        [whole(parts.shape)],
        [jax.ShapeDtypeStruct(parts.shape, jnp.bfloat16)],
    )[0]


def join_kernel(place, *refs, offsets, aliased):
    pieces = refs[: len(offsets)]
    out, sems = refs[len(offsets) + aliased :]
    width = pieces[0].shape[2]
    copies = []
    for entry, offset in enumerate(offsets):
        for half in range(2):
            column = (place[0] ^ offset ^ (half * pair_bit)) * width
            copies.append(
                pltpu.make_async_copy(
                    pieces[entry].at[half],
                    out.at[:, pl.ds(pl.multiple_of(column, width), width)],
                    sems.at[2 * entry + half],
                )
            )
    run(copies)


def join_columns(place, pieces, offsets, columns, before=None):
    rows = pieces[0].shape[1]
    rest = [] if before is None else [before]
    return pl.pallas_call(
        functools.partial(join_kernel, offsets=offsets, aliased=len(rest)),
        out_shape=jax.ShapeDtypeStruct((rows, columns), pieces[0].dtype),
        grid_spec=pltpu.PrefetchScalarGridSpec(
            num_scalar_prefetch=1,
            grid=(1,),
            in_specs=[whole(piece.shape) for piece in pieces]
            + [pl.BlockSpec(memory_space=pl.ANY)] * len(rest),
            out_specs=pl.BlockSpec(memory_space=pltpu.HBM),
            scratch_shapes=[pltpu.SemaphoreType.DMA((2 * len(pieces),))],
        ),
        input_output_aliases={1 + len(pieces): 0} if rest else {},
        compiler_params=params(),
        name="join_columns",
    )(place, *pieces, *rest)


def list_members(adapters, place, members, head, following):
    def clear(adapter, carry):
        head[adapter] = -1
        return carry

    lax.fori_loop(0, head.shape[0], clear, 0)
    for entry in reversed(range(2 * members)):
        side, own = divmod(entry, members)
        adapter = adapters[place_of(own, place[0], side, members)]
        following[entry] = head[adapter]
        head[adapter] = entry


def write_sums(head, following, products, ready, zero, out, sems, finish):
    num_adapters = out.shape[0]
    zero[...] = jnp.zeros_like(zero)

    def write(adapter, carry):
        first = head[adapter]

        @pl.when(first < 0)
        def _():
            pltpu.make_async_copy(zero, out.at[adapter], sems.at[adapter]).start()

        @pl.when(first >= 0)
        def _():
            def more(entry):
                products[first] += products[entry]
                return following[entry]

            lax.while_loop(lambda entry: entry >= 0, more, following[first])
            ready[first] = finish(adapter, products[first]).astype(out.dtype)
            pltpu.make_async_copy(ready.at[first], out.at[adapter], sems.at[adapter]).start()

        return carry

    lax.fori_loop(0, num_adapters, write, 0)

    def wait(adapter, carry):
        pltpu.make_async_copy(zero, out.at[adapter], sems.at[adapter]).wait()
        return carry

    lax.fori_loop(0, num_adapters, wait, 0)


def by_rows(left, right):
    return lax.dot_general(
        left, right, (((0,), (0,)), ((), ())), preferred_element_type=jnp.float32
    )


def sums_call(kernel, name, prefetch, operands, num_adapters, entries, product, scratch=()):
    return pl.pallas_call(
        kernel,
        out_shape=jax.ShapeDtypeStruct((num_adapters,) + product, jnp.bfloat16),
        grid_spec=pltpu.PrefetchScalarGridSpec(
            num_scalar_prefetch=len(prefetch),
            grid=(1,),
            in_specs=[whole(operand.shape) for operand in operands],
            out_specs=pl.BlockSpec(memory_space=pltpu.HBM),
            scratch_shapes=[
                pltpu.SMEM((num_adapters,), jnp.int32),
                pltpu.SMEM((entries,), jnp.int32),
                pltpu.VMEM((entries,) + product, jnp.float32),
                pltpu.VMEM((entries,) + product, jnp.bfloat16),
                pltpu.VMEM(product, jnp.bfloat16),
                pltpu.SemaphoreType.DMA((num_adapters,)),
                *scratch,
            ],
        ),
        compiler_params=params(),
        name=name,
    )(*prefetch, *operands)


def down_gradient_kernel(
    adapters, place, backs, backs_pair, own, other, out, head, following, products, ready, zero, sems
):
    members = own.shape[0]
    list_members(adapters, place, members, head, following)
    for slot in range(members):
        products[slot] = by_rows(backs[slot], own[slot])
        products[members + slot] = by_rows(backs_pair[slot], other[slot])
    write_sums(
        head, following, products, ready, zero, out, sems, lambda adapter, total: total
    )


def down_gradients(adapters, place, backs, backs_pair, own, other, num_adapters):
    members, _, width = own.shape
    return sums_call(
        down_gradient_kernel,
        "down_gradients",
        (adapters, place),
        (backs, backs_pair, own, other),
        num_adapters,
        2 * members,
        (backs.shape[2], width),
    )


def up_gradient_kernel(
    adapters,
    place,
    ranks,
    gradients,
    gradients_pair,
    hiddens,
    hiddens_pair,
    out,
    head,
    following,
    products,
    ready,
    zero,
    sems,
    lines,
):
    members, _, lanes = gradients.shape
    width, extent = out.shape[1:]
    list_members(adapters, place, members, head, following)
    inside = pl.multiple_of(lax.rem(place[0], lanes // width) * width, width)
    for slot in range(members):
        lines[slot] = by_rows(gradients[slot], hiddens[slot])
        lines[members + slot] = by_rows(gradients_pair[slot], hiddens_pair[slot])
    for entry in range(2 * members):
        products[entry] = lines[entry, pl.ds(inside, width), :]

    def finish(adapter, total):
        _, factor = rank_row(ranks, adapter, extent)
        return factor * total

    write_sums(head, following, products, ready, zero, out, sems, finish)


def up_gradients(adapters, place, ranks, gradients, gradients_pair, hiddens, hiddens_pair, width):
    members, _, lanes = gradients.shape
    extent = hiddens.shape[2]
    return sums_call(
        up_gradient_kernel,
        "up_gradients",
        (adapters, place, ranks),
        (gradients, gradients_pair, hiddens, hiddens_pair),
        ranks.shape[0],
        2 * members,
        (width, extent),
        [pltpu.VMEM((2 * members, lanes, extent), jnp.float32)],
    )


def exchange(pieces, groups):
    return lax.all_to_all(
        pieces, "dp", split_axis=0, concat_axis=0, axis_index_groups=groups, tiled=True
    )


def exchange_line(pieces):
    groups = [
        [line * line_bit + first for line in range(pieces.shape[0])] for first in range(line_bit)
    ]
    return exchange(pieces, groups)


def exchange_side(pieces):
    members = pieces.shape[0]
    groups = [
        [(index // 2) * line_bit + side * pair_bit + index % 2 for index in range(members)]
        for side in range(2)
    ]
    return exchange(pieces, groups)


def swap(array, flip):
    devices = lax.axis_size("dp")
    return lax.ppermute(array, "dp", [(i, i ^ flip) for i in range(devices)])


def tie(first, second):
    return lax.optimization_barrier((first, second))


def both_cores(held):
    return jnp.concatenate([held, swap(held, 1)], axis=0)


def local(tokens, output_gradient, value_weight, down_maps, up_maps, adapter_per_block, ranks):
    devices = lax.axis_size("dp")
    members = devices // 2
    lines = members // 2
    steps = members.bit_length() - 1
    num_adapters, extent, width = down_maps.shape
    rows, depth = output_gradient.shape
    place = lax.axis_index("dp").astype(jnp.int32).reshape(1)
    adapters = adapter_per_block
    offsets = [line_offset(slot, members) for slot in range(members)]
    barrier = lax.optimization_barrier

    far = [slot for slot in range(members) if slot % 2]
    quarter = max(1, len(far) // 4)
    far = [far[at : at + quarter] for at in range(0, len(far), quarter)]
    near = [slot for slot in range(2, members, 2)]

    def send(packs, portion):
        return {slot: swap(packs[slot], offsets[slot]) for slot in portion}

    def taken(pieces, portion):
        return [pieces[slot] for slot in portion]

    own_gradient = output_gradient.reshape(1, rows, depth)
    gradients = [own_gradient] + [None] * (lines - 1)
    for step in range(steps - 1):
        gradients[1 << step] = swap(own_gradient, offsets[1 << step])
    ups, ups_pair = gather_up(adapters, place, up_maps, members)
    ups_other = swap(ups_pair, pair_bit)
    pair = for_pair(adapters, place, value_weight, down_maps, members)
    ups_other, pair = barrier((ups_other, pair))
    pair = swap(pair, pair_bit)
    early = near[:1] + far[0] + far[1]
    packs = dict(zip(early, pack_tokens(place, tokens, taken(offsets, early), width)))
    firsts = [gradients[1 << step] for step in range(steps - 1)]
    firsts, ups_other, packs = barrier((firsts, ups_other, packs))

    ups = exchange_side(jnp.stack([ups, ups_other], axis=1))
    arrived = send(packs, early)
    ups, firsts, tokens, done = barrier((ups, firsts, tokens, taken(arrived, early)))
    arrived.update(zip(early, done))
    for step in range(steps - 1):
        gradients[1 << step] = firsts[step]

    late = [slot for slot in range(members) if slot not in early]
    packs = dict(zip(late, pack_tokens(place, tokens, taken(offsets, late), width)))
    arrived.update(send(packs, late[1:]))
    arrived[0] = packs[0]
    backs = exchange_line(back_rows(adapters, place, ranks, output_gradient, ups))
    backs = both_cores(backs)
    for step in range(1, steps - 1):
        for slot in range(1, 1 << step):
            gradients[slot + (1 << step)] = swap(gradients[slot], offsets[1 << step])
    gradients.append(swap(jnp.concatenate(gradients, axis=0), 1))
    backs, gradients, pair, arrived = barrier(
        (backs, gradients, pair, taken(arrived, range(members)))
    )

    parts, tokens_own, tokens_pair = hidden_parts(adapters, place, down_maps, pair, arrived)
    parts, gradients = barrier((parts, gradients))
    tokens_other = swap(tokens_pair, pair_bit)
    *slices, columns, columns_pair = input_slices(
        adapters, place, gradients, backs, value_weight, pair, down_maps
    )
    results = {0: slices[0]}
    results.update(send(slices, far[0]))
    parts = exchange_line(parts[:lines] + swap(parts[lines:], 1))
    parts, done, slices, columns_pair, backs = barrier(
        (parts, taken(results, far[0]), slices, columns_pair, backs)
    )
    results.update(zip(far[0], done))

    window = near[:1] + far[1] + far[2]
    results.update(send(slices, window))
    hiddens = exchange_line(hidden_rows(adapters, place, ranks, parts))
    backs_pair = swap(backs, pair_bit)
    columns_other = swap(columns_pair, pair_bit)
    down_gradient = down_gradients(
        adapters, place, backs, backs_pair, tokens_own, tokens_other, num_adapters
    )
    hiddens, done, slices, columns_other, down_gradient = barrier(
        (hiddens, taken(results, window), slices, columns_other, down_gradient)
    )
    results.update(zip(window, done))

    results.update(send(slices, near[1:] + far[3]))
    hiddens = both_cores(hiddens)
    hiddens_pair = swap(hiddens, pair_bit)
    up_gradient = up_gradients(
        adapters, place, ranks, columns, columns_other, hiddens, hiddens_pair, depth // devices
    )

    def joined(slots, before=None):
        return join_columns(
            place, taken(results, slots), taken(offsets, slots), tokens.shape[1], before
        )

    most = joined([slot for slot in range(members) if slot not in far[3]])
    up_gradient, most = barrier((up_gradient, most))
    input_grad = joined(far[3], most)
    return (input_grad, down_gradient, up_gradient)


def solution(mesh):
    in_specs = (
        P(("groups", "dp"), None),
        P(("groups", "dp"), None),
        P(None, "dp"),
        P(None, None, "dp"),
        P(None, "dp", None),
        P("groups"),
        P(),
    )
    out_specs = (P(("groups", "dp"), None), P("groups", None, "dp"), P("groups", "dp", None))
    return jax.shard_map(local, mesh=mesh, in_specs=in_specs, out_specs=out_specs, check_vma=False)
```

```python
import functools

import jax
import jax.numpy as jnp
from jax import lax
from jax.experimental import pallas as pl
from jax.experimental.pallas import tpu as pltpu
from jax.sharding import PartitionSpec as P

adapter_alpha = 32.0
vmem_limit = 48 * 1024 * 1024
pair_bit = 2
line_bit = 4


def line_offset(slot, members):
    bits = members.bit_length() - 1
    order = 0
    for bit in range(bits):
        order |= ((slot >> bit) & 1) << (bits - 1 - bit)
    return ((order // 2) * line_bit) | (order % 2)


def side_of(place):
    return place % line_bit // pair_bit


def side_index(place):
    return place // line_bit * pair_bit + place % pair_bit


def side_place(index, side):
    return index // pair_bit * line_bit + side * pair_bit + index % pair_bit


def params():
    return pltpu.CompilerParams(vmem_limit_bytes=vmem_limit)


def whole(shape):
    return pl.BlockSpec(shape, lambda *_: (0,) * len(shape))


def picked(maps, flip):
    return pl.BlockSpec(
        (1,) + maps.shape[1:], lambda i, adapters, place, *_: (adapters[place[0] ^ flip], 0, 0)
    )


def call(kernel, name, prefetch, operands, in_specs, out_shapes, scratch=(), grid=(1,), out_specs=None):
    if out_specs is None:
        out_specs = [whole(shape.shape) for shape in out_shapes]
    return pl.pallas_call(
        kernel,
        out_shape=out_shapes,
        grid_spec=pltpu.PrefetchScalarGridSpec(
            num_scalar_prefetch=len(prefetch),
            grid=grid,
            in_specs=in_specs,
            out_specs=out_specs,
            scratch_shapes=list(scratch),
        ),
        compiler_params=params(),
        name=name,
    )(*prefetch, *operands)


def run(copies):
    for copy in copies:
        copy.start()
    for copy in copies:
        copy.wait()


def copy_call(kernel, name, prefetch, operands, out_shapes, copies):
    return pl.pallas_call(
        kernel,
        out_shape=out_shapes,
        grid_spec=pltpu.PrefetchScalarGridSpec(
            num_scalar_prefetch=len(prefetch),
            grid=(1,),
            in_specs=[pl.BlockSpec(memory_space=pl.ANY)] * len(operands),
            out_specs=[whole(shape.shape) for shape in out_shapes],
            scratch_shapes=[pltpu.SemaphoreType.DMA((copies,))],
        ),
        compiler_params=params(),
        name=name,
    )(*prefetch, *operands)


weight_cuts = 4


def pair_kernel(adapters, place, weight, down_maps, out, sems):
    extent = down_maps.shape[1]
    depth = weight.shape[0]
    members = (out.shape[0] - depth) // extent
    copies = []
    for slot in range(members):
        block = place[0] ^ line_offset(slot, members) ^ pair_bit
        copies.append((down_maps.at[adapters[block]], slot * extent, extent))
    cut = depth // weight_cuts
    for at in range(0, depth, cut):
        copies.append((weight.at[pl.ds(at, cut)], members * extent + at, cut))
    run(
        [
            pltpu.make_async_copy(source, out.at[pl.ds(at, rows)], sems.at[number])
            for number, (source, at, rows) in enumerate(copies)
        ]
    )


def for_pair(adapters, place, weight, down_maps, members):
    extent, width = down_maps.shape[1:]
    shape = jax.ShapeDtypeStruct((members * extent + weight.shape[0], width), weight.dtype)
    return copy_call(
        pair_kernel,
        "for_pair",
        (adapters, place),
        (weight, down_maps),
        [shape],
        members + weight_cuts,
    )[0]


def gather_up_kernel(adapters, up_maps, out, sems):
    run(
        [
            pltpu.make_async_copy(up_maps.at[adapters[block]], out.at[block], sems.at[block])
            for block in range(out.shape[0])
        ]
    )


def gather_up(adapters, up_maps):
    shape = jax.ShapeDtypeStruct((adapters.shape[0],) + up_maps.shape[1:], up_maps.dtype)
    return copy_call(
        gather_up_kernel, "gather_up", (adapters,), (up_maps,), [shape], adapters.shape[0]
    )[0]


def pack_kernel(place, tokens, out, sems):
    members, _, _, width = out.shape
    copies = []
    for index in range(members):
        for half in range(2):
            column = side_place(index, side_of(place[0]) ^ half) * width
            copies.append(
                pltpu.make_async_copy(
                    tokens.at[:, pl.ds(pl.multiple_of(column, width), width)],
                    out.at[index, half],
                    sems.at[2 * index + half],
                )
            )
    run(copies)


def pack_tokens(place, tokens, members, width):
    shape = jax.ShapeDtypeStruct((members, 2, tokens.shape[0], width), tokens.dtype)
    return copy_call(pack_kernel, "pack_tokens", (place,), (tokens,), [shape], 2 * members)[0]


def rank_row(ranks, adapter, extent):
    rank = jnp.full((1, extent), ranks[adapter], jnp.int32)
    alive = (lax.broadcasted_iota(jnp.int32, (1, extent), 1) < rank).astype(jnp.float32)
    return alive, adapter_alpha / rank.astype(jnp.float32)


def back_kernel(adapters, place, ranks, gradient, up, out):
    alive, factor = rank_row(ranks, adapters[place[0]], up.shape[1])
    back = jnp.dot(gradient[...], up[...], preferred_element_type=jnp.float32)
    out[0] = (factor * back * alive).astype(out.dtype)


def back_rows(adapters, place, ranks, gradient, up):
    return call(
        back_kernel,
        "back_low",
        (adapters, place, ranks),
        (gradient, up),
        [whole(gradient.shape), whole(up.shape)],
        [jax.ShapeDtypeStruct((1, gradient.shape[0], up.shape[1]), jnp.bfloat16)],
    )[0]


def input_kernel(adapters, place, backs, pair, *refs):
    members, rows, _ = backs.shape
    apart = members // 2
    gradients = [ref.at[0] for ref in refs[:apart]]
    gradients += [refs[apart].at[slot] for slot in range(members - apart)]
    downs = refs[apart + 1 : apart + 1 + members]
    weight = refs[apart + 1 + members]
    out, *columns = refs[-3:]
    extent = downs[0].shape[1]
    lanes = columns[0].shape[2]
    value_width = gradients[0].shape[1] // (2 * members)
    some = min(4, members)
    for first in range(0, members, some):
        slots = range(first, first + some)
        lines = jnp.concatenate([gradients[slot][...] for slot in slots], axis=0)
        for half in range(2):
            right = weight[...] if half == 0 else pair[members * extent :]
            frozen = jnp.dot(lines, right, preferred_element_type=jnp.float32)
            for slot in slots:
                down = downs[slot][0] if half == 0 else pair[slot * extent : (slot + 1) * extent]
                index = side_index(place[0] ^ line_offset(slot, members))
                low = jnp.dot(backs[slot], down, preferred_element_type=jnp.float32)
                at = (slot - first) * rows
                out[index, half] = (frozen[at : at + rows] + low).astype(jnp.bfloat16)
    for side in range(2):
        column = (place[0] ^ (side * pair_bit)) * value_width // lanes * lanes
        for slot in range(members):
            columns[side][slot] = gradients[slot][:, pl.ds(pl.multiple_of(column, lanes), lanes)]


def input_slices(adapters, place, gradients, backs, weight, pair, down_maps):
    members, rows, _ = backs.shape
    width = weight.shape[1]
    lanes = max(128, gradients[0].shape[2] // (2 * members))
    shape = jax.ShapeDtypeStruct((members, 2, rows, width), jnp.bfloat16)
    columns = jax.ShapeDtypeStruct((members, rows, lanes), jnp.bfloat16)
    return call(
        input_kernel,
        "input_slices",
        (adapters, place),
        [backs, pair] + list(gradients) + [down_maps] * members + [weight],
        [whole(backs.shape), whole(pair.shape)]
        + [whole(gradient.shape) for gradient in gradients]
        + [picked(down_maps, line_offset(slot, members)) for slot in range(members)]
        + [whole(weight.shape)],
        [shape, columns, columns],
    )


def hidden_kernel(adapters, place, pair, tokens, *refs):
    parts, own, other = refs[-3:]
    members = own.shape[0]
    downs = refs[:members]
    extent = downs[0].shape[1]
    across = (((1,), (1,)), ((), ()))
    for slot in range(members):
        index = side_index(place[0] ^ line_offset(slot, members))
        own[slot] = tokens[index, 0]
        other[slot] = tokens[index, 1]
        parts[slot] = lax.dot_general(
            tokens[index, 0], downs[slot][0], across, preferred_element_type=jnp.float32
        ) + lax.dot_general(
            tokens[index, 1],
            pair[slot * extent : (slot + 1) * extent],
            across,
            preferred_element_type=jnp.float32,
        )


def hidden_parts(adapters, place, down_maps, pair, tokens):
    members, _, rows, width = tokens.shape
    extent = down_maps.shape[1]
    tokens_shape = jax.ShapeDtypeStruct((members, rows, width), tokens.dtype)
    return call(
        hidden_kernel,
        "hidden_parts",
        (adapters, place),
        [pair, tokens] + [down_maps] * members,
        [whole(pair.shape), whole(tokens.shape)]
        + [picked(down_maps, line_offset(slot, members)) for slot in range(members)],
        [
            jax.ShapeDtypeStruct((members, rows, extent), jnp.float32),
            tokens_shape,
            tokens_shape,
        ],
    )


def sum_kernel(total, received, *outs, flip):
    for slot in range(outs[0].shape[0]):
        value = total[slot] + received[slot ^ flip].astype(jnp.float32)
        for out in outs:
            out[slot] = value.astype(out.dtype)


def slot_sums(total, received, flip, types):
    shape = received.shape
    return call(
        functools.partial(sum_kernel, flip=flip),
        "slot_sums",
        (),
        (total, received),
        [whole(shape)] * 2,
        [jax.ShapeDtypeStruct(shape, kind) for kind in types],
    )


def hidden_low_kernel(adapters, place, ranks, total, received, out, *, flip, members):
    for slot in range(out.shape[0]):
        block = place[0] ^ line_offset(slot, members)
        alive, _ = rank_row(ranks, adapters[block], out.shape[2])
        value = total[slot] + received[slot ^ flip].astype(jnp.float32)
        out[slot] = (value * alive).astype(out.dtype)


def hidden_rows(adapters, place, ranks, total, received, flip, members):
    return call(
        functools.partial(hidden_low_kernel, flip=flip, members=members),
        "hidden_low",
        (adapters, place, ranks),
        (total, received),
        [whole(total.shape)] * 2,
        [jax.ShapeDtypeStruct(total.shape, jnp.bfloat16)],
    )[0]


def join_kernel(place, source, out, sems):
    members, _, _, width = source.shape
    copies = []
    for index in range(members):
        for half in range(2):
            column = side_place(index, side_of(place[0]) ^ half) * width
            copies.append(
                pltpu.make_async_copy(
                    source.at[index, half],
                    out.at[:, pl.ds(pl.multiple_of(column, width), width)],
                    sems.at[2 * index + half],
                )
            )
    run(copies)


def join_columns(place, source):
    members, _, rows, width = source.shape
    return pl.pallas_call(
        join_kernel,
        out_shape=jax.ShapeDtypeStruct((rows, 2 * members * width), source.dtype),
        grid_spec=pltpu.PrefetchScalarGridSpec(
            num_scalar_prefetch=1,
            grid=(1,),
            in_specs=[whole(source.shape)],
            out_specs=pl.BlockSpec(memory_space=pl.ANY),
            scratch_shapes=[pltpu.SemaphoreType.DMA((2 * members,))],
        ),
        compiler_params=params(),
        name="join_columns",
    )(place, source)


def list_members(adapters, place, members, head, following):
    def clear(adapter, carry):
        head[adapter] = -1
        return carry

    lax.fori_loop(0, head.shape[0], clear, 0)
    for entry in reversed(range(2 * members)):
        side, own = divmod(entry, members)
        adapter = adapters[place[0] ^ line_offset(own, members) ^ (side * pair_bit)]
        following[entry] = head[adapter]
        head[adapter] = entry


def write_sums(head, following, products, ready, zero, out, sems, finish):
    num_adapters = out.shape[0]
    zero[...] = jnp.zeros_like(zero)

    def write(adapter, carry):
        first = head[adapter]

        @pl.when(first < 0)
        def _():
            pltpu.make_async_copy(zero, out.at[adapter], sems.at[adapter]).start()

        @pl.when(first >= 0)
        def _():
            def more(entry):
                products[first] += products[entry]
                return following[entry]

            lax.while_loop(lambda entry: entry >= 0, more, following[first])
            ready[first] = finish(adapter, products[first]).astype(out.dtype)
            pltpu.make_async_copy(ready.at[first], out.at[adapter], sems.at[adapter]).start()

        return carry

    lax.fori_loop(0, num_adapters, write, 0)

    def wait(adapter, carry):
        pltpu.make_async_copy(zero, out.at[adapter], sems.at[adapter]).wait()
        return carry

    lax.fori_loop(0, num_adapters, wait, 0)


def by_rows(left, right):
    return lax.dot_general(
        left, right, (((0,), (0,)), ((), ())), preferred_element_type=jnp.float32
    )


def sums_call(kernel, name, prefetch, operands, num_adapters, entries, product, scratch=()):
    return pl.pallas_call(
        kernel,
        out_shape=jax.ShapeDtypeStruct((num_adapters,) + product, jnp.bfloat16),
        grid_spec=pltpu.PrefetchScalarGridSpec(
            num_scalar_prefetch=len(prefetch),
            grid=(1,),
            in_specs=[whole(operand.shape) for operand in operands],
            out_specs=pl.BlockSpec(memory_space=pltpu.HBM),
            scratch_shapes=[
                pltpu.SMEM((num_adapters,), jnp.int32),
                pltpu.SMEM((entries,), jnp.int32),
                pltpu.VMEM((entries,) + product, jnp.float32),
                pltpu.VMEM((entries,) + product, jnp.bfloat16),
                pltpu.VMEM(product, jnp.bfloat16),
                pltpu.SemaphoreType.DMA((num_adapters,)),
                *scratch,
            ],
        ),
        compiler_params=params(),
        name=name,
    )(*prefetch, *operands)


def down_gradient_kernel(
    adapters, place, backs, backs_pair, own, other, out, head, following, products, ready, zero, sems
):
    members = own.shape[0]
    list_members(adapters, place, members, head, following)
    for slot in range(members):
        products[slot] = by_rows(backs[slot], own[slot])
        products[members + slot] = by_rows(backs_pair[slot], other[slot])
    write_sums(
        head, following, products, ready, zero, out, sems, lambda adapter, total: total
    )


def down_gradients(adapters, place, backs, backs_pair, own, other, num_adapters):
    members, _, width = own.shape
    return sums_call(
        down_gradient_kernel,
        "down_gradients",
        (adapters, place),
        (backs, backs_pair, own, other),
        num_adapters,
        2 * members,
        (backs.shape[2], width),
    )


def up_gradient_kernel(
    adapters,
    place,
    ranks,
    gradients,
    gradients_pair,
    hiddens,
    hiddens_pair,
    out,
    head,
    following,
    products,
    ready,
    zero,
    sems,
    lines,
):
    members, _, lanes = gradients.shape
    width, extent = out.shape[1:]
    list_members(adapters, place, members, head, following)
    inside = pl.multiple_of(lax.rem(place[0], lanes // width) * width, width)
    for slot in range(members):
        lines[slot] = by_rows(gradients[slot], hiddens[slot])
        lines[members + slot] = by_rows(gradients_pair[slot], hiddens_pair[slot])
    for entry in range(2 * members):
        products[entry] = lines[entry, pl.ds(inside, width), :]

    def finish(adapter, total):
        _, factor = rank_row(ranks, adapter, extent)
        return factor * total

    write_sums(head, following, products, ready, zero, out, sems, finish)


def up_gradients(adapters, place, ranks, gradients, gradients_pair, hiddens, hiddens_pair, width):
    members, _, lanes = gradients.shape
    extent = hiddens.shape[2]
    return sums_call(
        up_gradient_kernel,
        "up_gradients",
        (adapters, place, ranks),
        (gradients, gradients_pair, hiddens, hiddens_pair),
        ranks.shape[0],
        2 * members,
        (width, extent),
        [pltpu.VMEM((2 * members, lanes, extent), jnp.float32)],
    )


def exchange(pieces):
    return lax.all_to_all(pieces, "dp", split_axis=0, concat_axis=0, tiled=True)


def exchange_side(pieces):
    members = pieces.shape[0]
    groups = [[side_place(index, side) for index in range(members)] for side in range(2)]
    return lax.all_to_all(
        pieces, "dp", split_axis=0, concat_axis=0, axis_index_groups=groups, tiled=True
    )


def swap(array, flip):
    devices = lax.axis_size("dp")
    return lax.ppermute(array, "dp", [(i, i ^ flip) for i in range(devices)])


def tie(first, second):
    return lax.optimization_barrier((first, second))


def gather_step(held, members):
    arrived = swap(held, line_offset(held.shape[0], members))
    return jnp.concatenate([held, arrived], axis=0)


def local(tokens, output_gradient, value_weight, down_maps, up_maps, adapter_per_block, ranks):
    devices = lax.axis_size("dp")
    members = devices // 2
    lines = members // 2
    steps = members.bit_length() - 1
    num_adapters, extent, width = down_maps.shape
    rows, depth = output_gradient.shape
    place = lax.axis_index("dp").astype(jnp.int32).reshape(1)
    adapters = adapter_per_block
    offsets = [line_offset(slot, members) for slot in range(members)]
    barrier = lax.optimization_barrier

    own_gradient = output_gradient.reshape(1, rows, depth)
    gradients = [own_gradient] + [None] * (lines - 1)
    for step in range(steps - 1):
        gradients[1 << step] = swap(own_gradient, offsets[1 << step])
    own_up = exchange(gather_up(adapters, up_maps)).reshape(depth, extent)
    packs = pack_tokens(place, tokens, members, width)
    pair = for_pair(adapters, place, value_weight, down_maps, members)
    firsts = [gradients[1 << step] for step in range(steps - 1)]
    firsts, own_up, packs, pair = barrier((firsts, own_up, packs, pair))
    for step in range(steps - 1):
        gradients[1 << step] = firsts[step]

    arrived = exchange_side(packs)
    pair = swap(pair, pair_bit)
    backs = back_rows(adapters, place, ranks, output_gradient, own_up)
    backs = gather_step(backs, members)
    for slot in range(1, 2):
        for step in range(1, min(2, steps - 1)):
            gradients[slot + (1 << step)] = swap(gradients[slot], offsets[1 << step])
    held = [gradients[slot] for slot in range(lines) if gradients[slot] is not None]
    arrived, backs, held, pair = barrier((arrived, backs, held, pair))
    known = [slot for slot in range(lines) if gradients[slot] is not None]
    for slot, block in zip(known, held):
        gradients[slot] = block

    parts, tokens_own, tokens_pair = hidden_parts(adapters, place, down_maps, pair, arrived)
    while backs.shape[0] < members:
        backs = gather_step(backs, members)
    for step in range(1, steps - 1):
        for slot in range(1, 1 << step):
            if gradients[slot + (1 << step)] is None:
                gradients[slot + (1 << step)] = swap(gradients[slot], offsets[1 << step])
    gradients.append(swap(jnp.concatenate(gradients, axis=0), 1))
    slices, columns, columns_pair = input_slices(
        adapters, place, gradients, backs, value_weight, pair, down_maps
    )
    received, flip = swap(parts[lines:], 1), 0
    total = parts
    for step in reversed(range(steps - 1)):
        flipped = 1 << step
        last = step == 0
        sums = slot_sums(
            total, received, flip, [jnp.float32] + [jnp.bfloat16] * last
        )
        total, flip = sums[0], flipped
        received = swap(sums[-1], offsets[flipped])
    received, slices, columns_pair, backs, tokens_pair = barrier(
        (received, slices, columns_pair, backs, tokens_pair)
    )

    result = exchange_side(slices)
    hiddens = hidden_rows(adapters, place, ranks, total, received, flip, members)
    hiddens = gather_step(hiddens, members)
    hiddens_pair = swap(hiddens, pair_bit)
    columns_other = swap(columns_pair, pair_bit)
    backs_pair = swap(backs, pair_bit)
    tokens_other = swap(tokens_pair, pair_bit)
    up_gradient = up_gradients(
        adapters, place, ranks, columns, columns_other, hiddens, hiddens_pair, depth // devices
    )
    down_gradient = down_gradients(
        adapters, place, backs, backs_pair, tokens_own, tokens_other, num_adapters
    )
    up_gradient, down_gradient, result = barrier((up_gradient, down_gradient, result))
    return (join_columns(place, result), down_gradient, up_gradient)


def solution(mesh):
    in_specs = (
        P(("groups", "dp"), None),
        P(("groups", "dp"), None),
        P(None, "dp"),
        P(None, None, "dp"),
        P(None, "dp", None),
        P("groups"),
        P(),
    )
    out_specs = (P(("groups", "dp"), None), P("groups", None, "dp"), P("groups", "dp", None))
    return jax.shard_map(local, mesh=mesh, in_specs=in_specs, out_specs=out_specs, check_vma=False)
```

```python
import functools

import jax
import jax.numpy as jnp
from jax import lax
from jax.experimental import pallas as pl
from jax.experimental.pallas import tpu as pltpu
from jax.sharding import PartitionSpec as P

adapter_alpha = 32.0
vmem_limit = 48 * 1024 * 1024
pair_bit = 2
line_bit = 4


def line_offset(slot, members):
    bits = members.bit_length() - 1
    order = 0
    for bit in range(bits):
        order |= ((slot >> bit) & 1) << (bits - 1 - bit)
    return ((order // 2) * line_bit) | (order % 2)


def side_of(place):
    return place % line_bit // pair_bit


def reversed_bits(number, count):
    bits = count.bit_length() - 1
    return sum(((number >> bit) & 1) << (bits - 1 - bit) for bit in range(bits))


def side_index(place, members):
    lines = members // 2
    return place % pair_bit * lines + reversed_bits(place // line_bit, lines)


def side_place(index, side, members):
    core, line = divmod(index, members // 2)
    return reversed_bits(line, members // 2) * line_bit + side * pair_bit + core


def params():
    return pltpu.CompilerParams(vmem_limit_bytes=vmem_limit)


def whole(shape):
    return pl.BlockSpec(shape, lambda *_: (0,) * len(shape))


def picked(maps, flip):
    return pl.BlockSpec(
        (1,) + maps.shape[1:], lambda i, adapters, place, *_: (adapters[place[0] ^ flip], 0, 0)
    )


def call(kernel, name, prefetch, operands, in_specs, out_shapes, scratch=(), grid=(1,), out_specs=None):
    if out_specs is None:
        out_specs = [whole(shape.shape) for shape in out_shapes]
    return pl.pallas_call(
        kernel,
        out_shape=out_shapes,
        grid_spec=pltpu.PrefetchScalarGridSpec(
            num_scalar_prefetch=len(prefetch),
            grid=grid,
            in_specs=in_specs,
            out_specs=out_specs,
            scratch_shapes=list(scratch),
        ),
        compiler_params=params(),
        name=name,
    )(*prefetch, *operands)


def run(copies):
    for copy in copies:
        copy.start()
    for copy in copies:
        copy.wait()


def copy_call(kernel, name, prefetch, operands, out_shapes, copies):
    return pl.pallas_call(
        kernel,
        out_shape=out_shapes,
        grid_spec=pltpu.PrefetchScalarGridSpec(
            num_scalar_prefetch=len(prefetch),
            grid=(1,),
            in_specs=[pl.BlockSpec(memory_space=pl.ANY)] * len(operands),
            out_specs=[whole(shape.shape) for shape in out_shapes],
            scratch_shapes=[pltpu.SemaphoreType.DMA((copies,))],
        ),
        compiler_params=params(),
        name=name,
    )(*prefetch, *operands)


weight_cuts = 4


def pair_kernel(adapters, place, weight, down_maps, out, sems):
    extent = down_maps.shape[1]
    depth = weight.shape[0]
    members = (out.shape[0] - depth) // extent
    copies = []
    for slot in range(members):
        block = place[0] ^ line_offset(slot, members) ^ pair_bit
        copies.append((down_maps.at[adapters[block]], slot * extent, extent))
    cut = depth // weight_cuts
    for at in range(0, depth, cut):
        copies.append((weight.at[pl.ds(at, cut)], members * extent + at, cut))
    run(
        [
            pltpu.make_async_copy(source, out.at[pl.ds(at, rows)], sems.at[number])
            for number, (source, at, rows) in enumerate(copies)
        ]
    )


def for_pair(adapters, place, weight, down_maps, members):
    extent, width = down_maps.shape[1:]
    shape = jax.ShapeDtypeStruct((members * extent + weight.shape[0], width), weight.dtype)
    return copy_call(
        pair_kernel,
        "for_pair",
        (adapters, place),
        (weight, down_maps),
        [shape],
        members + weight_cuts,
    )[0]


def gather_up_kernel(adapters, up_maps, out, sems):
    run(
        [
            pltpu.make_async_copy(up_maps.at[adapters[block]], out.at[block], sems.at[block])
            for block in range(out.shape[0])
        ]
    )


def gather_up(adapters, up_maps):
    shape = jax.ShapeDtypeStruct((adapters.shape[0],) + up_maps.shape[1:], up_maps.dtype)
    return copy_call(
        gather_up_kernel, "gather_up", (adapters,), (up_maps,), [shape], adapters.shape[0]
    )[0]


def pack_kernel(place, tokens, out, sems):
    members, _, _, width = out.shape
    copies = []
    for index in range(members):
        for half in range(2):
            column = side_place(index, side_of(place[0]) ^ half, members) * width
            copies.append(
                pltpu.make_async_copy(
                    tokens.at[:, pl.ds(pl.multiple_of(column, width), width)],
                    out.at[index, half],
                    sems.at[2 * index + half],
                )
            )
    run(copies)


def pack_tokens(place, tokens, members, width):
    shape = jax.ShapeDtypeStruct((members, 2, tokens.shape[0], width), tokens.dtype)
    return copy_call(pack_kernel, "pack_tokens", (place,), (tokens,), [shape], 2 * members)[0]


def rank_row(ranks, adapter, extent):
    rank = jnp.full((1, extent), ranks[adapter], jnp.int32)
    alive = (lax.broadcasted_iota(jnp.int32, (1, extent), 1) < rank).astype(jnp.float32)
    return alive, adapter_alpha / rank.astype(jnp.float32)


def back_kernel(adapters, place, ranks, gradient, up, out):
    alive, factor = rank_row(ranks, adapters[place[0]], up.shape[1])
    back = jnp.dot(gradient[...], up[...], preferred_element_type=jnp.float32)
    out[0] = (factor * back * alive).astype(out.dtype)


def back_rows(adapters, place, ranks, gradient, up):
    return call(
        back_kernel,
        "back_low",
        (adapters, place, ranks),
        (gradient, up),
        [whole(gradient.shape), whole(up.shape)],
        [jax.ShapeDtypeStruct((1, gradient.shape[0], up.shape[1]), jnp.bfloat16)],
    )[0]


def input_kernel(adapters, place, backs, pair, *refs):
    members, rows, _ = backs.shape
    apart = members // 2
    gradients = [ref.at[0] for ref in refs[:apart]]
    gradients += [refs[apart].at[slot] for slot in range(members - apart)]
    downs = refs[apart + 1 : apart + 1 + members]
    weight = refs[apart + 1 + members]
    out, *columns = refs[-3:]
    extent = downs[0].shape[1]
    lanes = columns[0].shape[2]
    value_width = gradients[0].shape[1] // (2 * members)
    some = min(4, members)
    for first in range(0, members, some):
        slots = range(first, first + some)
        lines = jnp.concatenate([gradients[slot][...] for slot in slots], axis=0)
        for half in range(2):
            right = weight[...] if half == 0 else pair[members * extent :]
            frozen = jnp.dot(lines, right, preferred_element_type=jnp.float32)
            for slot in slots:
                down = downs[slot][0] if half == 0 else pair[slot * extent : (slot + 1) * extent]
                index = side_index(place[0] ^ line_offset(slot, members), members)
                low = jnp.dot(backs[slot], down, preferred_element_type=jnp.float32)
                at = (slot - first) * rows
                out[index, half] = (frozen[at : at + rows] + low).astype(jnp.bfloat16)
    for side in range(2):
        column = (place[0] ^ (side * pair_bit)) * value_width // lanes * lanes
        for slot in range(members):
            columns[side][slot] = gradients[slot][:, pl.ds(pl.multiple_of(column, lanes), lanes)]


def input_slices(adapters, place, gradients, backs, weight, pair, down_maps):
    members, rows, _ = backs.shape
    width = weight.shape[1]
    lanes = max(128, gradients[0].shape[2] // (2 * members))
    shape = jax.ShapeDtypeStruct((members, 2, rows, width), jnp.bfloat16)
    columns = jax.ShapeDtypeStruct((members, rows, lanes), jnp.bfloat16)
    return call(
        input_kernel,
        "input_slices",
        (adapters, place),
        [backs, pair] + list(gradients) + [down_maps] * members + [weight],
        [whole(backs.shape), whole(pair.shape)]
        + [whole(gradient.shape) for gradient in gradients]
        + [picked(down_maps, line_offset(slot, members)) for slot in range(members)]
        + [whole(weight.shape)],
        [shape, columns, columns],
    )


def hidden_kernel(adapters, place, pair, tokens, *refs):
    parts, own, *others = refs[-4:]
    members = own.shape[0]
    downs = refs[:members]
    extent = downs[0].shape[1]
    across = (((1,), (1,)), ((), ()))
    for slot in range(members):
        index = side_index(place[0] ^ line_offset(slot, members), members)
        own[slot] = tokens[index, 0]
        others[slot // (members // 2)][slot % (members // 2)] = tokens[index, 1]
        parts[slot] = lax.dot_general(
            tokens[index, 0], downs[slot][0], across, preferred_element_type=jnp.float32
        ) + lax.dot_general(
            tokens[index, 1],
            pair[slot * extent : (slot + 1) * extent],
            across,
            preferred_element_type=jnp.float32,
        )


def hidden_parts(adapters, place, down_maps, pair, tokens):
    members, _, rows, width = tokens.shape
    extent = down_maps.shape[1]
    others = jax.ShapeDtypeStruct((members // 2, rows, width), tokens.dtype)
    return call(
        hidden_kernel,
        "hidden_parts",
        (adapters, place),
        [pair, tokens] + [down_maps] * members,
        [whole(pair.shape), whole(tokens.shape)]
        + [picked(down_maps, line_offset(slot, members)) for slot in range(members)],
        [
            jax.ShapeDtypeStruct((members, rows, extent), jnp.float32),
            jax.ShapeDtypeStruct((members, rows, width), tokens.dtype),
            others,
            others,
        ],
    )


def sum_kernel(total, received, *outs, flip):
    for slot in range(outs[0].shape[0]):
        value = total[slot] + received[slot ^ flip].astype(jnp.float32)
        for out in outs:
            out[slot] = value.astype(out.dtype)


def slot_sums(total, received, flip, types):
    shape = received.shape
    return call(
        functools.partial(sum_kernel, flip=flip),
        "slot_sums",
        (),
        (total, received),
        [whole(shape)] * 2,
        [jax.ShapeDtypeStruct(shape, kind) for kind in types],
    )


def hidden_low_kernel(adapters, place, ranks, total, received, out, *, flip, members):
    for slot in range(out.shape[0]):
        block = place[0] ^ line_offset(slot, members)
        alive, _ = rank_row(ranks, adapters[block], out.shape[2])
        value = total[slot] + received[slot ^ flip].astype(jnp.float32)
        out[slot] = (value * alive).astype(out.dtype)


def hidden_rows(adapters, place, ranks, total, received, flip, members):
    return call(
        functools.partial(hidden_low_kernel, flip=flip, members=members),
        "hidden_low",
        (adapters, place, ranks),
        (total, received),
        [whole(total.shape)] * 2,
        [jax.ShapeDtypeStruct(total.shape, jnp.bfloat16)],
    )[0]


def join_kernel(place, source, out, sems):
    members, _, _, width = source.shape
    copies = []
    for index in range(members):
        for half in range(2):
            column = side_place(index, side_of(place[0]) ^ half, members) * width
            copies.append(
                pltpu.make_async_copy(
                    source.at[index, half],
                    out.at[:, pl.ds(pl.multiple_of(column, width), width)],
                    sems.at[2 * index + half],
                )
            )
    run(copies)


def join_columns(place, source):
    members, _, rows, width = source.shape
    return pl.pallas_call(
        join_kernel,
        out_shape=jax.ShapeDtypeStruct((rows, 2 * members * width), source.dtype),
        grid_spec=pltpu.PrefetchScalarGridSpec(
            num_scalar_prefetch=1,
            grid=(1,),
            in_specs=[whole(source.shape)],
            out_specs=pl.BlockSpec(memory_space=pl.ANY),
            scratch_shapes=[pltpu.SemaphoreType.DMA((2 * members,))],
        ),
        compiler_params=params(),
        name="join_columns",
    )(place, source)


def list_members(adapters, place, members, head, following):
    def clear(adapter, carry):
        head[adapter] = -1
        return carry

    lax.fori_loop(0, head.shape[0], clear, 0)
    for entry in reversed(range(2 * members)):
        side, own = divmod(entry, members)
        adapter = adapters[place[0] ^ line_offset(own, members) ^ (side * pair_bit)]
        following[entry] = head[adapter]
        head[adapter] = entry


def write_sums(head, following, products, ready, zero, out, sems, finish):
    num_adapters = out.shape[0]
    zero[...] = jnp.zeros_like(zero)

    def write(adapter, carry):
        first = head[adapter]

        @pl.when(first < 0)
        def _():
            pltpu.make_async_copy(zero, out.at[adapter], sems.at[adapter]).start()

        @pl.when(first >= 0)
        def _():
            def more(entry):
                products[first] += products[entry]
                return following[entry]

            lax.while_loop(lambda entry: entry >= 0, more, following[first])
            ready[first] = finish(adapter, products[first]).astype(out.dtype)
            pltpu.make_async_copy(ready.at[first], out.at[adapter], sems.at[adapter]).start()

        return carry

    lax.fori_loop(0, num_adapters, write, 0)

    def wait(adapter, carry):
        pltpu.make_async_copy(zero, out.at[adapter], sems.at[adapter]).wait()
        return carry

    lax.fori_loop(0, num_adapters, wait, 0)


def by_rows(left, right):
    return lax.dot_general(
        left, right, (((0,), (0,)), ((), ())), preferred_element_type=jnp.float32
    )


def sums_call(kernel, name, prefetch, operands, num_adapters, entries, product, scratch=()):
    return pl.pallas_call(
        kernel,
        out_shape=jax.ShapeDtypeStruct((num_adapters,) + product, jnp.bfloat16),
        grid_spec=pltpu.PrefetchScalarGridSpec(
            num_scalar_prefetch=len(prefetch),
            grid=(1,),
            in_specs=[whole(operand.shape) for operand in operands],
            out_specs=pl.BlockSpec(memory_space=pltpu.HBM),
            scratch_shapes=[
                pltpu.SMEM((num_adapters,), jnp.int32),
                pltpu.SMEM((entries,), jnp.int32),
                pltpu.VMEM((entries,) + product, jnp.float32),
                pltpu.VMEM((entries,) + product, jnp.bfloat16),
                pltpu.VMEM(product, jnp.bfloat16),
                pltpu.SemaphoreType.DMA((num_adapters,)),
                *scratch,
            ],
        ),
        compiler_params=params(),
        name=name,
    )(*prefetch, *operands)


def down_gradient_kernel(
    adapters,
    place,
    backs,
    backs_pair,
    own,
    other_first,
    other_second,
    out,
    head,
    following,
    products,
    ready,
    zero,
    sems,
):
    members = own.shape[0]
    others = (other_first, other_second)
    list_members(adapters, place, members, head, following)
    for slot in range(members):
        products[slot] = by_rows(backs[slot], own[slot])
        core, line = divmod(slot, members // 2)
        products[members + slot] = by_rows(backs_pair[slot], others[core][line])
    write_sums(
        head, following, products, ready, zero, out, sems, lambda adapter, total: total
    )


def down_gradients(adapters, place, backs, backs_pair, own, others, num_adapters):
    members, _, width = own.shape
    return sums_call(
        down_gradient_kernel,
        "down_gradients",
        (adapters, place),
        (backs, backs_pair, own, *others),
        num_adapters,
        2 * members,
        (backs.shape[2], width),
    )


def up_gradient_kernel(
    adapters,
    place,
    ranks,
    gradients,
    gradients_pair,
    hiddens,
    hiddens_pair,
    out,
    head,
    following,
    products,
    ready,
    zero,
    sems,
    lines,
):
    members, _, lanes = gradients.shape
    width, extent = out.shape[1:]
    list_members(adapters, place, members, head, following)
    inside = pl.multiple_of(lax.rem(place[0], lanes // width) * width, width)
    for slot in range(members):
        lines[slot] = by_rows(gradients[slot], hiddens[slot])
        lines[members + slot] = by_rows(gradients_pair[slot], hiddens_pair[slot])
    for entry in range(2 * members):
        products[entry] = lines[entry, pl.ds(inside, width), :]

    def finish(adapter, total):
        _, factor = rank_row(ranks, adapter, extent)
        return factor * total

    write_sums(head, following, products, ready, zero, out, sems, finish)


def up_gradients(adapters, place, ranks, gradients, gradients_pair, hiddens, hiddens_pair, width):
    members, _, lanes = gradients.shape
    extent = hiddens.shape[2]
    return sums_call(
        up_gradient_kernel,
        "up_gradients",
        (adapters, place, ranks),
        (gradients, gradients_pair, hiddens, hiddens_pair),
        ranks.shape[0],
        2 * members,
        (width, extent),
        [pltpu.VMEM((2 * members, lanes, extent), jnp.float32)],
    )


def exchange(pieces):
    return lax.all_to_all(pieces, "dp", split_axis=0, concat_axis=0, tiled=True)


def exchange_side(pieces):
    members = pieces.shape[0]
    groups = [[side_place(index, side, members) for index in range(members)] for side in range(2)]
    return lax.all_to_all(
        pieces, "dp", split_axis=0, concat_axis=0, axis_index_groups=groups, tiled=True
    )


def swap(array, flip):
    devices = lax.axis_size("dp")
    return lax.ppermute(array, "dp", [(i, i ^ flip) for i in range(devices)])


def tie(first, second):
    return lax.optimization_barrier((first, second))


def gather_step(held, members):
    arrived = swap(held, line_offset(held.shape[0], members))
    return jnp.concatenate([held, arrived], axis=0)


def local(tokens, output_gradient, value_weight, down_maps, up_maps, adapter_per_block, ranks):
    devices = lax.axis_size("dp")
    members = devices // 2
    lines = members // 2
    steps = members.bit_length() - 1
    num_adapters, extent, width = down_maps.shape
    rows, depth = output_gradient.shape
    place = lax.axis_index("dp").astype(jnp.int32).reshape(1)
    adapters = adapter_per_block
    offsets = [line_offset(slot, members) for slot in range(members)]
    barrier = lax.optimization_barrier

    own_gradient = output_gradient.reshape(1, rows, depth)
    gradients = [own_gradient] + [None] * (lines - 1)
    for step in range(steps - 1):
        gradients[1 << step] = swap(own_gradient, offsets[1 << step])
    own_up = exchange(gather_up(adapters, up_maps)).reshape(depth, extent)
    packs = pack_tokens(place, tokens, members, width)
    pair = for_pair(adapters, place, value_weight, down_maps, members)
    for step in range(1, steps - 1):
        for slot in range(1, 1 << step):
            gradients[slot + (1 << step)] = swap(gradients[slot], offsets[1 << step])
    gradients, own_up, packs, pair = barrier((gradients, own_up, packs, pair))

    arrived = exchange_side(packs)
    pair = swap(pair, pair_bit)
    gradients.append(swap(jnp.concatenate(gradients, axis=0), 1))
    backs = back_rows(adapters, place, ranks, output_gradient, own_up)
    backs = gather_step(backs, members)
    arrived, backs, gradients, pair = barrier((arrived, backs, gradients, pair))

    parts, tokens_own, *tokens_pair = hidden_parts(
        adapters, place, down_maps, pair, arrived
    )
    tokens_other = [swap(tokens_pair[0], pair_bit)]
    while backs.shape[0] < members:
        backs = gather_step(backs, members)
    slices, columns, columns_pair = input_slices(
        adapters, place, gradients, backs, value_weight, pair, down_maps
    )
    total, flip = parts, 0
    received = swap(parts[lines:], 1)
    for step in reversed(range(steps - 1)):
        kinds = [jnp.float32] if step else [jnp.float32, jnp.bfloat16]
        sums = slot_sums(total, received, flip, kinds)
        total, flip = sums[0], 1 << step
        received = swap(sums[-1], offsets[flip])
    received, slices, columns_pair, backs, tokens_pair, tokens_other = barrier(
        (received, slices, columns_pair, backs, tokens_pair, tokens_other)
    )

    result = exchange_side(slices)
    hiddens = hidden_rows(adapters, place, ranks, total, received, flip, members)
    hiddens = gather_step(hiddens, members)
    hiddens_pair = swap(hiddens, pair_bit)
    columns_other = swap(columns_pair, pair_bit)
    backs_pair = swap(backs, pair_bit)
    hiddens_pair, columns_other, backs_pair, tokens_pair = barrier(
        (hiddens_pair, columns_other, backs_pair, tokens_pair)
    )
    tokens_other.append(swap(tokens_pair[1], pair_bit))
    up_gradient = up_gradients(
        adapters, place, ranks, columns, columns_other, hiddens, hiddens_pair, depth // devices
    )
    down_gradient = down_gradients(
        adapters, place, backs, backs_pair, tokens_own, tokens_other, num_adapters
    )
    up_gradient, down_gradient, result = barrier((up_gradient, down_gradient, result))
    return (join_columns(place, result), down_gradient, up_gradient)


def solution(mesh):
    in_specs = (
        P(("groups", "dp"), None),
        P(("groups", "dp"), None),
        P(None, "dp"),
        P(None, None, "dp"),
        P(None, "dp", None),
        P("groups"),
        P(),
    )
    out_specs = (P(("groups", "dp"), None), P("groups", None, "dp"), P("groups", "dp", None))
    return jax.shard_map(local, mesh=mesh, in_specs=in_specs, out_specs=out_specs, check_vma=False)
```

```python
import functools

import jax
import jax.numpy as jnp
from jax import lax
from jax.experimental import pallas as pl
from jax.experimental.pallas import tpu as pltpu
from jax.sharding import PartitionSpec as P

adapter_alpha = 32.0
vmem_limit = 48 * 1024 * 1024
pair_bit = 2
line_bit = 4


def line_offset(slot, members):
    bits = members.bit_length() - 1
    order = 0
    for bit in range(bits):
        order |= ((slot >> bit) & 1) << (bits - 1 - bit)
    return ((order // 2) * line_bit) | (order % 2)


def side_of(place):
    return place % line_bit // pair_bit


def reversed_bits(number, count):
    bits = count.bit_length() - 1
    return sum(((number >> bit) & 1) << (bits - 1 - bit) for bit in range(bits))


def side_index(place, members):
    lines = members // 2
    return place % pair_bit * lines + reversed_bits(place // line_bit, lines)


def side_place(index, side, members):
    core, line = divmod(index, members // 2)
    return reversed_bits(line, members // 2) * line_bit + side * pair_bit + core


def params():
    return pltpu.CompilerParams(vmem_limit_bytes=vmem_limit)


def whole(shape):
    return pl.BlockSpec(shape, lambda *_: (0,) * len(shape))


def picked(maps, flip):
    return pl.BlockSpec(
        (1,) + maps.shape[1:], lambda i, adapters, place, *_: (adapters[place[0] ^ flip], 0, 0)
    )


def call(kernel, name, prefetch, operands, in_specs, out_shapes, scratch=(), grid=(1,), out_specs=None):
    if out_specs is None:
        out_specs = [whole(shape.shape) for shape in out_shapes]
    return pl.pallas_call(
        kernel,
        out_shape=out_shapes,
        grid_spec=pltpu.PrefetchScalarGridSpec(
            num_scalar_prefetch=len(prefetch),
            grid=grid,
            in_specs=in_specs,
            out_specs=out_specs,
            scratch_shapes=list(scratch),
        ),
        compiler_params=params(),
        name=name,
    )(*prefetch, *operands)


def run(copies):
    for copy in copies:
        copy.start()
    for copy in copies:
        copy.wait()


def copy_call(kernel, name, prefetch, operands, out_shapes, copies):
    return pl.pallas_call(
        kernel,
        out_shape=out_shapes,
        grid_spec=pltpu.PrefetchScalarGridSpec(
            num_scalar_prefetch=len(prefetch),
            grid=(1,),
            in_specs=[pl.BlockSpec(memory_space=pl.ANY)] * len(operands),
            out_specs=[whole(shape.shape) for shape in out_shapes],
            scratch_shapes=[pltpu.SemaphoreType.DMA((copies,))],
        ),
        compiler_params=params(),
        name=name,
    )(*prefetch, *operands)


weight_cuts = 4


def pair_kernel(adapters, place, weight, down_maps, out, sems):
    extent = down_maps.shape[1]
    depth = weight.shape[0]
    members = (out.shape[0] - depth) // extent
    copies = []
    for slot in range(members):
        block = place[0] ^ line_offset(slot, members) ^ pair_bit
        copies.append((down_maps.at[adapters[block]], slot * extent, extent))
    cut = depth // weight_cuts
    for at in range(0, depth, cut):
        copies.append((weight.at[pl.ds(at, cut)], members * extent + at, cut))
    run(
        [
            pltpu.make_async_copy(source, out.at[pl.ds(at, rows)], sems.at[number])
            for number, (source, at, rows) in enumerate(copies)
        ]
    )


def for_pair(adapters, place, weight, down_maps, members):
    extent, width = down_maps.shape[1:]
    shape = jax.ShapeDtypeStruct((members * extent + weight.shape[0], width), weight.dtype)
    return copy_call(
        pair_kernel,
        "for_pair",
        (adapters, place),
        (weight, down_maps),
        [shape],
        members + weight_cuts,
    )[0]


def gather_up_kernel(adapters, up_maps, out, sems):
    run(
        [
            pltpu.make_async_copy(up_maps.at[adapters[block]], out.at[block], sems.at[block])
            for block in range(out.shape[0])
        ]
    )


def gather_up(adapters, up_maps):
    shape = jax.ShapeDtypeStruct((adapters.shape[0],) + up_maps.shape[1:], up_maps.dtype)
    return copy_call(
        gather_up_kernel, "gather_up", (adapters,), (up_maps,), [shape], adapters.shape[0]
    )[0]


def pack_kernel(place, tokens, out, sems):
    members, _, _, width = out.shape
    copies = []
    for index in range(members):
        for half in range(2):
            column = side_place(index, side_of(place[0]) ^ half, members) * width
            copies.append(
                pltpu.make_async_copy(
                    tokens.at[:, pl.ds(pl.multiple_of(column, width), width)],
                    out.at[index, half],
                    sems.at[2 * index + half],
                )
            )
    run(copies)


def pack_tokens(place, tokens, members, width):
    shape = jax.ShapeDtypeStruct((members, 2, tokens.shape[0], width), tokens.dtype)
    return copy_call(pack_kernel, "pack_tokens", (place,), (tokens,), [shape], 2 * members)[0]


def rank_row(ranks, adapter, extent):
    rank = jnp.full((1, extent), ranks[adapter], jnp.int32)
    alive = (lax.broadcasted_iota(jnp.int32, (1, extent), 1) < rank).astype(jnp.float32)
    return alive, adapter_alpha / rank.astype(jnp.float32)


def back_kernel(adapters, place, ranks, gradient, up, out):
    alive, factor = rank_row(ranks, adapters[place[0]], up.shape[1])
    back = jnp.dot(gradient[...], up[...], preferred_element_type=jnp.float32)
    out[0] = (factor * back * alive).astype(out.dtype)


def back_rows(adapters, place, ranks, gradient, up):
    return call(
        back_kernel,
        "back_low",
        (adapters, place, ranks),
        (gradient, up),
        [whole(gradient.shape), whole(up.shape)],
        [jax.ShapeDtypeStruct((1, gradient.shape[0], up.shape[1]), jnp.bfloat16)],
    )[0]


def input_kernel(adapters, place, backs, pair, *refs):
    members, rows, _ = backs.shape
    apart = members // 2
    gradients = [ref.at[0] for ref in refs[:apart]]
    for ref in refs[apart : apart + 2]:
        gradients += [ref.at[slot] for slot in range(ref.shape[0])]
    downs = refs[apart + 2 : apart + 2 + members]
    weight = refs[apart + 2 + members]
    out, *columns = refs[-3:]
    extent = downs[0].shape[1]
    lanes = columns[0].shape[2]
    value_width = gradients[0].shape[1] // (2 * members)
    some = min(4, members)
    for first in range(0, members, some):
        slots = range(first, first + some)
        lines = jnp.concatenate([gradients[slot][...] for slot in slots], axis=0)
        for half in range(2):
            right = weight[...] if half == 0 else pair[members * extent :]
            frozen = jnp.dot(lines, right, preferred_element_type=jnp.float32)
            for slot in slots:
                down = downs[slot][0] if half == 0 else pair[slot * extent : (slot + 1) * extent]
                index = side_index(place[0] ^ line_offset(slot, members), members)
                low = jnp.dot(backs[slot], down, preferred_element_type=jnp.float32)
                at = (slot - first) * rows
                out[index, half] = (frozen[at : at + rows] + low).astype(jnp.bfloat16)
    for side in range(2):
        column = (place[0] ^ (side * pair_bit)) * value_width // lanes * lanes
        for slot in range(members):
            columns[side][slot] = gradients[slot][:, pl.ds(pl.multiple_of(column, lanes), lanes)]


def input_slices(adapters, place, gradients, backs, weight, pair, down_maps):
    members, rows, _ = backs.shape
    width = weight.shape[1]
    lanes = max(128, gradients[0].shape[2] // (2 * members))
    shape = jax.ShapeDtypeStruct((members, 2, rows, width), jnp.bfloat16)
    columns = jax.ShapeDtypeStruct((members, rows, lanes), jnp.bfloat16)
    return call(
        input_kernel,
        "input_slices",
        (adapters, place),
        [backs, pair] + list(gradients) + [down_maps] * members + [weight],
        [whole(backs.shape), whole(pair.shape)]
        + [whole(gradient.shape) for gradient in gradients]
        + [picked(down_maps, line_offset(slot, members)) for slot in range(members)]
        + [whole(weight.shape)],
        [shape, columns, columns],
    )


def hidden_kernel(adapters, place, pair, tokens, *refs):
    parts, own, *others = refs[-4:]
    members = own.shape[0]
    downs = refs[:members]
    extent = downs[0].shape[1]
    across = (((1,), (1,)), ((), ()))
    for slot in range(members):
        index = side_index(place[0] ^ line_offset(slot, members), members)
        own[slot] = tokens[index, 0]
        others[slot // (members // 2)][slot % (members // 2)] = tokens[index, 1]
        parts[slot] = lax.dot_general(
            tokens[index, 0], downs[slot][0], across, preferred_element_type=jnp.float32
        ) + lax.dot_general(
            tokens[index, 1],
            pair[slot * extent : (slot + 1) * extent],
            across,
            preferred_element_type=jnp.float32,
        )


def hidden_parts(adapters, place, down_maps, pair, tokens):
    members, _, rows, width = tokens.shape
    extent = down_maps.shape[1]
    others = jax.ShapeDtypeStruct((members // 2, rows, width), tokens.dtype)
    return call(
        hidden_kernel,
        "hidden_parts",
        (adapters, place),
        [pair, tokens] + [down_maps] * members,
        [whole(pair.shape), whole(tokens.shape)]
        + [picked(down_maps, line_offset(slot, members)) for slot in range(members)],
        [
            jax.ShapeDtypeStruct((members, rows, extent), jnp.float32),
            jax.ShapeDtypeStruct((members, rows, width), tokens.dtype),
            others,
            others,
        ],
    )


def sum_kernel(total, received, *outs, flip):
    for slot in range(outs[0].shape[0]):
        value = total[slot] + received[slot ^ flip].astype(jnp.float32)
        for out in outs:
            out[slot] = value.astype(out.dtype)


def slot_sums(total, received, flip, types):
    shape = received.shape
    return call(
        functools.partial(sum_kernel, flip=flip),
        "slot_sums",
        (),
        (total, received),
        [whole(shape)] * 2,
        [jax.ShapeDtypeStruct(shape, kind) for kind in types],
    )


def hidden_low_kernel(adapters, place, ranks, total, received, out, *, flip, members):
    for slot in range(out.shape[0]):
        block = place[0] ^ line_offset(slot, members)
        alive, _ = rank_row(ranks, adapters[block], out.shape[2])
        value = total[slot] + received[slot ^ flip].astype(jnp.float32)
        out[slot] = (value * alive).astype(out.dtype)


def hidden_rows(adapters, place, ranks, total, received, flip, members):
    return call(
        functools.partial(hidden_low_kernel, flip=flip, members=members),
        "hidden_low",
        (adapters, place, ranks),
        (total, received),
        [whole(total.shape)] * 2,
        [jax.ShapeDtypeStruct(total.shape, jnp.bfloat16)],
    )[0]


def join_kernel(place, source, out, sems):
    members, _, _, width = source.shape
    copies = []
    for index in range(members):
        for half in range(2):
            column = side_place(index, side_of(place[0]) ^ half, members) * width
            copies.append(
                pltpu.make_async_copy(
                    source.at[index, half],
                    out.at[:, pl.ds(pl.multiple_of(column, width), width)],
                    sems.at[2 * index + half],
                )
            )
    run(copies)


def join_columns(place, source):
    members, _, rows, width = source.shape
    return pl.pallas_call(
        join_kernel,
        out_shape=jax.ShapeDtypeStruct((rows, 2 * members * width), source.dtype),
        grid_spec=pltpu.PrefetchScalarGridSpec(
            num_scalar_prefetch=1,
            grid=(1,),
            in_specs=[whole(source.shape)],
            out_specs=pl.BlockSpec(memory_space=pl.ANY),
            scratch_shapes=[pltpu.SemaphoreType.DMA((2 * members,))],
        ),
        compiler_params=params(),
        name="join_columns",
    )(place, source)


def list_members(adapters, place, members, head, following):
    def clear(adapter, carry):
        head[adapter] = -1
        return carry

    lax.fori_loop(0, head.shape[0], clear, 0)
    for entry in reversed(range(2 * members)):
        side, own = divmod(entry, members)
        adapter = adapters[place[0] ^ line_offset(own, members) ^ (side * pair_bit)]
        following[entry] = head[adapter]
        head[adapter] = entry


def write_sums(head, following, products, ready, zero, out, sems, finish):
    num_adapters = out.shape[0]
    zero[...] = jnp.zeros_like(zero)

    def write(adapter, carry):
        first = head[adapter]

        @pl.when(first < 0)
        def _():
            pltpu.make_async_copy(zero, out.at[adapter], sems.at[adapter]).start()

        @pl.when(first >= 0)
        def _():
            def more(entry):
                products[first] += products[entry]
                return following[entry]

            lax.while_loop(lambda entry: entry >= 0, more, following[first])
            ready[first] = finish(adapter, products[first]).astype(out.dtype)
            pltpu.make_async_copy(ready.at[first], out.at[adapter], sems.at[adapter]).start()

        return carry

    lax.fori_loop(0, num_adapters, write, 0)

    def wait(adapter, carry):
        pltpu.make_async_copy(zero, out.at[adapter], sems.at[adapter]).wait()
        return carry

    lax.fori_loop(0, num_adapters, wait, 0)


def by_rows(left, right):
    return lax.dot_general(
        left, right, (((0,), (0,)), ((), ())), preferred_element_type=jnp.float32
    )


def sums_call(kernel, name, prefetch, operands, num_adapters, entries, product, scratch=()):
    return pl.pallas_call(
        kernel,
        out_shape=jax.ShapeDtypeStruct((num_adapters,) + product, jnp.bfloat16),
        grid_spec=pltpu.PrefetchScalarGridSpec(
            num_scalar_prefetch=len(prefetch),
            grid=(1,),
            in_specs=[whole(operand.shape) for operand in operands],
            out_specs=pl.BlockSpec(memory_space=pltpu.HBM),
            scratch_shapes=[
                pltpu.SMEM((num_adapters,), jnp.int32),
                pltpu.SMEM((entries,), jnp.int32),
                pltpu.VMEM((entries,) + product, jnp.float32),
                pltpu.VMEM((entries,) + product, jnp.bfloat16),
                pltpu.VMEM(product, jnp.bfloat16),
                pltpu.SemaphoreType.DMA((num_adapters,)),
                *scratch,
            ],
        ),
        compiler_params=params(),
        name=name,
    )(*prefetch, *operands)


def down_gradient_kernel(
    adapters,
    place,
    backs,
    backs_pair,
    own,
    other_first,
    other_second,
    out,
    head,
    following,
    products,
    ready,
    zero,
    sems,
):
    members = own.shape[0]
    others = (other_first, other_second)
    list_members(adapters, place, members, head, following)
    for slot in range(members):
        products[slot] = by_rows(backs[slot], own[slot])
        core, line = divmod(slot, members // 2)
        products[members + slot] = by_rows(backs_pair[slot], others[core][line])
    write_sums(
        head, following, products, ready, zero, out, sems, lambda adapter, total: total
    )


def down_gradients(adapters, place, backs, backs_pair, own, others, num_adapters):
    members, _, width = own.shape
    return sums_call(
        down_gradient_kernel,
        "down_gradients",
        (adapters, place),
        (backs, backs_pair, own, *others),
        num_adapters,
        2 * members,
        (backs.shape[2], width),
    )


def up_gradient_kernel(
    adapters,
    place,
    ranks,
    gradients,
    gradients_pair,
    hiddens,
    hiddens_pair,
    out,
    head,
    following,
    products,
    ready,
    zero,
    sems,
    lines,
):
    members, _, lanes = gradients.shape
    width, extent = out.shape[1:]
    list_members(adapters, place, members, head, following)
    inside = pl.multiple_of(lax.rem(place[0], lanes // width) * width, width)
    for slot in range(members):
        lines[slot] = by_rows(gradients[slot], hiddens[slot])
        lines[members + slot] = by_rows(gradients_pair[slot], hiddens_pair[slot])
    for entry in range(2 * members):
        products[entry] = lines[entry, pl.ds(inside, width), :]

    def finish(adapter, total):
        _, factor = rank_row(ranks, adapter, extent)
        return factor * total

    write_sums(head, following, products, ready, zero, out, sems, finish)


def up_gradients(adapters, place, ranks, gradients, gradients_pair, hiddens, hiddens_pair, width):
    members, _, lanes = gradients.shape
    extent = hiddens.shape[2]
    return sums_call(
        up_gradient_kernel,
        "up_gradients",
        (adapters, place, ranks),
        (gradients, gradients_pair, hiddens, hiddens_pair),
        ranks.shape[0],
        2 * members,
        (width, extent),
        [pltpu.VMEM((2 * members, lanes, extent), jnp.float32)],
    )


def exchange(pieces):
    return lax.all_to_all(pieces, "dp", split_axis=0, concat_axis=0, tiled=True)


def exchange_side(pieces):
    members = pieces.shape[0]
    groups = [[side_place(index, side, members) for index in range(members)] for side in range(2)]
    return lax.all_to_all(
        pieces, "dp", split_axis=0, concat_axis=0, axis_index_groups=groups, tiled=True
    )


def swap(array, flip):
    devices = lax.axis_size("dp")
    return lax.ppermute(array, "dp", [(i, i ^ flip) for i in range(devices)])


def tie(first, second):
    return lax.optimization_barrier((first, second))


def gather_step(held, members):
    arrived = swap(held, line_offset(held.shape[0], members))
    return jnp.concatenate([held, arrived], axis=0)


def local(tokens, output_gradient, value_weight, down_maps, up_maps, adapter_per_block, ranks):
    devices = lax.axis_size("dp")
    members = devices // 2
    lines = members // 2
    steps = members.bit_length() - 1
    num_adapters, extent, width = down_maps.shape
    rows, depth = output_gradient.shape
    place = lax.axis_index("dp").astype(jnp.int32).reshape(1)
    adapters = adapter_per_block
    offsets = [line_offset(slot, members) for slot in range(members)]
    barrier = lax.optimization_barrier

    own_gradient = output_gradient.reshape(1, rows, depth)
    gradients = [own_gradient] + [None] * (lines - 1)
    for step in range(steps - 1):
        gradients[1 << step] = swap(own_gradient, offsets[1 << step])
    own_up = exchange(gather_up(adapters, up_maps)).reshape(depth, extent)
    packs = pack_tokens(place, tokens, members, width)
    pair = for_pair(adapters, place, value_weight, down_maps, members)
    across = [swap(jnp.concatenate(gradients[:2], axis=0), 1)]
    firsts = [gradients[1 << step] for step in range(steps - 1)]
    firsts, across, own_up, packs, pair = barrier((firsts, across, own_up, packs, pair))
    for step in range(steps - 1):
        gradients[1 << step] = firsts[step]

    arrived = exchange_side(packs)
    pair = swap(pair, pair_bit)
    for step in range(1, steps - 1):
        for slot in range(1, 1 << step):
            gradients[slot + (1 << step)] = swap(gradients[slot], offsets[1 << step])
    across.append(swap(jnp.concatenate(gradients[2:], axis=0), 1))
    backs = back_rows(adapters, place, ranks, output_gradient, own_up)
    backs = [backs] + [swap(backs, offset) for offset in offsets[1:lines]]
    arrived, backs, gradients, across, pair = barrier(
        (arrived, backs, gradients, across, pair)
    )

    parts, tokens_own, *tokens_pair = hidden_parts(
        adapters, place, down_maps, pair, arrived
    )
    backs = gather_step(jnp.concatenate(backs, axis=0), members)
    slices, columns, columns_pair = input_slices(
        adapters, place, gradients + across, backs, value_weight, pair, down_maps
    )
    total, received, flip = parts, swap(parts[lines:], 1), 0
    for step in range(steps - 1):
        kinds = [jnp.float32] if step else [jnp.float32, jnp.bfloat16]
        sums = slot_sums(total, received, flip, kinds)
        total, flip = sums[0], 1 << step
        received = swap(sums[-1], offsets[flip])
        if step == 0:
            received, slices, columns_pair, backs, tokens_pair = barrier(
                (received, slices, columns_pair, backs, tokens_pair)
            )
            result = exchange_side(slices)

    hiddens = hidden_rows(adapters, place, ranks, total, received, flip, members)
    hiddens = gather_step(hiddens, members)
    columns_other = swap(columns_pair, pair_bit)
    backs_pair = swap(backs, pair_bit)
    tokens_other = [swap(half, pair_bit) for half in tokens_pair]
    hiddens_pair = swap(hiddens, pair_bit)
    up_gradient = up_gradients(
        adapters, place, ranks, columns, columns_other, hiddens, hiddens_pair, depth // devices
    )
    down_gradient = down_gradients(
        adapters, place, backs, backs_pair, tokens_own, tokens_other, num_adapters
    )
    up_gradient, down_gradient, result = barrier((up_gradient, down_gradient, result))
    return (join_columns(place, result), down_gradient, up_gradient)


def solution(mesh):
    in_specs = (
        P(("groups", "dp"), None),
        P(("groups", "dp"), None),
        P(None, "dp"),
        P(None, None, "dp"),
        P(None, "dp", None),
        P("groups"),
        P(),
    )
    out_specs = (P(("groups", "dp"), None), P("groups", None, "dp"), P("groups", "dp", None))
    return jax.shard_map(local, mesh=mesh, in_specs=in_specs, out_specs=out_specs, check_vma=False)
```

```python
import functools

import jax
import jax.numpy as jnp
from jax import lax
from jax.experimental import pallas as pl
from jax.experimental.pallas import tpu as pltpu
from jax.sharding import PartitionSpec as P

adapter_alpha = 32.0
vmem_limit = 48 * 1024 * 1024
pair_bit = 2
line_bit = 4


def line_offset(slot, members):
    bits = members.bit_length() - 1
    order = 0
    for bit in range(bits):
        order |= ((slot >> bit) & 1) << (bits - 1 - bit)
    return ((order // 2) * line_bit) | (order % 2)


def side_of(place):
    return place % line_bit // pair_bit


def reversed_bits(number, count):
    bits = count.bit_length() - 1
    return sum(((number >> bit) & 1) << (bits - 1 - bit) for bit in range(bits))


def side_index(place, members):
    lines = members // 2
    return place % pair_bit * lines + reversed_bits(place // line_bit, lines)


def side_place(index, side, members):
    core, line = divmod(index, members // 2)
    return reversed_bits(line, members // 2) * line_bit + side * pair_bit + core


def params():
    return pltpu.CompilerParams(vmem_limit_bytes=vmem_limit)


def whole(shape):
    return pl.BlockSpec(shape, lambda *_: (0,) * len(shape))


def picked(maps, flip):
    return pl.BlockSpec(
        (1,) + maps.shape[1:], lambda i, adapters, place, *_: (adapters[place[0] ^ flip], 0, 0)
    )


def call(kernel, name, prefetch, operands, in_specs, out_shapes, scratch=(), grid=(1,), out_specs=None):
    if out_specs is None:
        out_specs = [whole(shape.shape) for shape in out_shapes]
    return pl.pallas_call(
        kernel,
        out_shape=out_shapes,
        grid_spec=pltpu.PrefetchScalarGridSpec(
            num_scalar_prefetch=len(prefetch),
            grid=grid,
            in_specs=in_specs,
            out_specs=out_specs,
            scratch_shapes=list(scratch),
        ),
        compiler_params=params(),
        name=name,
    )(*prefetch, *operands)


def run(copies):
    for copy in copies:
        copy.start()
    for copy in copies:
        copy.wait()


def copy_call(kernel, name, prefetch, operands, out_shapes, copies):
    return pl.pallas_call(
        kernel,
        out_shape=out_shapes,
        grid_spec=pltpu.PrefetchScalarGridSpec(
            num_scalar_prefetch=len(prefetch),
            grid=(1,),
            in_specs=[pl.BlockSpec(memory_space=pl.ANY)] * len(operands),
            out_specs=[whole(shape.shape) for shape in out_shapes],
            scratch_shapes=[pltpu.SemaphoreType.DMA((copies,))],
        ),
        compiler_params=params(),
        name=name,
    )(*prefetch, *operands)


weight_cuts = 4


def pair_kernel(adapters, place, weight, down_maps, out, sems):
    extent = down_maps.shape[1]
    depth = weight.shape[0]
    members = (out.shape[0] - depth) // extent
    copies = []
    for slot in range(members):
        block = place[0] ^ line_offset(slot, members) ^ pair_bit
        copies.append((down_maps.at[adapters[block]], slot * extent, extent))
    cut = depth // weight_cuts
    for at in range(0, depth, cut):
        copies.append((weight.at[pl.ds(at, cut)], members * extent + at, cut))
    run(
        [
            pltpu.make_async_copy(source, out.at[pl.ds(at, rows)], sems.at[number])
            for number, (source, at, rows) in enumerate(copies)
        ]
    )


def for_pair(adapters, place, weight, down_maps, members):
    extent, width = down_maps.shape[1:]
    shape = jax.ShapeDtypeStruct((members * extent + weight.shape[0], width), weight.dtype)
    return copy_call(
        pair_kernel,
        "for_pair",
        (adapters, place),
        (weight, down_maps),
        [shape],
        members + weight_cuts,
    )[0]


def gather_up_kernel(adapters, up_maps, out, sems):
    run(
        [
            pltpu.make_async_copy(up_maps.at[adapters[block]], out.at[block], sems.at[block])
            for block in range(out.shape[0])
        ]
    )


def gather_up(adapters, up_maps):
    shape = jax.ShapeDtypeStruct((adapters.shape[0],) + up_maps.shape[1:], up_maps.dtype)
    return copy_call(
        gather_up_kernel, "gather_up", (adapters,), (up_maps,), [shape], adapters.shape[0]
    )[0]


def pack_kernel(place, tokens, out, sems):
    members, _, _, width = out.shape
    copies = []
    for index in range(members):
        for half in range(2):
            column = side_place(index, side_of(place[0]) ^ half, members) * width
            copies.append(
                pltpu.make_async_copy(
                    tokens.at[:, pl.ds(pl.multiple_of(column, width), width)],
                    out.at[index, half],
                    sems.at[2 * index + half],
                )
            )
    run(copies)


def pack_tokens(place, tokens, members, width):
    shape = jax.ShapeDtypeStruct((members, 2, tokens.shape[0], width), tokens.dtype)
    return copy_call(pack_kernel, "pack_tokens", (place,), (tokens,), [shape], 2 * members)[0]


def rank_row(ranks, adapter, extent):
    rank = jnp.full((1, extent), ranks[adapter], jnp.int32)
    alive = (lax.broadcasted_iota(jnp.int32, (1, extent), 1) < rank).astype(jnp.float32)
    return alive, adapter_alpha / rank.astype(jnp.float32)


def back_kernel(adapters, place, ranks, gradient, up, out):
    alive, factor = rank_row(ranks, adapters[place[0]], up.shape[1])
    back = jnp.dot(gradient[...], up[...], preferred_element_type=jnp.float32)
    out[0] = (factor * back * alive).astype(out.dtype)


def back_rows(adapters, place, ranks, gradient, up):
    return call(
        back_kernel,
        "back_low",
        (adapters, place, ranks),
        (gradient, up),
        [whole(gradient.shape), whole(up.shape)],
        [jax.ShapeDtypeStruct((1, gradient.shape[0], up.shape[1]), jnp.bfloat16)],
    )[0]


def input_kernel(adapters, place, backs, pair, *refs):
    members, rows, _ = backs.shape
    gradients = [ref.at[0] for ref in refs[:members]]
    downs = refs[members : 2 * members]
    weight = refs[2 * members]
    out, *columns = refs[-3:]
    extent = downs[0].shape[1]
    lanes = columns[0].shape[2]
    value_width = gradients[0].shape[1] // (2 * members)
    some = min(4, members)
    for first in range(0, members, some):
        slots = range(first, first + some)
        lines = jnp.concatenate([gradients[slot][...] for slot in slots], axis=0)
        for half in range(2):
            right = weight[...] if half == 0 else pair[members * extent :]
            frozen = jnp.dot(lines, right, preferred_element_type=jnp.float32)
            for slot in slots:
                down = downs[slot][0] if half == 0 else pair[slot * extent : (slot + 1) * extent]
                index = side_index(place[0] ^ line_offset(slot, members), members)
                low = jnp.dot(backs[slot], down, preferred_element_type=jnp.float32)
                at = (slot - first) * rows
                out[index, half] = (frozen[at : at + rows] + low).astype(jnp.bfloat16)
    for side in range(2):
        column = (place[0] ^ (side * pair_bit)) * value_width // lanes * lanes
        for slot in range(members):
            columns[side][slot] = gradients[slot][:, pl.ds(pl.multiple_of(column, lanes), lanes)]


def input_slices(adapters, place, gradients, backs, weight, pair, down_maps):
    members, rows, _ = backs.shape
    width = weight.shape[1]
    lanes = max(128, gradients[0].shape[2] // (2 * members))
    shape = jax.ShapeDtypeStruct((members, 2, rows, width), jnp.bfloat16)
    columns = jax.ShapeDtypeStruct((members, rows, lanes), jnp.bfloat16)
    return call(
        input_kernel,
        "input_slices",
        (adapters, place),
        [backs, pair] + list(gradients) + [down_maps] * members + [weight],
        [whole(backs.shape), whole(pair.shape)]
        + [whole(gradient.shape) for gradient in gradients]
        + [picked(down_maps, line_offset(slot, members)) for slot in range(members)]
        + [whole(weight.shape)],
        [shape, columns, columns],
    )


def hidden_kernel(adapters, place, pair, tokens, *refs):
    parts, own, *others = refs[-4:]
    members = own.shape[0]
    downs = refs[:members]
    extent = downs[0].shape[1]
    across = (((1,), (1,)), ((), ()))
    for slot in range(members):
        index = side_index(place[0] ^ line_offset(slot, members), members)
        own[slot] = tokens[index, 0]
        others[slot // (members // 2)][slot % (members // 2)] = tokens[index, 1]
        parts[slot] = lax.dot_general(
            tokens[index, 0], downs[slot][0], across, preferred_element_type=jnp.float32
        ) + lax.dot_general(
            tokens[index, 1],
            pair[slot * extent : (slot + 1) * extent],
            across,
            preferred_element_type=jnp.float32,
        )


def hidden_parts(adapters, place, down_maps, pair, tokens):
    members, _, rows, width = tokens.shape
    extent = down_maps.shape[1]
    others = jax.ShapeDtypeStruct((members // 2, rows, width), tokens.dtype)
    return call(
        hidden_kernel,
        "hidden_parts",
        (adapters, place),
        [pair, tokens] + [down_maps] * members,
        [whole(pair.shape), whole(tokens.shape)]
        + [picked(down_maps, line_offset(slot, members)) for slot in range(members)],
        [
            jax.ShapeDtypeStruct((members, rows, extent), jnp.float32),
            jax.ShapeDtypeStruct((members, rows, width), tokens.dtype),
            others,
            others,
        ],
    )


def sum_kernel(total, received, *outs, flip):
    for slot in range(outs[0].shape[0]):
        value = total[slot] + received[slot ^ flip].astype(jnp.float32)
        for out in outs:
            out[slot] = value.astype(out.dtype)


def slot_sums(total, received, flip, types):
    shape = received.shape
    return call(
        functools.partial(sum_kernel, flip=flip),
        "slot_sums",
        (),
        (total, received),
        [whole(shape)] * 2,
        [jax.ShapeDtypeStruct(shape, kind) for kind in types],
    )


def hidden_low_kernel(adapters, place, ranks, total, received, out, *, flip, members):
    for slot in range(out.shape[0]):
        block = place[0] ^ line_offset(slot, members)
        alive, _ = rank_row(ranks, adapters[block], out.shape[2])
        value = total[slot] + received[slot ^ flip].astype(jnp.float32)
        out[slot] = (value * alive).astype(out.dtype)


def hidden_rows(adapters, place, ranks, total, received, flip, members):
    return call(
        functools.partial(hidden_low_kernel, flip=flip, members=members),
        "hidden_low",
        (adapters, place, ranks),
        (total, received),
        [whole(total.shape)] * 2,
        [jax.ShapeDtypeStruct(total.shape, jnp.bfloat16)],
    )[0]


def join_kernel(place, source, out, sems):
    members, _, _, width = source.shape
    copies = []
    for index in range(members):
        for half in range(2):
            column = side_place(index, side_of(place[0]) ^ half, members) * width
            copies.append(
                pltpu.make_async_copy(
                    source.at[index, half],
                    out.at[:, pl.ds(pl.multiple_of(column, width), width)],
                    sems.at[2 * index + half],
                )
            )
    run(copies)


def join_columns(place, source):
    members, _, rows, width = source.shape
    return pl.pallas_call(
        join_kernel,
        out_shape=jax.ShapeDtypeStruct((rows, 2 * members * width), source.dtype),
        grid_spec=pltpu.PrefetchScalarGridSpec(
            num_scalar_prefetch=1,
            grid=(1,),
            in_specs=[whole(source.shape)],
            out_specs=pl.BlockSpec(memory_space=pl.ANY),
            scratch_shapes=[pltpu.SemaphoreType.DMA((2 * members,))],
        ),
        compiler_params=params(),
        name="join_columns",
    )(place, source)


def list_members(adapters, place, members, head, following):
    def clear(adapter, carry):
        head[adapter] = -1
        return carry

    lax.fori_loop(0, head.shape[0], clear, 0)
    for entry in reversed(range(2 * members)):
        side, own = divmod(entry, members)
        adapter = adapters[place[0] ^ line_offset(own, members) ^ (side * pair_bit)]
        following[entry] = head[adapter]
        head[adapter] = entry


def write_sums(head, following, products, ready, zero, out, sems, finish):
    num_adapters = out.shape[0]
    zero[...] = jnp.zeros_like(zero)

    def write(adapter, carry):
        first = head[adapter]

        @pl.when(first < 0)
        def _():
            pltpu.make_async_copy(zero, out.at[adapter], sems.at[adapter]).start()

        @pl.when(first >= 0)
        def _():
            def more(entry):
                products[first] += products[entry]
                return following[entry]

            lax.while_loop(lambda entry: entry >= 0, more, following[first])
            ready[first] = finish(adapter, products[first]).astype(out.dtype)
            pltpu.make_async_copy(ready.at[first], out.at[adapter], sems.at[adapter]).start()

        return carry

    lax.fori_loop(0, num_adapters, write, 0)

    def wait(adapter, carry):
        pltpu.make_async_copy(zero, out.at[adapter], sems.at[adapter]).wait()
        return carry

    lax.fori_loop(0, num_adapters, wait, 0)


def by_rows(left, right):
    return lax.dot_general(
        left, right, (((0,), (0,)), ((), ())), preferred_element_type=jnp.float32
    )


def sums_call(kernel, name, prefetch, operands, num_adapters, entries, product, scratch=()):
    return pl.pallas_call(
        kernel,
        out_shape=jax.ShapeDtypeStruct((num_adapters,) + product, jnp.bfloat16),
        grid_spec=pltpu.PrefetchScalarGridSpec(
            num_scalar_prefetch=len(prefetch),
            grid=(1,),
            in_specs=[whole(operand.shape) for operand in operands],
            out_specs=pl.BlockSpec(memory_space=pltpu.HBM),
            scratch_shapes=[
                pltpu.SMEM((num_adapters,), jnp.int32),
                pltpu.SMEM((entries,), jnp.int32),
                pltpu.VMEM((entries,) + product, jnp.float32),
                pltpu.VMEM((entries,) + product, jnp.bfloat16),
                pltpu.VMEM(product, jnp.bfloat16),
                pltpu.SemaphoreType.DMA((num_adapters,)),
                *scratch,
            ],
        ),
        compiler_params=params(),
        name=name,
    )(*prefetch, *operands)


def down_gradient_kernel(
    adapters,
    place,
    backs,
    backs_pair,
    own,
    other_first,
    other_second,
    out,
    head,
    following,
    products,
    ready,
    zero,
    sems,
):
    members = own.shape[0]
    others = (other_first, other_second)
    list_members(adapters, place, members, head, following)
    for slot in range(members):
        products[slot] = by_rows(backs[slot], own[slot])
        core, line = divmod(slot, members // 2)
        products[members + slot] = by_rows(backs_pair[slot], others[core][line])
    write_sums(
        head, following, products, ready, zero, out, sems, lambda adapter, total: total
    )


def down_gradients(adapters, place, backs, backs_pair, own, others, num_adapters):
    members, _, width = own.shape
    return sums_call(
        down_gradient_kernel,
        "down_gradients",
        (adapters, place),
        (backs, backs_pair, own, *others),
        num_adapters,
        2 * members,
        (backs.shape[2], width),
    )


def up_gradient_kernel(
    adapters,
    place,
    ranks,
    gradients,
    gradients_pair,
    hiddens,
    hiddens_pair,
    out,
    head,
    following,
    products,
    ready,
    zero,
    sems,
    lines,
):
    members, _, lanes = gradients.shape
    width, extent = out.shape[1:]
    list_members(adapters, place, members, head, following)
    inside = pl.multiple_of(lax.rem(place[0], lanes // width) * width, width)
    for slot in range(members):
        lines[slot] = by_rows(gradients[slot], hiddens[slot])
        lines[members + slot] = by_rows(gradients_pair[slot], hiddens_pair[slot])
    for entry in range(2 * members):
        products[entry] = lines[entry, pl.ds(inside, width), :]

    def finish(adapter, total):
        _, factor = rank_row(ranks, adapter, extent)
        return factor * total

    write_sums(head, following, products, ready, zero, out, sems, finish)


def up_gradients(adapters, place, ranks, gradients, gradients_pair, hiddens, hiddens_pair, width):
    members, _, lanes = gradients.shape
    extent = hiddens.shape[2]
    return sums_call(
        up_gradient_kernel,
        "up_gradients",
        (adapters, place, ranks),
        (gradients, gradients_pair, hiddens, hiddens_pair),
        ranks.shape[0],
        2 * members,
        (width, extent),
        [pltpu.VMEM((2 * members, lanes, extent), jnp.float32)],
    )


def exchange(pieces):
    return lax.all_to_all(pieces, "dp", split_axis=0, concat_axis=0, tiled=True)


def exchange_side(pieces):
    members = pieces.shape[0]
    groups = [[side_place(index, side, members) for index in range(members)] for side in range(2)]
    return lax.all_to_all(
        pieces, "dp", split_axis=0, concat_axis=0, axis_index_groups=groups, tiled=True
    )


def swap(array, flip):
    devices = lax.axis_size("dp")
    return lax.ppermute(array, "dp", [(i, i ^ flip) for i in range(devices)])


def tie(first, second):
    return lax.optimization_barrier((first, second))


def gather_step(held, members):
    arrived = swap(held, line_offset(held.shape[0], members))
    return jnp.concatenate([held, arrived], axis=0)


def local(tokens, output_gradient, value_weight, down_maps, up_maps, adapter_per_block, ranks):
    devices = lax.axis_size("dp")
    members = devices // 2
    lines = members // 2
    steps = members.bit_length() - 1
    num_adapters, extent, width = down_maps.shape
    rows, depth = output_gradient.shape
    place = lax.axis_index("dp").astype(jnp.int32).reshape(1)
    adapters = adapter_per_block
    offsets = [line_offset(slot, members) for slot in range(members)]
    barrier = lax.optimization_barrier

    own_gradient = output_gradient.reshape(1, rows, depth)
    gradients = [own_gradient] + [None] * (lines - 1)
    for step in range(steps - 1):
        gradients[1 << step] = swap(own_gradient, offsets[1 << step])
    own_up = exchange(gather_up(adapters, up_maps)).reshape(depth, extent)
    packs = pack_tokens(place, tokens, members, width)
    firsts = [1 << step for step in range(steps - 1)]
    across = {slot: swap(gradients[slot], 1) for slot in [0] + firsts}
    held, crossed, own_up, packs, adapters = barrier(
        ([gradients[slot] for slot in firsts], across, own_up, packs, adapters)
    )
    across = dict(crossed)
    for slot, block in zip(firsts, held):
        gradients[slot] = block

    arrived = exchange_side(packs)
    pair = swap(for_pair(adapters, place, value_weight, down_maps, members), pair_bit)
    for step in range(1, steps - 1):
        for slot in range(1, 1 << step):
            gradients[slot + (1 << step)] = swap(gradients[slot], offsets[1 << step])
    backs = back_rows(adapters, place, ranks, output_gradient, own_up)
    backs = [backs] + [swap(backs, offset) for offset in offsets[1:lines]]
    arrived, backs, gradients, pair = barrier((arrived, backs, gradients, pair))

    parts, tokens_own, *tokens_pair = hidden_parts(
        adapters, place, down_maps, pair, arrived
    )
    for slot in range(lines):
        if slot not in across:
            across[slot] = swap(gradients[slot], 1)
    backs = gather_step(jnp.concatenate(backs, axis=0), members)
    slices, columns, columns_pair = input_slices(
        adapters,
        place,
        gradients + [across[slot] for slot in range(lines)],
        backs,
        value_weight,
        pair,
        down_maps,
    )
    total, received, flip = parts, swap(parts[lines:], 1), 0
    for step in reversed(range(steps - 1)):
        kinds = [jnp.float32] if step else [jnp.float32, jnp.bfloat16]
        sums = slot_sums(total, received, flip, kinds)
        total, flip = sums[0], 1 << step
        received = swap(sums[-1], offsets[flip])
    received, slices, columns_pair, backs, tokens_pair = barrier(
        (received, slices, columns_pair, backs, tokens_pair)
    )

    result = exchange_side(slices)
    hiddens = hidden_rows(adapters, place, ranks, total, received, flip, members)
    hiddens = gather_step(hiddens, members)
    columns_other = swap(columns_pair, pair_bit)
    backs_pair = swap(backs, pair_bit)
    tokens_other = [swap(half, pair_bit) for half in tokens_pair]
    hiddens_pair = swap(hiddens, pair_bit)
    up_gradient = up_gradients(
        adapters, place, ranks, columns, columns_other, hiddens, hiddens_pair, depth // devices
    )
    down_gradient = down_gradients(
        adapters, place, backs, backs_pair, tokens_own, tokens_other, num_adapters
    )
    up_gradient, down_gradient, result = barrier((up_gradient, down_gradient, result))
    return (join_columns(place, result), down_gradient, up_gradient)


def solution(mesh):
    in_specs = (
        P(("groups", "dp"), None),
        P(("groups", "dp"), None),
        P(None, "dp"),
        P(None, None, "dp"),
        P(None, "dp", None),
        P("groups"),
        P(),
    )
    out_specs = (P(("groups", "dp"), None), P("groups", None, "dp"), P("groups", "dp", None))
    return jax.shard_map(local, mesh=mesh, in_specs=in_specs, out_specs=out_specs, check_vma=False)
```

```python
import functools

import jax
import jax.numpy as jnp
from jax import lax
from jax.experimental import pallas as pl
from jax.experimental.pallas import tpu as pltpu
from jax.sharding import PartitionSpec as P

adapter_alpha = 32.0
vmem_limit = 48 * 1024 * 1024
pair_bit = 2
line_bit = 4


def line_offset(slot, members):
    bits = members.bit_length() - 1
    order = 0
    for bit in range(bits):
        order |= ((slot >> bit) & 1) << (bits - 1 - bit)
    return ((order // 2) * line_bit) | (order % 2)


def side_of(place):
    return place % line_bit // pair_bit


def reversed_bits(number, count):
    bits = count.bit_length() - 1
    return sum(((number >> bit) & 1) << (bits - 1 - bit) for bit in range(bits))


def side_index(place, members):
    lines = members // 2
    return place % pair_bit * lines + reversed_bits(place // line_bit, lines)


def side_place(index, side, members):
    core, line = divmod(index, members // 2)
    return reversed_bits(line, members // 2) * line_bit + side * pair_bit + core


def params():
    return pltpu.CompilerParams(vmem_limit_bytes=vmem_limit)


def whole(shape):
    return pl.BlockSpec(shape, lambda *_: (0,) * len(shape))


def picked(maps, flip):
    return pl.BlockSpec(
        (1,) + maps.shape[1:], lambda i, adapters, place, *_: (adapters[place[0] ^ flip], 0, 0)
    )


def call(kernel, name, prefetch, operands, in_specs, out_shapes, scratch=(), grid=(1,), out_specs=None):
    if out_specs is None:
        out_specs = [whole(shape.shape) for shape in out_shapes]
    return pl.pallas_call(
        kernel,
        out_shape=out_shapes,
        grid_spec=pltpu.PrefetchScalarGridSpec(
            num_scalar_prefetch=len(prefetch),
            grid=grid,
            in_specs=in_specs,
            out_specs=out_specs,
            scratch_shapes=list(scratch),
        ),
        compiler_params=params(),
        name=name,
    )(*prefetch, *operands)


def run(copies):
    for copy in copies:
        copy.start()
    for copy in copies:
        copy.wait()


def copy_call(kernel, name, prefetch, operands, out_shapes, copies):
    return pl.pallas_call(
        kernel,
        out_shape=out_shapes,
        grid_spec=pltpu.PrefetchScalarGridSpec(
            num_scalar_prefetch=len(prefetch),
            grid=(1,),
            in_specs=[pl.BlockSpec(memory_space=pl.ANY)] * len(operands),
            out_specs=[whole(shape.shape) for shape in out_shapes],
            scratch_shapes=[pltpu.SemaphoreType.DMA((copies,))],
        ),
        compiler_params=params(),
        name=name,
    )(*prefetch, *operands)


weight_cuts = 4


def pair_kernel(adapters, place, weight, down_maps, out, sems):
    extent = down_maps.shape[1]
    depth = weight.shape[0]
    members = (out.shape[0] - depth) // extent
    copies = []
    for slot in range(members):
        block = place[0] ^ line_offset(slot, members) ^ pair_bit
        copies.append((down_maps.at[adapters[block]], slot * extent, extent))
    cut = depth // weight_cuts
    for at in range(0, depth, cut):
        copies.append((weight.at[pl.ds(at, cut)], members * extent + at, cut))
    run(
        [
            pltpu.make_async_copy(source, out.at[pl.ds(at, rows)], sems.at[number])
            for number, (source, at, rows) in enumerate(copies)
        ]
    )


def for_pair(adapters, place, weight, down_maps, members):
    extent, width = down_maps.shape[1:]
    shape = jax.ShapeDtypeStruct((members * extent + weight.shape[0], width), weight.dtype)
    return copy_call(
        pair_kernel,
        "for_pair",
        (adapters, place),
        (weight, down_maps),
        [shape],
        members + weight_cuts,
    )[0]


def gather_up_kernel(adapters, up_maps, out, sems):
    run(
        [
            pltpu.make_async_copy(up_maps.at[adapters[block]], out.at[block], sems.at[block])
            for block in range(out.shape[0])
        ]
    )


def gather_up(adapters, up_maps):
    shape = jax.ShapeDtypeStruct((adapters.shape[0],) + up_maps.shape[1:], up_maps.dtype)
    return copy_call(
        gather_up_kernel, "gather_up", (adapters,), (up_maps,), [shape], adapters.shape[0]
    )[0]


def pack_kernel(place, tokens, out, sems):
    members, _, _, width = out.shape
    copies = []
    for index in range(members):
        for half in range(2):
            column = side_place(index, side_of(place[0]) ^ half, members) * width
            copies.append(
                pltpu.make_async_copy(
                    tokens.at[:, pl.ds(pl.multiple_of(column, width), width)],
                    out.at[index, half],
                    sems.at[2 * index + half],
                )
            )
    run(copies)


def pack_tokens(place, tokens, members, width):
    shape = jax.ShapeDtypeStruct((members, 2, tokens.shape[0], width), tokens.dtype)
    return copy_call(pack_kernel, "pack_tokens", (place,), (tokens,), [shape], 2 * members)[0]


def rank_row(ranks, adapter, extent):
    rank = jnp.full((1, extent), ranks[adapter], jnp.int32)
    alive = (lax.broadcasted_iota(jnp.int32, (1, extent), 1) < rank).astype(jnp.float32)
    return alive, adapter_alpha / rank.astype(jnp.float32)


def back_kernel(adapters, place, ranks, gradient, up, out):
    alive, factor = rank_row(ranks, adapters[place[0]], up.shape[1])
    back = jnp.dot(gradient[...], up[...], preferred_element_type=jnp.float32)
    out[0] = (factor * back * alive).astype(out.dtype)


def back_rows(adapters, place, ranks, gradient, up):
    return call(
        back_kernel,
        "back_low",
        (adapters, place, ranks),
        (gradient, up),
        [whole(gradient.shape), whole(up.shape)],
        [jax.ShapeDtypeStruct((1, gradient.shape[0], up.shape[1]), jnp.bfloat16)],
    )[0]


def input_kernel(adapters, place, backs, pair, *refs):
    members, rows, _ = backs.shape
    gradients, downs = refs[:members], refs[members : 2 * members]
    weight, out = refs[2 * members :]
    extent = downs[0].shape[1]
    some = min(4, members)
    for first in range(0, members, some):
        slots = range(first, first + some)
        lines = jnp.concatenate([gradients[slot][0] for slot in slots], axis=0)
        for half in range(2):
            right = weight[...] if half == 0 else pair[members * extent :]
            frozen = jnp.dot(lines, right, preferred_element_type=jnp.float32)
            for slot in slots:
                down = downs[slot][0] if half == 0 else pair[slot * extent : (slot + 1) * extent]
                index = side_index(place[0] ^ line_offset(slot, members), members)
                low = jnp.dot(backs[slot], down, preferred_element_type=jnp.float32)
                at = (slot - first) * rows
                out[index, half] = (frozen[at : at + rows] + low).astype(jnp.bfloat16)


def input_slices(adapters, place, gradients, backs, weight, pair, down_maps, part, parts):
    members, rows, extent = backs.shape
    depth, width = weight.shape
    rows //= parts
    return call(
        input_kernel,
        "input_slices",
        (adapters, place),
        [backs, pair] + list(gradients) + [down_maps] * members + [weight],
        [pl.BlockSpec((members, rows, extent), lambda *_: (0, part, 0)), whole(pair.shape)]
        + [pl.BlockSpec((1, rows, depth), lambda *_: (0, part, 0))] * members
        + [picked(down_maps, line_offset(slot, members)) for slot in range(members)]
        + [whole(weight.shape)],
        [jax.ShapeDtypeStruct((members, 2, rows, width), jnp.bfloat16)],
    )[0]


def columns_kernel(place, *refs):
    *gradients, own, pair = refs
    for slot in range(own.shape[0]):
        own[slot] = gradients[2 * slot][0]
        pair[slot] = gradients[2 * slot + 1][0]


def gradient_columns(place, gradients, value_width):
    members = len(gradients)
    rows = gradients[0].shape[1]
    lanes = max(128, value_width)

    def spec(side):
        return pl.BlockSpec(
            (1, rows, lanes),
            lambda i, place: (0, 0, (place[0] ^ (side * pair_bit)) * value_width // lanes),
        )

    shape = jax.ShapeDtypeStruct((members, rows, lanes), gradients[0].dtype)
    return call(
        columns_kernel,
        "gradient_columns",
        (place,),
        [gradient for gradient in gradients for _ in range(2)],
        [spec(0), spec(1)] * members,
        [shape, shape],
    )


def hidden_kernel(adapters, place, pair, tokens, *refs):
    parts, own, *others = refs[-4:]
    members = own.shape[0]
    downs = refs[:members]
    extent = downs[0].shape[1]
    across = (((1,), (1,)), ((), ()))
    for slot in range(members):
        index = side_index(place[0] ^ line_offset(slot, members), members)
        own[slot] = tokens[index, 0]
        others[slot // (members // 2)][slot % (members // 2)] = tokens[index, 1]
        parts[slot] = lax.dot_general(
            tokens[index, 0], downs[slot][0], across, preferred_element_type=jnp.float32
        ) + lax.dot_general(
            tokens[index, 1],
            pair[slot * extent : (slot + 1) * extent],
            across,
            preferred_element_type=jnp.float32,
        )


def hidden_parts(adapters, place, down_maps, pair, tokens):
    members, _, rows, width = tokens.shape
    extent = down_maps.shape[1]
    others = jax.ShapeDtypeStruct((members // 2, rows, width), tokens.dtype)
    return call(
        hidden_kernel,
        "hidden_parts",
        (adapters, place),
        [pair, tokens] + [down_maps] * members,
        [whole(pair.shape), whole(tokens.shape)]
        + [picked(down_maps, line_offset(slot, members)) for slot in range(members)],
        [
            jax.ShapeDtypeStruct((members, rows, extent), jnp.float32),
            jax.ShapeDtypeStruct((members, rows, width), tokens.dtype),
            others,
            others,
        ],
    )


def sum_kernel(total, received, *outs, flip):
    for slot in range(outs[0].shape[0]):
        value = total[slot] + received[slot ^ flip].astype(jnp.float32)
        for out in outs:
            out[slot] = value.astype(out.dtype)


def slot_sums(total, received, flip, types):
    shape = received.shape
    return call(
        functools.partial(sum_kernel, flip=flip),
        "slot_sums",
        (),
        (total, received),
        [whole(shape)] * 2,
        [jax.ShapeDtypeStruct(shape, kind) for kind in types],
    )


def hidden_low_kernel(adapters, place, ranks, total, received, out, *, flip, members):
    for slot in range(out.shape[0]):
        block = place[0] ^ line_offset(slot, members)
        alive, _ = rank_row(ranks, adapters[block], out.shape[2])
        value = total[slot] + received[slot ^ flip].astype(jnp.float32)
        out[slot] = (value * alive).astype(out.dtype)


def hidden_rows(adapters, place, ranks, total, received, flip, members):
    return call(
        functools.partial(hidden_low_kernel, flip=flip, members=members),
        "hidden_low",
        (adapters, place, ranks),
        (total, received),
        [whole(total.shape)] * 2,
        [jax.ShapeDtypeStruct(total.shape, jnp.bfloat16)],
    )[0]


def join_kernel(place, source, *refs, part):
    out, sems = refs[-2:]
    members, _, rows, width = source.shape
    copies = []
    for index in range(members):
        for half in range(2):
            column = side_place(index, side_of(place[0]) ^ half, members) * width
            columns = pl.ds(pl.multiple_of(column, width), width)
            copies.append(
                pltpu.make_async_copy(
                    source.at[index, half],
                    out.at[pl.ds(part * rows, rows), columns],
                    sems.at[2 * index + half],
                )
            )
    run(copies)


def join_columns(place, source, part, parts, before=()):
    members, _, rows, width = source.shape
    shape = jax.ShapeDtypeStruct((parts * rows, 2 * members * width), source.dtype)
    return pl.pallas_call(
        functools.partial(join_kernel, part=part),
        out_shape=shape,
        grid_spec=pltpu.PrefetchScalarGridSpec(
            num_scalar_prefetch=1,
            grid=(1,),
            in_specs=[whole(source.shape)] + [pl.BlockSpec(memory_space=pl.ANY)] * len(before),
            out_specs=pl.BlockSpec(memory_space=pl.ANY),
            scratch_shapes=[pltpu.SemaphoreType.DMA((2 * members,))],
        ),
        input_output_aliases={2: 0} if before else {},
        compiler_params=params(),
        name="join_columns",
    )(place, source, *before)


def list_members(adapters, place, members, head, following):
    def clear(adapter, carry):
        head[adapter] = -1
        return carry

    lax.fori_loop(0, head.shape[0], clear, 0)
    for entry in reversed(range(2 * members)):
        side, own = divmod(entry, members)
        adapter = adapters[place[0] ^ line_offset(own, members) ^ (side * pair_bit)]
        following[entry] = head[adapter]
        head[adapter] = entry


def write_sums(head, following, products, ready, zero, out, sems, finish):
    num_adapters = out.shape[0]
    zero[...] = jnp.zeros_like(zero)

    def write(adapter, carry):
        first = head[adapter]

        @pl.when(first < 0)
        def _():
            pltpu.make_async_copy(zero, out.at[adapter], sems.at[adapter]).start()

        @pl.when(first >= 0)
        def _():
            def more(entry):
                products[first] += products[entry]
                return following[entry]

            lax.while_loop(lambda entry: entry >= 0, more, following[first])
            ready[first] = finish(adapter, products[first]).astype(out.dtype)
            pltpu.make_async_copy(ready.at[first], out.at[adapter], sems.at[adapter]).start()

        return carry

    lax.fori_loop(0, num_adapters, write, 0)

    def wait(adapter, carry):
        pltpu.make_async_copy(zero, out.at[adapter], sems.at[adapter]).wait()
        return carry

    lax.fori_loop(0, num_adapters, wait, 0)


def by_rows(left, right):
    return lax.dot_general(
        left, right, (((0,), (0,)), ((), ())), preferred_element_type=jnp.float32
    )


def sums_call(kernel, name, prefetch, operands, num_adapters, entries, product, scratch=()):
    return pl.pallas_call(
        kernel,
        out_shape=jax.ShapeDtypeStruct((num_adapters,) + product, jnp.bfloat16),
        grid_spec=pltpu.PrefetchScalarGridSpec(
            num_scalar_prefetch=len(prefetch),
            grid=(1,),
            in_specs=[whole(operand.shape) for operand in operands],
            out_specs=pl.BlockSpec(memory_space=pltpu.HBM),
            scratch_shapes=[
                pltpu.SMEM((num_adapters,), jnp.int32),
                pltpu.SMEM((entries,), jnp.int32),
                pltpu.VMEM((entries,) + product, jnp.float32),
                pltpu.VMEM((entries,) + product, jnp.bfloat16),
                pltpu.VMEM(product, jnp.bfloat16),
                pltpu.SemaphoreType.DMA((num_adapters,)),
                *scratch,
            ],
        ),
        compiler_params=params(),
        name=name,
    )(*prefetch, *operands)


def down_gradient_kernel(
    adapters,
    place,
    backs,
    backs_pair,
    own,
    other_first,
    other_second,
    out,
    head,
    following,
    products,
    ready,
    zero,
    sems,
):
    members = own.shape[0]
    others = (other_first, other_second)
    list_members(adapters, place, members, head, following)
    for slot in range(members):
        products[slot] = by_rows(backs[slot], own[slot])
        core, line = divmod(slot, members // 2)
        products[members + slot] = by_rows(backs_pair[slot], others[core][line])
    write_sums(
        head, following, products, ready, zero, out, sems, lambda adapter, total: total
    )


def down_gradients(adapters, place, backs, backs_pair, own, others, num_adapters):
    members, _, width = own.shape
    return sums_call(
        down_gradient_kernel,
        "down_gradients",
        (adapters, place),
        (backs, backs_pair, own, *others),
        num_adapters,
        2 * members,
        (backs.shape[2], width),
    )


def up_gradient_kernel(
    adapters,
    place,
    ranks,
    gradients,
    gradients_pair,
    hiddens,
    hiddens_pair,
    out,
    head,
    following,
    products,
    ready,
    zero,
    sems,
    lines,
):
    members, _, lanes = gradients.shape
    width, extent = out.shape[1:]
    list_members(adapters, place, members, head, following)
    inside = pl.multiple_of(lax.rem(place[0], lanes // width) * width, width)
    for slot in range(members):
        lines[slot] = by_rows(gradients[slot], hiddens[slot])
        lines[members + slot] = by_rows(gradients_pair[slot], hiddens_pair[slot])
    for entry in range(2 * members):
        products[entry] = lines[entry, pl.ds(inside, width), :]

    def finish(adapter, total):
        _, factor = rank_row(ranks, adapter, extent)
        return factor * total

    write_sums(head, following, products, ready, zero, out, sems, finish)


def up_gradients(adapters, place, ranks, gradients, gradients_pair, hiddens, hiddens_pair, width):
    members, _, lanes = gradients.shape
    extent = hiddens.shape[2]
    return sums_call(
        up_gradient_kernel,
        "up_gradients",
        (adapters, place, ranks),
        (gradients, gradients_pair, hiddens, hiddens_pair),
        ranks.shape[0],
        2 * members,
        (width, extent),
        [pltpu.VMEM((2 * members, lanes, extent), jnp.float32)],
    )


def exchange(pieces):
    return lax.all_to_all(pieces, "dp", split_axis=0, concat_axis=0, tiled=True)


def exchange_side(pieces):
    members = pieces.shape[0]
    groups = [[side_place(index, side, members) for index in range(members)] for side in range(2)]
    return lax.all_to_all(
        pieces, "dp", split_axis=0, concat_axis=0, axis_index_groups=groups, tiled=True
    )


def swap(array, flip):
    devices = lax.axis_size("dp")
    return lax.ppermute(array, "dp", [(i, i ^ flip) for i in range(devices)])


def tie(first, second):
    return lax.optimization_barrier((first, second))


def gather_step(held, members):
    arrived = swap(held, line_offset(held.shape[0], members))
    return jnp.concatenate([held, arrived], axis=0)


def local(tokens, output_gradient, value_weight, down_maps, up_maps, adapter_per_block, ranks):
    devices = lax.axis_size("dp")
    members = devices // 2
    lines = members // 2
    steps = members.bit_length() - 1
    num_adapters, extent, width = down_maps.shape
    rows, depth = output_gradient.shape
    place = lax.axis_index("dp").astype(jnp.int32).reshape(1)
    adapters = adapter_per_block
    offsets = [line_offset(slot, members) for slot in range(members)]
    barrier = lax.optimization_barrier

    own_gradient = output_gradient.reshape(1, rows, depth)
    gradients = [own_gradient] + [None] * (lines - 1)
    for step in range(steps - 1):
        gradients[1 << step] = swap(own_gradient, offsets[1 << step])
    own_up = exchange(gather_up(adapters, up_maps)).reshape(depth, extent)
    packs = pack_tokens(place, tokens, members, width)
    firsts = [1 << step for step in range(steps - 1)]
    across = {slot: swap(gradients[slot], 1) for slot in [0] + firsts}
    held, crossed, own_up, packs, adapters = barrier(
        ([gradients[slot] for slot in firsts], across, own_up, packs, adapters)
    )
    across = dict(crossed)
    for slot, block in zip(firsts, held):
        gradients[slot] = block

    arrived = exchange_side(packs)
    pair = swap(for_pair(adapters, place, value_weight, down_maps, members), pair_bit)
    for step in range(1, steps - 1):
        for slot in range(1, 1 << step):
            gradients[slot + (1 << step)] = swap(gradients[slot], offsets[1 << step])
    backs = back_rows(adapters, place, ranks, output_gradient, own_up)
    backs = [backs] + [swap(backs, offset) for offset in offsets[1:lines]]
    arrived, backs, gradients, pair = barrier((arrived, backs, gradients, pair))

    for slot in range(lines):
        if slot not in across:
            across[slot] = swap(gradients[slot], 1)
    gradients = gradients + [across[slot] for slot in range(lines)]
    backs = gather_step(jnp.concatenate(backs, axis=0), members)
    slices = input_slices(
        adapters, place, gradients, backs, value_weight, pair, down_maps, 0, 2
    )
    slices, arrived = barrier((slices, arrived))
    first = exchange_side(slices)

    parts, tokens_own, *tokens_pair = hidden_parts(
        adapters, place, down_maps, pair, arrived
    )
    columns, columns_other = gradient_columns(place, gradients, depth // devices)
    columns_other = swap(columns_other, pair_bit)
    backs_pair = swap(backs, pair_bit)
    tokens_other = [swap(tokens_pair[0], pair_bit)]
    total, received, flip = parts, swap(parts[lines:], 1), 0
    for step in reversed(range(steps - 1)):
        kinds = [jnp.float32] if step else [jnp.float32, jnp.bfloat16]
        sums = slot_sums(total, received, flip, kinds)
        total, flip = sums[0], 1 << step
        received = swap(sums[-1], offsets[flip])
        if step == 1:
            received, backs, columns_other, backs_pair, tokens_other, tokens_pair = barrier(
                (received, backs, columns_other, backs_pair, tokens_other, tokens_pair)
            )
            slices = input_slices(
                adapters, place, gradients, backs, value_weight, pair, down_maps, 1, 2
            )
    second = exchange_side(slices)

    hiddens = hidden_rows(adapters, place, ranks, total, received, flip, members)
    hiddens = gather_step(hiddens, members)
    hiddens_pair = swap(hiddens, pair_bit)
    tokens_other.append(swap(tokens_pair[1], pair_bit))
    up_gradient = up_gradients(
        adapters, place, ranks, columns, columns_other, hiddens, hiddens_pair, depth // devices
    )
    down_gradient = down_gradients(
        adapters, place, backs, backs_pair, tokens_own, tokens_other, num_adapters
    )
    joined = join_columns(place, first, 0, 2)
    up_gradient, down_gradient, joined, second = barrier(
        (up_gradient, down_gradient, joined, second)
    )
    input_grad = join_columns(place, second, 1, 2, (joined,))
    return (input_grad, down_gradient, up_gradient)


def solution(mesh):
    in_specs = (
        P(("groups", "dp"), None),
        P(("groups", "dp"), None),
        P(None, "dp"),
        P(None, None, "dp"),
        P(None, "dp", None),
        P("groups"),
        P(),
    )
    out_specs = (P(("groups", "dp"), None), P("groups", None, "dp"), P("groups", "dp", None))
    return jax.shard_map(local, mesh=mesh, in_specs=in_specs, out_specs=out_specs, check_vma=False)
```

```python
import functools

import jax
import jax.numpy as jnp
from jax import lax
from jax.experimental import pallas as pl
from jax.experimental.pallas import tpu as pltpu
from jax.sharding import PartitionSpec as P

adapter_alpha = 32.0
vmem_limit = 60 * 1024 * 1024
pair_bit = 2
line_bit = 4


def line_offset(slot, members):
    bits = members.bit_length() - 1
    order = 0
    for bit in range(bits):
        order |= ((slot >> bit) & 1) << (bits - 1 - bit)
    return ((order // 2) * line_bit) | (order % 2)


def side_of(place):
    return place % line_bit // pair_bit


def reversed_bits(number, count):
    bits = count.bit_length() - 1
    return sum(((number >> bit) & 1) << (bits - 1 - bit) for bit in range(bits))


def side_index(place, members):
    lines = members // 2
    return place % pair_bit * lines + reversed_bits(place // line_bit, lines)


def side_place(index, side, members):
    core, line = divmod(index, members // 2)
    return reversed_bits(line, members // 2) * line_bit + side * pair_bit + core


def params():
    return pltpu.CompilerParams(vmem_limit_bytes=vmem_limit)


def whole(shape):
    return pl.BlockSpec(shape, lambda *_: (0,) * len(shape))


def picked(maps, flip):
    return pl.BlockSpec(
        (1,) + maps.shape[1:], lambda i, adapters, place, *_: (adapters[place[0] ^ flip], 0, 0)
    )


def call(kernel, name, prefetch, operands, in_specs, out_shapes, scratch=(), grid=(1,), out_specs=None):
    if out_specs is None:
        out_specs = [whole(shape.shape) for shape in out_shapes]
    return pl.pallas_call(
        kernel,
        out_shape=out_shapes,
        grid_spec=pltpu.PrefetchScalarGridSpec(
            num_scalar_prefetch=len(prefetch),
            grid=grid,
            in_specs=in_specs,
            out_specs=out_specs,
            scratch_shapes=list(scratch),
        ),
        compiler_params=params(),
        name=name,
    )(*prefetch, *operands)


def run(copies):
    for copy in copies:
        copy.start()
    for copy in copies:
        copy.wait()


def copy_call(kernel, name, prefetch, operands, out_shapes, copies):
    return pl.pallas_call(
        kernel,
        out_shape=out_shapes,
        grid_spec=pltpu.PrefetchScalarGridSpec(
            num_scalar_prefetch=len(prefetch),
            grid=(1,),
            in_specs=[pl.BlockSpec(memory_space=pl.ANY)] * len(operands),
            out_specs=[whole(shape.shape) for shape in out_shapes],
            scratch_shapes=[pltpu.SemaphoreType.DMA((copies,))],
        ),
        compiler_params=params(),
        name=name,
    )(*prefetch, *operands)


weight_cuts = 4


def pair_kernel(adapters, place, weight, down_maps, out, sems):
    extent = down_maps.shape[1]
    depth = weight.shape[0]
    members = (out.shape[0] - depth) // extent
    copies = []
    for slot in range(members):
        block = place[0] ^ line_offset(slot, members) ^ pair_bit
        copies.append((down_maps.at[adapters[block]], slot * extent, extent))
    cut = depth // weight_cuts
    for at in range(0, depth, cut):
        copies.append((weight.at[pl.ds(at, cut)], members * extent + at, cut))
    run(
        [
            pltpu.make_async_copy(source, out.at[pl.ds(at, rows)], sems.at[number])
            for number, (source, at, rows) in enumerate(copies)
        ]
    )


def for_pair(adapters, place, weight, down_maps, members):
    extent, width = down_maps.shape[1:]
    shape = jax.ShapeDtypeStruct((members * extent + weight.shape[0], width), weight.dtype)
    return copy_call(
        pair_kernel,
        "for_pair",
        (adapters, place),
        (weight, down_maps),
        [shape],
        members + weight_cuts,
    )[0]


def gather_up_kernel(adapters, up_maps, out, sems):
    run(
        [
            pltpu.make_async_copy(up_maps.at[adapters[block]], out.at[block], sems.at[block])
            for block in range(out.shape[0])
        ]
    )


def gather_up(adapters, up_maps):
    shape = jax.ShapeDtypeStruct((adapters.shape[0],) + up_maps.shape[1:], up_maps.dtype)
    return copy_call(
        gather_up_kernel, "gather_up", (adapters,), (up_maps,), [shape], adapters.shape[0]
    )[0]


def pack_kernel(place, tokens, out, sems):
    members, _, _, width = out.shape
    copies = []
    for index in range(members):
        for half in range(2):
            column = side_place(index, side_of(place[0]) ^ half, members) * width
            copies.append(
                pltpu.make_async_copy(
                    tokens.at[:, pl.ds(pl.multiple_of(column, width), width)],
                    out.at[index, half],
                    sems.at[2 * index + half],
                )
            )
    run(copies)


def pack_tokens(place, tokens, members, width):
    shape = jax.ShapeDtypeStruct((members, 2, tokens.shape[0], width), tokens.dtype)
    return copy_call(pack_kernel, "pack_tokens", (place,), (tokens,), [shape], 2 * members)[0]


def rank_row(ranks, adapter, extent):
    rank = jnp.full((1, extent), ranks[adapter], jnp.int32)
    alive = (lax.broadcasted_iota(jnp.int32, (1, extent), 1) < rank).astype(jnp.float32)
    return alive, adapter_alpha / rank.astype(jnp.float32)


def back_kernel(adapters, place, ranks, gradient, up, out):
    alive, factor = rank_row(ranks, adapters[place[0]], up.shape[1])
    back = jnp.dot(gradient[...], up[...], preferred_element_type=jnp.float32)
    out[0] = (factor * back * alive).astype(out.dtype)


def back_rows(adapters, place, ranks, gradient, up):
    return call(
        back_kernel,
        "back_low",
        (adapters, place, ranks),
        (gradient, up),
        [whole(gradient.shape), whole(up.shape)],
        [jax.ShapeDtypeStruct((1, gradient.shape[0], up.shape[1]), jnp.bfloat16)],
    )[0]


def input_kernel(adapters, place, backs, pair, *refs):
    members, rows, _ = backs.shape
    gradients, downs = refs[:members], refs[members : 2 * members]
    weight, out = refs[2 * members :]
    extent = downs[0].shape[1]
    some = min(4, members)
    for first in range(0, members, some):
        slots = range(first, first + some)
        lines = jnp.concatenate([gradients[slot][0] for slot in slots], axis=0)
        for half in range(2):
            right = weight[...] if half == 0 else pair[members * extent :]
            frozen = jnp.dot(lines, right, preferred_element_type=jnp.float32)
            for slot in slots:
                down = downs[slot][0] if half == 0 else pair[slot * extent : (slot + 1) * extent]
                index = side_index(place[0] ^ line_offset(slot, members), members)
                low = jnp.dot(backs[slot], down, preferred_element_type=jnp.float32)
                at = (slot - first) * rows
                out[index, half] = (frozen[at : at + rows] + low).astype(jnp.bfloat16)


def input_slices(adapters, place, gradients, backs, weight, pair, down_maps, part, parts):
    members, rows, extent = backs.shape
    depth, width = weight.shape
    rows //= parts
    return call(
        input_kernel,
        "input_slices",
        (adapters, place),
        [backs, pair] + list(gradients) + [down_maps] * members + [weight],
        [pl.BlockSpec((members, rows, extent), lambda *_: (0, part, 0)), whole(pair.shape)]
        + [pl.BlockSpec((1, rows, depth), lambda *_: (0, part, 0))] * members
        + [picked(down_maps, line_offset(slot, members)) for slot in range(members)]
        + [whole(weight.shape)],
        [jax.ShapeDtypeStruct((members, 2, rows, width), jnp.bfloat16)],
    )[0]


def columns_kernel(place, *refs):
    *gradients, own, pair = refs
    for slot in range(own.shape[0]):
        own[slot] = gradients[2 * slot][0]
        pair[slot] = gradients[2 * slot + 1][0]


def gradient_columns(place, gradients, value_width):
    members = len(gradients)
    rows = gradients[0].shape[1]
    lanes = max(128, value_width)

    def spec(side):
        return pl.BlockSpec(
            (1, rows, lanes),
            lambda i, place: (0, 0, (place[0] ^ (side * pair_bit)) * value_width // lanes),
        )

    shape = jax.ShapeDtypeStruct((members, rows, lanes), gradients[0].dtype)
    return call(
        columns_kernel,
        "gradient_columns",
        (place,),
        [gradient for gradient in gradients for _ in range(2)],
        [spec(0), spec(1)] * members,
        [shape, shape],
    )


def hidden_kernel(adapters, place, pair, tokens, *refs):
    *downs, parts = refs
    members = parts.shape[0]
    extent = downs[0].shape[1]
    across = (((1,), (1,)), ((), ()))
    for slot in range(members):
        index = side_index(place[0] ^ line_offset(slot, members), members)
        parts[slot] = lax.dot_general(
            tokens[index, 0], downs[slot][0], across, preferred_element_type=jnp.float32
        ) + lax.dot_general(
            tokens[index, 1],
            pair[slot * extent : (slot + 1) * extent],
            across,
            preferred_element_type=jnp.float32,
        )


def hidden_parts(adapters, place, down_maps, pair, tokens):
    members, _, rows, _ = tokens.shape
    extent = down_maps.shape[1]
    return call(
        hidden_kernel,
        "hidden_parts",
        (adapters, place),
        [pair, tokens] + [down_maps] * members,
        [whole(pair.shape), whole(tokens.shape)]
        + [picked(down_maps, line_offset(slot, members)) for slot in range(members)],
        [jax.ShapeDtypeStruct((members, rows, extent), jnp.float32)],
    )[0]


def pair_tokens_kernel(tokens, first, second):
    half = first.shape[0]
    for index in range(half):
        first[index] = tokens[index, 0]
        second[index] = tokens[half + index, 0]


def pair_tokens(tokens):
    members, _, rows, width = tokens.shape
    shape = jax.ShapeDtypeStruct((members // 2, rows, width), tokens.dtype)
    return call(
        pair_tokens_kernel,
        "pair_tokens",
        (),
        (tokens,),
        [pl.BlockSpec((members, 1, rows, width), lambda *_: (0, 1, 0, 0))],
        [shape, shape],
    )


def sum_kernel(total, received, *outs, flip):
    for slot in range(outs[0].shape[0]):
        value = total[slot] + received[slot ^ flip].astype(jnp.float32)
        for out in outs:
            out[slot] = value.astype(out.dtype)


def slot_sums(total, received, flip, types):
    shape = received.shape
    return call(
        functools.partial(sum_kernel, flip=flip),
        "slot_sums",
        (),
        (total, received),
        [whole(shape)] * 2,
        [jax.ShapeDtypeStruct(shape, kind) for kind in types],
    )


def hidden_low_kernel(adapters, place, ranks, total, received, out, *, flip, members):
    for slot in range(out.shape[0]):
        block = place[0] ^ line_offset(slot, members)
        alive, _ = rank_row(ranks, adapters[block], out.shape[2])
        value = total[slot] + received[slot ^ flip].astype(jnp.float32)
        out[slot] = (value * alive).astype(out.dtype)


def hidden_rows(adapters, place, ranks, total, received, flip, members):
    return call(
        functools.partial(hidden_low_kernel, flip=flip, members=members),
        "hidden_low",
        (adapters, place, ranks),
        (total, received),
        [whole(total.shape)] * 2,
        [jax.ShapeDtypeStruct(total.shape, jnp.bfloat16)],
    )[0]


def join_kernel(place, source, out, sems):
    members, _, _, width = source.shape
    copies = []
    for index in range(members):
        for half in range(2):
            column = side_place(index, side_of(place[0]) ^ half, members) * width
            copies.append(
                pltpu.make_async_copy(
                    source.at[index, half],
                    out.at[:, pl.ds(pl.multiple_of(column, width), width)],
                    sems.at[2 * index + half],
                )
            )
    run(copies)


def join_columns(place, source):
    members, _, rows, width = source.shape
    return pl.pallas_call(
        join_kernel,
        out_shape=jax.ShapeDtypeStruct((rows, 2 * members * width), source.dtype),
        grid_spec=pltpu.PrefetchScalarGridSpec(
            num_scalar_prefetch=1,
            grid=(1,),
            in_specs=[whole(source.shape)],
            out_specs=pl.BlockSpec(memory_space=pl.ANY),
            scratch_shapes=[pltpu.SemaphoreType.DMA((2 * members,))],
        ),
        compiler_params=params(),
        name="join_columns",
    )(place, source)


def list_members(adapters, place, members, head, following):
    def clear(adapter, carry):
        head[adapter] = -1
        return carry

    lax.fori_loop(0, head.shape[0], clear, 0)
    for entry in reversed(range(2 * members)):
        side, own = divmod(entry, members)
        adapter = adapters[place[0] ^ line_offset(own, members) ^ (side * pair_bit)]
        following[entry] = head[adapter]
        head[adapter] = entry


def write_sums(head, following, products, ready, zero, out, sems, finish):
    num_adapters = out.shape[0]
    zero[...] = jnp.zeros_like(zero)

    def write(adapter, carry):
        first = head[adapter]

        @pl.when(first < 0)
        def _():
            pltpu.make_async_copy(zero, out.at[adapter], sems.at[adapter]).start()

        @pl.when(first >= 0)
        def _():
            def more(entry):
                products[first] += products[entry]
                return following[entry]

            lax.while_loop(lambda entry: entry >= 0, more, following[first])
            ready[first] = finish(adapter, products[first]).astype(out.dtype)
            pltpu.make_async_copy(ready.at[first], out.at[adapter], sems.at[adapter]).start()

        return carry

    lax.fori_loop(0, num_adapters, write, 0)

    def wait(adapter, carry):
        pltpu.make_async_copy(zero, out.at[adapter], sems.at[adapter]).wait()
        return carry

    lax.fori_loop(0, num_adapters, wait, 0)


def by_rows(left, right):
    return lax.dot_general(
        left, right, (((0,), (0,)), ((), ())), preferred_element_type=jnp.float32
    )


def sums_call(kernel, name, prefetch, operands, num_adapters, entries, product, scratch=(), specs=None):
    return pl.pallas_call(
        kernel,
        out_shape=jax.ShapeDtypeStruct((num_adapters,) + product, jnp.bfloat16),
        grid_spec=pltpu.PrefetchScalarGridSpec(
            num_scalar_prefetch=len(prefetch),
            grid=(1,),
            in_specs=specs or [whole(operand.shape) for operand in operands],
            out_specs=pl.BlockSpec(memory_space=pltpu.HBM),
            scratch_shapes=[
                pltpu.SMEM((num_adapters,), jnp.int32),
                pltpu.SMEM((entries,), jnp.int32),
                pltpu.VMEM((entries,) + product, jnp.float32),
                pltpu.VMEM((entries,) + product, jnp.bfloat16),
                pltpu.VMEM(product, jnp.bfloat16),
                pltpu.SemaphoreType.DMA((num_adapters,)),
                *scratch,
            ],
        ),
        compiler_params=params(),
        name=name,
    )(*prefetch, *operands)


def down_gradient_kernel(
    adapters,
    place,
    backs,
    backs_pair,
    tokens,
    other_first,
    other_second,
    out,
    head,
    following,
    products,
    ready,
    zero,
    sems,
):
    members = tokens.shape[0]
    half = members // 2
    list_members(adapters, place, members, head, following)
    for slot in range(members):
        index = side_index(place[0] ^ line_offset(slot, members), members)
        products[slot] = by_rows(backs[slot], tokens[index, 0])
        for number, other in enumerate((other_first, other_second)):

            @pl.when(index // half == number)
            def _(slot=slot, index=index, other=other):
                products[members + slot] = by_rows(backs_pair[slot], other[lax.rem(index, half)])

    write_sums(
        head, following, products, ready, zero, out, sems, lambda adapter, total: total
    )


def down_gradients(adapters, place, backs, backs_pair, tokens, others, num_adapters):
    members, _, rows, width = tokens.shape
    extent = backs.shape[2]
    operands = (backs, backs_pair, tokens, *others)
    specs = [whole(operand.shape) for operand in operands]
    specs[2] = pl.BlockSpec((members, 1, rows, width), lambda *_: (0, 0, 0, 0))
    return sums_call(
        down_gradient_kernel,
        "down_gradients",
        (adapters, place),
        operands,
        num_adapters,
        2 * members,
        (extent, width),
        specs=specs,
    )


def up_gradient_kernel(
    adapters,
    place,
    ranks,
    gradients,
    gradients_pair,
    hiddens,
    hiddens_pair,
    out,
    head,
    following,
    products,
    ready,
    zero,
    sems,
    lines,
):
    members, _, lanes = gradients.shape
    width, extent = out.shape[1:]
    list_members(adapters, place, members, head, following)
    inside = pl.multiple_of(lax.rem(place[0], lanes // width) * width, width)
    for slot in range(members):
        lines[slot] = by_rows(gradients[slot], hiddens[slot])
        lines[members + slot] = by_rows(gradients_pair[slot], hiddens_pair[slot])
    for entry in range(2 * members):
        products[entry] = lines[entry, pl.ds(inside, width), :]

    def finish(adapter, total):
        _, factor = rank_row(ranks, adapter, extent)
        return factor * total

    write_sums(head, following, products, ready, zero, out, sems, finish)


def up_gradients(adapters, place, ranks, gradients, gradients_pair, hiddens, hiddens_pair, width):
    members, _, lanes = gradients.shape
    extent = hiddens.shape[2]
    return sums_call(
        up_gradient_kernel,
        "up_gradients",
        (adapters, place, ranks),
        (gradients, gradients_pair, hiddens, hiddens_pair),
        ranks.shape[0],
        2 * members,
        (width, extent),
        [pltpu.VMEM((2 * members, lanes, extent), jnp.float32)],
    )


def exchange(pieces):
    return lax.all_to_all(pieces, "dp", split_axis=0, concat_axis=0, tiled=True)


def exchange_side(pieces):
    members = pieces.shape[0]
    groups = [[side_place(index, side, members) for index in range(members)] for side in range(2)]
    return lax.all_to_all(
        pieces, "dp", split_axis=0, concat_axis=0, axis_index_groups=groups, tiled=True
    )


def swap(array, flip):
    devices = lax.axis_size("dp")
    return lax.ppermute(array, "dp", [(i, i ^ flip) for i in range(devices)])


def tie(first, second):
    return lax.optimization_barrier((first, second))


def gather_step(held, members):
    arrived = swap(held, line_offset(held.shape[0], members))
    return jnp.concatenate([held, arrived], axis=0)


def local(tokens, output_gradient, value_weight, down_maps, up_maps, adapter_per_block, ranks):
    devices = lax.axis_size("dp")
    members = devices // 2
    lines = members // 2
    steps = members.bit_length() - 1
    num_adapters, extent, width = down_maps.shape
    rows, depth = output_gradient.shape
    place = lax.axis_index("dp").astype(jnp.int32).reshape(1)
    adapters = adapter_per_block
    offsets = [line_offset(slot, members) for slot in range(members)]
    barrier = lax.optimization_barrier

    own_gradient = output_gradient.reshape(1, rows, depth)
    gradients = [own_gradient] + [None] * (lines - 1)
    for step in range(steps - 1):
        gradients[1 << step] = swap(own_gradient, offsets[1 << step])
    own_up = exchange(gather_up(adapters, up_maps)).reshape(depth, extent)
    packs = pack_tokens(place, tokens, members, width)
    firsts = [1 << step for step in range(steps - 1)]
    across = {slot: swap(gradients[slot], 1) for slot in [0] + firsts}
    held, crossed, own_up, packs, adapters = barrier(
        ([gradients[slot] for slot in firsts], across, own_up, packs, adapters)
    )
    across = dict(crossed)
    for slot, block in zip(firsts, held):
        gradients[slot] = block

    arrived = exchange_side(packs)
    pair = swap(for_pair(adapters, place, value_weight, down_maps, members), pair_bit)
    for step in range(1, steps - 1):
        for slot in range(1, 1 << step):
            gradients[slot + (1 << step)] = swap(gradients[slot], offsets[1 << step])
    backs = back_rows(adapters, place, ranks, output_gradient, own_up)
    backs = [backs] + [swap(backs, offset) for offset in offsets[1:lines]]
    arrived, backs[0], gradients, pair = barrier((arrived, backs[0], gradients, pair))

    parts = hidden_parts(adapters, place, down_maps, pair, arrived)
    for slot in range(lines):
        if slot not in across:
            across[slot] = swap(gradients[slot], 1)
    backs = gather_step(jnp.concatenate(backs, axis=0), members)
    gradients = gradients + [across[slot] for slot in range(lines)]
    slices = input_slices(
        adapters, place, gradients, backs, value_weight, pair, down_maps, 0, 1
    )
    total, received, flip = parts, swap(parts[lines:], 1), 0
    for step in reversed(range(steps - 1)):
        kinds = [jnp.float32] if step else [jnp.float32, jnp.bfloat16]
        sums = slot_sums(total, received, flip, kinds)
        total, flip = sums[0], 1 << step
        received = swap(sums[-1], offsets[flip])
    received, slices, backs, gradients, arrived = barrier(
        (received, slices, backs, gradients, arrived)
    )

    result = exchange_side(slices)
    hiddens = hidden_rows(adapters, place, ranks, total, received, flip, members)
    hiddens = gather_step(hiddens, members)
    columns, columns_other = gradient_columns(place, gradients, depth // devices)
    columns_other = swap(columns_other, pair_bit)
    backs_pair = swap(backs, pair_bit)
    tokens_other = [swap(half, pair_bit) for half in pair_tokens(arrived)]
    hiddens_pair = swap(hiddens, pair_bit)
    up_gradient = up_gradients(
        adapters, place, ranks, columns, columns_other, hiddens, hiddens_pair, depth // devices
    )
    down_gradient = down_gradients(
        adapters, place, backs, backs_pair, arrived, tokens_other, num_adapters
    )
    up_gradient, down_gradient, result = barrier((up_gradient, down_gradient, result))
    return (join_columns(place, result), down_gradient, up_gradient)


def solution(mesh):
    in_specs = (
        P(("groups", "dp"), None),
        P(("groups", "dp"), None),
        P(None, "dp"),
        P(None, None, "dp"),
        P(None, "dp", None),
        P("groups"),
        P(),
    )
    out_specs = (P(("groups", "dp"), None), P("groups", None, "dp"), P("groups", "dp", None))
    return jax.shard_map(local, mesh=mesh, in_specs=in_specs, out_specs=out_specs, check_vma=False)
```

```python
import functools

import jax
import jax.numpy as jnp
from jax import lax
from jax.experimental import pallas as pl
from jax.experimental.pallas import tpu as pltpu
from jax.sharding import PartitionSpec as P

adapter_alpha = 32.0
vmem_limit = 48 * 1024 * 1024
pair_bit = 2
line_bit = 4


def line_offset(slot, members):
    bits = members.bit_length() - 1
    order = 0
    for bit in range(bits):
        order |= ((slot >> bit) & 1) << (bits - 1 - bit)
    return ((order // 2) * line_bit) | (order % 2)


def side_of(place):
    return place % line_bit // pair_bit


def reversed_bits(number, count):
    bits = count.bit_length() - 1
    return sum(((number >> bit) & 1) << (bits - 1 - bit) for bit in range(bits))


def side_index(place, members):
    lines = members // 2
    return place % pair_bit * lines + reversed_bits(place // line_bit, lines)


def side_place(index, side, members):
    core, line = divmod(index, members // 2)
    return reversed_bits(line, members // 2) * line_bit + side * pair_bit + core


def params():
    return pltpu.CompilerParams(vmem_limit_bytes=vmem_limit)


def whole(shape):
    return pl.BlockSpec(shape, lambda *_: (0,) * len(shape))


def picked(maps, flip):
    return pl.BlockSpec(
        (1,) + maps.shape[1:], lambda i, adapters, place, *_: (adapters[place[0] ^ flip], 0, 0)
    )


def call(kernel, name, prefetch, operands, in_specs, out_shapes, scratch=(), grid=(1,), out_specs=None):
    if out_specs is None:
        out_specs = [whole(shape.shape) for shape in out_shapes]
    return pl.pallas_call(
        kernel,
        out_shape=out_shapes,
        grid_spec=pltpu.PrefetchScalarGridSpec(
            num_scalar_prefetch=len(prefetch),
            grid=grid,
            in_specs=in_specs,
            out_specs=out_specs,
            scratch_shapes=list(scratch),
        ),
        compiler_params=params(),
        name=name,
    )(*prefetch, *operands)


def run(copies):
    for copy in copies:
        copy.start()
    for copy in copies:
        copy.wait()


def copy_call(kernel, name, prefetch, operands, out_shapes, copies):
    return pl.pallas_call(
        kernel,
        out_shape=out_shapes,
        grid_spec=pltpu.PrefetchScalarGridSpec(
            num_scalar_prefetch=len(prefetch),
            grid=(1,),
            in_specs=[pl.BlockSpec(memory_space=pl.ANY)] * len(operands),
            out_specs=[whole(shape.shape) for shape in out_shapes],
            scratch_shapes=[pltpu.SemaphoreType.DMA((copies,))],
        ),
        compiler_params=params(),
        name=name,
    )(*prefetch, *operands)


weight_cuts = 4


def pair_kernel(adapters, place, weight, down_maps, out, sems):
    extent = down_maps.shape[1]
    depth = weight.shape[0]
    members = (out.shape[0] - depth) // extent
    copies = []
    for slot in range(members):
        block = place[0] ^ line_offset(slot, members) ^ pair_bit
        copies.append((down_maps.at[adapters[block]], slot * extent, extent))
    cut = depth // weight_cuts
    for at in range(0, depth, cut):
        copies.append((weight.at[pl.ds(at, cut)], members * extent + at, cut))
    run(
        [
            pltpu.make_async_copy(source, out.at[pl.ds(at, rows)], sems.at[number])
            for number, (source, at, rows) in enumerate(copies)
        ]
    )


def for_pair(adapters, place, weight, down_maps, members):
    extent, width = down_maps.shape[1:]
    shape = jax.ShapeDtypeStruct((members * extent + weight.shape[0], width), weight.dtype)
    return copy_call(
        pair_kernel,
        "for_pair",
        (adapters, place),
        (weight, down_maps),
        [shape],
        members + weight_cuts,
    )[0]


def gather_up_kernel(adapters, up_maps, out, sems):
    run(
        [
            pltpu.make_async_copy(up_maps.at[adapters[block]], out.at[block], sems.at[block])
            for block in range(out.shape[0])
        ]
    )


def gather_up(adapters, up_maps):
    shape = jax.ShapeDtypeStruct((adapters.shape[0],) + up_maps.shape[1:], up_maps.dtype)
    return copy_call(
        gather_up_kernel, "gather_up", (adapters,), (up_maps,), [shape], adapters.shape[0]
    )[0]


def pack_kernel(place, tokens, out, sems):
    members, _, _, width = out.shape
    copies = []
    for index in range(members):
        for half in range(2):
            column = side_place(index, side_of(place[0]) ^ half, members) * width
            copies.append(
                pltpu.make_async_copy(
                    tokens.at[:, pl.ds(pl.multiple_of(column, width), width)],
                    out.at[index, half],
                    sems.at[2 * index + half],
                )
            )
    run(copies)


def pack_tokens(place, tokens, members, width):
    shape = jax.ShapeDtypeStruct((members, 2, tokens.shape[0], width), tokens.dtype)
    return copy_call(pack_kernel, "pack_tokens", (place,), (tokens,), [shape], 2 * members)[0]


def rank_row(ranks, adapter, extent):
    rank = jnp.full((1, extent), ranks[adapter], jnp.int32)
    alive = (lax.broadcasted_iota(jnp.int32, (1, extent), 1) < rank).astype(jnp.float32)
    return alive, adapter_alpha / rank.astype(jnp.float32)


def back_kernel(adapters, place, ranks, gradient, up, out):
    alive, factor = rank_row(ranks, adapters[place[0]], up.shape[1])
    back = jnp.dot(gradient[...], up[...], preferred_element_type=jnp.float32)
    out[0] = (factor * back * alive).astype(out.dtype)


def back_rows(adapters, place, ranks, gradient, up):
    return call(
        back_kernel,
        "back_low",
        (adapters, place, ranks),
        (gradient, up),
        [whole(gradient.shape), whole(up.shape)],
        [jax.ShapeDtypeStruct((1, gradient.shape[0], up.shape[1]), jnp.bfloat16)],
    )[0]


def input_kernel(adapters, place, backs, pair, *refs):
    members, rows, _ = backs.shape
    gradients, downs = refs[:members], refs[members : 2 * members]
    weight, out = refs[2 * members :]
    extent = downs[0].shape[1]
    some = min(4, members)
    for first in range(0, members, some):
        slots = range(first, first + some)
        lines = jnp.concatenate([gradients[slot][0] for slot in slots], axis=0)
        for half in range(2):
            right = weight[...] if half == 0 else pair[members * extent :]
            frozen = jnp.dot(lines, right, preferred_element_type=jnp.float32)
            for slot in slots:
                down = downs[slot][0] if half == 0 else pair[slot * extent : (slot + 1) * extent]
                index = side_index(place[0] ^ line_offset(slot, members), members)
                low = jnp.dot(backs[slot], down, preferred_element_type=jnp.float32)
                at = (slot - first) * rows
                out[index, half] = (frozen[at : at + rows] + low).astype(jnp.bfloat16)


def input_slices(adapters, place, gradients, backs, weight, pair, down_maps, part, parts):
    members, rows, extent = backs.shape
    depth, width = weight.shape
    rows //= parts
    return call(
        input_kernel,
        "input_slices",
        (adapters, place),
        [backs, pair] + list(gradients) + [down_maps] * members + [weight],
        [pl.BlockSpec((members, rows, extent), lambda *_: (0, part, 0)), whole(pair.shape)]
        + [pl.BlockSpec((1, rows, depth), lambda *_: (0, part, 0))] * members
        + [picked(down_maps, line_offset(slot, members)) for slot in range(members)]
        + [whole(weight.shape)],
        [jax.ShapeDtypeStruct((members, 2, rows, width), jnp.bfloat16)],
    )[0]


def columns_kernel(place, *refs):
    *gradients, own, pair = refs
    for slot in range(own.shape[0]):
        own[slot] = gradients[2 * slot][0]
        pair[slot] = gradients[2 * slot + 1][0]


def gradient_columns(place, gradients, value_width):
    members = len(gradients)
    rows = gradients[0].shape[1]
    lanes = max(128, value_width)

    def spec(side):
        return pl.BlockSpec(
            (1, rows, lanes),
            lambda i, place: (0, 0, (place[0] ^ (side * pair_bit)) * value_width // lanes),
        )

    shape = jax.ShapeDtypeStruct((members, rows, lanes), gradients[0].dtype)
    return call(
        columns_kernel,
        "gradient_columns",
        (place,),
        [gradient for gradient in gradients for _ in range(2)],
        [spec(0), spec(1)] * members,
        [shape, shape],
    )


def hidden_kernel(adapters, place, pair, tokens, *refs):
    *downs, parts = refs
    members = parts.shape[0]
    extent = downs[0].shape[1]
    across = (((1,), (1,)), ((), ()))
    for slot in range(members):
        index = side_index(place[0] ^ line_offset(slot, members), members)
        parts[slot] = lax.dot_general(
            tokens[index, 0], downs[slot][0], across, preferred_element_type=jnp.float32
        ) + lax.dot_general(
            tokens[index, 1],
            pair[slot * extent : (slot + 1) * extent],
            across,
            preferred_element_type=jnp.float32,
        )


def hidden_parts(adapters, place, down_maps, pair, tokens):
    members, _, rows, _ = tokens.shape
    extent = down_maps.shape[1]
    return call(
        hidden_kernel,
        "hidden_parts",
        (adapters, place),
        [pair, tokens] + [down_maps] * members,
        [whole(pair.shape), whole(tokens.shape)]
        + [picked(down_maps, line_offset(slot, members)) for slot in range(members)],
        [jax.ShapeDtypeStruct((members, rows, extent), jnp.float32)],
    )[0]


def pair_tokens_kernel(tokens, first, second):
    half = first.shape[0]
    for index in range(half):
        first[index] = tokens[index, 0]
        second[index] = tokens[half + index, 0]


def pair_tokens(tokens):
    members, _, rows, width = tokens.shape
    shape = jax.ShapeDtypeStruct((members // 2, rows, width), tokens.dtype)
    return call(
        pair_tokens_kernel,
        "pair_tokens",
        (),
        (tokens,),
        [pl.BlockSpec((members, 1, rows, width), lambda *_: (0, 1, 0, 0))],
        [shape, shape],
    )


def sum_kernel(total, received, *outs, flip):
    for slot in range(outs[0].shape[0]):
        value = total[slot] + received[slot ^ flip].astype(jnp.float32)
        for out in outs:
            out[slot] = value.astype(out.dtype)


def slot_sums(total, received, flip, types):
    shape = received.shape
    return call(
        functools.partial(sum_kernel, flip=flip),
        "slot_sums",
        (),
        (total, received),
        [whole(shape)] * 2,
        [jax.ShapeDtypeStruct(shape, kind) for kind in types],
    )


def hidden_low_kernel(adapters, place, ranks, total, received, out, *, flip, members):
    for slot in range(out.shape[0]):
        block = place[0] ^ line_offset(slot, members)
        alive, _ = rank_row(ranks, adapters[block], out.shape[2])
        value = total[slot] + received[slot ^ flip].astype(jnp.float32)
        out[slot] = (value * alive).astype(out.dtype)


def hidden_rows(adapters, place, ranks, total, received, flip, members):
    return call(
        functools.partial(hidden_low_kernel, flip=flip, members=members),
        "hidden_low",
        (adapters, place, ranks),
        (total, received),
        [whole(total.shape)] * 2,
        [jax.ShapeDtypeStruct(total.shape, jnp.bfloat16)],
    )[0]


def join_kernel(place, source, out, sems):
    members, _, _, width = source.shape
    copies = []
    for index in range(members):
        for half in range(2):
            column = side_place(index, side_of(place[0]) ^ half, members) * width
            copies.append(
                pltpu.make_async_copy(
                    source.at[index, half],
                    out.at[:, pl.ds(pl.multiple_of(column, width), width)],
                    sems.at[2 * index + half],
                )
            )
    run(copies)


def join_columns(place, source):
    members, _, rows, width = source.shape
    return pl.pallas_call(
        join_kernel,
        out_shape=jax.ShapeDtypeStruct((rows, 2 * members * width), source.dtype),
        grid_spec=pltpu.PrefetchScalarGridSpec(
            num_scalar_prefetch=1,
            grid=(1,),
            in_specs=[whole(source.shape)],
            out_specs=pl.BlockSpec(memory_space=pl.ANY),
            scratch_shapes=[pltpu.SemaphoreType.DMA((2 * members,))],
        ),
        compiler_params=params(),
        name="join_columns",
    )(place, source)


def list_members(adapters, place, members, head, following):
    def clear(adapter, carry):
        head[adapter] = -1
        return carry

    lax.fori_loop(0, head.shape[0], clear, 0)
    for entry in reversed(range(2 * members)):
        side, own = divmod(entry, members)
        adapter = adapters[place[0] ^ line_offset(own, members) ^ (side * pair_bit)]
        following[entry] = head[adapter]
        head[adapter] = entry


def write_sums(head, following, products, ready, zero, out, sems, finish):
    num_adapters = out.shape[0]
    zero[...] = jnp.zeros_like(zero)

    def write(adapter, carry):
        first = head[adapter]

        @pl.when(first < 0)
        def _():
            pltpu.make_async_copy(zero, out.at[adapter], sems.at[adapter]).start()

        @pl.when(first >= 0)
        def _():
            def more(entry):
                products[first] += products[entry]
                return following[entry]

            lax.while_loop(lambda entry: entry >= 0, more, following[first])
            ready[first] = finish(adapter, products[first]).astype(out.dtype)
            pltpu.make_async_copy(ready.at[first], out.at[adapter], sems.at[adapter]).start()

        return carry

    lax.fori_loop(0, num_adapters, write, 0)

    def wait(adapter, carry):
        pltpu.make_async_copy(zero, out.at[adapter], sems.at[adapter]).wait()
        return carry

    lax.fori_loop(0, num_adapters, wait, 0)


def by_rows(left, right):
    return lax.dot_general(
        left, right, (((0,), (0,)), ((), ())), preferred_element_type=jnp.float32
    )


def sums_call(kernel, name, prefetch, operands, num_adapters, entries, product, scratch=(), specs=None):
    return pl.pallas_call(
        kernel,
        out_shape=jax.ShapeDtypeStruct((num_adapters,) + product, jnp.bfloat16),
        grid_spec=pltpu.PrefetchScalarGridSpec(
            num_scalar_prefetch=len(prefetch),
            grid=(1,),
            in_specs=specs or [whole(operand.shape) for operand in operands],
            out_specs=pl.BlockSpec(memory_space=pltpu.HBM),
            scratch_shapes=[
                pltpu.SMEM((num_adapters,), jnp.int32),
                pltpu.SMEM((entries,), jnp.int32),
                pltpu.VMEM((entries,) + product, jnp.float32),
                pltpu.VMEM((entries,) + product, jnp.bfloat16),
                pltpu.VMEM(product, jnp.bfloat16),
                pltpu.SemaphoreType.DMA((num_adapters,)),
                *scratch,
            ],
        ),
        compiler_params=params(),
        name=name,
    )(*prefetch, *operands)


def down_gradient_kernel(
    adapters,
    place,
    backs,
    backs_pair,
    tokens,
    other_first,
    other_second,
    out,
    head,
    following,
    products,
    ready,
    zero,
    sems,
):
    members = tokens.shape[0]
    half = members // 2
    list_members(adapters, place, members, head, following)
    for slot in range(members):
        index = side_index(place[0] ^ line_offset(slot, members), members)
        products[slot] = by_rows(backs[slot], tokens[index, 0])
        for number, other in enumerate((other_first, other_second)):

            @pl.when(index // half == number)
            def _(slot=slot, index=index, other=other):
                products[members + slot] = by_rows(backs_pair[slot], other[lax.rem(index, half)])

    write_sums(
        head, following, products, ready, zero, out, sems, lambda adapter, total: total
    )


def down_gradients(adapters, place, backs, backs_pair, tokens, others, num_adapters):
    members, _, rows, width = tokens.shape
    extent = backs.shape[2]
    operands = (backs, backs_pair, tokens, *others)
    specs = [whole(operand.shape) for operand in operands]
    specs[2] = pl.BlockSpec((members, 1, rows, width), lambda *_: (0, 0, 0, 0))
    return sums_call(
        down_gradient_kernel,
        "down_gradients",
        (adapters, place),
        operands,
        num_adapters,
        2 * members,
        (extent, width),
        specs=specs,
    )


def up_gradient_kernel(
    adapters,
    place,
    ranks,
    gradients,
    gradients_pair,
    hiddens,
    hiddens_pair,
    out,
    head,
    following,
    products,
    ready,
    zero,
    sems,
    lines,
):
    members, _, lanes = gradients.shape
    width, extent = out.shape[1:]
    list_members(adapters, place, members, head, following)
    inside = pl.multiple_of(lax.rem(place[0], lanes // width) * width, width)
    for slot in range(members):
        lines[slot] = by_rows(gradients[slot], hiddens[slot])
        lines[members + slot] = by_rows(gradients_pair[slot], hiddens_pair[slot])
    for entry in range(2 * members):
        products[entry] = lines[entry, pl.ds(inside, width), :]

    def finish(adapter, total):
        _, factor = rank_row(ranks, adapter, extent)
        return factor * total

    write_sums(head, following, products, ready, zero, out, sems, finish)


def up_gradients(adapters, place, ranks, gradients, gradients_pair, hiddens, hiddens_pair, width):
    members, _, lanes = gradients.shape
    extent = hiddens.shape[2]
    return sums_call(
        up_gradient_kernel,
        "up_gradients",
        (adapters, place, ranks),
        (gradients, gradients_pair, hiddens, hiddens_pair),
        ranks.shape[0],
        2 * members,
        (width, extent),
        [pltpu.VMEM((2 * members, lanes, extent), jnp.float32)],
    )


def exchange(pieces):
    return lax.all_to_all(pieces, "dp", split_axis=0, concat_axis=0, tiled=True)


def exchange_side(pieces):
    members = pieces.shape[0]
    groups = [[side_place(index, side, members) for index in range(members)] for side in range(2)]
    return lax.all_to_all(
        pieces, "dp", split_axis=0, concat_axis=0, axis_index_groups=groups, tiled=True
    )


def swap(array, flip):
    devices = lax.axis_size("dp")
    return lax.ppermute(array, "dp", [(i, i ^ flip) for i in range(devices)])


def tie(first, second):
    return lax.optimization_barrier((first, second))


def gather_step(held, members):
    arrived = swap(held, line_offset(held.shape[0], members))
    return jnp.concatenate([held, arrived], axis=0)


def local(tokens, output_gradient, value_weight, down_maps, up_maps, adapter_per_block, ranks):
    devices = lax.axis_size("dp")
    members = devices // 2
    lines = members // 2
    steps = members.bit_length() - 1
    num_adapters, extent, width = down_maps.shape
    rows, depth = output_gradient.shape
    place = lax.axis_index("dp").astype(jnp.int32).reshape(1)
    adapters = adapter_per_block
    offsets = [line_offset(slot, members) for slot in range(members)]
    barrier = lax.optimization_barrier

    own_gradient = output_gradient.reshape(1, rows, depth)
    gradients = [own_gradient] + [None] * (lines - 1)
    for step in range(steps - 1):
        gradients[1 << step] = swap(own_gradient, offsets[1 << step])
    own_up = exchange(gather_up(adapters, up_maps)).reshape(depth, extent)
    packs = pack_tokens(place, tokens, members, width)
    firsts = [1 << step for step in range(steps - 1)]
    across = {slot: swap(gradients[slot], 1) for slot in [0] + firsts}
    pair = for_pair(adapters, place, value_weight, down_maps, members)
    gradients[2], pair = barrier((gradients[2], pair))
    pair = swap(pair, pair_bit)
    held, crossed, own_up, packs = barrier(
        ([gradients[slot] for slot in firsts], across, own_up, packs)
    )
    across = dict(crossed)
    for slot, block in zip(firsts, held):
        gradients[slot] = block

    arrived = exchange_side(packs)
    for step in range(1, steps - 1):
        for slot in range(1, 1 << step):
            gradients[slot + (1 << step)] = swap(gradients[slot], offsets[1 << step])
    backs = back_rows(adapters, place, ranks, output_gradient, own_up)
    backs = [backs] + [swap(backs, offset) for offset in offsets[1:lines]]
    arrived, backs, gradients, pair = barrier((arrived, backs, gradients, pair))

    parts = hidden_parts(adapters, place, down_maps, pair, arrived)
    for slot in range(lines):
        if slot not in across:
            across[slot] = swap(gradients[slot], 1)
    backs = gather_step(jnp.concatenate(backs, axis=0), members)
    gradients = gradients + [across[slot] for slot in range(lines)]
    slices = input_slices(
        adapters, place, gradients, backs, value_weight, pair, down_maps, 0, 1
    )
    total, received, flip = parts, swap(parts[lines:], 1), 0
    for step in reversed(range(steps - 1)):
        kinds = [jnp.float32] if step else [jnp.float32, jnp.bfloat16]
        sums = slot_sums(total, received, flip, kinds)
        total, flip = sums[0], 1 << step
        received = swap(sums[-1], offsets[flip])
    received, slices, backs, gradients, arrived = barrier(
        (received, slices, backs, gradients, arrived)
    )

    result = exchange_side(slices)
    hiddens = hidden_rows(adapters, place, ranks, total, received, flip, members)
    hiddens = gather_step(hiddens, members)
    columns, columns_other = gradient_columns(place, gradients, depth // devices)
    columns_other = swap(columns_other, pair_bit)
    backs_pair = swap(backs, pair_bit)
    tokens_other = [swap(half, pair_bit) for half in pair_tokens(arrived)]
    hiddens_pair = swap(hiddens, pair_bit)
    up_gradient = up_gradients(
        adapters, place, ranks, columns, columns_other, hiddens, hiddens_pair, depth // devices
    )
    down_gradient = down_gradients(
        adapters, place, backs, backs_pair, arrived, tokens_other, num_adapters
    )
    up_gradient, down_gradient, result = barrier((up_gradient, down_gradient, result))
    return (join_columns(place, result), down_gradient, up_gradient)


def solution(mesh):
    in_specs = (
        P(("groups", "dp"), None),
        P(("groups", "dp"), None),
        P(None, "dp"),
        P(None, None, "dp"),
        P(None, "dp", None),
        P("groups"),
        P(),
    )
    out_specs = (P(("groups", "dp"), None), P("groups", None, "dp"), P("groups", "dp", None))
    return jax.shard_map(local, mesh=mesh, in_specs=in_specs, out_specs=out_specs, check_vma=False)
```

```python
import functools

import jax
import jax.numpy as jnp
from jax import lax
from jax.experimental import pallas as pl
from jax.experimental.pallas import tpu as pltpu
from jax.sharding import PartitionSpec as P

adapter_alpha = 32.0
vmem_limit = 48 * 1024 * 1024
pair_bit = 2
line_bit = 4


def line_offset(slot, members):
    bits = members.bit_length() - 1
    order = 0
    for bit in range(bits):
        order |= ((slot >> bit) & 1) << (bits - 1 - bit)
    return ((order // 2) * line_bit) | (order % 2)


def side_of(place):
    return place % line_bit // pair_bit


def reversed_bits(number, count):
    bits = count.bit_length() - 1
    return sum(((number >> bit) & 1) << (bits - 1 - bit) for bit in range(bits))


def side_index(place, members):
    lines = members // 2
    return place % pair_bit * lines + reversed_bits(place // line_bit, lines)


def side_place(index, side, members):
    core, line = divmod(index, members // 2)
    return reversed_bits(line, members // 2) * line_bit + side * pair_bit + core


def params():
    return pltpu.CompilerParams(vmem_limit_bytes=vmem_limit)


def whole(shape):
    return pl.BlockSpec(shape, lambda *_: (0,) * len(shape))


def picked(maps, flip):
    return pl.BlockSpec(
        (1,) + maps.shape[1:], lambda i, adapters, place, *_: (adapters[place[0] ^ flip], 0, 0)
    )


def call(kernel, name, prefetch, operands, in_specs, out_shapes, scratch=(), grid=(1,), out_specs=None):
    if out_specs is None:
        out_specs = [whole(shape.shape) for shape in out_shapes]
    return pl.pallas_call(
        kernel,
        out_shape=out_shapes,
        grid_spec=pltpu.PrefetchScalarGridSpec(
            num_scalar_prefetch=len(prefetch),
            grid=grid,
            in_specs=in_specs,
            out_specs=out_specs,
            scratch_shapes=list(scratch),
        ),
        compiler_params=params(),
        name=name,
    )(*prefetch, *operands)


def run(copies):
    for copy in copies:
        copy.start()
    for copy in copies:
        copy.wait()


def copy_call(kernel, name, prefetch, operands, out_shapes, copies):
    return pl.pallas_call(
        kernel,
        out_shape=out_shapes,
        grid_spec=pltpu.PrefetchScalarGridSpec(
            num_scalar_prefetch=len(prefetch),
            grid=(1,),
            in_specs=[pl.BlockSpec(memory_space=pl.ANY)] * len(operands),
            out_specs=[whole(shape.shape) for shape in out_shapes],
            scratch_shapes=[pltpu.SemaphoreType.DMA((copies,))],
        ),
        compiler_params=params(),
        name=name,
    )(*prefetch, *operands)


weight_cuts = 4


def pair_kernel(adapters, place, weight, down_maps, out, sems):
    extent = down_maps.shape[1]
    depth = weight.shape[0]
    members = (out.shape[0] - depth) // extent
    copies = []
    for slot in range(members):
        block = place[0] ^ line_offset(slot, members) ^ pair_bit
        copies.append((down_maps.at[adapters[block]], slot * extent, extent))
    cut = depth // weight_cuts
    for at in range(0, depth, cut):
        copies.append((weight.at[pl.ds(at, cut)], members * extent + at, cut))
    run(
        [
            pltpu.make_async_copy(source, out.at[pl.ds(at, rows)], sems.at[number])
            for number, (source, at, rows) in enumerate(copies)
        ]
    )


def for_pair(adapters, place, weight, down_maps, members):
    extent, width = down_maps.shape[1:]
    shape = jax.ShapeDtypeStruct((members * extent + weight.shape[0], width), weight.dtype)
    return copy_call(
        pair_kernel,
        "for_pair",
        (adapters, place),
        (weight, down_maps),
        [shape],
        members + weight_cuts,
    )[0]


def gather_up_kernel(adapters, up_maps, out, sems):
    run(
        [
            pltpu.make_async_copy(up_maps.at[adapters[block]], out.at[block], sems.at[block])
            for block in range(out.shape[0])
        ]
    )


def gather_up(adapters, up_maps):
    shape = jax.ShapeDtypeStruct((adapters.shape[0],) + up_maps.shape[1:], up_maps.dtype)
    return copy_call(
        gather_up_kernel, "gather_up", (adapters,), (up_maps,), [shape], adapters.shape[0]
    )[0]


def pack_kernel(place, tokens, out, sems):
    members, _, _, width = out.shape
    copies = []
    for index in range(members):
        for half in range(2):
            column = side_place(index, side_of(place[0]) ^ half, members) * width
            copies.append(
                pltpu.make_async_copy(
                    tokens.at[:, pl.ds(pl.multiple_of(column, width), width)],
                    out.at[index, half],
                    sems.at[2 * index + half],
                )
            )
    run(copies)


def pack_tokens(place, tokens, members, width):
    shape = jax.ShapeDtypeStruct((members, 2, tokens.shape[0], width), tokens.dtype)
    return copy_call(pack_kernel, "pack_tokens", (place,), (tokens,), [shape], 2 * members)[0]


def rank_row(ranks, adapter, extent):
    rank = jnp.full((1, extent), ranks[adapter], jnp.int32)
    alive = (lax.broadcasted_iota(jnp.int32, (1, extent), 1) < rank).astype(jnp.float32)
    return alive, adapter_alpha / rank.astype(jnp.float32)


def back_kernel(adapters, place, ranks, gradient, up, out):
    alive, factor = rank_row(ranks, adapters[place[0]], up.shape[1])
    back = jnp.dot(gradient[...], up[...], preferred_element_type=jnp.float32)
    out[0] = (factor * back * alive).astype(out.dtype)


def back_rows(adapters, place, ranks, gradient, up):
    return call(
        back_kernel,
        "back_low",
        (adapters, place, ranks),
        (gradient, up),
        [whole(gradient.shape), whole(up.shape)],
        [jax.ShapeDtypeStruct((1, gradient.shape[0], up.shape[1]), jnp.bfloat16)],
    )[0]


def input_kernel(adapters, place, backs, pair, *refs):
    members, rows, _ = backs.shape
    gradients = [ref.at[0] for ref in refs[:members]]
    downs = refs[members : 2 * members]
    weight = refs[2 * members]
    out, *columns = refs[-3:]
    extent = downs[0].shape[1]
    lanes = columns[0].shape[2]
    value_width = gradients[0].shape[1] // (2 * members)
    some = min(4, members)
    for first in range(0, members, some):
        slots = range(first, first + some)
        lines = jnp.concatenate([gradients[slot][...] for slot in slots], axis=0)
        for half in range(2):
            right = weight[...] if half == 0 else pair[members * extent :]
            frozen = jnp.dot(lines, right, preferred_element_type=jnp.float32)
            for slot in slots:
                down = downs[slot][0] if half == 0 else pair[slot * extent : (slot + 1) * extent]
                index = side_index(place[0] ^ line_offset(slot, members), members)
                low = jnp.dot(backs[slot], down, preferred_element_type=jnp.float32)
                at = (slot - first) * rows
                out[index, half] = (frozen[at : at + rows] + low).astype(jnp.bfloat16)
    for side in range(2):
        column = (place[0] ^ (side * pair_bit)) * value_width // lanes * lanes
        for slot in range(members):
            columns[side][slot] = gradients[slot][:, pl.ds(pl.multiple_of(column, lanes), lanes)]


def input_slices(adapters, place, gradients, backs, weight, pair, down_maps):
    members, rows, _ = backs.shape
    width = weight.shape[1]
    lanes = max(128, gradients[0].shape[2] // (2 * members))
    shape = jax.ShapeDtypeStruct((members, 2, rows, width), jnp.bfloat16)
    columns = jax.ShapeDtypeStruct((members, rows, lanes), jnp.bfloat16)
    return call(
        input_kernel,
        "input_slices",
        (adapters, place),
        [backs, pair] + list(gradients) + [down_maps] * members + [weight],
        [whole(backs.shape), whole(pair.shape)]
        + [whole(gradient.shape) for gradient in gradients]
        + [picked(down_maps, line_offset(slot, members)) for slot in range(members)]
        + [whole(weight.shape)],
        [shape, columns, columns],
    )


def hidden_kernel(adapters, place, pair, tokens, *refs):
    parts, own, *others = refs[-4:]
    members = own.shape[0]
    downs = refs[:members]
    extent = downs[0].shape[1]
    across = (((1,), (1,)), ((), ()))
    for slot in range(members):
        index = side_index(place[0] ^ line_offset(slot, members), members)
        own[slot] = tokens[index, 0]
        others[slot // (members // 2)][slot % (members // 2)] = tokens[index, 1]
        parts[slot] = lax.dot_general(
            tokens[index, 0], downs[slot][0], across, preferred_element_type=jnp.float32
        ) + lax.dot_general(
            tokens[index, 1],
            pair[slot * extent : (slot + 1) * extent],
            across,
            preferred_element_type=jnp.float32,
        )


def hidden_parts(adapters, place, down_maps, pair, tokens):
    members, _, rows, width = tokens.shape
    extent = down_maps.shape[1]
    others = jax.ShapeDtypeStruct((members // 2, rows, width), tokens.dtype)
    return call(
        hidden_kernel,
        "hidden_parts",
        (adapters, place),
        [pair, tokens] + [down_maps] * members,
        [whole(pair.shape), whole(tokens.shape)]
        + [picked(down_maps, line_offset(slot, members)) for slot in range(members)],
        [
            jax.ShapeDtypeStruct((members, rows, extent), jnp.float32),
            jax.ShapeDtypeStruct((members, rows, width), tokens.dtype),
            others,
            others,
        ],
    )


def sum_kernel(total, received, *outs, flip):
    for slot in range(outs[0].shape[0]):
        value = total[slot] + received[slot ^ flip].astype(jnp.float32)
        for out in outs:
            out[slot] = value.astype(out.dtype)


def slot_sums(total, received, flip, types):
    shape = received.shape
    return call(
        functools.partial(sum_kernel, flip=flip),
        "slot_sums",
        (),
        (total, received),
        [whole(shape)] * 2,
        [jax.ShapeDtypeStruct(shape, kind) for kind in types],
    )


def hidden_low_kernel(adapters, place, ranks, total, received, out, *, flip, members):
    for slot in range(out.shape[0]):
        block = place[0] ^ line_offset(slot, members)
        alive, _ = rank_row(ranks, adapters[block], out.shape[2])
        value = total[slot] + received[slot ^ flip].astype(jnp.float32)
        out[slot] = (value * alive).astype(out.dtype)


def hidden_rows(adapters, place, ranks, total, received, flip, members):
    return call(
        functools.partial(hidden_low_kernel, flip=flip, members=members),
        "hidden_low",
        (adapters, place, ranks),
        (total, received),
        [whole(total.shape)] * 2,
        [jax.ShapeDtypeStruct(total.shape, jnp.bfloat16)],
    )[0]


def join_kernel(place, source, out, sems):
    members, _, _, width = source.shape
    copies = []
    for index in range(members):
        for half in range(2):
            column = side_place(index, side_of(place[0]) ^ half, members) * width
            copies.append(
                pltpu.make_async_copy(
                    source.at[index, half],
                    out.at[:, pl.ds(pl.multiple_of(column, width), width)],
                    sems.at[2 * index + half],
                )
            )
    run(copies)


def join_columns(place, source):
    members, _, rows, width = source.shape
    return pl.pallas_call(
        join_kernel,
        out_shape=jax.ShapeDtypeStruct((rows, 2 * members * width), source.dtype),
        grid_spec=pltpu.PrefetchScalarGridSpec(
            num_scalar_prefetch=1,
            grid=(1,),
            in_specs=[whole(source.shape)],
            out_specs=pl.BlockSpec(memory_space=pl.ANY),
            scratch_shapes=[pltpu.SemaphoreType.DMA((2 * members,))],
        ),
        compiler_params=params(),
        name="join_columns",
    )(place, source)


def list_members(adapters, place, members, head, following):
    def clear(adapter, carry):
        head[adapter] = -1
        return carry

    lax.fori_loop(0, head.shape[0], clear, 0)
    for entry in reversed(range(2 * members)):
        side, own = divmod(entry, members)
        adapter = adapters[place[0] ^ line_offset(own, members) ^ (side * pair_bit)]
        following[entry] = head[adapter]
        head[adapter] = entry


def write_sums(head, following, products, ready, zero, out, sems, finish):
    num_adapters = out.shape[0]
    zero[...] = jnp.zeros_like(zero)

    def write(adapter, carry):
        first = head[adapter]

        @pl.when(first < 0)
        def _():
            pltpu.make_async_copy(zero, out.at[adapter], sems.at[adapter]).start()

        @pl.when(first >= 0)
        def _():
            def more(entry):
                products[first] += products[entry]
                return following[entry]

            lax.while_loop(lambda entry: entry >= 0, more, following[first])
            ready[first] = finish(adapter, products[first]).astype(out.dtype)
            pltpu.make_async_copy(ready.at[first], out.at[adapter], sems.at[adapter]).start()

        return carry

    lax.fori_loop(0, num_adapters, write, 0)

    def wait(adapter, carry):
        pltpu.make_async_copy(zero, out.at[adapter], sems.at[adapter]).wait()
        return carry

    lax.fori_loop(0, num_adapters, wait, 0)


def by_rows(left, right):
    return lax.dot_general(
        left, right, (((0,), (0,)), ((), ())), preferred_element_type=jnp.float32
    )


def sums_call(kernel, name, prefetch, operands, num_adapters, entries, product, scratch=()):
    return pl.pallas_call(
        kernel,
        out_shape=jax.ShapeDtypeStruct((num_adapters,) + product, jnp.bfloat16),
        grid_spec=pltpu.PrefetchScalarGridSpec(
            num_scalar_prefetch=len(prefetch),
            grid=(1,),
            in_specs=[whole(operand.shape) for operand in operands],
            out_specs=pl.BlockSpec(memory_space=pltpu.HBM),
            scratch_shapes=[
                pltpu.SMEM((num_adapters,), jnp.int32),
                pltpu.SMEM((entries,), jnp.int32),
                pltpu.VMEM((entries,) + product, jnp.float32),
                pltpu.VMEM((entries,) + product, jnp.bfloat16),
                pltpu.VMEM(product, jnp.bfloat16),
                pltpu.SemaphoreType.DMA((num_adapters,)),
                *scratch,
            ],
        ),
        compiler_params=params(),
        name=name,
    )(*prefetch, *operands)


def down_gradient_kernel(
    adapters,
    place,
    backs,
    backs_pair,
    own,
    other_first,
    other_second,
    out,
    head,
    following,
    products,
    ready,
    zero,
    sems,
):
    members = own.shape[0]
    others = (other_first, other_second)
    list_members(adapters, place, members, head, following)
    for slot in range(members):
        products[slot] = by_rows(backs[slot], own[slot])
        core, line = divmod(slot, members // 2)
        products[members + slot] = by_rows(backs_pair[slot], others[core][line])
    write_sums(
        head, following, products, ready, zero, out, sems, lambda adapter, total: total
    )


def down_gradients(adapters, place, backs, backs_pair, own, others, num_adapters):
    members, _, width = own.shape
    return sums_call(
        down_gradient_kernel,
        "down_gradients",
        (adapters, place),
        (backs, backs_pair, own, *others),
        num_adapters,
        2 * members,
        (backs.shape[2], width),
    )


def up_gradient_kernel(
    adapters,
    place,
    ranks,
    gradients,
    gradients_pair,
    hiddens,
    hiddens_pair,
    out,
    head,
    following,
    products,
    ready,
    zero,
    sems,
    lines,
):
    members, _, lanes = gradients.shape
    width, extent = out.shape[1:]
    list_members(adapters, place, members, head, following)
    inside = pl.multiple_of(lax.rem(place[0], lanes // width) * width, width)
    for slot in range(members):
        lines[slot] = by_rows(gradients[slot], hiddens[slot])
        lines[members + slot] = by_rows(gradients_pair[slot], hiddens_pair[slot])
    for entry in range(2 * members):
        products[entry] = lines[entry, pl.ds(inside, width), :]

    def finish(adapter, total):
        _, factor = rank_row(ranks, adapter, extent)
        return factor * total

    write_sums(head, following, products, ready, zero, out, sems, finish)


def up_gradients(adapters, place, ranks, gradients, gradients_pair, hiddens, hiddens_pair, width):
    members, _, lanes = gradients.shape
    extent = hiddens.shape[2]
    return sums_call(
        up_gradient_kernel,
        "up_gradients",
        (adapters, place, ranks),
        (gradients, gradients_pair, hiddens, hiddens_pair),
        ranks.shape[0],
        2 * members,
        (width, extent),
        [pltpu.VMEM((2 * members, lanes, extent), jnp.float32)],
    )


def exchange(pieces):
    return lax.all_to_all(pieces, "dp", split_axis=0, concat_axis=0, tiled=True)


def exchange_side(pieces):
    members = pieces.shape[0]
    groups = [[side_place(index, side, members) for index in range(members)] for side in range(2)]
    return lax.all_to_all(
        pieces, "dp", split_axis=0, concat_axis=0, axis_index_groups=groups, tiled=True
    )


def swap(array, flip):
    devices = lax.axis_size("dp")
    return lax.ppermute(array, "dp", [(i, i ^ flip) for i in range(devices)])


def tie(first, second):
    return lax.optimization_barrier((first, second))


def gather_step(held, members):
    arrived = swap(held, line_offset(held.shape[0], members))
    return jnp.concatenate([held, arrived], axis=0)


def local(tokens, output_gradient, value_weight, down_maps, up_maps, adapter_per_block, ranks):
    devices = lax.axis_size("dp")
    members = devices // 2
    lines = members // 2
    steps = members.bit_length() - 1
    num_adapters, extent, width = down_maps.shape
    rows, depth = output_gradient.shape
    place = lax.axis_index("dp").astype(jnp.int32).reshape(1)
    adapters = adapter_per_block
    offsets = [line_offset(slot, members) for slot in range(members)]
    barrier = lax.optimization_barrier

    own_gradient = output_gradient.reshape(1, rows, depth)
    gradients = [own_gradient] + [None] * (lines - 1)
    for step in range(steps - 1):
        gradients[1 << step] = swap(own_gradient, offsets[1 << step])
    own_up = exchange(gather_up(adapters, up_maps)).reshape(depth, extent)
    packs = pack_tokens(place, tokens, members, width)
    firsts = [1 << step for step in range(steps - 1)]
    across = {slot: swap(gradients[slot], 1) for slot in [0] + firsts}
    held, crossed, own_up, packs, adapters = barrier(
        ([gradients[slot] for slot in firsts], across, own_up, packs, adapters)
    )
    across = dict(crossed)
    for slot, block in zip(firsts, held):
        gradients[slot] = block

    arrived = exchange_side(packs)
    pair = swap(for_pair(adapters, place, value_weight, down_maps, members), pair_bit)
    for step in range(1, steps - 1):
        for slot in range(1, 1 << step):
            gradients[slot + (1 << step)] = swap(gradients[slot], offsets[1 << step])
    backs = back_rows(adapters, place, ranks, output_gradient, own_up)
    backs = [backs] + [swap(backs, offset) for offset in offsets[1:lines]]
    arrived, backs, gradients, pair = barrier((arrived, backs, gradients, pair))

    parts, tokens_own, *tokens_pair = hidden_parts(
        adapters, place, down_maps, pair, arrived
    )
    tokens_other = [swap(tokens_pair[0], pair_bit)]
    for slot in range(lines):
        if slot not in across:
            across[slot] = swap(gradients[slot], 1)
    backs = gather_step(jnp.concatenate(backs, axis=0), members)
    slices, columns, columns_pair = input_slices(
        adapters,
        place,
        gradients + [across[slot] for slot in range(lines)],
        backs,
        value_weight,
        pair,
        down_maps,
    )
    total, received, flip = parts, swap(parts[lines:], 1), 0
    for step in reversed(range(steps - 1)):
        sums = slot_sums(total, received, flip, [jnp.float32, jnp.bfloat16])
        total, flip = sums[0], 1 << step
        received = swap(sums[-1], offsets[flip])
    received, slices, columns_pair, backs, tokens_pair, tokens_other = barrier(
        (received, slices, columns_pair, backs, tokens_pair, tokens_other)
    )

    result = exchange_side(slices)
    hiddens = hidden_rows(adapters, place, ranks, total, received, flip, members)
    hiddens = gather_step(hiddens, members)
    columns_other = swap(columns_pair, pair_bit)
    backs_pair = swap(backs, pair_bit)
    tokens_other.append(swap(tokens_pair[1], pair_bit))
    hiddens_pair = swap(hiddens, pair_bit)
    up_gradient = up_gradients(
        adapters, place, ranks, columns, columns_other, hiddens, hiddens_pair, depth // devices
    )
    down_gradient = down_gradients(
        adapters, place, backs, backs_pair, tokens_own, tokens_other, num_adapters
    )
    up_gradient, down_gradient, result = barrier((up_gradient, down_gradient, result))
    return (join_columns(place, result), down_gradient, up_gradient)


def solution(mesh):
    in_specs = (
        P(("groups", "dp"), None),
        P(("groups", "dp"), None),
        P(None, "dp"),
        P(None, None, "dp"),
        P(None, "dp", None),
        P("groups"),
        P(),
    )
    out_specs = (P(("groups", "dp"), None), P("groups", None, "dp"), P("groups", "dp", None))
    return jax.shard_map(local, mesh=mesh, in_specs=in_specs, out_specs=out_specs, check_vma=False)
```

```python
import functools

import jax
import jax.numpy as jnp
from jax import lax
from jax.experimental import pallas as pl
from jax.experimental.pallas import tpu as pltpu
from jax.sharding import PartitionSpec as P

adapter_alpha = 32.0
vmem_limit = 48 * 1024 * 1024
pair_bit = 2
line_bit = 4


def line_offset(slot, members):
    bits = members.bit_length() - 1
    order = 0
    for bit in range(bits):
        order |= ((slot >> bit) & 1) << (bits - 1 - bit)
    return ((order // 2) * line_bit) | (order % 2)


def side_of(place):
    return place % line_bit // pair_bit


def side_index(place, members):
    lines = members // 2
    return place % pair_bit * lines + place // line_bit


def side_place(index, side, members):
    core, line = divmod(index, members // 2)
    return line * line_bit + side * pair_bit + core


def params():
    return pltpu.CompilerParams(vmem_limit_bytes=vmem_limit)


def whole(shape):
    return pl.BlockSpec(shape, lambda *_: (0,) * len(shape))


def picked(maps, flip):
    return pl.BlockSpec(
        (1,) + maps.shape[1:], lambda i, adapters, place, *_: (adapters[place[0] ^ flip], 0, 0)
    )


def call(kernel, name, prefetch, operands, in_specs, out_shapes, scratch=(), grid=(1,), out_specs=None):
    if out_specs is None:
        out_specs = [whole(shape.shape) for shape in out_shapes]
    return pl.pallas_call(
        kernel,
        out_shape=out_shapes,
        grid_spec=pltpu.PrefetchScalarGridSpec(
            num_scalar_prefetch=len(prefetch),
            grid=grid,
            in_specs=in_specs,
            out_specs=out_specs,
            scratch_shapes=list(scratch),
        ),
        compiler_params=params(),
        name=name,
    )(*prefetch, *operands)


def run(copies):
    for copy in copies:
        copy.start()
    for copy in copies:
        copy.wait()


def copy_call(kernel, name, prefetch, operands, out_shapes, copies):
    return pl.pallas_call(
        kernel,
        out_shape=out_shapes,
        grid_spec=pltpu.PrefetchScalarGridSpec(
            num_scalar_prefetch=len(prefetch),
            grid=(1,),
            in_specs=[pl.BlockSpec(memory_space=pl.ANY)] * len(operands),
            out_specs=[whole(shape.shape) for shape in out_shapes],
            scratch_shapes=[pltpu.SemaphoreType.DMA((copies,))],
        ),
        compiler_params=params(),
        name=name,
    )(*prefetch, *operands)


weight_cuts = 4


def pair_kernel(adapters, place, weight, down_maps, out, sems):
    extent = down_maps.shape[1]
    depth = weight.shape[0]
    members = (out.shape[0] - depth) // extent
    copies = []
    for slot in range(members):
        block = place[0] ^ line_offset(slot, members) ^ pair_bit
        copies.append((down_maps.at[adapters[block]], slot * extent, extent))
    cut = depth // weight_cuts
    for at in range(0, depth, cut):
        copies.append((weight.at[pl.ds(at, cut)], members * extent + at, cut))
    run(
        [
            pltpu.make_async_copy(source, out.at[pl.ds(at, rows)], sems.at[number])
            for number, (source, at, rows) in enumerate(copies)
        ]
    )


def for_pair(adapters, place, weight, down_maps, members):
    extent, width = down_maps.shape[1:]
    shape = jax.ShapeDtypeStruct((members * extent + weight.shape[0], width), weight.dtype)
    return copy_call(
        pair_kernel,
        "for_pair",
        (adapters, place),
        (weight, down_maps),
        [shape],
        members + weight_cuts,
    )[0]


def gather_up_kernel(adapters, up_maps, out, sems):
    run(
        [
            pltpu.make_async_copy(up_maps.at[adapters[block]], out.at[block], sems.at[block])
            for block in range(out.shape[0])
        ]
    )


def gather_up(adapters, up_maps):
    shape = jax.ShapeDtypeStruct((adapters.shape[0],) + up_maps.shape[1:], up_maps.dtype)
    return copy_call(
        gather_up_kernel, "gather_up", (adapters,), (up_maps,), [shape], adapters.shape[0]
    )[0]


def pack_kernel(place, tokens, out, sems):
    members, _, _, width = out.shape
    copies = []
    for index in range(members):
        for half in range(2):
            column = side_place(index, side_of(place[0]) ^ half, members) * width
            copies.append(
                pltpu.make_async_copy(
                    tokens.at[:, pl.ds(pl.multiple_of(column, width), width)],
                    out.at[index, half],
                    sems.at[2 * index + half],
                )
            )
    run(copies)


def pack_tokens(place, tokens, members, width):
    shape = jax.ShapeDtypeStruct((members, 2, tokens.shape[0], width), tokens.dtype)
    return copy_call(pack_kernel, "pack_tokens", (place,), (tokens,), [shape], 2 * members)[0]


def rank_row(ranks, adapter, extent):
    rank = jnp.full((1, extent), ranks[adapter], jnp.int32)
    alive = (lax.broadcasted_iota(jnp.int32, (1, extent), 1) < rank).astype(jnp.float32)
    return alive, adapter_alpha / rank.astype(jnp.float32)


def back_kernel(adapters, place, ranks, gradient, up, out):
    alive, factor = rank_row(ranks, adapters[place[0]], up.shape[1])
    back = jnp.dot(gradient[...], up[...], preferred_element_type=jnp.float32)
    out[0] = (factor * back * alive).astype(out.dtype)


def back_rows(adapters, place, ranks, gradient, up):
    return call(
        back_kernel,
        "back_low",
        (adapters, place, ranks),
        (gradient, up),
        [whole(gradient.shape), whole(up.shape)],
        [jax.ShapeDtypeStruct((1, gradient.shape[0], up.shape[1]), jnp.bfloat16)],
    )[0]


def input_kernel(adapters, place, backs, pair, *refs):
    members, rows, _ = backs.shape
    gradients = [ref.at[0] for ref in refs[:members]]
    downs = refs[members : 2 * members]
    weight = refs[2 * members]
    out, *columns = refs[-3:]
    extent = downs[0].shape[1]
    lanes = columns[0].shape[2]
    value_width = gradients[0].shape[1] // (2 * members)
    some = min(4, members)
    for first in range(0, members, some):
        slots = range(first, first + some)
        lines = jnp.concatenate([gradients[slot][...] for slot in slots], axis=0)
        for half in range(2):
            right = weight[...] if half == 0 else pair[members * extent :]
            frozen = jnp.dot(lines, right, preferred_element_type=jnp.float32)
            for slot in slots:
                down = downs[slot][0] if half == 0 else pair[slot * extent : (slot + 1) * extent]
                index = side_index(place[0] ^ line_offset(slot, members), members)
                low = jnp.dot(backs[slot], down, preferred_element_type=jnp.float32)
                at = (slot - first) * rows
                out[index, half] = (frozen[at : at + rows] + low).astype(jnp.bfloat16)
    for side in range(2):
        column = (place[0] ^ (side * pair_bit)) * value_width // lanes * lanes
        for slot in range(members):
            columns[side][slot] = gradients[slot][:, pl.ds(pl.multiple_of(column, lanes), lanes)]


def input_slices(adapters, place, gradients, backs, weight, pair, down_maps):
    members, rows, _ = backs.shape
    width = weight.shape[1]
    lanes = max(128, gradients[0].shape[2] // (2 * members))
    shape = jax.ShapeDtypeStruct((members, 2, rows, width), jnp.bfloat16)
    columns = jax.ShapeDtypeStruct((members, rows, lanes), jnp.bfloat16)
    return call(
        input_kernel,
        "input_slices",
        (adapters, place),
        [backs, pair] + list(gradients) + [down_maps] * members + [weight],
        [whole(backs.shape), whole(pair.shape)]
        + [whole(gradient.shape) for gradient in gradients]
        + [picked(down_maps, line_offset(slot, members)) for slot in range(members)]
        + [whole(weight.shape)],
        [shape, columns, columns],
    )


def hidden_kernel(adapters, place, pair, tokens, *refs):
    parts, own, *others = refs[-4:]
    members = own.shape[0]
    downs = refs[:members]
    extent = downs[0].shape[1]
    across = (((1,), (1,)), ((), ()))
    for slot in range(members):
        index = side_index(place[0] ^ line_offset(slot, members), members)
        own[slot] = tokens[index, 0]
        others[slot // (members // 2)][slot % (members // 2)] = tokens[index, 1]
        parts[slot] = lax.dot_general(
            tokens[index, 0], downs[slot][0], across, preferred_element_type=jnp.float32
        ) + lax.dot_general(
            tokens[index, 1],
            pair[slot * extent : (slot + 1) * extent],
            across,
            preferred_element_type=jnp.float32,
        )


def hidden_parts(adapters, place, down_maps, pair, tokens):
    members, _, rows, width = tokens.shape
    extent = down_maps.shape[1]
    others = jax.ShapeDtypeStruct((members // 2, rows, width), tokens.dtype)
    return call(
        hidden_kernel,
        "hidden_parts",
        (adapters, place),
        [pair, tokens] + [down_maps] * members,
        [whole(pair.shape), whole(tokens.shape)]
        + [picked(down_maps, line_offset(slot, members)) for slot in range(members)],
        [
            jax.ShapeDtypeStruct((members, rows, extent), jnp.float32),
            jax.ShapeDtypeStruct((members, rows, width), tokens.dtype),
            others,
            others,
        ],
    )


def sum_kernel(total, received, *outs, flip):
    for slot in range(outs[0].shape[0]):
        value = total[slot] + received[slot ^ flip].astype(jnp.float32)
        for out in outs:
            out[slot] = value.astype(out.dtype)


def slot_sums(total, received, flip, types):
    shape = received.shape
    return call(
        functools.partial(sum_kernel, flip=flip),
        "slot_sums",
        (),
        (total, received),
        [whole(shape)] * 2,
        [jax.ShapeDtypeStruct(shape, kind) for kind in types],
    )


def hidden_low_kernel(adapters, place, ranks, total, received, out, *, flip, members):
    for slot in range(out.shape[0]):
        block = place[0] ^ line_offset(slot, members)
        alive, _ = rank_row(ranks, adapters[block], out.shape[2])
        value = total[slot] + received[slot ^ flip].astype(jnp.float32)
        out[slot] = (value * alive).astype(out.dtype)


def hidden_rows(adapters, place, ranks, total, received, flip, members):
    return call(
        functools.partial(hidden_low_kernel, flip=flip, members=members),
        "hidden_low",
        (adapters, place, ranks),
        (total, received),
        [whole(total.shape)] * 2,
        [jax.ShapeDtypeStruct(total.shape, jnp.bfloat16)],
    )[0]


def join_kernel(place, source, out, sems):
    members, _, _, width = source.shape
    copies = []
    for index in range(members):
        for half in range(2):
            column = side_place(index, side_of(place[0]) ^ half, members) * width
            copies.append(
                pltpu.make_async_copy(
                    source.at[index, half],
                    out.at[:, pl.ds(pl.multiple_of(column, width), width)],
                    sems.at[2 * index + half],
                )
            )
    run(copies)


def join_columns(place, source):
    members, _, rows, width = source.shape
    return pl.pallas_call(
        join_kernel,
        out_shape=jax.ShapeDtypeStruct((rows, 2 * members * width), source.dtype),
        grid_spec=pltpu.PrefetchScalarGridSpec(
            num_scalar_prefetch=1,
            grid=(1,),
            in_specs=[whole(source.shape)],
            out_specs=pl.BlockSpec(memory_space=pl.ANY),
            scratch_shapes=[pltpu.SemaphoreType.DMA((2 * members,))],
        ),
        compiler_params=params(),
        name="join_columns",
    )(place, source)


def list_members(adapters, place, members, head, following):
    def clear(adapter, carry):
        head[adapter] = -1
        return carry

    lax.fori_loop(0, head.shape[0], clear, 0)
    for entry in reversed(range(2 * members)):
        side, own = divmod(entry, members)
        adapter = adapters[place[0] ^ line_offset(own, members) ^ (side * pair_bit)]
        following[entry] = head[adapter]
        head[adapter] = entry


def write_sums(head, following, products, ready, zero, out, sems, finish):
    num_adapters = out.shape[0]
    zero[...] = jnp.zeros_like(zero)

    def write(adapter, carry):
        first = head[adapter]

        @pl.when(first < 0)
        def _():
            pltpu.make_async_copy(zero, out.at[adapter], sems.at[adapter]).start()

        @pl.when(first >= 0)
        def _():
            def more(entry):
                products[first] += products[entry]
                return following[entry]

            lax.while_loop(lambda entry: entry >= 0, more, following[first])
            ready[first] = finish(adapter, products[first]).astype(out.dtype)
            pltpu.make_async_copy(ready.at[first], out.at[adapter], sems.at[adapter]).start()

        return carry

    lax.fori_loop(0, num_adapters, write, 0)

    def wait(adapter, carry):
        pltpu.make_async_copy(zero, out.at[adapter], sems.at[adapter]).wait()
        return carry

    lax.fori_loop(0, num_adapters, wait, 0)


def by_rows(left, right):
    return lax.dot_general(
        left, right, (((0,), (0,)), ((), ())), preferred_element_type=jnp.float32
    )


def sums_call(kernel, name, prefetch, operands, num_adapters, entries, product, scratch=()):
    return pl.pallas_call(
        kernel,
        out_shape=jax.ShapeDtypeStruct((num_adapters,) + product, jnp.bfloat16),
        grid_spec=pltpu.PrefetchScalarGridSpec(
            num_scalar_prefetch=len(prefetch),
            grid=(1,),
            in_specs=[whole(operand.shape) for operand in operands],
            out_specs=pl.BlockSpec(memory_space=pltpu.HBM),
            scratch_shapes=[
                pltpu.SMEM((num_adapters,), jnp.int32),
                pltpu.SMEM((entries,), jnp.int32),
                pltpu.VMEM((entries,) + product, jnp.float32),
                pltpu.VMEM((entries,) + product, jnp.bfloat16),
                pltpu.VMEM(product, jnp.bfloat16),
                pltpu.SemaphoreType.DMA((num_adapters,)),
                *scratch,
            ],
        ),
        compiler_params=params(),
        name=name,
    )(*prefetch, *operands)


def down_gradient_kernel(
    adapters,
    place,
    backs,
    backs_pair,
    own,
    other_first,
    other_second,
    out,
    head,
    following,
    products,
    ready,
    zero,
    sems,
):
    members = own.shape[0]
    others = (other_first, other_second)
    list_members(adapters, place, members, head, following)
    for slot in range(members):
        products[slot] = by_rows(backs[slot], own[slot])
        core, line = divmod(slot, members // 2)
        products[members + slot] = by_rows(backs_pair[slot], others[core][line])
    write_sums(
        head, following, products, ready, zero, out, sems, lambda adapter, total: total
    )


def down_gradients(adapters, place, backs, backs_pair, own, others, num_adapters):
    members, _, width = own.shape
    return sums_call(
        down_gradient_kernel,
        "down_gradients",
        (adapters, place),
        (backs, backs_pair, own, *others),
        num_adapters,
        2 * members,
        (backs.shape[2], width),
    )


def up_gradient_kernel(
    adapters,
    place,
    ranks,
    gradients,
    gradients_pair,
    hiddens,
    hiddens_pair,
    out,
    head,
    following,
    products,
    ready,
    zero,
    sems,
    lines,
):
    members, _, lanes = gradients.shape
    width, extent = out.shape[1:]
    list_members(adapters, place, members, head, following)
    inside = pl.multiple_of(lax.rem(place[0], lanes // width) * width, width)
    for slot in range(members):
        lines[slot] = by_rows(gradients[slot], hiddens[slot])
        lines[members + slot] = by_rows(gradients_pair[slot], hiddens_pair[slot])
    for entry in range(2 * members):
        products[entry] = lines[entry, pl.ds(inside, width), :]

    def finish(adapter, total):
        _, factor = rank_row(ranks, adapter, extent)
        return factor * total

    write_sums(head, following, products, ready, zero, out, sems, finish)


def up_gradients(adapters, place, ranks, gradients, gradients_pair, hiddens, hiddens_pair, width):
    members, _, lanes = gradients.shape
    extent = hiddens.shape[2]
    return sums_call(
        up_gradient_kernel,
        "up_gradients",
        (adapters, place, ranks),
        (gradients, gradients_pair, hiddens, hiddens_pair),
        ranks.shape[0],
        2 * members,
        (width, extent),
        [pltpu.VMEM((2 * members, lanes, extent), jnp.float32)],
    )


def exchange(pieces):
    return lax.all_to_all(pieces, "dp", split_axis=0, concat_axis=0, tiled=True)


def exchange_side(pieces):
    members = pieces.shape[0]
    groups = [[side_place(index, side, members) for index in range(members)] for side in range(2)]
    return lax.all_to_all(
        pieces, "dp", split_axis=0, concat_axis=0, axis_index_groups=groups, tiled=True
    )


def swap(array, flip):
    devices = lax.axis_size("dp")
    return lax.ppermute(array, "dp", [(i, i ^ flip) for i in range(devices)])


def tie(first, second):
    return lax.optimization_barrier((first, second))


def gather_step(held, members):
    arrived = swap(held, line_offset(held.shape[0], members))
    return jnp.concatenate([held, arrived], axis=0)


def local(tokens, output_gradient, value_weight, down_maps, up_maps, adapter_per_block, ranks):
    devices = lax.axis_size("dp")
    members = devices // 2
    lines = members // 2
    steps = members.bit_length() - 1
    num_adapters, extent, width = down_maps.shape
    rows, depth = output_gradient.shape
    place = lax.axis_index("dp").astype(jnp.int32).reshape(1)
    adapters = adapter_per_block
    offsets = [line_offset(slot, members) for slot in range(members)]
    barrier = lax.optimization_barrier

    own_gradient = output_gradient.reshape(1, rows, depth)
    gradients = [own_gradient] + [None] * (lines - 1)
    for step in range(steps - 1):
        gradients[1 << step] = swap(own_gradient, offsets[1 << step])
    own_up = exchange(gather_up(adapters, up_maps)).reshape(depth, extent)
    packs = pack_tokens(place, tokens, members, width)
    firsts = [1 << step for step in range(steps - 1)]
    across = {slot: swap(gradients[slot], 1) for slot in [0] + firsts}
    held, crossed, own_up, packs, adapters = barrier(
        ([gradients[slot] for slot in firsts], across, own_up, packs, adapters)
    )
    across = dict(crossed)
    for slot, block in zip(firsts, held):
        gradients[slot] = block

    arrived = exchange_side(packs)
    pair = swap(for_pair(adapters, place, value_weight, down_maps, members), pair_bit)
    for step in range(1, steps - 1):
        for slot in range(1, 1 << step):
            gradients[slot + (1 << step)] = swap(gradients[slot], offsets[1 << step])
    backs = back_rows(adapters, place, ranks, output_gradient, own_up)
    backs = [backs] + [swap(backs, offset) for offset in offsets[1:lines]]
    arrived, backs, gradients, pair = barrier((arrived, backs, gradients, pair))

    parts, tokens_own, *tokens_pair = hidden_parts(
        adapters, place, down_maps, pair, arrived
    )
    tokens_other = [swap(tokens_pair[0], pair_bit)]
    for slot in range(lines):
        if slot not in across:
            across[slot] = swap(gradients[slot], 1)
    backs = gather_step(jnp.concatenate(backs, axis=0), members)
    slices, columns, columns_pair = input_slices(
        adapters,
        place,
        gradients + [across[slot] for slot in range(lines)],
        backs,
        value_weight,
        pair,
        down_maps,
    )
    total, received, flip = parts, swap(parts[lines:], 1), 0
    for step in reversed(range(steps - 1)):
        sums = slot_sums(total, received, flip, [jnp.float32, jnp.bfloat16])
        total, flip = sums[0], 1 << step
        received = swap(sums[-1], offsets[flip])
    received, slices, columns_pair, backs, tokens_pair, tokens_other = barrier(
        (received, slices, columns_pair, backs, tokens_pair, tokens_other)
    )

    result = exchange_side(slices)
    hiddens = hidden_rows(adapters, place, ranks, total, received, flip, members)
    hiddens = gather_step(hiddens, members)
    columns_other = swap(columns_pair, pair_bit)
    backs_pair = swap(backs, pair_bit)
    tokens_other.append(swap(tokens_pair[1], pair_bit))
    hiddens_pair = swap(hiddens, pair_bit)
    up_gradient = up_gradients(
        adapters, place, ranks, columns, columns_other, hiddens, hiddens_pair, depth // devices
    )
    down_gradient = down_gradients(
        adapters, place, backs, backs_pair, tokens_own, tokens_other, num_adapters
    )
    up_gradient, down_gradient, result = barrier((up_gradient, down_gradient, result))
    return (join_columns(place, result), down_gradient, up_gradient)


def solution(mesh):
    in_specs = (
        P(("groups", "dp"), None),
        P(("groups", "dp"), None),
        P(None, "dp"),
        P(None, None, "dp"),
        P(None, "dp", None),
        P("groups"),
        P(),
    )
    out_specs = (P(("groups", "dp"), None), P("groups", None, "dp"), P("groups", "dp", None))
    return jax.shard_map(local, mesh=mesh, in_specs=in_specs, out_specs=out_specs, check_vma=False)
```

```python
import functools

import jax
import jax.numpy as jnp
from jax import lax
from jax.experimental import pallas as pl
from jax.experimental.pallas import tpu as pltpu
from jax.sharding import PartitionSpec as P

adapter_alpha = 32.0
vmem_limit = 48 * 1024 * 1024
pair_bit = 2
line_bit = 4


def line_offset(slot, members):
    bits = members.bit_length() - 1
    order = 0
    for bit in range(bits):
        order |= ((slot >> bit) & 1) << (bits - 1 - bit)
    return ((order // 2) * line_bit) | (order % 2)


def side_of(place):
    return place % line_bit // pair_bit


def side_index(place, members):
    lines = members // 2
    line = place // line_bit
    order = line
    for shift in range(1, lines.bit_length() - 1):
        order = order ^ (line >> shift)
    return place % pair_bit * lines + order


def side_place(index, side, members):
    core, line = divmod(index, members // 2)
    return (line ^ (line >> 1)) * line_bit + side * pair_bit + core


def params():
    return pltpu.CompilerParams(vmem_limit_bytes=vmem_limit)


def whole(shape):
    return pl.BlockSpec(shape, lambda *_: (0,) * len(shape))


def picked(maps, flip):
    return pl.BlockSpec(
        (1,) + maps.shape[1:], lambda i, adapters, place, *_: (adapters[place[0] ^ flip], 0, 0)
    )


def call(kernel, name, prefetch, operands, in_specs, out_shapes, scratch=(), grid=(1,), out_specs=None):
    if out_specs is None:
        out_specs = [whole(shape.shape) for shape in out_shapes]
    return pl.pallas_call(
        kernel,
        out_shape=out_shapes,
        grid_spec=pltpu.PrefetchScalarGridSpec(
            num_scalar_prefetch=len(prefetch),
            grid=grid,
            in_specs=in_specs,
            out_specs=out_specs,
            scratch_shapes=list(scratch),
        ),
        compiler_params=params(),
        name=name,
    )(*prefetch, *operands)


def run(copies):
    for copy in copies:
        copy.start()
    for copy in copies:
        copy.wait()


def copy_call(kernel, name, prefetch, operands, out_shapes, copies):
    return pl.pallas_call(
        kernel,
        out_shape=out_shapes,
        grid_spec=pltpu.PrefetchScalarGridSpec(
            num_scalar_prefetch=len(prefetch),
            grid=(1,),
            in_specs=[pl.BlockSpec(memory_space=pl.ANY)] * len(operands),
            out_specs=[whole(shape.shape) for shape in out_shapes],
            scratch_shapes=[pltpu.SemaphoreType.DMA((copies,))],
        ),
        compiler_params=params(),
        name=name,
    )(*prefetch, *operands)


weight_cuts = 4


def pair_kernel(adapters, place, weight, down_maps, out, sems):
    extent = down_maps.shape[1]
    depth = weight.shape[0]
    members = (out.shape[0] - depth) // extent
    copies = []
    for slot in range(members):
        block = place[0] ^ line_offset(slot, members) ^ pair_bit
        copies.append((down_maps.at[adapters[block]], slot * extent, extent))
    cut = depth // weight_cuts
    for at in range(0, depth, cut):
        copies.append((weight.at[pl.ds(at, cut)], members * extent + at, cut))
    run(
        [
            pltpu.make_async_copy(source, out.at[pl.ds(at, rows)], sems.at[number])
            for number, (source, at, rows) in enumerate(copies)
        ]
    )


def for_pair(adapters, place, weight, down_maps, members):
    extent, width = down_maps.shape[1:]
    shape = jax.ShapeDtypeStruct((members * extent + weight.shape[0], width), weight.dtype)
    return copy_call(
        pair_kernel,
        "for_pair",
        (adapters, place),
        (weight, down_maps),
        [shape],
        members + weight_cuts,
    )[0]


def gather_up_kernel(adapters, up_maps, out, sems):
    run(
        [
            pltpu.make_async_copy(up_maps.at[adapters[block]], out.at[block], sems.at[block])
            for block in range(out.shape[0])
        ]
    )


def gather_up(adapters, up_maps):
    shape = jax.ShapeDtypeStruct((adapters.shape[0],) + up_maps.shape[1:], up_maps.dtype)
    return copy_call(
        gather_up_kernel, "gather_up", (adapters,), (up_maps,), [shape], adapters.shape[0]
    )[0]


def pack_kernel(place, tokens, out, sems):
    members, _, _, width = out.shape
    copies = []
    for index in range(members):
        for half in range(2):
            column = side_place(index, side_of(place[0]) ^ half, members) * width
            copies.append(
                pltpu.make_async_copy(
                    tokens.at[:, pl.ds(pl.multiple_of(column, width), width)],
                    out.at[index, half],
                    sems.at[2 * index + half],
                )
            )
    run(copies)


def pack_tokens(place, tokens, members, width):
    shape = jax.ShapeDtypeStruct((members, 2, tokens.shape[0], width), tokens.dtype)
    return copy_call(pack_kernel, "pack_tokens", (place,), (tokens,), [shape], 2 * members)[0]


def rank_row(ranks, adapter, extent):
    rank = jnp.full((1, extent), ranks[adapter], jnp.int32)
    alive = (lax.broadcasted_iota(jnp.int32, (1, extent), 1) < rank).astype(jnp.float32)
    return alive, adapter_alpha / rank.astype(jnp.float32)


def back_kernel(adapters, place, ranks, gradient, up, out):
    alive, factor = rank_row(ranks, adapters[place[0]], up.shape[1])
    back = jnp.dot(gradient[...], up[...], preferred_element_type=jnp.float32)
    out[0] = (factor * back * alive).astype(out.dtype)


def back_rows(adapters, place, ranks, gradient, up):
    return call(
        back_kernel,
        "back_low",
        (adapters, place, ranks),
        (gradient, up),
        [whole(gradient.shape), whole(up.shape)],
        [jax.ShapeDtypeStruct((1, gradient.shape[0], up.shape[1]), jnp.bfloat16)],
    )[0]


def input_kernel(adapters, place, backs, pair, *refs):
    members, rows, _ = backs.shape
    gradients = [ref.at[0] for ref in refs[:members]]
    downs = refs[members : 2 * members]
    weight = refs[2 * members]
    out, *columns = refs[-3:]
    extent = downs[0].shape[1]
    lanes = columns[0].shape[2]
    value_width = gradients[0].shape[1] // (2 * members)
    some = min(4, members)
    for first in range(0, members, some):
        slots = range(first, first + some)
        lines = jnp.concatenate([gradients[slot][...] for slot in slots], axis=0)
        for half in range(2):
            right = weight[...] if half == 0 else pair[members * extent :]
            frozen = jnp.dot(lines, right, preferred_element_type=jnp.float32)
            for slot in slots:
                down = downs[slot][0] if half == 0 else pair[slot * extent : (slot + 1) * extent]
                index = side_index(place[0] ^ line_offset(slot, members), members)
                low = jnp.dot(backs[slot], down, preferred_element_type=jnp.float32)
                at = (slot - first) * rows
                out[index, half] = (frozen[at : at + rows] + low).astype(jnp.bfloat16)
    for side in range(2):
        column = (place[0] ^ (side * pair_bit)) * value_width // lanes * lanes
        for slot in range(members):
            columns[side][slot] = gradients[slot][:, pl.ds(pl.multiple_of(column, lanes), lanes)]


def input_slices(adapters, place, gradients, backs, weight, pair, down_maps):
    members, rows, _ = backs.shape
    width = weight.shape[1]
    lanes = max(128, gradients[0].shape[2] // (2 * members))
    shape = jax.ShapeDtypeStruct((members, 2, rows, width), jnp.bfloat16)
    columns = jax.ShapeDtypeStruct((members, rows, lanes), jnp.bfloat16)
    return call(
        input_kernel,
        "input_slices",
        (adapters, place),
        [backs, pair] + list(gradients) + [down_maps] * members + [weight],
        [whole(backs.shape), whole(pair.shape)]
        + [whole(gradient.shape) for gradient in gradients]
        + [picked(down_maps, line_offset(slot, members)) for slot in range(members)]
        + [whole(weight.shape)],
        [shape, columns, columns],
    )


def hidden_kernel(adapters, place, pair, tokens, *refs):
    parts, own, *others = refs[-4:]
    members = own.shape[0]
    downs = refs[:members]
    extent = downs[0].shape[1]
    across = (((1,), (1,)), ((), ()))
    for slot in range(members):
        index = side_index(place[0] ^ line_offset(slot, members), members)
        own[slot] = tokens[index, 0]
        others[slot // (members // 2)][slot % (members // 2)] = tokens[index, 1]
        parts[slot] = lax.dot_general(
            tokens[index, 0], downs[slot][0], across, preferred_element_type=jnp.float32
        ) + lax.dot_general(
            tokens[index, 1],
            pair[slot * extent : (slot + 1) * extent],
            across,
            preferred_element_type=jnp.float32,
        )


def hidden_parts(adapters, place, down_maps, pair, tokens):
    members, _, rows, width = tokens.shape
    extent = down_maps.shape[1]
    others = jax.ShapeDtypeStruct((members // 2, rows, width), tokens.dtype)
    return call(
        hidden_kernel,
        "hidden_parts",
        (adapters, place),
        [pair, tokens] + [down_maps] * members,
        [whole(pair.shape), whole(tokens.shape)]
        + [picked(down_maps, line_offset(slot, members)) for slot in range(members)],
        [
            jax.ShapeDtypeStruct((members, rows, extent), jnp.float32),
            jax.ShapeDtypeStruct((members, rows, width), tokens.dtype),
            others,
            others,
        ],
    )


def sum_kernel(total, received, *outs, flip):
    for slot in range(outs[0].shape[0]):
        value = total[slot] + received[slot ^ flip].astype(jnp.float32)
        for out in outs:
            out[slot] = value.astype(out.dtype)


def slot_sums(total, received, flip, types):
    shape = received.shape
    return call(
        functools.partial(sum_kernel, flip=flip),
        "slot_sums",
        (),
        (total, received),
        [whole(shape)] * 2,
        [jax.ShapeDtypeStruct(shape, kind) for kind in types],
    )


def hidden_low_kernel(adapters, place, ranks, total, received, out, *, flip, members):
    for slot in range(out.shape[0]):
        block = place[0] ^ line_offset(slot, members)
        alive, _ = rank_row(ranks, adapters[block], out.shape[2])
        value = total[slot] + received[slot ^ flip].astype(jnp.float32)
        out[slot] = (value * alive).astype(out.dtype)


def hidden_rows(adapters, place, ranks, total, received, flip, members):
    return call(
        functools.partial(hidden_low_kernel, flip=flip, members=members),
        "hidden_low",
        (adapters, place, ranks),
        (total, received),
        [whole(total.shape)] * 2,
        [jax.ShapeDtypeStruct(total.shape, jnp.bfloat16)],
    )[0]


def join_kernel(place, source, out, sems):
    members, _, _, width = source.shape
    copies = []
    for index in range(members):
        for half in range(2):
            column = side_place(index, side_of(place[0]) ^ half, members) * width
            copies.append(
                pltpu.make_async_copy(
                    source.at[index, half],
                    out.at[:, pl.ds(pl.multiple_of(column, width), width)],
                    sems.at[2 * index + half],
                )
            )
    run(copies)


def join_columns(place, source):
    members, _, rows, width = source.shape
    return pl.pallas_call(
        join_kernel,
        out_shape=jax.ShapeDtypeStruct((rows, 2 * members * width), source.dtype),
        grid_spec=pltpu.PrefetchScalarGridSpec(
            num_scalar_prefetch=1,
            grid=(1,),
            in_specs=[whole(source.shape)],
            out_specs=pl.BlockSpec(memory_space=pl.ANY),
            scratch_shapes=[pltpu.SemaphoreType.DMA((2 * members,))],
        ),
        compiler_params=params(),
        name="join_columns",
    )(place, source)


def list_members(adapters, place, members, head, following):
    def clear(adapter, carry):
        head[adapter] = -1
        return carry

    lax.fori_loop(0, head.shape[0], clear, 0)
    for entry in reversed(range(2 * members)):
        side, own = divmod(entry, members)
        adapter = adapters[place[0] ^ line_offset(own, members) ^ (side * pair_bit)]
        following[entry] = head[adapter]
        head[adapter] = entry


def write_sums(head, following, products, ready, zero, out, sems, finish):
    num_adapters = out.shape[0]
    zero[...] = jnp.zeros_like(zero)

    def write(adapter, carry):
        first = head[adapter]

        @pl.when(first < 0)
        def _():
            pltpu.make_async_copy(zero, out.at[adapter], sems.at[adapter]).start()

        @pl.when(first >= 0)
        def _():
            def more(entry):
                products[first] += products[entry]
                return following[entry]

            lax.while_loop(lambda entry: entry >= 0, more, following[first])
            ready[first] = finish(adapter, products[first]).astype(out.dtype)
            pltpu.make_async_copy(ready.at[first], out.at[adapter], sems.at[adapter]).start()

        return carry

    lax.fori_loop(0, num_adapters, write, 0)

    def wait(adapter, carry):
        pltpu.make_async_copy(zero, out.at[adapter], sems.at[adapter]).wait()
        return carry

    lax.fori_loop(0, num_adapters, wait, 0)


def by_rows(left, right):
    return lax.dot_general(
        left, right, (((0,), (0,)), ((), ())), preferred_element_type=jnp.float32
    )


def sums_call(kernel, name, prefetch, operands, num_adapters, entries, product, scratch=()):
    return pl.pallas_call(
        kernel,
        out_shape=jax.ShapeDtypeStruct((num_adapters,) + product, jnp.bfloat16),
        grid_spec=pltpu.PrefetchScalarGridSpec(
            num_scalar_prefetch=len(prefetch),
            grid=(1,),
            in_specs=[whole(operand.shape) for operand in operands],
            out_specs=pl.BlockSpec(memory_space=pltpu.HBM),
            scratch_shapes=[
                pltpu.SMEM((num_adapters,), jnp.int32),
                pltpu.SMEM((entries,), jnp.int32),
                pltpu.VMEM((entries,) + product, jnp.float32),
                pltpu.VMEM((entries,) + product, jnp.bfloat16),
                pltpu.VMEM(product, jnp.bfloat16),
                pltpu.SemaphoreType.DMA((num_adapters,)),
                *scratch,
            ],
        ),
        compiler_params=params(),
        name=name,
    )(*prefetch, *operands)


def down_gradient_kernel(
    adapters,
    place,
    backs,
    backs_pair,
    own,
    other_first,
    other_second,
    out,
    head,
    following,
    products,
    ready,
    zero,
    sems,
):
    members = own.shape[0]
    others = (other_first, other_second)
    list_members(adapters, place, members, head, following)
    for slot in range(members):
        products[slot] = by_rows(backs[slot], own[slot])
        core, line = divmod(slot, members // 2)
        products[members + slot] = by_rows(backs_pair[slot], others[core][line])
    write_sums(
        head, following, products, ready, zero, out, sems, lambda adapter, total: total
    )


def down_gradients(adapters, place, backs, backs_pair, own, others, num_adapters):
    members, _, width = own.shape
    return sums_call(
        down_gradient_kernel,
        "down_gradients",
        (adapters, place),
        (backs, backs_pair, own, *others),
        num_adapters,
        2 * members,
        (backs.shape[2], width),
    )


def up_gradient_kernel(
    adapters,
    place,
    ranks,
    gradients,
    gradients_pair,
    hiddens,
    hiddens_pair,
    out,
    head,
    following,
    products,
    ready,
    zero,
    sems,
    lines,
):
    members, _, lanes = gradients.shape
    width, extent = out.shape[1:]
    list_members(adapters, place, members, head, following)
    inside = pl.multiple_of(lax.rem(place[0], lanes // width) * width, width)
    for slot in range(members):
        lines[slot] = by_rows(gradients[slot], hiddens[slot])
        lines[members + slot] = by_rows(gradients_pair[slot], hiddens_pair[slot])
    for entry in range(2 * members):
        products[entry] = lines[entry, pl.ds(inside, width), :]

    def finish(adapter, total):
        _, factor = rank_row(ranks, adapter, extent)
        return factor * total

    write_sums(head, following, products, ready, zero, out, sems, finish)


def up_gradients(adapters, place, ranks, gradients, gradients_pair, hiddens, hiddens_pair, width):
    members, _, lanes = gradients.shape
    extent = hiddens.shape[2]
    return sums_call(
        up_gradient_kernel,
        "up_gradients",
        (adapters, place, ranks),
        (gradients, gradients_pair, hiddens, hiddens_pair),
        ranks.shape[0],
        2 * members,
        (width, extent),
        [pltpu.VMEM((2 * members, lanes, extent), jnp.float32)],
    )


def exchange(pieces):
    return lax.all_to_all(pieces, "dp", split_axis=0, concat_axis=0, tiled=True)


def exchange_side(pieces):
    members = pieces.shape[0]
    groups = [[side_place(index, side, members) for index in range(members)] for side in range(2)]
    return lax.all_to_all(
        pieces, "dp", split_axis=0, concat_axis=0, axis_index_groups=groups, tiled=True
    )


def swap(array, flip):
    devices = lax.axis_size("dp")
    return lax.ppermute(array, "dp", [(i, i ^ flip) for i in range(devices)])


def tie(first, second):
    return lax.optimization_barrier((first, second))


def gather_step(held, members):
    arrived = swap(held, line_offset(held.shape[0], members))
    return jnp.concatenate([held, arrived], axis=0)


def local(tokens, output_gradient, value_weight, down_maps, up_maps, adapter_per_block, ranks):
    devices = lax.axis_size("dp")
    members = devices // 2
    lines = members // 2
    steps = members.bit_length() - 1
    num_adapters, extent, width = down_maps.shape
    rows, depth = output_gradient.shape
    place = lax.axis_index("dp").astype(jnp.int32).reshape(1)
    adapters = adapter_per_block
    offsets = [line_offset(slot, members) for slot in range(members)]
    barrier = lax.optimization_barrier

    own_gradient = output_gradient.reshape(1, rows, depth)
    gradients = [own_gradient] + [None] * (lines - 1)
    for step in range(steps - 1):
        gradients[1 << step] = swap(own_gradient, offsets[1 << step])
    own_up = exchange(gather_up(adapters, up_maps)).reshape(depth, extent)
    packs = pack_tokens(place, tokens, members, width)
    firsts = [1 << step for step in range(steps - 1)]
    across = {slot: swap(gradients[slot], 1) for slot in [0] + firsts}
    held, crossed, own_up, packs, adapters = barrier(
        ([gradients[slot] for slot in firsts], across, own_up, packs, adapters)
    )
    across = dict(crossed)
    for slot, block in zip(firsts, held):
        gradients[slot] = block

    arrived = exchange_side(packs)
    pair = swap(for_pair(adapters, place, value_weight, down_maps, members), pair_bit)
    for step in range(1, steps - 1):
        for slot in range(1, 1 << step):
            gradients[slot + (1 << step)] = swap(gradients[slot], offsets[1 << step])
    backs = back_rows(adapters, place, ranks, output_gradient, own_up)
    backs = [backs] + [swap(backs, offset) for offset in offsets[1:lines]]
    arrived, backs, gradients, pair = barrier((arrived, backs, gradients, pair))

    parts, tokens_own, *tokens_pair = hidden_parts(
        adapters, place, down_maps, pair, arrived
    )
    tokens_other = [swap(tokens_pair[0], pair_bit)]
    for slot in range(lines):
        if slot not in across:
            across[slot] = swap(gradients[slot], 1)
    backs = gather_step(jnp.concatenate(backs, axis=0), members)
    slices, columns, columns_pair = input_slices(
        adapters,
        place,
        gradients + [across[slot] for slot in range(lines)],
        backs,
        value_weight,
        pair,
        down_maps,
    )
    total, received, flip = parts, swap(parts[lines:], 1), 0
    for step in reversed(range(steps - 1)):
        sums = slot_sums(total, received, flip, [jnp.float32, jnp.bfloat16])
        total, flip = sums[0], 1 << step
        received = swap(sums[-1], offsets[flip])
    received, slices, columns_pair, backs, tokens_pair, tokens_other = barrier(
        (received, slices, columns_pair, backs, tokens_pair, tokens_other)
    )

    result = exchange_side(slices)
    hiddens = hidden_rows(adapters, place, ranks, total, received, flip, members)
    hiddens = gather_step(hiddens, members)
    columns_other = swap(columns_pair, pair_bit)
    backs_pair = swap(backs, pair_bit)
    tokens_other.append(swap(tokens_pair[1], pair_bit))
    hiddens_pair = swap(hiddens, pair_bit)
    up_gradient = up_gradients(
        adapters, place, ranks, columns, columns_other, hiddens, hiddens_pair, depth // devices
    )
    down_gradient = down_gradients(
        adapters, place, backs, backs_pair, tokens_own, tokens_other, num_adapters
    )
    up_gradient, down_gradient, result = barrier((up_gradient, down_gradient, result))
    return (join_columns(place, result), down_gradient, up_gradient)


def solution(mesh):
    in_specs = (
        P(("groups", "dp"), None),
        P(("groups", "dp"), None),
        P(None, "dp"),
        P(None, None, "dp"),
        P(None, "dp", None),
        P("groups"),
        P(),
    )
    out_specs = (P(("groups", "dp"), None), P("groups", None, "dp"), P("groups", "dp", None))
    return jax.shard_map(local, mesh=mesh, in_specs=in_specs, out_specs=out_specs, check_vma=False)
```
